32 devices in a mesh: dop: 8 (over z, y), rng: 4 (over x, core).
Axes of the slice: x: 2, y: 2, z: 4, core: 2. Of those that a mesh axis runs over, the one named last changes fastest.
Arguments:
- raw_echo: float32 [2, 512, 512, 128], P(None, 'dop', 'rng'), may hold values from -6 to 6
- replica: float32 [2, 64], replicated, may hold values from -0.5 to 0.5
- beam_weights: bfloat16 [2, 512, 192], replicated, may hold values from -0.1875 to 0.1875
- pivots: int32 [128, 192], replicated, may hold values from 0 to 191, each once within a row
- owner_counts: int32 [8], replicated, may hold values from 1 to 32, 128 in all
- train_gates: int32 [128, 256], P(None, 'rng'), may hold values from 0 to 511, as said below
Outputs:
- factor: float32 [256, 384, 384], P('dop', 'rng')
The draws below stay inside these ranges and needn't reach their ends.
Inputs may be any that keep to these rules, and one draw needn't show every extreme that they name: Owner o holds the run of owner_counts[o] consecutive Doppler bins that follows the bins of the owners below it; the counts sum to 128, and the largest is exactly 32 in every draw. `pivots`: each row is a permutation of 0 to 191. `train_gates`: in each row, columns r * 64 to (r + 1) * 64 - 1 hold distinct gates of range block r, that is of r * 128 to (r + 1) * 128 - 1.
All inputs are finite; a program needn't handle non-finite values.
Results may differ from the reference program's by a relative error of at most 0.005.
Values may be sent and summed in bfloat16 or wider, within the bound.
No kernel may reach another device: no remote copies, remote signals or barrier semaphores. Data moves between devices by JAX's collectives and lax.ppermute only.
A program may use at most 128 MiB of HBM per device.

```python
import math
import jax
import jax.numpy as jnp
import numpy as np
from jax import lax

CH = 512
PULSES = 128
DOF = 192
TAPS = 64
GATES_DEV = 128
GATES = 512
TRAIN_DEV = 64
MOST = 32
N_DOP = 8


def draw_train_gates(key, part):
    block_count = GATES // GATES_DEV
    key_list = jax.random.split(key, PULSES * block_count)

    def choose_gates(one_key):
        return jax.random.permutation(one_key, GATES_DEV)[:TRAIN_DEV].astype(jnp.int32)
    local_gates = jax.vmap(choose_gates)(key_list).reshape(PULSES, block_count, TRAIN_DEV)
    block_start = (jnp.arange(block_count, dtype=jnp.int32) * GATES_DEV)[None, :, None]
    return (local_gates + block_start).reshape(PULSES, block_count * TRAIN_DEV)


def block_scale(rng, extent, cuts, low, top_value):
    loudness = 1.0
    for position, parts in cuts:
        draws = jax.random.uniform(jax.random.fold_in(jax.random.fold_in(rng, 6), position), (parts,), jnp.float32, low / len(cuts), top_value / len(cuts))
        loudness = loudness * jnp.repeat(jnp.exp(draws), extent[position] // parts).reshape((-1,) + (1,) * (len(extent) - 1 - position))
    return loudness


def length_profile(count, total, most, slope):
    weights = [(1 << 20) // math.isqrt(standing ** slope) + 1 for standing in range(2, count + 1)]
    rest, given = total - most - (count - 1), [1] * (count - 1)
    while rest > 0:
        movable = [i for i in range(count - 1) if given[i] < most]
        mass, budget = sum([weights[i] for i in movable]), rest
        for i in movable:
            addition = min(most - given[i], max(1, budget * weights[i] // mass), rest)
            given[i] = given[i] + addition
            rest = rest - addition
    return np.array([most] + given)


def ragged_sizes(own_key, number_of, total, reach, skew):
    if number_of == 2:
        one = jax.random.randint(own_key, (), max(1, total - reach), min(reach, total - 1) + 1)
        return jnp.stack([one, total - one])
    lengths = jnp.asarray(length_profile(number_of, total, reach, skew), jnp.int32)
    twos = (number_of - 1) // 2
    donor, sink = lengths[1:1 + 2 * twos:2], lengths[2:2 + 2 * twos:2]
    margin = jnp.minimum(donor - 1, reach - sink)
    passed = jax.random.randint(jax.random.fold_in(own_key, 1), (twos,), 0, 1 << 20) % (margin + 1)
    lengths = lengths.at[1:1 + 2 * twos:2].set(donor - passed).at[2:2 + 2 * twos:2].set(sink + passed)
    return lengths[jax.random.permutation(jax.random.fold_in(own_key, 2), number_of)]


def noise(rng, dims, width, bound, cuts=(), kind=jnp.bfloat16):
    loudness = block_scale(rng, dims, cuts, -0.22, 0.18) if cuts else 1.0
    result = jax.random.normal(rng, dims, jnp.float32) * width * loudness
    return jnp.minimum(jnp.maximum(result, -bound), bound).astype(kind)


def setup_inputs(seed: int = 0) -> dict:
    splits = jax.random.split(jax.random.key(seed), 7)
    return {
        "raw_echo": noise(splits[0], (2, CH, GATES, PULSES), 1.0, 6.0, ((1, 8), (2, 4)), jnp.float32),
        "replica": noise(splits[1], (2, TAPS), (2 * TAPS) ** -0.5, 0.5, (), jnp.float32),
        "beam_weights": noise(splits[2], (2, CH, DOF), (2 * CH) ** -0.5, 0.1875),
        "pivots": jax.vmap(lambda own: jax.random.permutation(own, DOF))(jax.random.split(splits[3], PULSES)).reshape((PULSES, DOF)).astype(jnp.int32),
        "owner_counts": ragged_sizes(splits[4], N_DOP, PULSES, MOST, 2).astype(jnp.int32),
        "train_gates": draw_train_gates(jax.random.fold_in(splits[6], 71), 0),
    }


LOADING = 0.25

def complex_block(real_part, imag_part):
    upper_row = jnp.stack([real_part, imag_part])
    lower_row = jnp.stack([-imag_part, real_part])
    return jnp.stack([upper_row, lower_row])

def doppler_table(pulse_count):
    pulse_index = jnp.arange(pulse_count, dtype=jnp.int32)
    phase_index = pulse_index[:, None] * pulse_index[None, :] % pulse_count
    angle_table = phase_index.astype(jnp.float32) * (2.0 * math.pi / pulse_count)
    norm_scale = 1.0 / math.sqrt(pulse_count)
    return complex_block(jnp.cos(angle_table) * norm_scale, jnp.sin(angle_table) * norm_scale)

def factor_matrix(real_part, imag_part, pivot_row, count_rows):
    real_part = real_part / count_rows
    imag_part = imag_part / count_rows
    real_pivot = jnp.take(jnp.take(real_part, pivot_row, axis=0), pivot_row, axis=1)
    imag_pivot = jnp.take(jnp.take(imag_part, pivot_row, axis=0), pivot_row, axis=1)
    upper_half = jnp.concatenate([real_pivot, -imag_pivot], axis=1)
    lower_half = jnp.concatenate([imag_pivot, real_pivot], axis=1)
    matrix = jnp.concatenate([upper_half, lower_half], axis=0)
    matrix = matrix + LOADING * jnp.eye(matrix.shape[0], dtype=matrix.dtype)
    return jnp.linalg.cholesky(matrix).T

def match_channel(echo_block, replica):
    tap_count = replica.shape[1]
    gate_count = echo_block.shape[1]
    padded = jnp.pad(echo_block, ((0, 0), (0, tap_count - 1), (0, 0)))
    real_sum = jnp.zeros(echo_block.shape[1:], echo_block.dtype)
    imag_sum = jnp.zeros(echo_block.shape[1:], echo_block.dtype)
    for tap_index in range(tap_count):
        window = padded[:, tap_index:tap_index + gate_count, :]
        real_sum = real_sum + replica[0, tap_index] * window[0] + replica[1, tap_index] * window[1]
        imag_sum = imag_sum + replica[0, tap_index] * window[1] - replica[1, tap_index] * window[0]
    return jnp.stack([real_sum, imag_sum])

def reference(raw_echo, replica, beam_weights, pivots, owner_counts, train_gates):
    dft_table = doppler_table(PULSES)

    def one_channel(channel_index):
        echo_block = lax.dynamic_index_in_dim(raw_echo, channel_index, 1, keepdims=False)
        matched = match_channel(echo_block, replica)
        spectra = jnp.einsum('abpk,bgp->kag', dft_table, matched, precision=lax.Precision.HIGHEST)
        return spectra.astype(jnp.bfloat16)
    spectrum = lax.map(one_channel, jnp.arange(CH, dtype=jnp.int32))
    weights = complex_block(beam_weights[0], beam_weights[1]).astype(jnp.float32)
    count_rows = float(train_gates.shape[1])

    def one_bin(bin_index):
        incoming = lax.dynamic_index_in_dim(spectrum, bin_index, 1, keepdims=False)
        gate_list = lax.dynamic_index_in_dim(train_gates, bin_index, 0, keepdims=False)
        chosen = jnp.take(incoming, gate_list, axis=2).astype(jnp.float32)
        beam_data = jnp.einsum('abcd,cbk->adk', weights, chosen).astype(jnp.bfloat16)
        stacked = beam_data.reshape(2 * DOF, -1)
        product = jnp.dot(stacked.astype(jnp.float32), stacked.T.astype(jnp.float32), preferred_element_type=jnp.float32)
        real_part = product[:DOF, :DOF] + product[DOF:, DOF:]
        imag_part = product[DOF:, :DOF] - product[:DOF, DOF:]
        pivot_row = lax.dynamic_index_in_dim(pivots, bin_index, 0, keepdims=False)
        return factor_matrix(real_part, imag_part, pivot_row, count_rows)
    factors = lax.map(one_bin, jnp.arange(PULSES, dtype=jnp.int32))
    starts = jnp.cumsum(owner_counts, dtype=jnp.int32) - owner_counts
    slot_index = jnp.arange(MOST, dtype=jnp.int32)
    slot_bins = jnp.minimum(starts[:, None] + slot_index[None, :], PULSES - 1).reshape(-1)
    filled = (slot_index[None, :] < owner_counts[:, None]).reshape(-1)
    placed = jnp.take(factors, slot_bins, axis=0)
    return jnp.where(filled[:, None, None], placed, 0.0)
```

```python
import functools
import math

import jax
import jax.numpy as jnp
from jax import lax
from jax.experimental import pallas as pl
from jax.experimental.pallas import tpu as pltpu
from jax.sharding import PartitionSpec as P

LOADING = 0.25
LANES = 128
PANEL = 16
BF16 = jnp.bfloat16
F32 = jnp.float32
PARAMS = pltpu.CompilerParams(vmem_limit_bytes=48 * 1024 * 1024)


def shifted(array, axis, by):
    count = lax.axis_size(axis)
    pairs = [(i, i + by) for i in range(count) if 0 <= i + by < count]
    return lax.ppermute(array, axis, pairs)


def complex_block(real_part, imag_part):
    upper_row = jnp.stack([real_part, imag_part])
    lower_row = jnp.stack([-imag_part, real_part])
    return jnp.stack([upper_row, lower_row])


def doppler_table(pulse_count):
    pulse_index = jnp.arange(pulse_count, dtype=jnp.int32)
    phase_index = pulse_index[:, None] * pulse_index[None, :] % pulse_count
    angle_table = phase_index.astype(jnp.float32) * (2.0 * math.pi / pulse_count)
    norm_scale = 1.0 / math.sqrt(pulse_count)
    return complex_block(jnp.cos(angle_table) * norm_scale, jnp.sin(angle_table) * norm_scale)


def filter_rows(replica, block_rows):
    tap_count = replica.shape[1]
    span_rows = block_rows + tap_count - 1
    offsets = (
        jnp.arange(span_rows, dtype=jnp.int32)[None, :]
        - jnp.arange(block_rows, dtype=jnp.int32)[:, None]
    )
    matches = offsets[:, :, None] == jnp.arange(tap_count, dtype=jnp.int32)[None, None, :]
    picked = jnp.sum(jnp.where(matches[None], replica[:, None, None, :], 0.0), axis=3)
    return complex_block(picked[0], picked[1])


def select_kernel(bins_ref, gates_ref, spectrum_ref, out_ref, *, pack, groups):
    owner = pl.program_id(0)
    gate_rows = spectrum_ref.shape[2]
    width = out_ref.shape[3]
    gate_index = lax.broadcasted_iota(jnp.int32, (gate_rows, width), 0)
    part_index = lax.broadcasted_iota(jnp.int32, (gate_rows, width), 1) // (width // pack)

    def one_group(group, carry):
        hit = gate_index == gates_ref[0, pl.ds(group, 1), :]
        total = jnp.zeros(out_ref.shape[2:], F32)
        for part in range(pack):
            bin_index = bins_ref[(owner * groups + group) * pack + part]
            chooser = jnp.where(hit & (part_index == part), 1.0, 0.0).astype(BF16)
            total += jnp.dot(spectrum_ref[bin_index], chooser, preferred_element_type=F32)
        out_ref[0, group] = total.astype(BF16)
        return carry

    lax.fori_loop(0, groups, one_group, 0)


def select_gates(spectrum, slot_bins, slot_gates, owners, pack):
    bins, rows, gate_rows = spectrum.shape
    groups = slot_bins.shape[0] // owners // pack
    width = slot_gates.shape[-1]
    return pl.pallas_call(
        functools.partial(select_kernel, pack=pack, groups=groups),
        out_shape=jax.ShapeDtypeStruct((owners, groups, rows, width), BF16),
        grid_spec=pltpu.PrefetchScalarGridSpec(
            num_scalar_prefetch=1,
            grid=(owners,),
            in_specs=[
                pl.BlockSpec((1, groups, width), lambda i, b: (i, 0, 0)),
                pl.BlockSpec((bins, rows, gate_rows), lambda i, b: (0, 0, 0)),
            ],
            out_specs=pl.BlockSpec((1, groups, rows, width), lambda i, b: (i, 0, 0, 0)),
        ),
        compiler_params=PARAMS,
        name="select_gates",
    )(slot_bins, slot_gates.reshape(owners, groups, width), spectrum)


def beam_kernel(weights_ref, arrived_ref, out_ref):
    sources, groups, rows, width = arrived_ref.shape
    packed = jnp.concatenate(
        [arrived_ref[:, g].reshape(sources * rows, width) for g in range(groups)], axis=1
    )
    beams = jnp.dot(weights_ref[...], packed, preferred_element_type=F32).astype(BF16)
    for g in range(groups):
        out_ref[g] = beams[:, g * width : (g + 1) * width]


def form_beams(arrived, weights):
    sources, groups, rows, width = arrived.shape
    step = 2 if groups % 2 == 0 else 1
    return pl.pallas_call(
        beam_kernel,
        out_shape=jax.ShapeDtypeStruct((groups, weights.shape[0], width), BF16),
        grid=(groups // step,),
        in_specs=[
            pl.BlockSpec(weights.shape, lambda i: (0, 0)),
            pl.BlockSpec((sources, step, rows, width), lambda i: (0, i, 0, 0)),
        ],
        out_specs=pl.BlockSpec((step, weights.shape[0], width), lambda i: (i, 0, 0)),
        compiler_params=PARAMS,
        name="form_beams",
    )(weights, arrived)


def split_terms(array):
    high = array.astype(BF16)
    return high, (array - high.astype(F32)).astype(BF16)


def cross_product(left, right):
    left_high, left_low = split_terms(left)
    right_high, right_low = split_terms(right)
    return lax.dot_general(
        jnp.concatenate([left_high, left_high, left_low], axis=0),
        jnp.concatenate([right_high, right_low, right_high], axis=0),
        (((0,), (0,)), ((), ())),
        preferred_element_type=F32,
    )


def loaded_covariance(beams, pivot_row, part, pack, count_rows):
    dof = pivot_row.shape[1]
    hot = lax.broadcasted_iota(jnp.int32, (dof, dof), 0) == pivot_row
    hot = jnp.where(hot, 1.0, 0.0).astype(BF16)
    picked = []
    for half in range(2):
        rows = jnp.concatenate([b[half * dof : (half + 1) * dof] for b in beams], axis=1)
        moved = lax.dot_general(hot, rows, (((0,), (0,)), ((), ())), preferred_element_type=F32)
        picked.append(moved)
    real_part, imag_part = picked
    upper = jnp.concatenate([real_part, imag_part], axis=1)
    lower = jnp.concatenate([imag_part, -real_part], axis=1)
    stacked = jnp.concatenate([upper, lower], axis=0)
    width = beams[0].shape[1]
    lane = lax.broadcasted_iota(jnp.int32, stacked.shape, 1)
    kept = jnp.where((lane % width) // (width // pack) == part, stacked, 0.0).astype(BF16)
    gram = lax.dot_general(
        kept, stacked.astype(BF16), (((1,), (1,)), ((), ())), preferred_element_type=F32
    )
    order = 2 * dof
    row = lax.broadcasted_iota(jnp.int32, (order, order), 0)
    col = lax.broadcasted_iota(jnp.int32, (order, order), 1)
    return gram / count_rows + jnp.where(row == col, LOADING, 0.0)


def eliminate(tiles):
    sub = lax.broadcasted_iota(jnp.int32, (8, LANES), 0)
    diagonal = [jnp.ones((8, LANES), F32) for _ in tiles]
    for t in range(PANEL):
        home, place = divmod(t, 8)
        column = jnp.broadcast_to(tiles[home][0][:, t : t + 1], (8, LANES))
        diagonal[home] = jnp.where(sub == place, column, diagonal[home])
        inverse = pl.reciprocal(column, approx=True)
        inverse = inverse * (2.0 - column * inverse)
        inverse = inverse[place : place + 1]
        scaled = [piece[place : place + 1] * inverse for piece in tiles[home]]
        for i in range(home, PANEL // 8):
            if i == home and place == 7:
                continue
            if i == home:
                factor = jnp.where(sub > place, column, 0.0)
            else:
                factor = jnp.broadcast_to(tiles[i][0][:, t : t + 1], (8, LANES))
            tiles[i] = [piece - factor * s for piece, s in zip(tiles[i], scaled)]
    scales = [lax.rsqrt(d) for d in diagonal]
    return [[piece * s for piece in row] for row, s in zip(tiles, scales)]


def factor_kernel(pivots_ref, beams_ref, out_ref, work, *, pack, count_rows):
    ranges, groups = beams_ref.shape[:2]
    slots, order, _ = work.shape

    for slot in range(slots):
        group, part = divmod(slot, pack)
        work[slot] = loaded_covariance(
            [beams_ref[r, group] for r in range(ranges)],
            pivots_ref[slot : slot + 1, :],
            part,
            pack,
            count_rows,
        )

    lane = lax.broadcasted_iota(jnp.int32, (PANEL, LANES), 1)
    for start in range(0, order, LANES):
        chunks = (order - start) // LANES

        def one_panel(p, carry, start=start, chunks=chunks):
            base = pl.multiple_of(start + p * PANEL, PANEL)
            back = p * PANEL
            for slot in range(slots):
                tiles = []
                for i in range(PANEL // 8):
                    piece = work[slot, pl.ds(pl.multiple_of(base + 8 * i, 8), 8), start:]
                    row = [piece[:, w * LANES : (w + 1) * LANES] for w in range(chunks)]
                    row[0] = pltpu.roll(row[0], (LANES - back) % LANES, 1)
                    tiles.append(row)
                tiles = eliminate(tiles)
                for row in tiles:
                    row[0] = pltpu.roll(row[0], back, 1)
                rows = [
                    jnp.concatenate([tiles[i][w] for i in range(PANEL // 8)], axis=0)
                    for w in range(chunks)
                ]
                panel = jnp.concatenate(rows, axis=1)
                work[slot, pl.ds(base, PANEL), start:] = panel
                below = jnp.where(lane >= back + PANEL, rows[0], 0.0)
                work[slot, start : start + LANES, start:] -= cross_product(below, panel)
            return carry

        lax.fori_loop(0, LANES // PANEL, one_panel, 0)
        if chunks > 1:
            after = start + LANES
            for slot in range(slots):
                ready = work[slot, start:after, after:]
                work[slot, after:, after:] -= cross_product(ready, ready)

    owners, _, share, _ = out_ref.shape
    for slot in range(slots):
        for r in range(owners):
            row = lax.broadcasted_iota(jnp.int32, (share, order), 0) + r * share
            col = lax.broadcasted_iota(jnp.int32, (share, order), 1)
            piece = work[slot, r * share : (r + 1) * share]
            out_ref[r, slot] = jnp.where(col >= row, piece, 0.0).astype(out_ref.dtype)


def factor_slots(beams, pivot_rows, pack, count_rows):
    ranges = beams.shape[0]
    slots, dof = pivot_rows.shape
    order = 2 * dof
    return pl.pallas_call(
        functools.partial(factor_kernel, pack=pack, count_rows=count_rows),
        out_shape=jax.ShapeDtypeStruct((ranges, slots, order // ranges, order), BF16),
        in_specs=[
            pl.BlockSpec(memory_space=pltpu.VMEM),
            pl.BlockSpec(memory_space=pltpu.VMEM),
        ],
        out_specs=pl.BlockSpec(memory_space=pltpu.VMEM),
        scratch_shapes=[pltpu.VMEM((slots, order, order), F32)],
        compiler_params=PARAMS,
        name="factor_slots",
    )(pivot_rows, beams)


def local(raw_echo, replica, beam_weights, pivots, owner_counts, train_gates):
    ch_local = raw_echo.shape[1]
    gate_rows = raw_echo.shape[2]
    pulse_count = raw_echo.shape[3]
    tap_count = replica.shape[1]
    train_local = train_gates.shape[1]
    owners = lax.axis_size("dop")
    ranges = lax.axis_size("rng")
    most_slots = 2 * (pulse_count // owners)
    share_slots = most_slots // ranges
    pack = max(1, min(LANES // train_local, share_slots))

    echo = raw_echo.astype(BF16)
    next_rows = shifted(echo[:, :, : tap_count - 1, :], "rng", -1)
    extended = jnp.concatenate([echo, next_rows], axis=2)
    matched = jnp.einsum(
        "abji,bcip->acjp",
        filter_rows(replica, gate_rows).astype(BF16),
        extended,
        preferred_element_type=F32,
    ).astype(BF16)
    spectrum = jnp.einsum(
        "abpk,bcgp->kacg",
        doppler_table(pulse_count).astype(BF16),
        matched,
        preferred_element_type=F32,
    ).astype(BF16)
    spectrum = spectrum.reshape(pulse_count, 2 * ch_local, gate_rows)

    starts = jnp.cumsum(owner_counts, dtype=jnp.int32) - owner_counts
    slot_index = jnp.arange(most_slots, dtype=jnp.int32)
    slot_bins = jnp.minimum(starts[:, None] + slot_index[None, :], pulse_count - 1).reshape(-1)
    slot_gates = jnp.take(train_gates % gate_rows, slot_bins, axis=0)
    slot_gates = slot_gates.reshape(-1, pack * train_local)
    outgoing = select_gates(spectrum, slot_bins, slot_gates, owners, pack)
    arrived = lax.all_to_all(outgoing, "dop", split_axis=0, concat_axis=0, tiled=True)

    dof = beam_weights.shape[2]
    weights = complex_block(beam_weights[0], beam_weights[1])
    weights = weights.reshape(2, 2, owners, ch_local, dof).transpose(0, 4, 2, 1, 3)
    weights = weights.reshape(2 * dof, -1)
    beams = form_beams(arrived, weights)
    beams = beams.reshape(ranges, -1, 2 * dof, beams.shape[-1])
    beams = lax.all_to_all(beams, "rng", split_axis=0, concat_axis=0, tiled=True)

    me = lax.axis_index("dop")
    my_start = lax.dynamic_index_in_dim(starts, me, 0, keepdims=False)
    my_count = lax.dynamic_index_in_dim(owner_counts, me, 0, keepdims=False)
    lead = lax.axis_index("rng") * share_slots
    share_bins = my_start + lead + jnp.arange(share_slots, dtype=jnp.int32)
    my_pivots = jnp.take(pivots, jnp.minimum(share_bins, pulse_count - 1), axis=0)
    count_rows = float(train_local * ranges)
    factors = factor_slots(beams, my_pivots, pack, count_rows)
    rows_done = lax.all_to_all(factors, "rng", split_axis=0, concat_axis=0, tiled=True)
    rows_done = rows_done.reshape(most_slots, *rows_done.shape[2:])
    filled = slot_index < my_count
    return jnp.where(filled[:, None, None], rows_done.astype(F32), 0.0)


def solution(mesh):
    return jax.shard_map(
        local,
        mesh=mesh,
        in_specs=(P(None, "dop", "rng", None), P(), P(), P(), P(), P(None, "rng")),
        out_specs=P("dop", "rng", None),
        check_vma=False,
    )
```

```python
import functools
import math

import jax
import jax.numpy as jnp
from jax import lax
from jax.experimental import pallas as pl
from jax.experimental.pallas import tpu as pltpu
from jax.sharding import PartitionSpec as P

LOADING = 0.25
LANES = 128
PANEL = 16
BF16 = jnp.bfloat16
F32 = jnp.float32
PARAMS = pltpu.CompilerParams(vmem_limit_bytes=48 * 1024 * 1024)


def shifted(array, axis, by):
    count = lax.axis_size(axis)
    pairs = [(i, i + by) for i in range(count) if 0 <= i + by < count]
    return lax.ppermute(array, axis, pairs)


def complex_block(real_part, imag_part):
    upper_row = jnp.stack([real_part, imag_part])
    lower_row = jnp.stack([-imag_part, real_part])
    return jnp.stack([upper_row, lower_row])


def doppler_table(pulse_count):
    pulse_index = jnp.arange(pulse_count, dtype=jnp.int32)
    phase_index = pulse_index[:, None] * pulse_index[None, :] % pulse_count
    angle_table = phase_index.astype(jnp.float32) * (2.0 * math.pi / pulse_count)
    norm_scale = 1.0 / math.sqrt(pulse_count)
    return complex_block(jnp.cos(angle_table) * norm_scale, jnp.sin(angle_table) * norm_scale)


def filter_rows(replica, block_rows):
    tap_count = replica.shape[1]
    span_rows = block_rows + tap_count - 1
    offsets = (
        jnp.arange(span_rows, dtype=jnp.int32)[None, :]
        - jnp.arange(block_rows, dtype=jnp.int32)[:, None]
    )
    matches = offsets[:, :, None] == jnp.arange(tap_count, dtype=jnp.int32)[None, None, :]
    picked = jnp.sum(jnp.where(matches[None], replica[:, None, None, :], 0.0), axis=3)
    return complex_block(picked[0], picked[1])


def select_kernel(bins_ref, gates_ref, spectrum_ref, out_ref, *, pack, groups):
    owner = pl.program_id(0)
    gate_rows = spectrum_ref.shape[2]
    width = out_ref.shape[3]
    gate_index = lax.broadcasted_iota(jnp.int32, (gate_rows, width), 0)
    part_index = lax.broadcasted_iota(jnp.int32, (gate_rows, width), 1) // (width // pack)

    unroll = math.gcd(groups, 4)
    masks = [part_index == part for part in range(pack)]

    def some_groups(step, carry):
        for inner in range(unroll):
            group = step * unroll + inner
            hit = gate_index == gates_ref[0, pl.ds(group, 1), :]
            total = jnp.zeros(out_ref.shape[2:], F32)
            for part in range(pack):
                bin_index = bins_ref[(owner * groups + group) * pack + part]
                chooser = jnp.where(hit & masks[part], 1.0, 0.0).astype(BF16)
                total += jnp.dot(spectrum_ref[bin_index], chooser, preferred_element_type=F32)
            out_ref[0, group] = total.astype(BF16)
        return carry

    lax.fori_loop(0, groups // unroll, some_groups, 0)


def select_gates(spectrum, slot_bins, slot_gates, owners, pack):
    bins, rows, gate_rows = spectrum.shape
    groups = slot_bins.shape[0] // owners // pack
    width = slot_gates.shape[-1]
    return pl.pallas_call(
        functools.partial(select_kernel, pack=pack, groups=groups),
        out_shape=jax.ShapeDtypeStruct((owners, groups, rows, width), BF16),
        grid_spec=pltpu.PrefetchScalarGridSpec(
            num_scalar_prefetch=1,
            grid=(owners,),
            in_specs=[
                pl.BlockSpec((1, groups, width), lambda i, b: (i, 0, 0)),
                pl.BlockSpec((bins, rows, gate_rows), lambda i, b: (0, 0, 0)),
            ],
            out_specs=pl.BlockSpec((1, groups, rows, width), lambda i, b: (i, 0, 0, 0)),
        ),
        compiler_params=PARAMS,
        name="select_gates",
    )(slot_bins, slot_gates.reshape(owners, groups, width), spectrum)


def beam_kernel(weights_ref, arrived_ref, out_ref):
    sources, groups, rows, width = arrived_ref.shape
    packed = jnp.concatenate(
        [arrived_ref[:, g].reshape(sources * rows, width) for g in range(groups)], axis=1
    )
    beams = jnp.dot(weights_ref[...], packed, preferred_element_type=F32).astype(BF16)
    for g in range(groups):
        out_ref[g] = beams[:, g * width : (g + 1) * width]


def form_beams(arrived, weights):
    sources, groups, rows, width = arrived.shape
    step = 2 if groups % 2 == 0 else 1
    return pl.pallas_call(
        beam_kernel,
        out_shape=jax.ShapeDtypeStruct((groups, weights.shape[0], width), BF16),
        grid=(groups // step,),
        in_specs=[
            pl.BlockSpec(weights.shape, lambda i: (0, 0)),
            pl.BlockSpec((sources, step, rows, width), lambda i: (0, i, 0, 0)),
        ],
        out_specs=pl.BlockSpec((step, weights.shape[0], width), lambda i: (i, 0, 0)),
        compiler_params=PARAMS,
        name="form_beams",
    )(weights, arrived)


def split_terms(array):
    high = array.astype(BF16)
    return high, (array - high.astype(F32)).astype(BF16)


def cross_product(left, right):
    left_high, left_low = split_terms(left)
    right_high, right_low = split_terms(right)
    return lax.dot_general(
        jnp.concatenate([left_high, left_high, left_low], axis=0),
        jnp.concatenate([right_high, right_low, right_high], axis=0),
        (((0,), (0,)), ((), ())),
        preferred_element_type=F32,
    )


def loaded_covariance(beams, pivot_row, part, pack, count_rows):
    dof = pivot_row.shape[1]
    width = beams[0].shape[1] // pack
    hot = lax.broadcasted_iota(jnp.int32, (dof, dof), 0) == pivot_row
    hot = jnp.where(hot, 1.0, 0.0).astype(BF16)
    own = jnp.concatenate([b[:, part * width : (part + 1) * width] for b in beams], axis=1)
    picked = [
        lax.dot_general(
            hot,
            own[half * dof : (half + 1) * dof],
            (((0,), (0,)), ((), ())),
            preferred_element_type=F32,
        )
        for half in range(2)
    ]
    upper = jnp.concatenate([picked[0], picked[1]], axis=1).astype(BF16)
    lower = jnp.concatenate([picked[1], -picked[0]], axis=1).astype(BF16)
    stacked = jnp.concatenate([upper, lower], axis=0)
    gram = lax.dot_general(
        stacked, stacked, (((1,), (1,)), ((), ())), preferred_element_type=F32
    )
    return gram * (1.0 / count_rows)


def lane_spread(piece, lane):
    return jnp.broadcast_to(piece[:, lane : lane + 1], piece.shape)


def eliminate(rows):
    scales = []
    for first in range(0, PANEL, 8):
        span = range(first, first + 8)
        small = {(i, j): lane_spread(rows[i][0], j) for i in span for j in span if j >= i}
        for t in span:
            pivot = small[t, t]
            inverse = pl.reciprocal(pivot, approx=True)
            inverse = inverse * (2.0 - pivot * inverse)
            scales.append(lax.rsqrt(pivot))
            for i in range(t + 1, first + 8):
                factor = small[t, i] * inverse
                for j in range(i, first + 8):
                    small[i, j] = small[i, j] - factor * small[t, j]
                rows[i] = [x - factor * y for x, y in zip(rows[i], rows[t])]
        for t in span:
            rows[t] = [x * scales[t] for x in rows[t]]
        for i in range(first + 8, PANEL):
            for t in span:
                factor = lane_spread(rows[t][0], i)
                rows[i] = [x - factor * y for x, y in zip(rows[i], rows[t])]
    return rows


def factor_kernel(pivots_ref, beams_ref, out_ref, panel_ref, *work, pack, count_rows):
    ranges, groups = beams_ref.shape[:2]
    slots = len(work)
    order = work[0].shape[0]
    height = panel_ref.shape[1] // PANEL

    row = lax.broadcasted_iota(jnp.int32, (LANES, LANES), 0)
    col = lax.broadcasted_iota(jnp.int32, (LANES, LANES), 1)
    loading = jnp.where(row == col, LOADING, 0.0)
    for slot in range(slots):
        group, part = divmod(slot, pack)
        work[slot][...] = loaded_covariance(
            [beams_ref[r, group] for r in range(ranges)],
            pivots_ref[slot : slot + 1, :],
            part,
            pack,
            count_rows,
        )
        for start in range(0, order, LANES):
            work[slot][start : start + LANES, start : start + LANES] += loading

    lane = lax.broadcasted_iota(jnp.int32, (PANEL, LANES), 1)
    eights = range(0, PANEL, 8)
    for start in range(0, order, LANES):
        chunks = (order - start) // LANES

        def one_panel(p, carry, start=start, chunks=chunks):
            base = pl.multiple_of(start + p * PANEL, PANEL)
            back = p * PANEL
            for slot in range(slots):
                for i in eights:
                    place = pl.ds(pl.multiple_of(base + i, 8), 8)
                    for w in range(chunks):
                        left = start + w * LANES
                        piece = work[slot][place, left : left + LANES]
                        panel_ref[w, pl.ds(i * height + slot, 8, stride=height), :] = piece
            rows = []
            for t in range(PANEL):
                pieces = [panel_ref[w, t * height : (t + 1) * height, :] for w in range(chunks)]
                pieces[0] = pltpu.roll(pieces[0], (LANES - back) % LANES, 1)
                rows.append(pieces)
            rows = eliminate(rows)
            for t in range(PANEL):
                rows[t][0] = pltpu.roll(rows[t][0], back, 1)
                for w in range(chunks):
                    panel_ref[w, t * height : (t + 1) * height, :] = rows[t][w]
            for slot in range(slots):
                parts = []
                for w in range(chunks):
                    pieces = [
                        panel_ref[w, pl.ds(i * height + slot, 8, stride=height), :] for i in eights
                    ]
                    parts.append(jnp.concatenate(pieces, axis=0))
                panel = jnp.concatenate(parts, axis=1)
                work[slot][pl.ds(base, PANEL), start:] = panel
                below = jnp.where(lane >= back + PANEL, parts[0], 0.0)
                work[slot][start : start + LANES, start:] -= cross_product(below, panel)
            return carry

        lax.fori_loop(0, LANES // PANEL, one_panel, 0)
        if chunks > 1:
            after = start + LANES
            for slot in range(slots):
                ready = work[slot][start:after, after:]
                work[slot][after:, after:] -= cross_product(ready, ready)

    owners, _, share, _ = out_ref.shape
    for slot in range(slots):
        for r in range(owners):
            row = lax.broadcasted_iota(jnp.int32, (share, order), 0) + r * share
            col = lax.broadcasted_iota(jnp.int32, (share, order), 1)
            piece = work[slot][r * share : (r + 1) * share]
            out_ref[r, slot] = jnp.where(col >= row, piece, 0.0).astype(out_ref.dtype)


def factor_slots(beams, pivot_rows, pack, count_rows):
    ranges = beams.shape[0]
    slots, dof = pivot_rows.shape
    order = 2 * dof
    height = -(-slots // 8) * 8
    return pl.pallas_call(
        functools.partial(factor_kernel, pack=pack, count_rows=count_rows),
        out_shape=jax.ShapeDtypeStruct((ranges, slots, order // ranges, order), BF16),
        in_specs=[
            pl.BlockSpec(memory_space=pltpu.VMEM),
            pl.BlockSpec(memory_space=pltpu.VMEM),
        ],
        out_specs=pl.BlockSpec(memory_space=pltpu.VMEM),
        scratch_shapes=[pltpu.VMEM((order // LANES, PANEL * height, LANES), F32)]
        + [pltpu.VMEM((order, order), F32) for _ in range(slots)],
        compiler_params=PARAMS,
        name="factor_slots",
    )(pivot_rows, beams)


def local(raw_echo, replica, beam_weights, pivots, owner_counts, train_gates):
    ch_local = raw_echo.shape[1]
    gate_rows = raw_echo.shape[2]
    pulse_count = raw_echo.shape[3]
    tap_count = replica.shape[1]
    train_local = train_gates.shape[1]
    owners = lax.axis_size("dop")
    ranges = lax.axis_size("rng")
    most_slots = 2 * (pulse_count // owners)
    share_slots = most_slots // ranges
    pack = max(1, min(LANES // train_local, share_slots))

    echo = raw_echo.astype(BF16)
    next_rows = shifted(echo[:, :, : tap_count - 1, :], "rng", -1)
    extended = jnp.concatenate([echo, next_rows], axis=2)
    matched = jnp.einsum(
        "abji,bcip->acjp",
        filter_rows(replica, gate_rows).astype(BF16),
        extended,
        preferred_element_type=F32,
    ).astype(BF16)
    spectrum = jnp.einsum(
        "abpk,bcgp->kacg",
        doppler_table(pulse_count).astype(BF16),
        matched,
        preferred_element_type=F32,
    ).astype(BF16)
    spectrum = spectrum.reshape(pulse_count, 2 * ch_local, gate_rows)

    starts = jnp.cumsum(owner_counts, dtype=jnp.int32) - owner_counts
    slot_index = jnp.arange(most_slots, dtype=jnp.int32)
    slot_bins = jnp.minimum(starts[:, None] + slot_index[None, :], pulse_count - 1).reshape(-1)
    slot_gates = jnp.take(train_gates % gate_rows, slot_bins, axis=0)
    slot_gates = slot_gates.reshape(-1, pack * train_local)
    outgoing = select_gates(spectrum, slot_bins, slot_gates, owners, pack)
    arrived = lax.all_to_all(outgoing, "dop", split_axis=0, concat_axis=0, tiled=True)

    dof = beam_weights.shape[2]
    weights = complex_block(beam_weights[0], beam_weights[1])
    weights = weights.reshape(2, 2, owners, ch_local, dof).transpose(0, 4, 2, 1, 3)
    weights = weights.reshape(2 * dof, -1)
    beams = form_beams(arrived, weights)
    beams = beams.reshape(ranges, -1, 2 * dof, beams.shape[-1])
    beams = lax.all_to_all(beams, "rng", split_axis=0, concat_axis=0, tiled=True)

    me = lax.axis_index("dop")
    my_start = lax.dynamic_index_in_dim(starts, me, 0, keepdims=False)
    my_count = lax.dynamic_index_in_dim(owner_counts, me, 0, keepdims=False)
    lead = lax.axis_index("rng") * share_slots
    share_bins = my_start + lead + jnp.arange(share_slots, dtype=jnp.int32)
    my_pivots = jnp.take(pivots, jnp.minimum(share_bins, pulse_count - 1), axis=0)
    count_rows = float(train_local * ranges)
    factors = factor_slots(beams, my_pivots, pack, count_rows)
    rows_done = lax.all_to_all(factors, "rng", split_axis=0, concat_axis=0, tiled=True)
    rows_done = rows_done.reshape(most_slots, *rows_done.shape[2:])
    filled = slot_index < my_count
    return jnp.where(filled[:, None, None], rows_done.astype(F32), 0.0)


def solution(mesh):
    return jax.shard_map(
        local,
        mesh=mesh,
        in_specs=(P(None, "dop", "rng", None), P(), P(), P(), P(), P(None, "rng")),
        out_specs=P("dop", "rng", None),
        check_vma=False,
    )
```

```python
import functools
import math

import jax
import jax.numpy as jnp
from jax import lax
from jax.experimental import pallas as pl
from jax.experimental.pallas import tpu as pltpu
from jax.sharding import PartitionSpec as P

LOADING = 0.25
LANES = 128
PANEL = 16
BF16 = jnp.bfloat16
F32 = jnp.float32
PARAMS = pltpu.CompilerParams(vmem_limit_bytes=48 * 1024 * 1024)


def shifted(array, axis, by):
    count = lax.axis_size(axis)
    pairs = [(i, i + by) for i in range(count) if 0 <= i + by < count]
    return lax.ppermute(array, axis, pairs)


def complex_block(real_part, imag_part):
    upper_row = jnp.stack([real_part, imag_part])
    lower_row = jnp.stack([-imag_part, real_part])
    return jnp.stack([upper_row, lower_row])


def doppler_table(pulse_count):
    pulse_index = jnp.arange(pulse_count, dtype=jnp.int32)
    phase_index = pulse_index[:, None] * pulse_index[None, :] % pulse_count
    angle_table = phase_index.astype(jnp.float32) * (2.0 * math.pi / pulse_count)
    norm_scale = 1.0 / math.sqrt(pulse_count)
    return complex_block(jnp.cos(angle_table) * norm_scale, jnp.sin(angle_table) * norm_scale)


def filter_rows(replica, block_rows):
    tap_count = replica.shape[1]
    span_rows = block_rows + tap_count - 1
    offsets = (
        jnp.arange(span_rows, dtype=jnp.int32)[None, :]
        - jnp.arange(block_rows, dtype=jnp.int32)[:, None]
    )
    matches = offsets[:, :, None] == jnp.arange(tap_count, dtype=jnp.int32)[None, None, :]
    picked = jnp.sum(jnp.where(matches[None], replica[:, None, None, :], 0.0), axis=3)
    return complex_block(picked[0], picked[1])


def select_kernel(bins_ref, gates_ref, spectrum_ref, out_ref, *, pack, groups):
    owner = pl.program_id(0)
    gate_rows = spectrum_ref.shape[2]
    width = out_ref.shape[3]
    gate_index = lax.broadcasted_iota(jnp.int32, (gate_rows, width), 0)
    part_index = lax.broadcasted_iota(jnp.int32, (gate_rows, width), 1) // (width // pack)

    unroll = math.gcd(groups, 4)
    masks = [part_index == part for part in range(pack)]

    def some_groups(step, carry):
        for inner in range(unroll):
            group = step * unroll + inner
            hit = gate_index == gates_ref[0, pl.ds(group, 1), :]
            total = jnp.zeros(out_ref.shape[2:], F32)
            for part in range(pack):
                bin_index = bins_ref[(owner * groups + group) * pack + part]
                chooser = jnp.where(hit & masks[part], 1.0, 0.0).astype(BF16)
                total += jnp.dot(spectrum_ref[bin_index], chooser, preferred_element_type=F32)
            out_ref[0, group] = total.astype(BF16)
        return carry

    lax.fori_loop(0, groups // unroll, some_groups, 0)


def select_gates(spectrum, slot_bins, slot_gates, owners, pack):
    bins, rows, gate_rows = spectrum.shape
    groups = slot_bins.shape[0] // owners // pack
    width = slot_gates.shape[-1]
    return pl.pallas_call(
        functools.partial(select_kernel, pack=pack, groups=groups),
        out_shape=jax.ShapeDtypeStruct((owners, groups, rows, width), BF16),
        grid_spec=pltpu.PrefetchScalarGridSpec(
            num_scalar_prefetch=1,
            grid=(owners,),
            in_specs=[
                pl.BlockSpec((1, groups, width), lambda i, b: (i, 0, 0)),
                pl.BlockSpec((bins, rows, gate_rows), lambda i, b: (0, 0, 0)),
            ],
            out_specs=pl.BlockSpec((1, groups, rows, width), lambda i, b: (i, 0, 0, 0)),
        ),
        compiler_params=PARAMS,
        cost_estimate=pl.CostEstimate(
            flops=2 * slot_bins.shape[0] * rows * gate_rows * width,
            bytes_accessed=spectrum.size * 2,
            transcendentals=0,
        ),
        name="select_gates",
    )(slot_bins, slot_gates.reshape(owners, groups, width), spectrum)


def beam_kernel(weights_ref, arrived_ref, out_ref):
    sources, groups, rows, width = arrived_ref.shape
    packed = jnp.concatenate(
        [arrived_ref[:, g].reshape(sources * rows, width) for g in range(groups)], axis=1
    )
    beams = jnp.dot(weights_ref[...], packed, preferred_element_type=F32).astype(BF16)
    for g in range(groups):
        out_ref[g] = beams[:, g * width : (g + 1) * width]


def form_beams(arrived, weights):
    sources, groups, rows, width = arrived.shape
    step = 2 if groups % 2 == 0 else 1
    return pl.pallas_call(
        beam_kernel,
        out_shape=jax.ShapeDtypeStruct((groups, weights.shape[0], width), BF16),
        grid=(groups // step,),
        in_specs=[
            pl.BlockSpec(weights.shape, lambda i: (0, 0)),
            pl.BlockSpec((sources, step, rows, width), lambda i: (0, i, 0, 0)),
        ],
        out_specs=pl.BlockSpec((step, weights.shape[0], width), lambda i: (i, 0, 0)),
        compiler_params=PARAMS,
        cost_estimate=pl.CostEstimate(
            flops=2 * arrived.size * weights.shape[0],
            bytes_accessed=arrived.size * 2,
            transcendentals=0,
        ),
        name="form_beams",
    )(weights, arrived)


def split_terms(array):
    high = array.astype(BF16)
    return high, (array - high.astype(F32)).astype(BF16)


def cross_product(left, right):
    left_high, left_low = split_terms(left)
    right_high, right_low = split_terms(right)
    return lax.dot_general(
        jnp.concatenate([left_high, left_high, left_low], axis=0),
        jnp.concatenate([right_high, right_low, right_high], axis=0),
        (((0,), (0,)), ((), ())),
        preferred_element_type=F32,
    )


def loaded_covariance(beams, pivot_row, part, pack, count_rows):
    dof = pivot_row.shape[1]
    width = beams[0].shape[1] // pack
    hot = lax.broadcasted_iota(jnp.int32, (dof, dof), 0) == pivot_row
    hot = jnp.where(hot, 1.0, 0.0).astype(BF16)
    own = jnp.concatenate([b[:, part * width : (part + 1) * width] for b in beams], axis=1)
    picked = [
        lax.dot_general(
            hot,
            own[half * dof : (half + 1) * dof],
            (((0,), (0,)), ((), ())),
            preferred_element_type=F32,
        )
        for half in range(2)
    ]
    upper = jnp.concatenate([picked[0], picked[1]], axis=1).astype(BF16)
    lower = jnp.concatenate([picked[1], -picked[0]], axis=1).astype(BF16)
    stacked = jnp.concatenate([upper, lower], axis=0)
    gram = lax.dot_general(
        stacked, stacked, (((1,), (1,)), ((), ())), preferred_element_type=F32
    )
    return gram * (1.0 / count_rows)


def lane_spread(piece, lane):
    return jnp.broadcast_to(piece[:, lane : lane + 1], piece.shape)


def eliminate(rows):
    scales = []
    for first in range(0, PANEL, 8):
        span = range(first, first + 8)
        small = {(i, j): lane_spread(rows[i][0], j) for i in span for j in span if j >= i}
        for t in span:
            pivot = small[t, t]
            inverse = pl.reciprocal(pivot, approx=True)
            inverse = inverse * (2.0 - pivot * inverse)
            scales.append(lax.rsqrt(pivot))
            for i in range(t + 1, first + 8):
                factor = small[t, i] * inverse
                for j in range(i, first + 8):
                    small[i, j] = small[i, j] - factor * small[t, j]
                rows[i] = [x - factor * y for x, y in zip(rows[i], rows[t])]
        for t in span:
            rows[t] = [x * scales[t] for x in rows[t]]
        for i in range(first + 8, PANEL):
            for t in span:
                factor = lane_spread(rows[t][0], i)
                rows[i] = [x - factor * y for x, y in zip(rows[i], rows[t])]
    return rows


def factor_kernel(pivots_ref, beams_ref, out_ref, panel_ref, *work, pack, count_rows):
    ranges, groups = beams_ref.shape[:2]
    slots = len(work)
    order = work[0].shape[0]
    height = panel_ref.shape[1] // PANEL

    row = lax.broadcasted_iota(jnp.int32, (LANES, LANES), 0)
    col = lax.broadcasted_iota(jnp.int32, (LANES, LANES), 1)
    loading = jnp.where(row == col, LOADING, 0.0)
    for slot in range(slots):
        group, part = divmod(slot, pack)
        work[slot][...] = loaded_covariance(
            [beams_ref[r, group] for r in range(ranges)],
            pivots_ref[slot : slot + 1, :],
            part,
            pack,
            count_rows,
        )
        for start in range(0, order, LANES):
            work[slot][start : start + LANES, start : start + LANES] += loading

    lane = lax.broadcasted_iota(jnp.int32, (PANEL, LANES), 1)
    eights = range(0, PANEL, 8)
    for start in range(0, order, LANES):
        chunks = (order - start) // LANES

        def one_panel(p, carry, start=start, chunks=chunks):
            base = pl.multiple_of(start + p * PANEL, PANEL)
            back = p * PANEL
            for slot in range(slots):
                for i in eights:
                    place = pl.ds(pl.multiple_of(base + i, 8), 8)
                    for w in range(chunks):
                        left = start + w * LANES
                        piece = work[slot][place, left : left + LANES]
                        panel_ref[w, pl.ds(i * height + slot, 8, stride=height), :] = piece
            rows = []
            for t in range(PANEL):
                pieces = [panel_ref[w, t * height : (t + 1) * height, :] for w in range(chunks)]
                pieces[0] = pltpu.roll(pieces[0], (LANES - back) % LANES, 1)
                rows.append(pieces)
            rows = eliminate(rows)
            for t in range(PANEL):
                rows[t][0] = pltpu.roll(rows[t][0], back, 1)
                for w in range(chunks):
                    panel_ref[w, t * height : (t + 1) * height, :] = rows[t][w]
            for slot in range(slots):
                parts = []
                for w in range(chunks):
                    pieces = [
                        panel_ref[w, pl.ds(i * height + slot, 8, stride=height), :] for i in eights
                    ]
                    parts.append(jnp.concatenate(pieces, axis=0))
                panel = jnp.concatenate(parts, axis=1)
                work[slot][pl.ds(base, PANEL), start:] = panel
                below = jnp.where(lane >= back + PANEL, parts[0], 0.0)
                work[slot][start : start + LANES, start:] -= cross_product(below, panel)
            return carry

        lax.fori_loop(0, LANES // PANEL, one_panel, 0)
        if chunks > 1:
            after = start + LANES
            for slot in range(slots):
                ready = work[slot][start:after, after:]
                work[slot][after:, after:] -= cross_product(ready, ready)

    owners, _, share, _ = out_ref.shape
    for slot in range(slots):
        for r in range(owners):
            row = lax.broadcasted_iota(jnp.int32, (share, order), 0) + r * share
            col = lax.broadcasted_iota(jnp.int32, (share, order), 1)
            piece = work[slot][r * share : (r + 1) * share]
            out_ref[r, slot] = jnp.where(col >= row, piece, 0.0).astype(out_ref.dtype)


def factor_slots(beams, pivot_rows, pack, count_rows):
    ranges = beams.shape[0]
    slots, dof = pivot_rows.shape
    order = 2 * dof
    height = -(-slots // 8) * 8
    return pl.pallas_call(
        functools.partial(factor_kernel, pack=pack, count_rows=count_rows),
        out_shape=jax.ShapeDtypeStruct((ranges, slots, order // ranges, order), BF16),
        in_specs=[
            pl.BlockSpec(memory_space=pltpu.VMEM),
            pl.BlockSpec(memory_space=pltpu.VMEM),
        ],
        out_specs=pl.BlockSpec(memory_space=pltpu.VMEM),
        scratch_shapes=[pltpu.VMEM((order // LANES, PANEL * height, LANES), F32)]
        + [pltpu.VMEM((order, order), F32) for _ in range(slots)],
        compiler_params=PARAMS,
        cost_estimate=pl.CostEstimate(
            flops=order * 60_000_000, bytes_accessed=beams.size * 2, transcendentals=0
        ),
        name="factor_slots",
    )(pivot_rows, beams)


def slot_parts(share_slots, pack):
    halves = 2 if share_slots % (2 * pack) == 0 else 1
    count = share_slots // halves
    return [(i * count, count) for i in range(halves)]


def local(raw_echo, replica, beam_weights, pivots, owner_counts, train_gates):
    ch_local = raw_echo.shape[1]
    gate_rows = raw_echo.shape[2]
    pulse_count = raw_echo.shape[3]
    tap_count = replica.shape[1]
    train_local = train_gates.shape[1]
    owners = lax.axis_size("dop")
    ranges = lax.axis_size("rng")
    most_slots = 2 * (pulse_count // owners)
    share_slots = most_slots // ranges
    pack = max(1, min(LANES // train_local, share_slots))

    echo = raw_echo.astype(BF16)
    next_rows = shifted(echo[:, :, : tap_count - 1, :], "rng", -1)
    extended = jnp.concatenate([echo, next_rows], axis=2)
    matched = jnp.einsum(
        "abji,bcip->acjp",
        filter_rows(replica, gate_rows).astype(BF16),
        extended,
        preferred_element_type=F32,
    ).astype(BF16)
    spectrum = jnp.einsum(
        "abpk,bcgp->kacg",
        doppler_table(pulse_count).astype(BF16),
        matched,
        preferred_element_type=F32,
    ).astype(BF16)
    spectrum = spectrum.reshape(pulse_count, 2 * ch_local, gate_rows)

    starts = jnp.cumsum(owner_counts, dtype=jnp.int32) - owner_counts
    me = lax.axis_index("dop")
    my_start = lax.dynamic_index_in_dim(starts, me, 0, keepdims=False)
    my_count = lax.dynamic_index_in_dim(owner_counts, me, 0, keepdims=False)
    my_lead = lax.axis_index("rng") * share_slots
    local_gates = train_gates % gate_rows
    count_rows = float(train_local * ranges)

    dof = beam_weights.shape[2]
    weights = complex_block(beam_weights[0], beam_weights[1])
    weights = weights.reshape(2, 2, owners, ch_local, dof).transpose(0, 4, 2, 1, 3)
    weights = weights.reshape(2 * dof, -1)

    lead_slots = jnp.arange(ranges, dtype=jnp.int32) * share_slots
    parts = slot_parts(share_slots, pack)
    sent = []
    for first, count in parts:
        some = first + jnp.arange(count, dtype=jnp.int32)
        slots = (lead_slots[:, None] + some[None, :]).reshape(-1)
        bins = jnp.minimum(starts[:, None] + slots[None, :], pulse_count - 1).reshape(-1)
        gates = jnp.take(local_gates, bins, axis=0).reshape(-1, pack * train_local)
        outgoing = select_gates(spectrum, bins, gates, owners, pack)
        sent.append(lax.all_to_all(outgoing, "dop", split_axis=0, concat_axis=0, tiled=True))
    done = []
    for (first, count), arrived in zip(parts, sent):
        beams = form_beams(arrived, weights)
        beams = beams.reshape(ranges, -1, 2 * dof, beams.shape[-1])
        beams = lax.all_to_all(beams, "rng", split_axis=0, concat_axis=0, tiled=True)
        bins = my_start + my_lead + first + jnp.arange(count, dtype=jnp.int32)
        my_pivots = jnp.take(pivots, jnp.minimum(bins, pulse_count - 1), axis=0)
        factors = factor_slots(beams, my_pivots, pack, count_rows)
        done.append(lax.all_to_all(factors, "rng", split_axis=0, concat_axis=0, tiled=True))
    rows_done = jnp.concatenate(done, axis=1)
    rows_done = rows_done.reshape(most_slots, *rows_done.shape[2:])
    filled = jnp.arange(most_slots, dtype=jnp.int32) < my_count
    return jnp.where(filled[:, None, None], rows_done.astype(F32), 0.0)


def solution(mesh):
    return jax.shard_map(
        local,
        mesh=mesh,
        in_specs=(P(None, "dop", "rng", None), P(), P(), P(), P(), P(None, "rng")),
        out_specs=P("dop", "rng", None),
        check_vma=False,
    )
```

```python
import functools
import math

import jax
import jax.numpy as jnp
from jax import lax
from jax.experimental import pallas as pl
from jax.experimental.pallas import tpu as pltpu
from jax.sharding import PartitionSpec as P

LOADING = 0.25
LANES = 128
PANEL = 16
BF16 = jnp.bfloat16
F32 = jnp.float32
PARAMS = pltpu.CompilerParams(vmem_limit_bytes=48 * 1024 * 1024)


def shifted(array, axis, by):
    count = lax.axis_size(axis)
    pairs = [(i, i + by) for i in range(count) if 0 <= i + by < count]
    return lax.ppermute(array, axis, pairs)


def complex_block(real_part, imag_part):
    upper_row = jnp.stack([real_part, imag_part])
    lower_row = jnp.stack([-imag_part, real_part])
    return jnp.stack([upper_row, lower_row])


def doppler_table(pulse_count):
    pulse_index = jnp.arange(pulse_count, dtype=jnp.int32)
    phase_index = pulse_index[:, None] * pulse_index[None, :] % pulse_count
    angle_table = phase_index.astype(jnp.float32) * (2.0 * math.pi / pulse_count)
    norm_scale = 1.0 / math.sqrt(pulse_count)
    return complex_block(jnp.cos(angle_table) * norm_scale, jnp.sin(angle_table) * norm_scale)


def filter_rows(replica, block_rows):
    tap_count = replica.shape[1]
    span_rows = block_rows + tap_count - 1
    offsets = (
        jnp.arange(span_rows, dtype=jnp.int32)[None, :]
        - jnp.arange(block_rows, dtype=jnp.int32)[:, None]
    )
    matches = offsets[:, :, None] == jnp.arange(tap_count, dtype=jnp.int32)[None, None, :]
    picked = jnp.sum(jnp.where(matches[None], replica[:, None, None, :], 0.0), axis=3)
    return complex_block(picked[0], picked[1])


def spectrum_kernel(rows_ref, table_ref, own_ref, next_ref, out_ref, turned):
    step = pl.program_id(0)
    _, channels, gate_rows, pulses = own_ref.shape
    bins, height, _ = out_ref.shape
    width = math.gcd(channels, 2)
    for first in range(0, channels, width):
        span = range(first, first + width)
        samples = []
        for part in range(2):
            own = jnp.concatenate([own_ref[part, c] for c in span], axis=1).astype(BF16)
            following = jnp.concatenate([next_ref[part, c] for c in span], axis=1)
            samples += [own, following]
        samples = jnp.concatenate(samples, axis=0)
        matched = jnp.dot(rows_ref[...], samples, preferred_element_type=F32).astype(BF16)
        stacked = jnp.concatenate(
            [
                jnp.concatenate(
                    [
                        matched[
                            part * gate_rows : (part + 1) * gate_rows, i * pulses : (i + 1) * pulses
                        ]
                        for part in range(2)
                    ],
                    axis=1,
                )
                for i in range(width)
            ],
            axis=0,
        )
        spectra = lax.dot_general(
            table_ref[...], stacked, (((1,), (1,)), ((), ())), preferred_element_type=F32
        )
        for part in range(2):
            for i in range(width):
                place = part * (height // 2) + step * channels + first + i
                turned[pl.ds(place, bins, stride=height), :] = spectra[
                    part * bins : (part + 1) * bins, i * gate_rows : (i + 1) * gate_rows
                ]

    @pl.when(step == pl.num_programs(0) - 1)
    def _():
        out_ref[...] = turned[...].astype(BF16).reshape(out_ref.shape)


def form_spectrum(rows, table, raw_echo, next_rows, chunk, chunks):
    _, ch_local, gate_rows, pulses = raw_echo.shape
    channels = ch_local // chunks
    step = math.gcd(channels, 4)
    steps = channels // step
    height = 2 * channels
    bins = table.shape[0] // 2
    return pl.pallas_call(
        spectrum_kernel,
        out_shape=jax.ShapeDtypeStruct((bins, height, gate_rows), BF16),
        grid=(steps,),
        in_specs=[
            pl.BlockSpec(rows.shape, lambda i: (0, 0)),
            pl.BlockSpec(table.shape, lambda i: (0, 0)),
            pl.BlockSpec((2, step, gate_rows, pulses), lambda i: (0, chunk * steps + i, 0, 0)),
            pl.BlockSpec((2, step) + next_rows.shape[2:], lambda i: (0, i, 0, 0)),
        ],
        out_specs=pl.BlockSpec((bins, height, gate_rows), lambda i: (0, 0, 0)),
        scratch_shapes=[pltpu.VMEM((bins * height, gate_rows), F32)],
        compiler_params=PARAMS,
        cost_estimate=pl.CostEstimate(
            flops=2 * rows.size * channels * pulses + 2 * table.size * channels * gate_rows,
            bytes_accessed=8 * channels * gate_rows * pulses,
            transcendentals=0,
        ),
        name="form_spectrum",
    )(rows, table, raw_echo, next_rows)


def select_kernel(bins_ref, gates_ref, *refs, pack):
    *spectrum_refs, out_ref = refs
    gate_rows = spectrum_refs[0].shape[2]
    owners, groups, rows, width = out_ref.shape
    gate_index = lax.broadcasted_iota(jnp.int32, (gate_rows, width), 0)
    part_index = lax.broadcasted_iota(jnp.int32, (gate_rows, width), 1) // (width // pack)
    unroll = math.gcd(groups, 4)
    masks = [part_index == part for part in range(pack)]

    def some_groups(step, carry):
        owner = step // (groups // unroll)
        lead = step % (groups // unroll) * unroll
        for inner in range(unroll):
            group = step * unroll + inner
            hit = gate_index == gates_ref[pl.ds(group, 1), :]
            total = jnp.zeros((rows, width), F32)
            for part in range(pack):
                bin_index = bins_ref[group * pack + part]
                chooser = jnp.where(hit & masks[part], 1.0, 0.0).astype(BF16)
                spectra = jnp.concatenate([ref[bin_index] for ref in spectrum_refs], axis=0)
                total += jnp.dot(spectra, chooser, preferred_element_type=F32)
            out_ref[owner, lead + inner] = total.astype(BF16)
        return carry

    lax.fori_loop(0, owners * groups // unroll, some_groups, 0)


def select_gates(spectra, slot_bins, slot_gates, owners, pack):
    rows = sum(spectrum.shape[1] for spectrum in spectra)
    gate_rows = spectra[0].shape[2]
    groups = slot_bins.shape[0] // owners // pack
    width = slot_gates.shape[-1]
    return pl.pallas_call(
        functools.partial(select_kernel, pack=pack),
        out_shape=jax.ShapeDtypeStruct((owners, groups, rows, width), BF16),
        in_specs=[pl.BlockSpec(memory_space=pltpu.SMEM)]
        + [pl.BlockSpec(memory_space=pltpu.VMEM)] * (1 + len(spectra)),
        out_specs=pl.BlockSpec(memory_space=pltpu.VMEM),
        compiler_params=PARAMS,
        cost_estimate=pl.CostEstimate(
            flops=2 * slot_bins.shape[0] * rows * gate_rows * width,
            bytes_accessed=owners * groups * rows * width * 2,
            transcendentals=0,
        ),
        name="select_gates",
    )(slot_bins, slot_gates, *spectra)


def beam_kernel(me_ref, weights_ref, arrived_ref, *out_refs):
    sources, groups, rows, width = arrived_ref.shape
    ranges = len(out_refs)
    share = groups // ranges
    for shift, out_ref in enumerate(out_refs):
        lead = lax.rem(me_ref[0] + shift, ranges) * share
        packed = jnp.concatenate(
            [arrived_ref[:, lead + g].reshape(sources * rows, width) for g in range(share)], axis=1
        )
        beams = lax.dot_general(
            weights_ref[...], packed, (((0,), (0,)), ((), ())), preferred_element_type=F32
        ).astype(BF16)
        for g in range(share):
            out_ref[g] = beams[:, g * width : (g + 1) * width]


def form_beams(arrived, weights, me, ranges):
    _, groups, _, width = arrived.shape
    shape = (groups // ranges, weights.shape[1], width)
    return pl.pallas_call(
        beam_kernel,
        out_shape=[jax.ShapeDtypeStruct(shape, BF16)] * ranges,
        in_specs=[
            pl.BlockSpec(memory_space=pltpu.SMEM),
            pl.BlockSpec(memory_space=pltpu.VMEM),
            pl.BlockSpec(memory_space=pltpu.VMEM),
        ],
        out_specs=[pl.BlockSpec(memory_space=pltpu.VMEM)] * ranges,
        compiler_params=PARAMS,
        cost_estimate=pl.CostEstimate(
            flops=2 * arrived.size * weights.shape[1],
            bytes_accessed=arrived.size * 2,
            transcendentals=0,
        ),
        name="form_beams",
    )(me, weights, arrived)


def exchange(arrays, axis):
    count = len(arrays)
    moved = [arrays[0]]
    for shift in range(1, count):
        pairs = [(i, (i + shift) % count) for i in range(count)]
        moved.append(lax.ppermute(arrays[shift], axis, pairs))
    return moved


def split_terms(array):
    high = array.astype(BF16)
    return high, (array - high.astype(F32)).astype(BF16)


def cross_product(left, right):
    left_high, left_low = split_terms(left)
    right_high, right_low = split_terms(right)
    return lax.dot_general(
        jnp.concatenate([left_high, left_high, left_low], axis=0),
        jnp.concatenate([right_high, right_low, right_high], axis=0),
        (((0,), (0,)), ((), ())),
        preferred_element_type=F32,
    )


def loaded_covariance(beams, pivot_row, part, pack, count_rows):
    dof = pivot_row.shape[1]
    width = beams[0].shape[1] // pack
    hot = lax.broadcasted_iota(jnp.int32, (dof, dof), 0) == pivot_row
    hot = jnp.where(hot, 1.0, 0.0).astype(BF16)
    own = jnp.concatenate([b[:, part * width : (part + 1) * width] for b in beams], axis=1)
    picked = [
        lax.dot_general(
            hot,
            own[half * dof : (half + 1) * dof],
            (((0,), (0,)), ((), ())),
            preferred_element_type=F32,
        )
        for half in range(2)
    ]
    upper = jnp.concatenate([picked[0], picked[1]], axis=1).astype(BF16)
    lower = jnp.concatenate([picked[1], -picked[0]], axis=1).astype(BF16)
    stacked = jnp.concatenate([upper, lower], axis=0)
    gram = lax.dot_general(
        stacked, stacked, (((1,), (1,)), ((), ())), preferred_element_type=F32
    )
    return gram * (1.0 / count_rows)


def lane_spread(piece, lane):
    return jnp.broadcast_to(piece[:, lane : lane + 1], piece.shape)


def eliminate(rows):
    scales = []
    for first in range(0, PANEL, 8):
        span = range(first, first + 8)
        small = {(i, j): lane_spread(rows[i][0], j) for i in span for j in span if j >= i}
        for t in span:
            pivot = small[t, t]
            inverse = pl.reciprocal(pivot, approx=True)
            inverse = inverse * (2.0 - pivot * inverse)
            scales.append(lax.rsqrt(pivot))
            for i in range(t + 1, first + 8):
                factor = small[t, i] * inverse
                for j in range(i, first + 8):
                    small[i, j] = small[i, j] - factor * small[t, j]
                rows[i] = [x - factor * y for x, y in zip(rows[i], rows[t])]
        for t in span:
            rows[t] = [x * scales[t] for x in rows[t]]
        for i in range(first + 8, PANEL):
            for t in span:
                factor = lane_spread(rows[t][0], i)
                rows[i] = [x - factor * y for x, y in zip(rows[i], rows[t])]
    return rows


def factor_kernel(me_ref, pivots_ref, *refs, ranges, pack, count_rows):
    beams_refs, out_refs = refs[:ranges], refs[ranges : 2 * ranges]
    panel_ref, *work = refs[2 * ranges :]
    slots = len(work)
    order = work[0].shape[0]
    height = panel_ref.shape[1] // PANEL

    row = lax.broadcasted_iota(jnp.int32, (LANES, LANES), 0)
    col = lax.broadcasted_iota(jnp.int32, (LANES, LANES), 1)
    loading = jnp.where(row == col, LOADING, 0.0)
    for slot in range(slots):
        group, part = divmod(slot, pack)
        work[slot][...] = loaded_covariance(
            [ref[group] for ref in beams_refs],
            pivots_ref[slot : slot + 1, :],
            part,
            pack,
            count_rows,
        )
        for start in range(0, order, LANES):
            work[slot][start : start + LANES, start : start + LANES] += loading

    lane = lax.broadcasted_iota(jnp.int32, (PANEL, LANES), 1)
    eights = range(0, PANEL, 8)
    for start in range(0, order, LANES):
        chunks = (order - start) // LANES

        def one_panel(p, carry, start=start, chunks=chunks):
            base = pl.multiple_of(start + p * PANEL, PANEL)
            back = p * PANEL
            for slot in range(slots):
                for i in eights:
                    place = pl.ds(pl.multiple_of(base + i, 8), 8)
                    for w in range(chunks):
                        left = start + w * LANES
                        piece = work[slot][place, left : left + LANES]
                        panel_ref[w, pl.ds(i * height + slot, 8, stride=height), :] = piece
            rows = []
            for t in range(PANEL):
                pieces = [panel_ref[w, t * height : (t + 1) * height, :] for w in range(chunks)]
                pieces[0] = pltpu.roll(pieces[0], (LANES - back) % LANES, 1)
                rows.append(pieces)
            rows = eliminate(rows)
            for t in range(PANEL):
                rows[t][0] = pltpu.roll(rows[t][0], back, 1)
                for w in range(chunks):
                    panel_ref[w, t * height : (t + 1) * height, :] = rows[t][w]
            for slot in range(slots):
                parts = []
                for w in range(chunks):
                    pieces = [
                        panel_ref[w, pl.ds(i * height + slot, 8, stride=height), :] for i in eights
                    ]
                    parts.append(jnp.concatenate(pieces, axis=0))
                panel = jnp.concatenate(parts, axis=1)
                work[slot][pl.ds(base, PANEL), start:] = panel
                below = jnp.where(lane >= back + PANEL, parts[0], 0.0)
                work[slot][start : start + LANES, start:] -= cross_product(below, panel)
            return carry

        lax.fori_loop(0, LANES // PANEL, one_panel, 0)
        if chunks > 1:
            after = start + LANES
            for slot in range(slots):
                ready = work[slot][start:after, after:]
                work[slot][after:, after:] -= cross_product(ready, ready)

    share = order // ranges
    row = lax.broadcasted_iota(jnp.int32, (share, order), 0)
    col = lax.broadcasted_iota(jnp.int32, (share, order), 1)
    for shift, out_ref in enumerate(out_refs):
        lead = pl.multiple_of(lax.rem(me_ref[0] + shift, ranges) * share, math.gcd(share, 16))
        upper = col >= row + lead
        for slot in range(slots):
            piece = work[slot][pl.ds(lead, share), :]
            out_ref[slot] = jnp.where(upper, piece, 0.0).astype(out_ref.dtype)


def factor_slots(beams, pivot_rows, me, pack, count_rows):
    ranges = len(beams)
    slots, dof = pivot_rows.shape
    order = 2 * dof
    height = -(-slots // 8) * 8
    return pl.pallas_call(
        functools.partial(factor_kernel, ranges=ranges, pack=pack, count_rows=count_rows),
        out_shape=[jax.ShapeDtypeStruct((slots, order // ranges, order), BF16)] * ranges,
        in_specs=[pl.BlockSpec(memory_space=pltpu.SMEM)]
        + [pl.BlockSpec(memory_space=pltpu.VMEM)] * (1 + ranges),
        out_specs=[pl.BlockSpec(memory_space=pltpu.VMEM)] * ranges,
        scratch_shapes=[pltpu.VMEM((order // LANES, PANEL * height, LANES), F32)]
        + [pltpu.VMEM((order, order), F32) for _ in range(slots)],
        compiler_params=PARAMS,
        cost_estimate=pl.CostEstimate(
            flops=order * 60_000_000,
            bytes_accessed=ranges * beams[0].size * 2,
            transcendentals=0,
        ),
        name="factor_slots",
    )(me, pivot_rows, *beams)


def place_kernel(place_ref, *refs, ranges, parts):
    *in_refs, out_ref = refs
    share_slots = out_ref.shape[0] // ranges
    for shift in range(ranges):
        lead = lax.rem(place_ref[0] + (ranges - shift), ranges) * share_slots
        for index, (first, count) in enumerate(parts):
            ref = in_refs[index * ranges + shift]
            for i in range(count):
                slot = lead + first + i
                keep = jnp.broadcast_to(slot < place_ref[1], out_ref.shape[1:])
                out_ref[slot] = jnp.where(keep, ref[i].astype(F32), 0.0)


def place_rows(place, done, parts, most_slots):
    ranges = len(done[0])
    arrays = [array for part in done for array in part]
    return pl.pallas_call(
        functools.partial(place_kernel, ranges=ranges, parts=parts),
        out_shape=jax.ShapeDtypeStruct((most_slots,) + arrays[0].shape[1:], F32),
        in_specs=[pl.BlockSpec(memory_space=pltpu.SMEM)]
        + [pl.BlockSpec(memory_space=pltpu.VMEM)] * len(arrays),
        out_specs=pl.BlockSpec(memory_space=pltpu.VMEM),
        compiler_params=PARAMS,
        name="place_rows",
    )(place, *arrays)


def slot_parts(share_slots, pack):
    halves = 2 if share_slots % (2 * pack) == 0 else 1
    count = share_slots // halves
    return [(i * count, count) for i in range(halves)]


def local(raw_echo, replica, beam_weights, pivots, owner_counts, train_gates):
    ch_local = raw_echo.shape[1]
    gate_rows = raw_echo.shape[2]
    pulse_count = raw_echo.shape[3]
    tap_count = replica.shape[1]
    train_local = train_gates.shape[1]
    owners = lax.axis_size("dop")
    ranges = lax.axis_size("rng")
    most_slots = 2 * (pulse_count // owners)
    share_slots = most_slots // ranges
    pack = max(1, min(LANES // train_local, share_slots))

    chunks = max(1, min(4, ch_local // 16))
    chunk_rows = ch_local // chunks
    rim = -(-(tap_count - 1) // 16) * 16
    filters = filter_rows(replica, gate_rows)
    filters = jnp.pad(filters, ((0, 0), (0, 0), (0, 0), (0, rim - tap_count + 1)))
    filters = filters.transpose(0, 2, 1, 3).reshape(2 * gate_rows, -1).astype(BF16)
    table = doppler_table(pulse_count).transpose(0, 3, 1, 2)
    table = table.reshape(2 * pulse_count, -1).astype(BF16)
    following = [
        shifted(raw_echo[:, c * chunk_rows : (c + 1) * chunk_rows, :rim, :].astype(BF16), "rng", -1)
        for c in range(chunks)
    ]
    spectra = [
        form_spectrum(filters, table, raw_echo, following[c], c, chunks) for c in range(chunks)
    ]

    starts = jnp.cumsum(owner_counts, dtype=jnp.int32) - owner_counts
    me = lax.axis_index("dop")
    my_start = lax.dynamic_index_in_dim(starts, me, 0, keepdims=False)
    my_count = lax.dynamic_index_in_dim(owner_counts, me, 0, keepdims=False)
    my_range = lax.axis_index("rng").astype(jnp.int32)
    my_lead = my_range * share_slots
    local_gates = train_gates % gate_rows
    count_rows = float(train_local * ranges)

    dof = beam_weights.shape[2]
    real_part, imag_part = beam_weights.reshape(2, owners, chunks, chunk_rows, dof)
    weights = jnp.stack(
        [
            jnp.concatenate([real_part, -imag_part], axis=3),
            jnp.concatenate([imag_part, real_part], axis=3),
        ],
        axis=2,
    ).reshape(-1, 2 * dof)

    lead_slots = jnp.arange(ranges, dtype=jnp.int32) * share_slots
    parts = slot_parts(share_slots, pack)
    sent = []
    for first, count in parts:
        some = first + jnp.arange(count, dtype=jnp.int32)
        slots = (lead_slots[:, None] + some[None, :]).reshape(-1)
        bins = jnp.minimum(starts[:, None] + slots[None, :], pulse_count - 1).reshape(-1)
        gates = jnp.take(local_gates, bins, axis=0).reshape(-1, pack * train_local)
        outgoing = select_gates(spectra, bins, gates, owners, pack)
        sent.append(lax.all_to_all(outgoing, "dop", split_axis=0, concat_axis=0, tiled=True))
    done = []
    for (first, count), arrived in zip(parts, sent):
        beams = exchange(form_beams(arrived, weights, my_range[None], ranges), "rng")
        bins = my_start + my_lead + first + jnp.arange(count, dtype=jnp.int32)
        my_pivots = jnp.take(pivots, jnp.minimum(bins, pulse_count - 1), axis=0)
        factors = factor_slots(beams, my_pivots, my_range[None], pack, count_rows)
        done.append(exchange(factors, "rng"))
    return place_rows(jnp.stack([my_range, my_count]), done, parts, most_slots)


def solution(mesh):
    return jax.shard_map(
        local,
        mesh=mesh,
        in_specs=(P(None, "dop", "rng", None), P(), P(), P(), P(), P(None, "rng")),
        out_specs=P("dop", "rng", None),
        check_vma=False,
    )
```

```python
import functools
import math

import jax
import jax.numpy as jnp
from jax import lax
from jax.experimental import pallas as pl
from jax.experimental.pallas import tpu as pltpu
from jax.sharding import PartitionSpec as P

LOADING = 0.25
LANES = 128
PANEL = 16
BF16 = jnp.bfloat16
F32 = jnp.float32
PARAMS = pltpu.CompilerParams(vmem_limit_bytes=48 * 1024 * 1024)


def shifted(array, axis, by):
    count = lax.axis_size(axis)
    pairs = [(i, i + by) for i in range(count) if 0 <= i + by < count]
    return lax.ppermute(array, axis, pairs)


def complex_block(real_part, imag_part):
    upper_row = jnp.stack([real_part, imag_part])
    lower_row = jnp.stack([-imag_part, real_part])
    return jnp.stack([upper_row, lower_row])


def doppler_table(pulse_count):
    pulse_index = jnp.arange(pulse_count, dtype=jnp.int32)
    phase_index = pulse_index[:, None] * pulse_index[None, :] % pulse_count
    angle_table = phase_index.astype(jnp.float32) * (2.0 * math.pi / pulse_count)
    norm_scale = 1.0 / math.sqrt(pulse_count)
    return complex_block(jnp.cos(angle_table) * norm_scale, jnp.sin(angle_table) * norm_scale)


def filter_kernel(replica_ref, out_ref):
    gate_rows, span = out_ref.shape[0] // 2, replica_ref.shape[1]
    banded = [
        pltpu.roll(
            jnp.broadcast_to(replica_ref[part : part + 1, :], (gate_rows, span)),
            0,
            1,
            stride=1,
            stride_axis=0,
        )
        for part in range(2)
    ]
    out_ref[:gate_rows, :span] = banded[0].astype(BF16)
    out_ref[:gate_rows, span:] = banded[1].astype(BF16)
    out_ref[gate_rows:, :span] = (-banded[1]).astype(BF16)
    out_ref[gate_rows:, span:] = banded[0].astype(BF16)


def filter_rows(replica, gate_rows):
    tap_count = replica.shape[1]
    span = -(-(gate_rows + tap_count) // LANES) * LANES
    return pl.pallas_call(
        filter_kernel,
        out_shape=jax.ShapeDtypeStruct((2 * gate_rows, 2 * span), BF16),
        in_specs=[pl.BlockSpec(memory_space=pltpu.VMEM)],
        out_specs=pl.BlockSpec(memory_space=pltpu.VMEM),
        compiler_params=PARAMS,
        name="filter_rows",
    )(jnp.pad(replica, ((0, 0), (0, span - tap_count))))


def rim_kernel(echo_ref, out_ref):
    out_ref[...] = echo_ref[...].astype(BF16)


def rim_rows(raw_echo, rim, chunk, chunks):
    _, ch_local, _, pulses = raw_echo.shape
    shape = (2, ch_local // chunks, rim, pulses)
    return pl.pallas_call(
        rim_kernel,
        out_shape=jax.ShapeDtypeStruct(shape, BF16),
        grid=(1,),
        in_specs=[pl.BlockSpec(shape, lambda i: (0, chunk, 0, 0))],
        out_specs=pl.BlockSpec(shape, lambda i: (0, 0, 0, 0)),
        compiler_params=PARAMS,
        name="rim_rows",
    )(raw_echo)


def spectrum_kernel(rows_ref, table_ref, own_ref, next_ref, out_ref, turned):
    step = pl.program_id(0)
    _, channels, gate_rows, pulses = own_ref.shape
    bins, height, _ = out_ref.shape
    rim = next_ref.shape[2]
    span = rows_ref.shape[1] // 2
    each = range(channels)
    samples = []
    for part in range(2):
        samples += [
            jnp.concatenate([own_ref[part, c] for c in each], axis=1).astype(BF16),
            jnp.concatenate([next_ref[part, c] for c in each], axis=1),
        ]
        if span > gate_rows + rim:
            samples.append(jnp.zeros((span - gate_rows - rim, channels * pulses), BF16))
    samples = jnp.concatenate(samples, axis=0)
    matched = jnp.dot(rows_ref[...], samples, preferred_element_type=F32).astype(BF16)
    halves = [matched[:gate_rows], matched[gate_rows:]]
    stacked = jnp.concatenate(
        [
            jnp.concatenate([half[:, c * pulses : (c + 1) * pulses] for half in halves], axis=1)
            for c in each
        ],
        axis=0,
    )
    spectra = lax.dot_general(
        table_ref[...], stacked, (((1,), (1,)), ((), ())), preferred_element_type=F32
    )
    for part in range(2):
        for c in each:
            place = part * (height // 2) + step * channels + c
            turned[pl.ds(place, bins, stride=height), :] = spectra[
                part * bins : (part + 1) * bins, c * gate_rows : (c + 1) * gate_rows
            ]

    @pl.when(step == pl.num_programs(0) - 1)
    def _():
        out_ref[...] = turned[...].astype(BF16).reshape(out_ref.shape)


def form_spectrum(rows, table, raw_echo, next_rows, chunk, chunks):
    _, ch_local, gate_rows, pulses = raw_echo.shape
    channels = ch_local // chunks
    step = math.gcd(channels, 8)
    steps = channels // step
    height = 2 * channels
    bins = table.shape[0] // 2
    return pl.pallas_call(
        spectrum_kernel,
        out_shape=jax.ShapeDtypeStruct((bins, height, gate_rows), BF16),
        grid=(steps,),
        in_specs=[
            pl.BlockSpec(rows.shape, lambda i: (0, 0)),
            pl.BlockSpec(table.shape, lambda i: (0, 0)),
            pl.BlockSpec((2, step, gate_rows, pulses), lambda i: (0, chunk * steps + i, 0, 0)),
            pl.BlockSpec((2, step) + next_rows.shape[2:], lambda i: (0, i, 0, 0)),
        ],
        out_specs=pl.BlockSpec((bins, height, gate_rows), lambda i: (0, 0, 0)),
        scratch_shapes=[pltpu.VMEM((bins * height, gate_rows), F32)],
        compiler_params=PARAMS,
        cost_estimate=pl.CostEstimate(
            flops=2 * rows.size * channels * pulses + 2 * table.size * channels * gate_rows,
            bytes_accessed=8 * channels * gate_rows * pulses,
            transcendentals=0,
        ),
        name="form_spectrum",
    )(rows, table, raw_echo, next_rows)


def select_kernel(bins_ref, gates_ref, *refs, pack):
    *spectrum_refs, out_ref = refs
    gate_rows = spectrum_refs[0].shape[2]
    owners, groups, rows, width = out_ref.shape
    gate_index = lax.broadcasted_iota(jnp.int32, (gate_rows, width), 0)
    part_index = lax.broadcasted_iota(jnp.int32, (gate_rows, width), 1) // (width // pack)
    unroll = math.gcd(groups, 4)
    masks = [part_index == part for part in range(pack)]

    def some_groups(step, carry):
        owner = step // (groups // unroll)
        lead = step % (groups // unroll) * unroll
        for inner in range(unroll):
            group = step * unroll + inner
            hit = gate_index == gates_ref[pl.ds(group, 1), :]
            total = jnp.zeros((rows, width), F32)
            for part in range(pack):
                bin_index = bins_ref[group * pack + part]
                chooser = jnp.where(hit & masks[part], 1.0, 0.0).astype(BF16)
                spectra = jnp.concatenate([ref[bin_index] for ref in spectrum_refs], axis=0)
                total += jnp.dot(spectra, chooser, preferred_element_type=F32)
            out_ref[owner, lead + inner] = total.astype(BF16)
        return carry

    lax.fori_loop(0, owners * groups // unroll, some_groups, 0)


def select_gates(spectra, slot_bins, slot_gates, owners, pack):
    rows = sum(spectrum.shape[1] for spectrum in spectra)
    gate_rows = spectra[0].shape[2]
    groups = slot_bins.shape[0] // owners // pack
    width = slot_gates.shape[-1]
    return pl.pallas_call(
        functools.partial(select_kernel, pack=pack),
        out_shape=jax.ShapeDtypeStruct((owners, groups, rows, width), BF16),
        in_specs=[pl.BlockSpec(memory_space=pltpu.SMEM)]
        + [pl.BlockSpec(memory_space=pltpu.VMEM)] * (1 + len(spectra)),
        out_specs=pl.BlockSpec(memory_space=pltpu.VMEM),
        compiler_params=PARAMS,
        cost_estimate=pl.CostEstimate(
            flops=2 * slot_bins.shape[0] * rows * gate_rows * width,
            bytes_accessed=owners * groups * rows * width * 2,
            transcendentals=0,
        ),
        name="select_gates",
    )(slot_bins, slot_gates, *spectra)


def beam_kernel(me_ref, weights_ref, arrived_ref, *refs, ranges):
    out_refs = refs[-ranges:]
    sources, groups, rows, width = arrived_ref.shape
    share = groups // ranges
    for shift, out_ref in enumerate(out_refs):
        lead = lax.rem(me_ref[0] + shift, ranges) * share
        packed = jnp.concatenate(
            [arrived_ref[:, lead + g].reshape(sources * rows, width) for g in range(share)], axis=1
        )
        beams = lax.dot_general(
            weights_ref[...], packed, (((0,), (0,)), ((), ())), preferred_element_type=F32
        ).astype(BF16)
        for g in range(share):
            out_ref[g] = beams[:, g * width : (g + 1) * width]


def form_beams(arrived, weights, me, ranges, earlier):
    _, groups, _, width = arrived.shape
    shape = (groups // ranges, weights.shape[1], width)
    return pl.pallas_call(
        functools.partial(beam_kernel, ranges=ranges),
        out_shape=[jax.ShapeDtypeStruct(shape, BF16)] * ranges,
        in_specs=[
            pl.BlockSpec(memory_space=pltpu.SMEM),
            pl.BlockSpec(memory_space=pltpu.VMEM),
            pl.BlockSpec(memory_space=pltpu.VMEM),
        ]
        + [pl.BlockSpec(memory_space=pl.ANY)] * len(earlier),
        out_specs=[pl.BlockSpec(memory_space=pltpu.VMEM)] * ranges,
        compiler_params=PARAMS,
        cost_estimate=pl.CostEstimate(
            flops=2 * arrived.size * weights.shape[1],
            bytes_accessed=arrived.size * 2,
            transcendentals=0,
        ),
        name="form_beams",
    )(me, weights, arrived, *earlier)


def exchange(arrays, axis):
    count = len(arrays)
    moved = [arrays[0]]
    for shift in range(1, count):
        pairs = [(i, (i + shift) % count) for i in range(count)]
        moved.append(lax.ppermute(arrays[shift], axis, pairs))
    return moved


def split_terms(array):
    high = array.astype(BF16)
    return high, (array - high.astype(F32)).astype(BF16)


def cross_product(left, right):
    left_high, left_low = split_terms(left)
    right_high, right_low = split_terms(right)
    return lax.dot_general(
        jnp.concatenate([left_high, left_high, left_low], axis=0),
        jnp.concatenate([right_high, right_low, right_high], axis=0),
        (((0,), (0,)), ((), ())),
        preferred_element_type=F32,
    )


def loaded_covariance(beams, pivot_row, part, pack, count_rows):
    dof = pivot_row.shape[1]
    width = beams[0].shape[1] // pack
    hot = lax.broadcasted_iota(jnp.int32, (dof, dof), 0) == pivot_row
    hot = jnp.where(hot, 1.0, 0.0).astype(BF16)
    own = jnp.concatenate([b[:, part * width : (part + 1) * width] for b in beams], axis=1)
    picked = [
        lax.dot_general(
            hot,
            own[half * dof : (half + 1) * dof],
            (((0,), (0,)), ((), ())),
            preferred_element_type=F32,
        )
        for half in range(2)
    ]
    upper = jnp.concatenate([picked[0], picked[1]], axis=1).astype(BF16)
    lower = jnp.concatenate([picked[1], -picked[0]], axis=1).astype(BF16)
    stacked = jnp.concatenate([upper, lower], axis=0)
    gram = lax.dot_general(
        stacked, stacked, (((1,), (1,)), ((), ())), preferred_element_type=F32
    )
    return gram * (1.0 / count_rows)


def lane_spread(piece, lane):
    return jnp.broadcast_to(piece[:, lane : lane + 1], piece.shape)


def refined_reciprocal(value):
    guess = pl.reciprocal(value, approx=True)
    return guess * (2.0 - value * guess)


def eliminate(rows):
    scales = []
    for first in range(0, PANEL, 8):
        span = range(first, first + 8)
        small = {(i, j): lane_spread(rows[i][0], j) for i in span for j in span if j >= i}
        for t in range(first, first + 8, 2):
            u = t + 1
            inverse = refined_reciprocal(small[t, t])
            cross = small[t, t] * small[u, u] - small[t, u] * small[t, u]
            second = refined_reciprocal(cross) * small[t, t]
            scales += [lax.rsqrt(small[t, t]), lax.rsqrt(cross * inverse)]
            factor = small[t, u] * inverse
            for j in range(u + 1, first + 8):
                small[u, j] = small[u, j] - factor * small[t, j]
            rows[u] = [x - factor * y for x, y in zip(rows[u], rows[t])]
            for i in range(u + 1, first + 8):
                one, two = small[t, i] * inverse, small[u, i] * second
                for j in range(i, first + 8):
                    small[i, j] = small[i, j] - one * small[t, j] - two * small[u, j]
                rows[i] = [
                    x - one * y - two * z for x, y, z in zip(rows[i], rows[t], rows[u])
                ]
        for t in span:
            rows[t] = [x * scales[t] for x in rows[t]]
        for i in range(first + 8, PANEL):
            for t in span:
                factor = lane_spread(rows[t][0], i)
                rows[i] = [x - factor * y for x, y in zip(rows[i], rows[t])]
    return rows


def factor_kernel(me_ref, pivots_ref, *refs, ranges, pack, count_rows):
    beams_refs, out_refs = refs[:ranges], refs[ranges : 2 * ranges]
    panel_ref, *work = refs[2 * ranges :]
    slots = len(work)
    order = work[0].shape[0]
    height = panel_ref.shape[1] // PANEL

    row = lax.broadcasted_iota(jnp.int32, (LANES, LANES), 0)
    col = lax.broadcasted_iota(jnp.int32, (LANES, LANES), 1)
    loading = jnp.where(row == col, LOADING, 0.0)
    for slot in range(slots):
        group, part = divmod(slot, pack)
        work[slot][...] = loaded_covariance(
            [ref[group] for ref in beams_refs],
            pivots_ref[slot : slot + 1, :],
            part,
            pack,
            count_rows,
        )
        for start in range(0, order, LANES):
            work[slot][start : start + LANES, start : start + LANES] += loading

    lane = lax.broadcasted_iota(jnp.int32, (PANEL, LANES), 1)
    eights = range(0, PANEL, 8)
    for start in range(0, order, LANES):
        chunks = (order - start) // LANES

        def one_panel(p, carry, start=start, chunks=chunks):
            base = pl.multiple_of(start + p * PANEL, PANEL)
            back = p * PANEL
            for slot in range(slots):
                for i in eights:
                    place = pl.ds(pl.multiple_of(base + i, 8), 8)
                    for w in range(chunks):
                        left = start + w * LANES
                        piece = work[slot][place, left : left + LANES]
                        panel_ref[w, pl.ds(i * height + slot, 8, stride=height), :] = piece
            rows = []
            for t in range(PANEL):
                pieces = [panel_ref[w, t * height : (t + 1) * height, :] for w in range(chunks)]
                pieces[0] = pltpu.roll(pieces[0], (LANES - back) % LANES, 1)
                rows.append(pieces)
            rows = eliminate(rows)
            for t in range(PANEL):
                rows[t][0] = pltpu.roll(rows[t][0], back, 1)
                for w in range(chunks):
                    panel_ref[w, t * height : (t + 1) * height, :] = rows[t][w]
            for slot in range(slots):
                parts = []
                for w in range(chunks):
                    pieces = [
                        panel_ref[w, pl.ds(i * height + slot, 8, stride=height), :] for i in eights
                    ]
                    parts.append(jnp.concatenate(pieces, axis=0))
                panel = jnp.concatenate(parts, axis=1)
                work[slot][pl.ds(base, PANEL), start:] = panel
                below = jnp.where(lane >= back + PANEL, parts[0], 0.0)
                work[slot][start : start + LANES, start:] -= cross_product(below, panel)
            return carry

        lax.fori_loop(0, LANES // PANEL, one_panel, 0)
        if chunks > 1:
            after = start + LANES
            for slot in range(slots):
                ready = work[slot][start:after, after:]
                work[slot][after:, after:] -= cross_product(ready, ready)

    share = order // ranges
    row = lax.broadcasted_iota(jnp.int32, (share, order), 0)
    col = lax.broadcasted_iota(jnp.int32, (share, order), 1)
    for shift, out_ref in enumerate(out_refs):
        lead = pl.multiple_of(lax.rem(me_ref[0] + shift, ranges) * share, math.gcd(share, 16))
        upper = col >= row + lead
        for slot in range(slots):
            piece = work[slot][pl.ds(lead, share), :]
            out_ref[slot] = jnp.where(upper, piece, 0.0).astype(out_ref.dtype)


def factor_slots(beams, pivot_rows, me, pack, count_rows):
    ranges = len(beams)
    slots, dof = pivot_rows.shape
    order = 2 * dof
    height = -(-slots // 8) * 8
    return pl.pallas_call(
        functools.partial(factor_kernel, ranges=ranges, pack=pack, count_rows=count_rows),
        out_shape=[jax.ShapeDtypeStruct((slots, order // ranges, order), BF16)] * ranges,
        in_specs=[pl.BlockSpec(memory_space=pltpu.SMEM)]
        + [pl.BlockSpec(memory_space=pltpu.VMEM)] * (1 + ranges),
        out_specs=[pl.BlockSpec(memory_space=pltpu.VMEM)] * ranges,
        scratch_shapes=[pltpu.VMEM((order // LANES, PANEL * height, LANES), F32)]
        + [pltpu.VMEM((order, order), F32) for _ in range(slots)],
        compiler_params=PARAMS,
        cost_estimate=pl.CostEstimate(
            flops=order * 60_000_000,
            bytes_accessed=ranges * beams[0].size * 2,
            transcendentals=0,
        ),
        name="factor_slots",
    )(me, pivot_rows, *beams)


def place_kernel(place_ref, *refs, ranges, parts):
    *in_refs, out_ref = refs
    share_slots = out_ref.shape[0] // ranges
    for shift in range(ranges):
        lead = lax.rem(place_ref[0] + (ranges - shift), ranges) * share_slots
        for index, (first, count) in enumerate(parts):
            ref = in_refs[index * ranges + shift]
            for i in range(count):
                slot = lead + first + i
                keep = jnp.broadcast_to(slot < place_ref[1], out_ref.shape[1:])
                out_ref[slot] = jnp.where(keep, ref[i].astype(F32), 0.0)


def place_rows(place, done, parts, most_slots):
    ranges = len(done[0])
    arrays = [array for part in done for array in part]
    return pl.pallas_call(
        functools.partial(place_kernel, ranges=ranges, parts=parts),
        out_shape=jax.ShapeDtypeStruct((most_slots,) + arrays[0].shape[1:], F32),
        in_specs=[pl.BlockSpec(memory_space=pltpu.SMEM)]
        + [pl.BlockSpec(memory_space=pltpu.VMEM)] * len(arrays),
        out_specs=pl.BlockSpec(memory_space=pltpu.VMEM),
        compiler_params=PARAMS,
        name="place_rows",
    )(place, *arrays)


def slot_parts(share_slots, pack):
    halves = 2 if share_slots % (2 * pack) == 0 else 1
    count = share_slots // halves
    return [(i * count, count) for i in range(halves)]


def local(raw_echo, replica, beam_weights, pivots, owner_counts, train_gates):
    ch_local = raw_echo.shape[1]
    gate_rows = raw_echo.shape[2]
    pulse_count = raw_echo.shape[3]
    tap_count = replica.shape[1]
    train_local = train_gates.shape[1]
    owners = lax.axis_size("dop")
    ranges = lax.axis_size("rng")
    most_slots = 2 * (pulse_count // owners)
    share_slots = most_slots // ranges
    pack = max(1, min(LANES // train_local, share_slots))

    chunks = max(1, min(4, ch_local // 16))
    chunk_rows = ch_local // chunks
    rim = -(-(tap_count - 1) // 16) * 16
    filters = filter_rows(replica, gate_rows)
    table = doppler_table(pulse_count).transpose(0, 3, 1, 2)
    table = table.reshape(2 * pulse_count, -1).astype(BF16)
    following = [shifted(rim_rows(raw_echo, rim, c, chunks), "rng", -1) for c in range(chunks)]
    spectra = [
        form_spectrum(filters, table, raw_echo, following[c], c, chunks) for c in range(chunks)
    ]

    starts = jnp.cumsum(owner_counts, dtype=jnp.int32) - owner_counts
    me = lax.axis_index("dop")
    my_start = lax.dynamic_index_in_dim(starts, me, 0, keepdims=False)
    my_count = lax.dynamic_index_in_dim(owner_counts, me, 0, keepdims=False)
    my_range = lax.axis_index("rng").astype(jnp.int32)
    my_lead = my_range * share_slots
    local_gates = train_gates % gate_rows
    count_rows = float(train_local * ranges)

    dof = beam_weights.shape[2]
    real_part, imag_part = beam_weights.reshape(2, owners, chunks, chunk_rows, dof)
    weights = jnp.stack(
        [
            jnp.concatenate([real_part, -imag_part], axis=3),
            jnp.concatenate([imag_part, real_part], axis=3),
        ],
        axis=2,
    ).reshape(-1, 2 * dof)

    lead_slots = jnp.arange(ranges, dtype=jnp.int32) * share_slots
    parts = slot_parts(share_slots, pack)
    sent = []
    for first, count in parts:
        some = first + jnp.arange(count, dtype=jnp.int32)
        slots = (lead_slots[:, None] + some[None, :]).reshape(-1)
        bins = jnp.minimum(starts[:, None] + slots[None, :], pulse_count - 1).reshape(-1)
        gates = jnp.take(local_gates, bins, axis=0).reshape(-1, pack * train_local)
        outgoing = select_gates(spectra, bins, gates, owners, pack)
        sent.append(lax.all_to_all(outgoing, "dop", split_axis=0, concat_axis=0, tiled=True))
    done, earlier = [], []
    for (first, count), arrived in zip(parts, sent):
        beams = exchange(form_beams(arrived, weights, my_range[None], ranges, earlier), "rng")
        bins = my_start + my_lead + first + jnp.arange(count, dtype=jnp.int32)
        my_pivots = jnp.take(pivots, jnp.minimum(bins, pulse_count - 1), axis=0)
        factors = factor_slots(beams, my_pivots, my_range[None], pack, count_rows)
        earlier = factors[:1]
        done.append(exchange(factors, "rng"))
    return place_rows(jnp.stack([my_range, my_count]), done, parts, most_slots)


def solution(mesh):
    return jax.shard_map(
        local,
        mesh=mesh,
        in_specs=(P(None, "dop", "rng", None), P(), P(), P(), P(), P(None, "rng")),
        out_specs=P("dop", "rng", None),
        check_vma=False,
    )
```

```python
import functools
import math

import jax
import jax.numpy as jnp
from jax import lax
from jax.experimental import pallas as pl
from jax.experimental.pallas import tpu as pltpu
from jax.sharding import PartitionSpec as P

LOADING = 0.25
LANES = 128
PANEL = 16
BF16 = jnp.bfloat16
F32 = jnp.float32
PARAMS = pltpu.CompilerParams(vmem_limit_bytes=48 * 1024 * 1024)


def shifted(array, axis, by):
    count = lax.axis_size(axis)
    pairs = [(i, i + by) for i in range(count) if 0 <= i + by < count]
    return lax.ppermute(array, axis, pairs)


def complex_block(real_part, imag_part):
    upper_row = jnp.stack([real_part, imag_part])
    lower_row = jnp.stack([-imag_part, real_part])
    return jnp.stack([upper_row, lower_row])


def doppler_table(pulse_count):
    pulse_index = jnp.arange(pulse_count, dtype=jnp.int32)
    phase_index = pulse_index[:, None] * pulse_index[None, :] % pulse_count
    angle_table = phase_index.astype(jnp.float32) * (2.0 * math.pi / pulse_count)
    norm_scale = 1.0 / math.sqrt(pulse_count)
    return complex_block(jnp.cos(angle_table) * norm_scale, jnp.sin(angle_table) * norm_scale)


def filter_kernel(replica_ref, out_ref):
    gate_rows, span = out_ref.shape[0] // 2, replica_ref.shape[1]
    banded = [
        pltpu.roll(
            jnp.broadcast_to(replica_ref[part : part + 1, :], (gate_rows, span)),
            0,
            1,
            stride=1,
            stride_axis=0,
        )
        for part in range(2)
    ]
    out_ref[:gate_rows, :span] = banded[0].astype(BF16)
    out_ref[:gate_rows, span:] = banded[1].astype(BF16)
    out_ref[gate_rows:, :span] = (-banded[1]).astype(BF16)
    out_ref[gate_rows:, span:] = banded[0].astype(BF16)


def filter_rows(replica, gate_rows):
    tap_count = replica.shape[1]
    span = -(-(gate_rows + tap_count) // LANES) * LANES
    return pl.pallas_call(
        filter_kernel,
        out_shape=jax.ShapeDtypeStruct((2 * gate_rows, 2 * span), BF16),
        in_specs=[pl.BlockSpec(memory_space=pltpu.VMEM)],
        out_specs=pl.BlockSpec(memory_space=pltpu.VMEM),
        compiler_params=PARAMS,
        name="filter_rows",
    )(jnp.pad(replica, ((0, 0), (0, span - tap_count))))


def rim_kernel(echo_ref, *out_refs):
    for chunk, out_ref in enumerate(out_refs):

        @pl.when(pl.program_id(0) == chunk)
        def _(out_ref=out_ref):
            out_ref[...] = echo_ref[...].astype(BF16)


def rim_rows(raw_echo, rim, chunks):
    _, ch_local, _, pulses = raw_echo.shape
    shape = (2, ch_local // chunks, rim, pulses)
    return pl.pallas_call(
        rim_kernel,
        out_shape=[jax.ShapeDtypeStruct(shape, BF16)] * chunks,
        grid=(chunks,),
        in_specs=[pl.BlockSpec(shape, lambda i: (0, i, 0, 0))],
        out_specs=[pl.BlockSpec(shape, lambda i: (0, 0, 0, 0))] * chunks,
        compiler_params=PARAMS,
        name="rim_rows",
    )(raw_echo)


def spectrum_kernel(rows_ref, table_ref, own_ref, next_ref, out_ref, turned):
    step = pl.program_id(0)
    _, channels, gate_rows, pulses = own_ref.shape
    bins, height, _ = out_ref.shape
    rim = next_ref.shape[2]
    span = rows_ref.shape[1] // 2
    each = range(channels)
    samples = []
    for part in range(2):
        samples += [
            jnp.concatenate([own_ref[part, c] for c in each], axis=1).astype(BF16),
            jnp.concatenate([next_ref[part, c] for c in each], axis=1),
        ]
        if span > gate_rows + rim:
            samples.append(jnp.zeros((span - gate_rows - rim, channels * pulses), BF16))
    samples = jnp.concatenate(samples, axis=0)
    matched = jnp.dot(rows_ref[...], samples, preferred_element_type=F32).astype(BF16)
    halves = [matched[:gate_rows], matched[gate_rows:]]
    stacked = jnp.concatenate(
        [
            jnp.concatenate([half[:, c * pulses : (c + 1) * pulses] for half in halves], axis=1)
            for c in each
        ],
        axis=0,
    )
    spectra = lax.dot_general(
        table_ref[...], stacked, (((1,), (1,)), ((), ())), preferred_element_type=F32
    )
    for part in range(2):
        for c in each:
            place = part * (height // 2) + step * channels + c
            turned[pl.ds(place, bins, stride=height), :] = spectra[
                part * bins : (part + 1) * bins, c * gate_rows : (c + 1) * gate_rows
            ]

    @pl.when(step == pl.num_programs(0) - 1)
    def _():
        out_ref[...] = turned[...].astype(BF16).reshape(out_ref.shape)


def form_spectrum(rows, table, raw_echo, next_rows, chunk, chunks):
    _, ch_local, gate_rows, pulses = raw_echo.shape
    channels = ch_local // chunks
    step = math.gcd(channels, 8)
    steps = channels // step
    height = 2 * channels
    bins = table.shape[0] // 2
    return pl.pallas_call(
        spectrum_kernel,
        out_shape=jax.ShapeDtypeStruct((bins, height, gate_rows), BF16),
        grid=(steps,),
        in_specs=[
            pl.BlockSpec(rows.shape, lambda i: (0, 0)),
            pl.BlockSpec(table.shape, lambda i: (0, 0)),
            pl.BlockSpec((2, step, gate_rows, pulses), lambda i: (0, chunk * steps + i, 0, 0)),
            pl.BlockSpec((2, step) + next_rows.shape[2:], lambda i: (0, i, 0, 0)),
        ],
        out_specs=pl.BlockSpec((bins, height, gate_rows), lambda i: (0, 0, 0)),
        scratch_shapes=[pltpu.VMEM((bins * height, gate_rows), F32)],
        compiler_params=PARAMS,
        cost_estimate=pl.CostEstimate(
            flops=2 * rows.size * channels * pulses + 2 * table.size * channels * gate_rows,
            bytes_accessed=8 * channels * gate_rows * pulses,
            transcendentals=0,
        ),
        name="form_spectrum",
    )(rows, table, raw_echo, next_rows)


def select_kernel(bins_ref, gates_ref, *refs, pack):
    *spectrum_refs, out_ref = refs
    gate_rows = spectrum_refs[0].shape[2]
    owners, groups, rows, width = out_ref.shape
    gate_index = lax.broadcasted_iota(jnp.int32, (pack * gate_rows, width), 0)
    unroll = math.gcd(groups, 4)

    def some_groups(step, carry):
        owner = step // (groups // unroll)
        lead = step % (groups // unroll) * unroll
        for inner in range(unroll):
            group = step * unroll + inner
            chooser = jnp.where(gate_index == gates_ref[pl.ds(group, 1), :], 1.0, 0.0)
            bins = [bins_ref[group * pack + part] for part in range(pack)]
            spectra = jnp.concatenate(
                [jnp.concatenate([ref[b] for b in bins], axis=1) for ref in spectrum_refs], axis=0
            )
            picked = jnp.dot(spectra, chooser.astype(BF16), preferred_element_type=F32)
            out_ref[owner, lead + inner] = picked.astype(BF16)
        return carry

    lax.fori_loop(0, owners * groups // unroll, some_groups, 0)


def select_gates(spectra, slot_bins, slot_gates, owners, pack):
    rows = sum(spectrum.shape[1] for spectrum in spectra)
    gate_rows = spectra[0].shape[2]
    groups = slot_bins.shape[0] // owners // pack
    width = slot_gates.shape[-1]
    return pl.pallas_call(
        functools.partial(select_kernel, pack=pack),
        out_shape=jax.ShapeDtypeStruct((owners, groups, rows, width), BF16),
        in_specs=[pl.BlockSpec(memory_space=pltpu.SMEM)]
        + [pl.BlockSpec(memory_space=pltpu.VMEM)] * (1 + len(spectra)),
        out_specs=pl.BlockSpec(memory_space=pltpu.VMEM),
        compiler_params=PARAMS,
        cost_estimate=pl.CostEstimate(
            flops=2 * slot_bins.shape[0] * rows * gate_rows * width,
            bytes_accessed=owners * groups * rows * width * 2,
            transcendentals=0,
        ),
        name="select_gates",
    )(slot_bins, slot_gates, *spectra)


def beam_kernel(me_ref, weights_ref, arrived_ref, *refs, ranges):
    out_refs = refs[-ranges:]
    sources, groups, rows, width = arrived_ref.shape
    share = groups // ranges
    for shift, out_ref in enumerate(out_refs):
        lead = lax.rem(me_ref[0] + shift, ranges) * share
        packed = jnp.concatenate(
            [arrived_ref[:, lead + g].reshape(sources * rows, width) for g in range(share)], axis=1
        )
        beams = lax.dot_general(
            weights_ref[...], packed, (((0,), (0,)), ((), ())), preferred_element_type=F32
        ).astype(BF16)
        for g in range(share):
            out_ref[g] = beams[:, g * width : (g + 1) * width]


def form_beams(arrived, weights, me, ranges, earlier):
    _, groups, _, width = arrived.shape
    shape = (groups // ranges, weights.shape[1], width)
    return pl.pallas_call(
        functools.partial(beam_kernel, ranges=ranges),
        out_shape=[jax.ShapeDtypeStruct(shape, BF16)] * ranges,
        in_specs=[
            pl.BlockSpec(memory_space=pltpu.SMEM),
            pl.BlockSpec(memory_space=pltpu.VMEM),
            pl.BlockSpec(memory_space=pltpu.VMEM),
        ]
        + [pl.BlockSpec(memory_space=pl.ANY)] * len(earlier),
        out_specs=[pl.BlockSpec(memory_space=pltpu.VMEM)] * ranges,
        compiler_params=PARAMS,
        cost_estimate=pl.CostEstimate(
            flops=2 * arrived.size * weights.shape[1],
            bytes_accessed=arrived.size * 2,
            transcendentals=0,
        ),
        name="form_beams",
    )(me, weights, arrived, *earlier)


def exchange(arrays, axis):
    count = len(arrays)
    moved = [arrays[0]]
    for shift in range(1, count):
        pairs = [(i, (i + shift) % count) for i in range(count)]
        moved.append(lax.ppermute(arrays[shift], axis, pairs))
    return moved


def split_terms(array):
    high = array.astype(BF16)
    return high, (array - high.astype(F32)).astype(BF16)


def cross_product(left, right):
    left_high, left_low = split_terms(left)
    right_high, right_low = split_terms(right)
    return lax.dot_general(
        jnp.concatenate([left_high, left_high, left_low], axis=0),
        jnp.concatenate([right_high, right_low, right_high], axis=0),
        (((0,), (0,)), ((), ())),
        preferred_element_type=F32,
    )


def loaded_covariance(beams, pivot_row, part, pack, count_rows):
    dof = pivot_row.shape[1]
    width = beams[0].shape[1] // pack
    hot = lax.broadcasted_iota(jnp.int32, (dof, dof), 0) == pivot_row
    hot = jnp.where(hot, 1.0, 0.0).astype(BF16)
    own = jnp.concatenate([b[:, part * width : (part + 1) * width] for b in beams], axis=1)
    picked = [
        lax.dot_general(
            hot,
            own[half * dof : (half + 1) * dof],
            (((0,), (0,)), ((), ())),
            preferred_element_type=F32,
        )
        for half in range(2)
    ]
    upper = jnp.concatenate([picked[0], picked[1]], axis=1).astype(BF16)
    lower = jnp.concatenate([picked[1], -picked[0]], axis=1).astype(BF16)
    stacked = jnp.concatenate([upper, lower], axis=0)
    gram = lax.dot_general(
        stacked, stacked, (((1,), (1,)), ((), ())), preferred_element_type=F32
    )
    return gram * (1.0 / count_rows)


def lane_spread(piece, lane):
    return jnp.broadcast_to(piece[:, lane : lane + 1], piece.shape)


def refined_reciprocal(value):
    guess = pl.reciprocal(value, approx=True)
    return guess * (2.0 - value * guess)


def eliminate(rows):
    scales = []
    for first in range(0, PANEL, 8):
        span = range(first, first + 8)
        small = {(i, j): lane_spread(rows[i][0], j) for i in span for j in span if j >= i}
        for t in range(first, first + 8, 2):
            u = t + 1
            inverse = refined_reciprocal(small[t, t])
            cross = small[t, t] * small[u, u] - small[t, u] * small[t, u]
            second = refined_reciprocal(cross) * small[t, t]
            scales += [lax.rsqrt(small[t, t]), lax.rsqrt(cross * inverse)]
            factor = small[t, u] * inverse
            for j in range(u + 1, first + 8):
                small[u, j] = small[u, j] - factor * small[t, j]
            rows[u] = [x - factor * y for x, y in zip(rows[u], rows[t])]
            for i in range(u + 1, first + 8):
                one, two = small[t, i] * inverse, small[u, i] * second
                for j in range(i, first + 8):
                    small[i, j] = small[i, j] - one * small[t, j] - two * small[u, j]
                rows[i] = [
                    x - one * y - two * z for x, y, z in zip(rows[i], rows[t], rows[u])
                ]
        for t in span:
            rows[t] = [x * scales[t] for x in rows[t]]
        for i in range(first + 8, PANEL):
            for t in span:
                factor = lane_spread(rows[t][0], i)
                rows[i] = [x - factor * y for x, y in zip(rows[i], rows[t])]
    return rows


def factor_kernel(me_ref, pivots_ref, *refs, ranges, pack, count_rows):
    beams_refs, out_refs = refs[:ranges], refs[ranges : 2 * ranges]
    panel_ref, *scratch = refs[2 * ranges :]
    slots = len(scratch) // 2
    work, last = scratch[:slots], scratch[slots:]
    order = work[0].shape[0]
    height = panel_ref.shape[1] // PANEL

    row = lax.broadcasted_iota(jnp.int32, (LANES, LANES), 0)
    col = lax.broadcasted_iota(jnp.int32, (LANES, LANES), 1)
    loading = jnp.where(row == col, LOADING, 0.0)
    for slot in range(slots):
        group, part = divmod(slot, pack)
        work[slot][...] = loaded_covariance(
            [ref[group] for ref in beams_refs],
            pivots_ref[slot : slot + 1, :],
            part,
            pack,
            count_rows,
        )
        for start in range(0, order, LANES):
            work[slot][start : start + LANES, start : start + LANES] += loading

    lane = lax.broadcasted_iota(jnp.int32, (PANEL, LANES), 1)
    eights = range(0, PANEL, 8)

    def spread_out(slot, rows, chunks):
        for i in eights:
            for w in range(chunks):
                piece = rows[i : i + 8, w * LANES : (w + 1) * LANES]
                panel_ref[w, pl.ds(i * height + slot, 8, stride=height), :] = piece

    for start in range(0, order, LANES):
        chunks = (order - start) // LANES
        stop = start + LANES
        for slot in range(slots):
            spread_out(slot, work[slot][start : start + PANEL, start:], chunks)
            last[slot][...] = jnp.zeros_like(last[slot])

        def one_panel(p, carry, start=start, stop=stop, chunks=chunks):
            base = pl.multiple_of(start + p * PANEL, PANEL)
            following = pl.multiple_of(jnp.minimum(base + PANEL, order - PANEL), PANEL)
            back = p * PANEL
            for slot in range(slots):
                before = last[slot][:, start:]
                below = jnp.where(lane >= back + PANEL, before[:, :LANES], 0.0)
                work[slot][start:stop, start:] -= cross_product(below, before)
            rows = []
            for t in range(PANEL):
                pieces = [panel_ref[w, t * height : (t + 1) * height, :] for w in range(chunks)]
                pieces[0] = pltpu.roll(pieces[0], (LANES - back) % LANES, 1)
                rows.append(pieces)
            rows = eliminate(rows)
            for t in range(PANEL):
                rows[t][0] = pltpu.roll(rows[t][0], back, 1)
                for w in range(chunks):
                    panel_ref[w, t * height : (t + 1) * height, :] = rows[t][w]
            for slot in range(slots):
                parts = []
                for w in range(chunks):
                    pieces = [
                        panel_ref[w, pl.ds(i * height + slot, 8, stride=height), :] for i in eights
                    ]
                    parts.append(jnp.concatenate(pieces, axis=0))
                panel = jnp.concatenate(parts, axis=1)
                ahead = pltpu.roll(parts[0], (2 * LANES - PANEL - back) % LANES, 1)[:, :PANEL]
                ready = work[slot][pl.ds(following, PANEL), start:] - cross_product(ahead, panel)
                spread_out(slot, ready, chunks)
                work[slot][pl.ds(base, PANEL), start:] = panel
                last[slot][:, start:] = panel
            return carry

        lax.fori_loop(0, LANES // PANEL, one_panel, 0)
        if chunks > 1:
            after = start + LANES
            for slot in range(slots):
                ready = work[slot][start:after, after:]
                work[slot][after:, after:] -= cross_product(ready, ready)

    share = order // ranges
    row = lax.broadcasted_iota(jnp.int32, (share, order), 0)
    col = lax.broadcasted_iota(jnp.int32, (share, order), 1)
    for shift, out_ref in enumerate(out_refs):
        lead = pl.multiple_of(lax.rem(me_ref[0] + shift, ranges) * share, math.gcd(share, 16))
        upper = col >= row + lead
        for slot in range(slots):
            piece = work[slot][pl.ds(lead, share), :]
            out_ref[slot] = jnp.where(upper, piece, 0.0).astype(out_ref.dtype)


def factor_slots(beams, pivot_rows, me, pack, count_rows):
    ranges = len(beams)
    slots, dof = pivot_rows.shape
    order = 2 * dof
    height = -(-slots // 8) * 8
    return pl.pallas_call(
        functools.partial(factor_kernel, ranges=ranges, pack=pack, count_rows=count_rows),
        out_shape=[jax.ShapeDtypeStruct((slots, order // ranges, order), BF16)] * ranges,
        in_specs=[pl.BlockSpec(memory_space=pltpu.SMEM)]
        + [pl.BlockSpec(memory_space=pltpu.VMEM)] * (1 + ranges),
        out_specs=[pl.BlockSpec(memory_space=pltpu.VMEM)] * ranges,
        scratch_shapes=[pltpu.VMEM((order // LANES, PANEL * height, LANES), F32)]
        + [pltpu.VMEM((order, order), F32) for _ in range(slots)]
        + [pltpu.VMEM((PANEL, order), F32) for _ in range(slots)],
        compiler_params=PARAMS,
        cost_estimate=pl.CostEstimate(
            flops=order * 60_000_000,
            bytes_accessed=ranges * beams[0].size * 2,
            transcendentals=0,
        ),
        name="factor_slots",
    )(me, pivot_rows, *beams)


def place_kernel(place_ref, *refs, ranges, parts):
    *in_refs, out_ref = refs
    share_slots = out_ref.shape[0] // ranges
    for shift in range(ranges):
        lead = lax.rem(place_ref[0] + (ranges - shift), ranges) * share_slots
        for index, (first, count) in enumerate(parts):
            ref = in_refs[index * ranges + shift]
            for i in range(count):
                slot = lead + first + i
                keep = jnp.broadcast_to(slot < place_ref[1], out_ref.shape[1:])
                out_ref[slot] = jnp.where(keep, ref[i].astype(F32), 0.0)


def place_rows(place, done, parts, most_slots):
    ranges = len(done[0])
    arrays = [array for part in done for array in part]
    return pl.pallas_call(
        functools.partial(place_kernel, ranges=ranges, parts=parts),
        out_shape=jax.ShapeDtypeStruct((most_slots,) + arrays[0].shape[1:], F32),
        in_specs=[pl.BlockSpec(memory_space=pltpu.SMEM)]
        + [pl.BlockSpec(memory_space=pltpu.VMEM)] * len(arrays),
        out_specs=pl.BlockSpec(memory_space=pltpu.VMEM),
        compiler_params=PARAMS,
        name="place_rows",
    )(place, *arrays)


def slot_parts(share_slots, pack):
    head = share_slots - pack
    return [(0, head), (head, pack)] if head > 0 else [(0, share_slots)]


def local(raw_echo, replica, beam_weights, pivots, owner_counts, train_gates):
    ch_local = raw_echo.shape[1]
    gate_rows = raw_echo.shape[2]
    pulse_count = raw_echo.shape[3]
    tap_count = replica.shape[1]
    train_local = train_gates.shape[1]
    owners = lax.axis_size("dop")
    ranges = lax.axis_size("rng")
    most_slots = 2 * (pulse_count // owners)
    share_slots = most_slots // ranges
    pack = max(1, min(LANES // train_local, share_slots))

    chunks = max(1, min(4, ch_local // 16))
    chunk_rows = ch_local // chunks
    rim = -(-(tap_count - 1) // 16) * 16
    filters = filter_rows(replica, gate_rows)
    table = doppler_table(pulse_count).transpose(0, 3, 1, 2)
    table = table.reshape(2 * pulse_count, -1).astype(BF16)
    following = [shifted(rows, "rng", -1) for rows in rim_rows(raw_echo, rim, chunks)]
    spectra = [
        form_spectrum(filters, table, raw_echo, following[c], c, chunks) for c in range(chunks)
    ]

    starts = jnp.cumsum(owner_counts, dtype=jnp.int32) - owner_counts
    me = lax.axis_index("dop")
    my_start = lax.dynamic_index_in_dim(starts, me, 0, keepdims=False)
    my_count = lax.dynamic_index_in_dim(owner_counts, me, 0, keepdims=False)
    my_range = lax.axis_index("rng").astype(jnp.int32)
    my_lead = my_range * share_slots
    local_gates = train_gates % gate_rows
    count_rows = float(train_local * ranges)

    dof = beam_weights.shape[2]
    real_part, imag_part = beam_weights.reshape(2, owners, chunks, chunk_rows, dof)
    weights = jnp.stack(
        [
            jnp.concatenate([real_part, -imag_part], axis=3),
            jnp.concatenate([imag_part, real_part], axis=3),
        ],
        axis=2,
    ).reshape(-1, 2 * dof)

    lead_slots = jnp.arange(ranges, dtype=jnp.int32) * share_slots
    parts = slot_parts(share_slots, pack)
    sent = []
    for first, count in parts:
        some = first + jnp.arange(count, dtype=jnp.int32)
        slots = (lead_slots[:, None] + some[None, :]).reshape(-1)
        bins = jnp.minimum(starts[:, None] + slots[None, :], pulse_count - 1).reshape(-1)
        gates = jnp.take(local_gates, bins, axis=0).reshape(-1, pack, train_local)
        gates = (gates + gate_rows * jnp.arange(pack, dtype=jnp.int32)[:, None]).reshape(
            -1, pack * train_local
        )
        outgoing = select_gates(spectra, bins, gates, owners, pack)
        sent.append(lax.all_to_all(outgoing, "dop", split_axis=0, concat_axis=0, tiled=True))
    done, earlier = [], []
    for (first, count), arrived in zip(parts, sent):
        beams = exchange(form_beams(arrived, weights, my_range[None], ranges, earlier), "rng")
        bins = my_start + my_lead + first + jnp.arange(count, dtype=jnp.int32)
        my_pivots = jnp.take(pivots, jnp.minimum(bins, pulse_count - 1), axis=0)
        factors = factor_slots(beams, my_pivots, my_range[None], pack, count_rows)
        earlier = factors[:1]
        done.append(exchange(factors, "rng"))
    return place_rows(jnp.stack([my_range, my_count]), done, parts, most_slots)


def solution(mesh):
    return jax.shard_map(
        local,
        mesh=mesh,
        in_specs=(P(None, "dop", "rng", None), P(), P(), P(), P(), P(None, "rng")),
        out_specs=P("dop", "rng", None),
        check_vma=False,
    )
```

```python
import functools
import math

import jax
import jax.numpy as jnp
from jax import lax
from jax.experimental import pallas as pl
from jax.experimental.pallas import tpu as pltpu
from jax.sharding import PartitionSpec as P

LOADING = 0.25
LANES = 128
PANEL = 32
BF16 = jnp.bfloat16
F32 = jnp.float32
PARAMS = pltpu.CompilerParams(vmem_limit_bytes=48 * 1024 * 1024)


def shifted(array, axis, by):
    count = lax.axis_size(axis)
    pairs = [(i, i + by) for i in range(count) if 0 <= i + by < count]
    return lax.ppermute(array, axis, pairs)


def complex_block(real_part, imag_part):
    upper_row = jnp.stack([real_part, imag_part])
    lower_row = jnp.stack([-imag_part, real_part])
    return jnp.stack([upper_row, lower_row])


def doppler_table(pulse_count):
    pulse_index = jnp.arange(pulse_count, dtype=jnp.int32)
    phase_index = pulse_index[:, None] * pulse_index[None, :] % pulse_count
    angle_table = phase_index.astype(jnp.float32) * (2.0 * math.pi / pulse_count)
    norm_scale = 1.0 / math.sqrt(pulse_count)
    return complex_block(jnp.cos(angle_table) * norm_scale, jnp.sin(angle_table) * norm_scale)


def filter_kernel(replica_ref, out_ref):
    gate_rows, span = out_ref.shape[0] // 2, replica_ref.shape[1]
    banded = [
        pltpu.roll(
            jnp.broadcast_to(replica_ref[part : part + 1, :], (gate_rows, span)),
            0,
            1,
            stride=1,
            stride_axis=0,
        )
        for part in range(2)
    ]
    out_ref[:gate_rows, :span] = banded[0].astype(BF16)
    out_ref[:gate_rows, span:] = banded[1].astype(BF16)
    out_ref[gate_rows:, :span] = (-banded[1]).astype(BF16)
    out_ref[gate_rows:, span:] = banded[0].astype(BF16)


def filter_rows(replica, gate_rows):
    tap_count = replica.shape[1]
    span = -(-(gate_rows + tap_count) // LANES) * LANES
    return pl.pallas_call(
        filter_kernel,
        out_shape=jax.ShapeDtypeStruct((2 * gate_rows, 2 * span), BF16),
        in_specs=[pl.BlockSpec(memory_space=pltpu.VMEM)],
        out_specs=pl.BlockSpec(memory_space=pltpu.VMEM),
        compiler_params=PARAMS,
        name="filter_rows",
    )(jnp.pad(replica, ((0, 0), (0, span - tap_count))))


def rim_kernel(echo_ref, out_ref):
    out_ref[...] = echo_ref[...].astype(BF16)


def rim_rows(raw_echo, rim, chunk, chunks):
    _, ch_local, _, pulses = raw_echo.shape
    shape = (2, ch_local // chunks, rim, pulses)
    return pl.pallas_call(
        rim_kernel,
        out_shape=jax.ShapeDtypeStruct(shape, BF16),
        grid=(1,),
        in_specs=[pl.BlockSpec(shape, lambda i: (0, chunk, 0, 0))],
        out_specs=pl.BlockSpec(shape, lambda i: (0, 0, 0, 0)),
        compiler_params=PARAMS,
        name="rim_rows",
    )(raw_echo)


def spectrum_kernel(rows_ref, table_ref, own_ref, next_ref, out_ref, turned):
    step = pl.program_id(0)
    _, channels, gate_rows, pulses = own_ref.shape
    bins, height, _ = out_ref.shape
    rim = next_ref.shape[2]
    span = rows_ref.shape[1] // 2
    each = range(channels)
    samples = []
    for part in range(2):
        samples += [
            jnp.concatenate([own_ref[part, c] for c in each], axis=1).astype(BF16),
            jnp.concatenate([next_ref[part, c] for c in each], axis=1),
        ]
        if span > gate_rows + rim:
            samples.append(jnp.zeros((span - gate_rows - rim, channels * pulses), BF16))
    samples = jnp.concatenate(samples, axis=0)
    matched = jnp.dot(rows_ref[...], samples, preferred_element_type=F32).astype(BF16)
    halves = [matched[:gate_rows], matched[gate_rows:]]
    stacked = jnp.concatenate(
        [
            jnp.concatenate([half[:, c * pulses : (c + 1) * pulses] for half in halves], axis=1)
            for c in each
        ],
        axis=0,
    )
    spectra = lax.dot_general(
        table_ref[...], stacked, (((1,), (1,)), ((), ())), preferred_element_type=F32
    )
    for part in range(2):
        for c in each:
            place = part * (height // 2) + step * channels + c
            turned[pl.ds(place, bins, stride=height), :] = spectra[
                part * bins : (part + 1) * bins, c * gate_rows : (c + 1) * gate_rows
            ]

    @pl.when(step == pl.num_programs(0) - 1)
    def _():
        out_ref[...] = turned[...].astype(BF16).reshape(out_ref.shape)


def form_spectrum(rows, table, raw_echo, next_rows, chunk, chunks):
    _, ch_local, gate_rows, pulses = raw_echo.shape
    channels = ch_local // chunks
    step = math.gcd(channels, 8)
    steps = channels // step
    height = 2 * channels
    bins = table.shape[0] // 2
    return pl.pallas_call(
        spectrum_kernel,
        out_shape=jax.ShapeDtypeStruct((bins, height, gate_rows), BF16),
        grid=(steps,),
        in_specs=[
            pl.BlockSpec(rows.shape, lambda i: (0, 0)),
            pl.BlockSpec(table.shape, lambda i: (0, 0)),
            pl.BlockSpec((2, step, gate_rows, pulses), lambda i: (0, chunk * steps + i, 0, 0)),
            pl.BlockSpec((2, step) + next_rows.shape[2:], lambda i: (0, i, 0, 0)),
        ],
        out_specs=pl.BlockSpec((bins, height, gate_rows), lambda i: (0, 0, 0)),
        scratch_shapes=[pltpu.VMEM((bins * height, gate_rows), F32)],
        compiler_params=PARAMS,
        cost_estimate=pl.CostEstimate(
            flops=2 * rows.size * channels * pulses + 2 * table.size * channels * gate_rows,
            bytes_accessed=8 * channels * gate_rows * pulses,
            transcendentals=0,
        ),
        name="form_spectrum",
    )(rows, table, raw_echo, next_rows)


def select_kernel(bins_ref, used_ref, gates_ref, *refs, pack):
    *spectrum_refs, out_ref, listed = refs
    gate_rows = spectrum_refs[0].shape[2]
    owners, groups, rows, width = out_ref.shape
    total = owners * groups
    gate_index = lax.broadcasted_iota(jnp.int32, (pack * gate_rows, width), 0)
    unroll = math.gcd(total, 4)

    def list_group(group, count):
        used = used_ref[group]
        listed[count] = group

        @pl.when(used == 0)
        def _():
            out_ref[group // groups, group % groups] = jnp.zeros((rows, width), BF16)

        return count + used

    count = lax.fori_loop(0, total, list_group, 0)
    for extra in range(unroll):
        listed[count + extra] = listed[0]

    def some_groups(step, carry):
        for inner in range(unroll):
            group = listed[step * unroll + inner]
            chooser = jnp.where(gate_index == gates_ref[pl.ds(group, 1), :], 1.0, 0.0)
            bins = [bins_ref[group * pack + part] for part in range(pack)]
            spectra = jnp.concatenate(
                [jnp.concatenate([ref[b] for b in bins], axis=1) for ref in spectrum_refs], axis=0
            )
            picked = jnp.dot(spectra, chooser.astype(BF16), preferred_element_type=F32)
            out_ref[group // groups, group % groups] = picked.astype(BF16)
        return carry

    lax.fori_loop(0, (count + unroll - 1) // unroll, some_groups, 0)


def select_gates(spectra, slot_bins, used, slot_gates, owners, pack):
    rows = sum(spectrum.shape[1] for spectrum in spectra)
    gate_rows = spectra[0].shape[2]
    groups = slot_bins.shape[0] // owners // pack
    width = slot_gates.shape[-1]
    return pl.pallas_call(
        functools.partial(select_kernel, pack=pack),
        out_shape=jax.ShapeDtypeStruct((owners, groups, rows, width), BF16),
        in_specs=[pl.BlockSpec(memory_space=pltpu.SMEM)] * 2
        + [pl.BlockSpec(memory_space=pltpu.VMEM)] * (1 + len(spectra)),
        out_specs=pl.BlockSpec(memory_space=pltpu.VMEM),
        scratch_shapes=[pltpu.SMEM((owners * groups + 8,), jnp.int32)],
        compiler_params=PARAMS,
        cost_estimate=pl.CostEstimate(
            flops=2 * slot_bins.shape[0] * rows * gate_rows * width,
            bytes_accessed=owners * groups * rows * width * 2,
            transcendentals=0,
        ),
        name="select_gates",
    )(slot_bins, used, slot_gates, *spectra)


def beam_kernel(me_ref, weights_ref, arrived_ref, *refs, ranges):
    out_refs = refs[-ranges:]
    sources, groups, rows, width = arrived_ref.shape
    share = groups // ranges
    for shift, out_ref in enumerate(out_refs):
        lead = lax.rem(me_ref[0] + shift, ranges) * share
        packed = jnp.concatenate(
            [arrived_ref[:, lead + g].reshape(sources * rows, width) for g in range(share)], axis=1
        )
        beams = lax.dot_general(
            weights_ref[...], packed, (((0,), (0,)), ((), ())), preferred_element_type=F32
        ).astype(BF16)
        for g in range(share):
            out_ref[g] = beams[:, g * width : (g + 1) * width]


def form_beams(arrived, weights, me, ranges, earlier):
    _, groups, _, width = arrived.shape
    shape = (groups // ranges, weights.shape[1], width)
    return pl.pallas_call(
        functools.partial(beam_kernel, ranges=ranges),
        out_shape=[jax.ShapeDtypeStruct(shape, BF16)] * ranges,
        in_specs=[
            pl.BlockSpec(memory_space=pltpu.SMEM),
            pl.BlockSpec(memory_space=pltpu.VMEM),
            pl.BlockSpec(memory_space=pltpu.VMEM),
        ]
        + [pl.BlockSpec(memory_space=pl.ANY)] * len(earlier),
        out_specs=[pl.BlockSpec(memory_space=pltpu.VMEM)] * ranges,
        compiler_params=PARAMS,
        cost_estimate=pl.CostEstimate(
            flops=2 * arrived.size * weights.shape[1],
            bytes_accessed=arrived.size * 2,
            transcendentals=0,
        ),
        name="form_beams",
    )(me, weights, arrived, *earlier)


def exchange(arrays, axis):
    count = len(arrays)
    moved = [arrays[0]]
    for shift in range(1, count):
        pairs = [(i, (i + shift) % count) for i in range(count)]
        moved.append(lax.ppermute(arrays[shift], axis, pairs))
    return moved


def split_terms(array):
    high = array.astype(BF16)
    return high, (array - high.astype(F32)).astype(BF16)


def left_terms(array):
    high, low = split_terms(array)
    high, low = high.astype(F32), low.astype(F32)
    return jnp.concatenate([high, high, low], axis=0).T.astype(BF16)


def right_terms(array):
    high, low = split_terms(array)
    return jnp.concatenate([high, low, high], axis=0)


def product(left, right):
    return jnp.dot(left, right, preferred_element_type=F32)


def loaded_covariance(beams, pivot_row, part, pack, count_rows):
    dof = pivot_row.shape[1]
    width = beams[0].shape[1] // pack
    hot = lax.broadcasted_iota(jnp.int32, (dof, dof), 0) == pivot_row
    hot = jnp.where(hot, 1.0, 0.0).astype(BF16)
    own = jnp.concatenate([b[:, part * width : (part + 1) * width] for b in beams], axis=1)
    picked = [
        lax.dot_general(
            hot,
            own[half * dof : (half + 1) * dof],
            (((0,), (0,)), ((), ())),
            preferred_element_type=F32,
        )
        for half in range(2)
    ]
    upper = jnp.concatenate([picked[0], picked[1]], axis=1).astype(BF16)
    lower = jnp.concatenate([picked[1], -picked[0]], axis=1).astype(BF16)
    stacked = jnp.concatenate([upper, lower], axis=0)
    gram = lax.dot_general(
        stacked, stacked, (((1,), (1,)), ((), ())), preferred_element_type=F32
    )
    return gram * (1.0 / count_rows)


def lane_spread(piece, lane):
    return jnp.broadcast_to(piece[:, lane : lane + 1], piece.shape)


def refined_reciprocal(value):
    guess = pl.reciprocal(value, approx=True)
    return guess * (2.0 - value * guess)


def eliminate(rows, lead):
    scales = []
    for first in range(0, PANEL, 8):
        span = range(first, first + 8)
        small = {(i, j): lane_spread(rows[i][0], lead + j) for i in span for j in span if j >= i}
        for t in range(first, first + 8, 2):
            u = t + 1
            inverse = refined_reciprocal(small[t, t])
            cross = small[t, t] * small[u, u] - small[t, u] * small[t, u]
            second = refined_reciprocal(cross) * small[t, t]
            scales += [lax.rsqrt(small[t, t]), lax.rsqrt(cross * inverse)]
            factor = small[t, u] * inverse
            for j in range(u + 1, first + 8):
                small[u, j] = small[u, j] - factor * small[t, j]
            rows[u] = [x - factor * y for x, y in zip(rows[u], rows[t])]
            for i in range(u + 1, first + 8):
                one, two = small[t, i] * inverse, small[u, i] * second
                for j in range(i, first + 8):
                    small[i, j] = small[i, j] - one * small[t, j] - two * small[u, j]
                rows[i] = [
                    x - one * y - two * z for x, y, z in zip(rows[i], rows[t], rows[u])
                ]
        for t in span:
            rows[t] = [x * scales[t] for x in rows[t]]
        for i in range(first + 8, PANEL):
            for t in span:
                factor = lane_spread(rows[t][0], lead + i)
                rows[i] = [x - factor * y for x, y in zip(rows[i], rows[t])]
    return rows


def factor_kernel(me_ref, pivots_ref, *refs, ranges, pack, count_rows):
    beams_refs, out_refs = refs[:ranges], refs[ranges : 2 * ranges]
    arriving, leaving, *work = refs[2 * ranges :]
    slots = len(work)
    order = work[0].shape[0]
    height = arriving.shape[1] // PANEL

    row = lax.broadcasted_iota(jnp.int32, (LANES, LANES), 0)
    col = lax.broadcasted_iota(jnp.int32, (LANES, LANES), 1)
    loading = jnp.where(row == col, LOADING, 0.0)
    for slot in range(slots):
        group, part = divmod(slot, pack)
        work[slot][...] = loaded_covariance(
            [ref[group] for ref in beams_refs],
            pivots_ref[slot : slot + 1, :],
            part,
            pack,
            count_rows,
        )
        for start in range(0, order, LANES):
            work[slot][start : start + LANES, start : start + LANES] += loading

    eights = range(0, PANEL, 8)

    def spread_out(slot, rows):
        for i in eights:
            for w in range(rows.shape[1] // LANES):
                piece = rows[i : i + 8, w * LANES : (w + 1) * LANES]
                arriving[w, pl.ds(i * height + slot, 8, stride=height), :] = piece

    for slot in range(slots):
        spread_out(slot, work[slot][:PANEL, :])
    for start in range(0, order, LANES):
        chunks = (order - start) // LANES
        stop = start + LANES
        delayed = None
        for lead in range(0, LANES, PANEL):
            base, after = start + lead, lead + PANEL
            rows = [
                [arriving[w, t * height : (t + 1) * height, :] for w in range(chunks)]
                for t in range(PANEL)
            ]
            if delayed is not None and after < LANES:
                for slot in range(slots):
                    left, right = delayed[slot]
                    work[slot][start + after : stop, start:] -= product(left[after:], right)
            rows = eliminate(rows, lead)
            for t in range(PANEL):
                for w in range(chunks):
                    leaving[w, t * height : (t + 1) * height, :] = rows[t][w]
            delayed = []
            for slot in range(slots):
                parts = []
                for w in range(chunks):
                    pieces = [
                        leaving[w, pl.ds(i * height + slot, 8, stride=height), :] for i in eights
                    ]
                    parts.append(jnp.concatenate(pieces, axis=0))
                panel = jnp.concatenate(parts, axis=1)
                work[slot][base : base + PANEL, start:] = panel
                if after < LANES:
                    left, right = left_terms(parts[0]), right_terms(panel)
                    ready = work[slot][base + PANEL : base + 2 * PANEL, start:]
                    spread_out(slot, ready - product(left[after : after + PANEL], right))
                    delayed.append((left, right))
        if chunks > 1:
            terms = []
            for slot in range(slots):
                done = work[slot][start:stop, stop:]
                left = jnp.concatenate(
                    [left_terms(done[:, w * LANES : (w + 1) * LANES]) for w in range(chunks - 1)],
                    axis=0,
                )
                right = right_terms(done)
                ready = work[slot][stop : stop + PANEL, stop:] - product(left[:PANEL], right)
                spread_out(slot, ready)
                terms.append((left, right))
            for slot in range(slots):
                left, right = terms[slot]
                work[slot][stop + PANEL :, stop:] -= product(left[PANEL:], right)

    share = order // ranges
    row = lax.broadcasted_iota(jnp.int32, (share, order), 0)
    col = lax.broadcasted_iota(jnp.int32, (share, order), 1)
    for shift, out_ref in enumerate(out_refs):
        lead = pl.multiple_of(lax.rem(me_ref[0] + shift, ranges) * share, math.gcd(share, 16))
        upper = col >= row + lead
        for slot in range(slots):
            piece = work[slot][pl.ds(lead, share), :]
            out_ref[slot] = jnp.where(upper, piece, 0.0).astype(out_ref.dtype)


def factor_slots(beams, pivot_rows, me, pack, count_rows):
    ranges = len(beams)
    slots, dof = pivot_rows.shape
    order = 2 * dof
    height = -(-slots // 8) * 8
    return pl.pallas_call(
        functools.partial(factor_kernel, ranges=ranges, pack=pack, count_rows=count_rows),
        out_shape=[jax.ShapeDtypeStruct((slots, order // ranges, order), BF16)] * ranges,
        in_specs=[pl.BlockSpec(memory_space=pltpu.SMEM)]
        + [pl.BlockSpec(memory_space=pltpu.VMEM)] * (1 + ranges),
        out_specs=[pl.BlockSpec(memory_space=pltpu.VMEM)] * ranges,
        scratch_shapes=[pltpu.VMEM((order // LANES, PANEL * height, LANES), F32)] * 2
        + [pltpu.VMEM((order, order), F32) for _ in range(slots)],
        compiler_params=PARAMS,
        cost_estimate=pl.CostEstimate(
            flops=slots * order**3,
            bytes_accessed=ranges * beams[0].size * 2,
            transcendentals=0,
        ),
        name="factor_slots",
    )(me, pivot_rows, *beams)


def place_kernel(place_ref, *refs, ranges, parts):
    *in_refs, out_ref = refs
    share_slots = out_ref.shape[0] // ranges
    for shift in range(ranges):
        lead = lax.rem(place_ref[0] + (ranges - shift), ranges) * share_slots
        for index, (first, count) in enumerate(parts):
            ref = in_refs[index * ranges + shift]
            for i in range(count):
                slot = lead + first + i
                keep = jnp.broadcast_to(slot < place_ref[1], out_ref.shape[1:])
                out_ref[slot] = jnp.where(keep, ref[i].astype(F32), 0.0)


def place_rows(place, done, parts, most_slots):
    ranges = len(done[0])
    arrays = [array for part in done for array in part]
    return pl.pallas_call(
        functools.partial(place_kernel, ranges=ranges, parts=parts),
        out_shape=jax.ShapeDtypeStruct((most_slots,) + arrays[0].shape[1:], F32),
        in_specs=[pl.BlockSpec(memory_space=pltpu.SMEM)]
        + [pl.BlockSpec(memory_space=pltpu.VMEM)] * len(arrays),
        out_specs=pl.BlockSpec(memory_space=pltpu.VMEM),
        compiler_params=PARAMS,
        name="place_rows",
    )(place, *arrays)


def slot_parts(share_slots, pack):
    head = share_slots - pack
    return [(0, head), (head, pack)] if head > 0 else [(0, share_slots)]


def local(raw_echo, replica, beam_weights, pivots, owner_counts, train_gates):
    ch_local = raw_echo.shape[1]
    gate_rows = raw_echo.shape[2]
    pulse_count = raw_echo.shape[3]
    tap_count = replica.shape[1]
    train_local = train_gates.shape[1]
    owners = lax.axis_size("dop")
    ranges = lax.axis_size("rng")
    most_slots = 2 * (pulse_count // owners)
    share_slots = most_slots // ranges
    pack = max(1, min(LANES // train_local, share_slots))

    chunks = max(1, min(4, ch_local // 16))
    chunk_rows = ch_local // chunks
    rim = -(-(tap_count - 1) // 16) * 16
    filters = filter_rows(replica, gate_rows)
    table = doppler_table(pulse_count).transpose(0, 3, 1, 2)
    table = table.reshape(2 * pulse_count, -1).astype(BF16)
    following = [shifted(rim_rows(raw_echo, rim, c, chunks), "rng", -1) for c in range(chunks)]
    spectra = [
        form_spectrum(filters, table, raw_echo, following[c], c, chunks) for c in range(chunks)
    ]

    starts = jnp.cumsum(owner_counts, dtype=jnp.int32) - owner_counts
    me = lax.axis_index("dop")
    my_start = lax.dynamic_index_in_dim(starts, me, 0, keepdims=False)
    my_count = lax.dynamic_index_in_dim(owner_counts, me, 0, keepdims=False)
    my_range = lax.axis_index("rng").astype(jnp.int32)
    my_lead = my_range * share_slots
    local_gates = train_gates % gate_rows
    count_rows = float(train_local * ranges)

    dof = beam_weights.shape[2]
    real_part, imag_part = beam_weights.reshape(2, owners, chunks, chunk_rows, dof)
    weights = jnp.stack(
        [
            jnp.concatenate([real_part, -imag_part], axis=3),
            jnp.concatenate([imag_part, real_part], axis=3),
        ],
        axis=2,
    ).reshape(-1, 2 * dof)

    lead_slots = jnp.arange(ranges, dtype=jnp.int32) * share_slots
    parts = slot_parts(share_slots, pack)
    sent, waiting = [], []
    for first, count in parts:
        some = first + jnp.arange(count, dtype=jnp.int32)
        slots = (lead_slots[:, None] + some[None, :]).reshape(-1)
        bins = jnp.minimum(starts[:, None] + slots[None, :], pulse_count - 1).reshape(-1)
        gates = jnp.take(local_gates, bins, axis=0).reshape(-1, pack, train_local)
        gates = (gates + gate_rows * jnp.arange(pack, dtype=jnp.int32)[:, None]).reshape(
            -1, pack * train_local
        )
        used = (slots[None, ::pack] < owner_counts[:, None]).astype(jnp.int32).reshape(-1)
        outgoing = select_gates(spectra, bins, used, gates, owners, pack)
        waiting.append(outgoing)
        sent.append(lax.all_to_all(outgoing, "dop", split_axis=0, concat_axis=0, tiled=True))
    done, earlier = [], waiting[1:]
    for (first, count), arrived in zip(parts, sent):
        beams = exchange(form_beams(arrived, weights, my_range[None], ranges, earlier), "rng")
        bins = my_start + my_lead + first + jnp.arange(count, dtype=jnp.int32)
        my_pivots = jnp.take(pivots, jnp.minimum(bins, pulse_count - 1), axis=0)
        factors = factor_slots(beams, my_pivots, my_range[None], pack, count_rows)
        earlier = factors[:1]
        done.append(exchange(factors, "rng"))
    return place_rows(jnp.stack([my_range, my_count]), done, parts, most_slots)


def solution(mesh):
    return jax.shard_map(
        local,
        mesh=mesh,
        in_specs=(P(None, "dop", "rng", None), P(), P(), P(), P(), P(None, "rng")),
        out_specs=P("dop", "rng", None),
        check_vma=False,
    )
```

```python
import functools
import math

import jax
import jax.numpy as jnp
from jax import lax
from jax.experimental import pallas as pl
from jax.experimental.pallas import tpu as pltpu
from jax.sharding import PartitionSpec as P

LOADING = 0.25
LANES = 128
PANEL = 32
BF16 = jnp.bfloat16
F32 = jnp.float32
PARAMS = pltpu.CompilerParams(vmem_limit_bytes=48 * 1024 * 1024)


def shifted(array, axis, by):
    count = lax.axis_size(axis)
    pairs = [(i, i + by) for i in range(count) if 0 <= i + by < count]
    return lax.ppermute(array, axis, pairs)


def complex_block(real_part, imag_part):
    upper_row = jnp.stack([real_part, imag_part])
    lower_row = jnp.stack([-imag_part, real_part])
    return jnp.stack([upper_row, lower_row])


def doppler_table(pulse_count):
    pulse_index = jnp.arange(pulse_count, dtype=jnp.int32)
    phase_index = pulse_index[:, None] * pulse_index[None, :] % pulse_count
    angle_table = phase_index.astype(jnp.float32) * (2.0 * math.pi / pulse_count)
    norm_scale = 1.0 / math.sqrt(pulse_count)
    return complex_block(jnp.cos(angle_table) * norm_scale, jnp.sin(angle_table) * norm_scale)


def filter_kernel(replica_ref, out_ref):
    gate_rows, span = out_ref.shape[0] // 2, replica_ref.shape[1]
    banded = [
        pltpu.roll(
            jnp.broadcast_to(replica_ref[part : part + 1, :], (gate_rows, span)),
            0,
            1,
            stride=1,
            stride_axis=0,
        )
        for part in range(2)
    ]
    out_ref[:gate_rows, :span] = banded[0].astype(BF16)
    out_ref[:gate_rows, span:] = banded[1].astype(BF16)
    out_ref[gate_rows:, :span] = (-banded[1]).astype(BF16)
    out_ref[gate_rows:, span:] = banded[0].astype(BF16)


def filter_rows(replica, gate_rows):
    tap_count = replica.shape[1]
    span = -(-(gate_rows + tap_count) // LANES) * LANES
    return pl.pallas_call(
        filter_kernel,
        out_shape=jax.ShapeDtypeStruct((2 * gate_rows, 2 * span), BF16),
        in_specs=[pl.BlockSpec(memory_space=pltpu.VMEM)],
        out_specs=pl.BlockSpec(memory_space=pltpu.VMEM),
        compiler_params=PARAMS,
        name="filter_rows",
    )(jnp.pad(replica, ((0, 0), (0, span - tap_count))))


def rim_kernel(echo_ref, out_ref):
    out_ref[...] = echo_ref[...].astype(BF16)


def rim_rows(raw_echo, rim, chunk, chunks):
    _, ch_local, _, pulses = raw_echo.shape
    shape = (2, ch_local // chunks, rim, pulses)
    return pl.pallas_call(
        rim_kernel,
        out_shape=jax.ShapeDtypeStruct(shape, BF16),
        grid=(1,),
        in_specs=[pl.BlockSpec(shape, lambda i: (0, chunk, 0, 0))],
        out_specs=pl.BlockSpec(shape, lambda i: (0, 0, 0, 0)),
        compiler_params=PARAMS,
        name="rim_rows",
    )(raw_echo)


def spectrum_kernel(rows_ref, table_ref, own_ref, next_ref, out_ref, turned):
    step = pl.program_id(0)
    _, channels, gate_rows, pulses = own_ref.shape
    bins, height, _ = out_ref.shape
    rim = next_ref.shape[2]
    span = rows_ref.shape[1] // 2
    each = range(channels)
    samples = []
    for part in range(2):
        samples += [
            jnp.concatenate([own_ref[part, c] for c in each], axis=1).astype(BF16),
            jnp.concatenate([next_ref[part, c] for c in each], axis=1),
        ]
        if span > gate_rows + rim:
            samples.append(jnp.zeros((span - gate_rows - rim, channels * pulses), BF16))
    samples = jnp.concatenate(samples, axis=0)
    matched = jnp.dot(rows_ref[...], samples, preferred_element_type=F32).astype(BF16)
    halves = [matched[:gate_rows], matched[gate_rows:]]
    stacked = jnp.concatenate(
        [
            jnp.concatenate([half[:, c * pulses : (c + 1) * pulses] for half in halves], axis=1)
            for c in each
        ],
        axis=0,
    )
    spectra = lax.dot_general(
        table_ref[...], stacked, (((1,), (1,)), ((), ())), preferred_element_type=F32
    )
    for part in range(2):
        for c in each:
            place = part * (height // 2) + step * channels + c
            turned[pl.ds(place, bins, stride=height), :] = spectra[
                part * bins : (part + 1) * bins, c * gate_rows : (c + 1) * gate_rows
            ]

    @pl.when(step == pl.num_programs(0) - 1)
    def _():
        out_ref[...] = turned[...].astype(BF16).reshape(out_ref.shape)


def form_spectrum(rows, table, raw_echo, next_rows, chunk, chunks):
    _, ch_local, gate_rows, pulses = raw_echo.shape
    channels = ch_local // chunks
    step = math.gcd(channels, 8)
    steps = channels // step
    height = 2 * channels
    bins = table.shape[0] // 2
    return pl.pallas_call(
        spectrum_kernel,
        out_shape=jax.ShapeDtypeStruct((bins, height, gate_rows), BF16),
        grid=(steps,),
        in_specs=[
            pl.BlockSpec(rows.shape, lambda i: (0, 0)),
            pl.BlockSpec(table.shape, lambda i: (0, 0)),
            pl.BlockSpec((2, step, gate_rows, pulses), lambda i: (0, chunk * steps + i, 0, 0)),
            pl.BlockSpec((2, step) + next_rows.shape[2:], lambda i: (0, i, 0, 0)),
        ],
        out_specs=pl.BlockSpec((bins, height, gate_rows), lambda i: (0, 0, 0)),
        scratch_shapes=[pltpu.VMEM((bins * height, gate_rows), F32)],
        compiler_params=PARAMS,
        cost_estimate=pl.CostEstimate(
            flops=2 * rows.size * channels * pulses + 2 * table.size * channels * gate_rows,
            bytes_accessed=8 * channels * gate_rows * pulses,
            transcendentals=0,
        ),
        name="form_spectrum",
    )(rows, table, raw_echo, next_rows)


def owner_count(index_ref, owner):
    return index_ref[2 + owner]


def owner_start(index_ref, owner, owners):
    return index_ref[2 + owners + owner]


def select_kernel(index_ref, gates_ref, *refs, first, share_slots, pack, ranges):
    *spectrum_refs, out_ref = refs
    bin_count, height, gate_rows = spectrum_refs[0].shape
    owners, groups, rows, width = out_ref.shape
    half = height // 2
    share = groups // ranges
    gate_index = lax.broadcasted_iota(jnp.int32, (pack * gate_rows, width), 0)
    part_index = lax.broadcasted_iota(jnp.int32, (1, width), 1) // (width // pack)

    def one_run(run, carry):
        owner, block = run // ranges, run % ranges
        lead = block * share_slots + first
        used = lead < owner_count(index_ref, owner)

        @pl.when(used)
        def _():
            for inner in range(share):
                slot = owner_start(index_ref, owner, owners) + lead + inner * pack
                bins = [jnp.minimum(slot + part, bin_count - 1) for part in range(pack)]
                gates = gates_ref[pl.ds(bins[0], 1), :]
                for part in range(1, pack):
                    gates = jnp.where(part_index == part, gates_ref[pl.ds(bins[part], 1), :], gates)
                chooser = jnp.where(gate_index == gates, 1.0, 0.0).astype(BF16)
                spectra = jnp.concatenate(
                    [
                        jnp.concatenate([ref[b, s * half : (s + 1) * half] for b in bins], axis=1)
                        for s in range(2)
                        for ref in spectrum_refs
                    ],
                    axis=0,
                )
                picked = jnp.dot(spectra, chooser, preferred_element_type=F32)
                out_ref[owner, block * share + inner] = picked.astype(BF16)

        @pl.when(jnp.logical_not(used))
        def _():
            for inner in range(share):
                out_ref[owner, block * share + inner] = jnp.zeros((rows, width), BF16)

        return carry

    lax.fori_loop(0, owners * ranges, one_run, 0)


def select_gates(spectra, index, gates, first, count, share_slots, owners, ranges, pack):
    rows = sum(spectrum.shape[1] for spectrum in spectra)
    gate_rows = spectra[0].shape[2]
    groups = ranges * count // pack
    width = gates.shape[1]
    return pl.pallas_call(
        functools.partial(
            select_kernel, first=first, share_slots=share_slots, pack=pack, ranges=ranges
        ),
        out_shape=jax.ShapeDtypeStruct((owners, groups, rows, width), BF16),
        in_specs=[pl.BlockSpec(memory_space=pltpu.SMEM)]
        + [pl.BlockSpec(memory_space=pltpu.VMEM)] * (1 + len(spectra)),
        out_specs=pl.BlockSpec(memory_space=pltpu.VMEM),
        compiler_params=PARAMS,
        cost_estimate=pl.CostEstimate(
            flops=2 * owners * groups * pack * rows * gate_rows * width,
            bytes_accessed=owners * groups * rows * width * 2,
            transcendentals=0,
        ),
        name="select_gates",
    )(index, gates, *spectra)


def beam_kernel(index_ref, weights_ref, arrived_ref, *refs, ranges):
    out_refs = refs[-ranges:]
    sources, groups, rows, width = arrived_ref.shape
    dof = weights_ref.shape[2]
    share = groups // ranges
    half = rows // 2
    for shift, out_ref in enumerate(out_refs):
        lead = lax.rem(index_ref[1] + shift, ranges) * share
        packed = jnp.concatenate(
            [
                arrived_ref[:, lead + g, s * half : (s + 1) * half].reshape(sources * half, width)
                for s in range(2)
                for g in range(share)
            ],
            axis=1,
        )
        by_real, by_imag = [
            lax.dot_general(
                weights_ref[part], packed, (((0,), (0,)), ((), ())), preferred_element_type=F32
            )
            for part in range(2)
        ]
        middle = share * width
        real_part = by_real[:, :middle] + by_imag[:, middle:]
        imag_part = by_real[:, middle:] - by_imag[:, :middle]
        for g in range(share):
            span = slice(g * width, (g + 1) * width)
            out_ref[g, :dof] = real_part[:, span].astype(BF16)
            out_ref[g, dof:] = imag_part[:, span].astype(BF16)


def form_beams(arrived, weights, index, ranges, earlier):
    _, groups, _, width = arrived.shape
    shape = (groups // ranges, 2 * weights.shape[2], width)
    return pl.pallas_call(
        functools.partial(beam_kernel, ranges=ranges),
        out_shape=[jax.ShapeDtypeStruct(shape, BF16)] * ranges,
        in_specs=[
            pl.BlockSpec(memory_space=pltpu.SMEM),
            pl.BlockSpec(memory_space=pltpu.VMEM),
            pl.BlockSpec(memory_space=pltpu.VMEM),
        ]
        + [pl.BlockSpec(memory_space=pl.ANY)] * len(earlier),
        out_specs=[pl.BlockSpec(memory_space=pltpu.VMEM)] * ranges,
        compiler_params=PARAMS,
        cost_estimate=pl.CostEstimate(
            flops=4 * arrived.size * weights.shape[2],
            bytes_accessed=arrived.size * 2,
            transcendentals=0,
        ),
        name="form_beams",
    )(index, weights, arrived, *earlier)


def exchange(arrays, axis):
    count = len(arrays)
    moved = [arrays[0]]
    for shift in range(1, count):
        pairs = [(i, (i + shift) % count) for i in range(count)]
        moved.append(lax.ppermute(arrays[shift], axis, pairs))
    return moved


def split_terms(array):
    high = array.astype(BF16)
    return high, (array - high.astype(F32)).astype(BF16)


def left_terms(array):
    high, low = split_terms(array)
    high, low = high.astype(F32), low.astype(F32)
    return jnp.concatenate([high, high, low], axis=0).T.astype(BF16)


def right_terms(array):
    high, low = split_terms(array)
    return jnp.concatenate([high, low, high], axis=0)


def product(left, right):
    return jnp.dot(left, right, preferred_element_type=F32)


def loaded_covariance(beams, pivot_row, part, pack, count_rows):
    dof = pivot_row.shape[1]
    width = beams[0].shape[1] // pack
    hot = lax.broadcasted_iota(jnp.int32, (dof, dof), 0) == pivot_row
    hot = jnp.where(hot, 1.0, 0.0).astype(BF16)
    own = jnp.concatenate([b[:, part * width : (part + 1) * width] for b in beams], axis=1)
    picked = [
        lax.dot_general(
            hot,
            own[half * dof : (half + 1) * dof],
            (((0,), (0,)), ((), ())),
            preferred_element_type=F32,
        )
        for half in range(2)
    ]
    upper = jnp.concatenate([picked[0], picked[1]], axis=1).astype(BF16)
    lower = jnp.concatenate([picked[1], -picked[0]], axis=1).astype(BF16)
    stacked = jnp.concatenate([upper, lower], axis=0)
    gram = lax.dot_general(
        stacked, stacked, (((1,), (1,)), ((), ())), preferred_element_type=F32
    )
    return gram * (1.0 / count_rows)


def lane_spread(piece, lane):
    return jnp.broadcast_to(piece[:, lane : lane + 1], piece.shape)


def refined_reciprocal(value):
    guess = pl.reciprocal(value, approx=True)
    return guess * (2.0 - value * guess)


def eliminate(rows, lead):
    scales = []
    for first in range(0, PANEL, 8):
        span = range(first, first + 8)
        small = {(i, j): lane_spread(rows[i][0], lead + j) for i in span for j in span if j >= i}
        for t in range(first, first + 8, 2):
            u = t + 1
            inverse = refined_reciprocal(small[t, t])
            cross = small[t, t] * small[u, u] - small[t, u] * small[t, u]
            second = refined_reciprocal(cross) * small[t, t]
            scales += [lax.rsqrt(small[t, t]), lax.rsqrt(cross * inverse)]
            factor = small[t, u] * inverse
            for j in range(u + 1, first + 8):
                small[u, j] = small[u, j] - factor * small[t, j]
            rows[u] = [x - factor * y for x, y in zip(rows[u], rows[t])]
            for i in range(u + 1, PANEL):
                if i < first + 8:
                    one, two = small[t, i] * inverse, small[u, i] * second
                    for j in range(i, first + 8):
                        small[i, j] = small[i, j] - one * small[t, j] - two * small[u, j]
                else:
                    one = lane_spread(rows[t][0], lead + i) * inverse
                    two = lane_spread(rows[u][0], lead + i) * second
                rows[i] = [
                    x - one * y - two * z for x, y, z in zip(rows[i], rows[t], rows[u])
                ]
    return [[x * scale for x in row] for row, scale in zip(rows, scales)]


def factor_kernel(index_ref, pivots_ref, *refs, first, share_slots, ranges, pack, count_rows):
    beams_refs, out_refs = refs[:ranges], refs[ranges : 2 * ranges]
    arriving, leaving, *work = refs[2 * ranges :]
    slots = len(work)
    order = work[0].shape[0]
    height = arriving.shape[1] // PANEL

    row = lax.broadcasted_iota(jnp.int32, (LANES, LANES), 0)
    col = lax.broadcasted_iota(jnp.int32, (LANES, LANES), 1)
    loading = jnp.where(row == col, LOADING, 0.0)
    owners = (index_ref.shape[0] - 2) // 2
    bin_lead = owner_start(index_ref, index_ref[0], owners) + index_ref[1] * share_slots + first
    for slot in range(slots):
        group, part = divmod(slot, pack)
        own_bin = jnp.minimum(bin_lead + slot, pivots_ref.shape[0] - 1)
        work[slot][...] = loaded_covariance(
            [ref[group] for ref in beams_refs],
            pivots_ref[pl.ds(own_bin, 1), :],
            part,
            pack,
            count_rows,
        )
        for start in range(0, order, LANES):
            work[slot][start : start + LANES, start : start + LANES] += loading

    eights = range(0, PANEL, 8)

    def spread_out(slot, rows):
        for i in eights:
            for w in range(rows.shape[1] // LANES):
                piece = rows[i : i + 8, w * LANES : (w + 1) * LANES]
                arriving[w, pl.ds(i * height + slot, 8, stride=height), :] = piece

    for slot in range(slots):
        spread_out(slot, work[slot][:PANEL, :])
    for start in range(0, order, LANES):
        chunks = (order - start) // LANES
        stop = start + LANES
        delayed = None
        for lead in range(0, LANES, PANEL):
            base, after = start + lead, lead + PANEL
            rows = [
                [arriving[w, t * height : (t + 1) * height, :] for w in range(chunks)]
                for t in range(PANEL)
            ]
            if delayed is not None and after < LANES:
                for slot in range(slots):
                    left, right = delayed[slot]
                    work[slot][start + after : stop, start:] -= product(left[after:], right)
            rows = eliminate(rows, lead)
            for t in range(PANEL):
                for w in range(chunks):
                    leaving[w, t * height : (t + 1) * height, :] = rows[t][w]
            delayed = []
            for slot in range(slots):
                parts = []
                for w in range(chunks):
                    pieces = [
                        leaving[w, pl.ds(i * height + slot, 8, stride=height), :] for i in eights
                    ]
                    parts.append(jnp.concatenate(pieces, axis=0))
                panel = jnp.concatenate(parts, axis=1)
                work[slot][base : base + PANEL, start:] = panel
                if after < LANES:
                    left, right = left_terms(parts[0]), right_terms(panel)
                    ready = work[slot][base + PANEL : base + 2 * PANEL, start:]
                    spread_out(slot, ready - product(left[after : after + PANEL], right))
                    delayed.append((left, right))
        if chunks > 1:
            terms = []
            for slot in range(slots):
                done = work[slot][start:stop, stop:]
                left = jnp.concatenate(
                    [left_terms(done[:, w * LANES : (w + 1) * LANES]) for w in range(chunks - 1)],
                    axis=0,
                )
                right = right_terms(done)
                ready = work[slot][stop : stop + PANEL, stop:] - product(left[:PANEL], right)
                spread_out(slot, ready)
                terms.append((left, right))
            for slot in range(slots):
                left, right = terms[slot]
                work[slot][stop + PANEL :, stop:] -= product(left[PANEL:], right)

    share = order // ranges
    row = lax.broadcasted_iota(jnp.int32, (share, order), 0)
    col = lax.broadcasted_iota(jnp.int32, (share, order), 1)
    for shift, out_ref in enumerate(out_refs):
        lead = pl.multiple_of(lax.rem(index_ref[1] + shift, ranges) * share, math.gcd(share, 16))
        upper = col >= row + lead
        for slot in range(slots):
            piece = work[slot][pl.ds(lead, share), :]
            out_ref[slot] = jnp.where(upper, piece, 0.0).astype(out_ref.dtype)


def factor_slots(beams, pivots, index, first, slots, share_slots, pack, count_rows):
    ranges = len(beams)
    order = beams[0].shape[1]
    height = -(-slots // 8) * 8
    return pl.pallas_call(
        functools.partial(
            factor_kernel,
            first=first,
            share_slots=share_slots,
            ranges=ranges,
            pack=pack,
            count_rows=count_rows,
        ),
        out_shape=[jax.ShapeDtypeStruct((slots, order // ranges, order), BF16)] * ranges,
        in_specs=[pl.BlockSpec(memory_space=pltpu.SMEM)]
        + [pl.BlockSpec(memory_space=pltpu.VMEM)] * (1 + ranges),
        out_specs=[pl.BlockSpec(memory_space=pltpu.VMEM)] * ranges,
        scratch_shapes=[pltpu.VMEM((order // LANES, PANEL * height, LANES), F32)] * 2
        + [pltpu.VMEM((order, order), F32) for _ in range(slots)],
        compiler_params=PARAMS,
        cost_estimate=pl.CostEstimate(
            flops=slots * order**3,
            bytes_accessed=ranges * beams[0].size * 2,
            transcendentals=0,
        ),
        name="factor_slots",
    )(index, pivots, *beams)


def place_kernel(index_ref, *refs, ranges, parts):
    *in_refs, out_ref = refs
    share_slots = out_ref.shape[0] // ranges
    for shift in range(ranges):
        lead = lax.rem(index_ref[1] + (ranges - shift), ranges) * share_slots
        for index, (first, count) in enumerate(parts):
            ref = in_refs[index * ranges + shift]
            for i in range(count):
                slot = lead + first + i
                keep = jnp.broadcast_to(slot < owner_count(index_ref, index_ref[0]), out_ref.shape[1:])
                out_ref[slot] = jnp.where(keep, ref[i].astype(F32), 0.0)


def place_rows(index, done, parts, most_slots):
    ranges = len(done[0])
    arrays = [array for part in done for array in part]
    return pl.pallas_call(
        functools.partial(place_kernel, ranges=ranges, parts=parts),
        out_shape=jax.ShapeDtypeStruct((most_slots,) + arrays[0].shape[1:], F32),
        in_specs=[pl.BlockSpec(memory_space=pltpu.SMEM)]
        + [pl.BlockSpec(memory_space=pltpu.VMEM)] * len(arrays),
        out_specs=pl.BlockSpec(memory_space=pltpu.VMEM),
        compiler_params=PARAMS,
        name="place_rows",
    )(index, *arrays)


def slot_parts(share_slots, pack):
    halves = 2 if share_slots % (2 * pack) == 0 else 1
    count = share_slots // halves
    return [(i * count, count) for i in range(halves)]


def local(raw_echo, replica, beam_weights, pivots, owner_counts, train_gates):
    ch_local = raw_echo.shape[1]
    gate_rows = raw_echo.shape[2]
    pulse_count = raw_echo.shape[3]
    tap_count = replica.shape[1]
    train_local = train_gates.shape[1]
    owners = lax.axis_size("dop")
    ranges = lax.axis_size("rng")
    most_slots = 2 * (pulse_count // owners)
    share_slots = most_slots // ranges
    pack = max(1, min(LANES // train_local, share_slots))

    chunks = max(1, min(4, ch_local // 16))
    chunk_rows = ch_local // chunks
    rim = -(-(tap_count - 1) // 16) * 16
    filters = filter_rows(replica, gate_rows)
    table = doppler_table(pulse_count).transpose(0, 3, 1, 2)
    table = table.reshape(2 * pulse_count, -1).astype(BF16)
    following = [shifted(rim_rows(raw_echo, rim, c, chunks), "rng", -1) for c in range(chunks)]
    spectra = [
        form_spectrum(filters, table, raw_echo, following[c], c, chunks) for c in range(chunks)
    ]

    starts = jnp.cumsum(owner_counts, dtype=jnp.int32) - owner_counts
    places = jnp.stack([lax.axis_index("dop"), lax.axis_index("rng")]).astype(jnp.int32)
    index = jnp.concatenate([places, owner_counts, starts])
    local_gates = train_gates % gate_rows
    gates = jnp.concatenate([local_gates + part * gate_rows for part in range(pack)], axis=1)
    count_rows = float(train_local * ranges)

    parts = slot_parts(share_slots, pack)
    outgoing = [
        select_gates(spectra, index, gates, first, count, share_slots, owners, ranges, pack)
        for first, count in parts
    ]
    sent = [
        lax.all_to_all(array, "dop", split_axis=0, concat_axis=0, tiled=True) for array in outgoing
    ]
    done, earlier = [], outgoing[1:]
    for (first, count), arrived in zip(parts, sent):
        beams = exchange(form_beams(arrived, beam_weights, index, ranges, earlier), "rng")
        factors = factor_slots(beams, pivots, index, first, count, share_slots, pack, count_rows)
        earlier = factors[:1]
        done.append(exchange(factors, "rng"))
    return place_rows(index, done, parts, most_slots)


def solution(mesh):
    return jax.shard_map(
        local,
        mesh=mesh,
        in_specs=(P(None, "dop", "rng", None), P(), P(), P(), P(), P(None, "rng")),
        out_specs=P("dop", "rng", None),
        check_vma=False,
    )
```

```python
import functools
import math

import jax
import jax.numpy as jnp
from jax import lax
from jax.experimental import pallas as pl
from jax.experimental.pallas import tpu as pltpu
from jax.sharding import PartitionSpec as P

LOADING = 0.25
LANES = 128
PANEL = 32
BF16 = jnp.bfloat16
F32 = jnp.float32
PARAMS = pltpu.CompilerParams(vmem_limit_bytes=48 * 1024 * 1024)


def shifted(array, axis, by):
    count = lax.axis_size(axis)
    pairs = [(i, i + by) for i in range(count) if 0 <= i + by < count]
    return lax.ppermute(array, axis, pairs)


def complex_block(real_part, imag_part):
    upper_row = jnp.stack([real_part, imag_part])
    lower_row = jnp.stack([-imag_part, real_part])
    return jnp.stack([upper_row, lower_row])


def doppler_table(pulse_count):
    pulse_index = jnp.arange(pulse_count, dtype=jnp.int32)
    phase_index = pulse_index[:, None] * pulse_index[None, :] % pulse_count
    angle_table = phase_index.astype(jnp.float32) * (2.0 * math.pi / pulse_count)
    norm_scale = 1.0 / math.sqrt(pulse_count)
    return complex_block(jnp.cos(angle_table) * norm_scale, jnp.sin(angle_table) * norm_scale)


def filter_kernel(replica_ref, out_ref):
    gate_rows, span = out_ref.shape[0] // 2, replica_ref.shape[1]
    banded = [
        pltpu.roll(
            jnp.broadcast_to(replica_ref[part : part + 1, :], (gate_rows, span)),
            0,
            1,
            stride=1,
            stride_axis=0,
        )
        for part in range(2)
    ]
    out_ref[:gate_rows, :span] = banded[0].astype(BF16)
    out_ref[:gate_rows, span:] = banded[1].astype(BF16)
    out_ref[gate_rows:, :span] = (-banded[1]).astype(BF16)
    out_ref[gate_rows:, span:] = banded[0].astype(BF16)


def filter_rows(replica, gate_rows):
    tap_count = replica.shape[1]
    span = -(-(gate_rows + tap_count) // LANES) * LANES
    return pl.pallas_call(
        filter_kernel,
        out_shape=jax.ShapeDtypeStruct((2 * gate_rows, 2 * span), BF16),
        in_specs=[pl.BlockSpec(memory_space=pltpu.VMEM)],
        out_specs=pl.BlockSpec(memory_space=pltpu.VMEM),
        compiler_params=PARAMS,
        name="filter_rows",
    )(jnp.pad(replica, ((0, 0), (0, span - tap_count))))


def rim_kernel(echo_ref, out_ref):
    out_ref[...] = echo_ref[...].astype(BF16)


def rim_rows(raw_echo, rim, chunk, chunks):
    _, ch_local, _, pulses = raw_echo.shape
    shape = (2, ch_local // chunks, rim, pulses)
    return pl.pallas_call(
        rim_kernel,
        out_shape=jax.ShapeDtypeStruct(shape, BF16),
        grid=(1,),
        in_specs=[pl.BlockSpec(shape, lambda i: (0, chunk, 0, 0))],
        out_specs=pl.BlockSpec(shape, lambda i: (0, 0, 0, 0)),
        compiler_params=PARAMS,
        name="rim_rows",
    )(raw_echo)


def spectrum_kernel(rows_ref, table_ref, own_ref, next_ref, out_ref, turned):
    step = pl.program_id(0)
    _, channels, gate_rows, pulses = own_ref.shape
    bins, height, _ = out_ref.shape
    rim = next_ref.shape[2]
    span = rows_ref.shape[1] // 2
    each = range(channels)
    samples = []
    for part in range(2):
        samples += [
            jnp.concatenate([own_ref[part, c] for c in each], axis=1).astype(BF16),
            jnp.concatenate([next_ref[part, c] for c in each], axis=1),
        ]
        if span > gate_rows + rim:
            samples.append(jnp.zeros((span - gate_rows - rim, channels * pulses), BF16))
    samples = jnp.concatenate(samples, axis=0)
    matched = jnp.dot(rows_ref[...], samples, preferred_element_type=F32).astype(BF16)
    halves = [matched[:gate_rows], matched[gate_rows:]]
    stacked = jnp.concatenate(
        [
            jnp.concatenate([half[:, c * pulses : (c + 1) * pulses] for half in halves], axis=1)
            for c in each
        ],
        axis=0,
    )
    spectra = lax.dot_general(
        table_ref[...], stacked, (((1,), (1,)), ((), ())), preferred_element_type=F32
    )
    for part in range(2):
        turned_part = jnp.stack(
            [
                spectra[part * bins : (part + 1) * bins, c * gate_rows : (c + 1) * gate_rows]
                for c in each
            ],
            axis=0,
        )
        place = pl.multiple_of(part * (height // 2) + step * channels, channels)
        turned[:, pl.ds(place, channels), :] = jnp.swapaxes(turned_part, 0, 1)

    @pl.when(step == pl.num_programs(0) - 1)
    def _():
        out_ref[...] = turned[...].astype(BF16)


def form_spectrum(rows, table, raw_echo, next_rows, chunk, chunks):
    _, ch_local, gate_rows, pulses = raw_echo.shape
    channels = ch_local // chunks
    step = math.gcd(channels, 8)
    steps = channels // step
    height = 2 * channels
    bins = table.shape[0] // 2
    return pl.pallas_call(
        spectrum_kernel,
        out_shape=jax.ShapeDtypeStruct((bins, height, gate_rows), BF16),
        grid=(steps,),
        in_specs=[
            pl.BlockSpec(rows.shape, lambda i: (0, 0)),
            pl.BlockSpec(table.shape, lambda i: (0, 0)),
            pl.BlockSpec((2, step, gate_rows, pulses), lambda i: (0, chunk * steps + i, 0, 0)),
            pl.BlockSpec((2, step) + next_rows.shape[2:], lambda i: (0, i, 0, 0)),
        ],
        out_specs=pl.BlockSpec((bins, height, gate_rows), lambda i: (0, 0, 0)),
        scratch_shapes=[pltpu.VMEM((bins, height, gate_rows), F32)],
        compiler_params=PARAMS,
        cost_estimate=pl.CostEstimate(
            flops=2 * rows.size * channels * pulses + 2 * table.size * channels * gate_rows,
            bytes_accessed=8 * channels * gate_rows * pulses,
            transcendentals=0,
        ),
        name="form_spectrum",
    )(rows, table, raw_echo, next_rows)


def owner_count(index_ref, owner):
    return index_ref[2 + owner]


def owner_start(index_ref, owner, owners):
    return index_ref[2 + owners + owner]


def select_kernel(index_ref, gates_ref, *refs, owners, pack):
    *spectrum_refs, out_ref = refs
    bin_count, height, gate_rows = spectrum_refs[0].shape
    some, groups, _, width = out_ref.shape
    half = height // 2
    gate_index = lax.broadcasted_iota(jnp.int32, (pack * gate_rows, width), 0)
    part_index = lax.broadcasted_iota(jnp.int32, (1, width), 1) // (width // pack)
    for inner in range(some):
        start = owner_start(index_ref, pl.program_id(0) * some + inner, owners)
        for group in range(groups):
            bins = [
                jnp.minimum(start + group * pack + part, bin_count - 1) for part in range(pack)
            ]
            gates = gates_ref[pl.ds(bins[0], 1), :]
            for part in range(1, pack):
                gates = jnp.where(part_index == part, gates_ref[pl.ds(bins[part], 1), :], gates)
            chooser = jnp.where(gate_index == gates, 1.0, 0.0).astype(BF16)
            spectra = jnp.concatenate(
                [
                    jnp.concatenate([ref[b, s * half : (s + 1) * half] for b in bins], axis=1)
                    for s in range(2)
                    for ref in spectrum_refs
                ],
                axis=0,
            )
            picked = jnp.dot(spectra, chooser, preferred_element_type=F32)
            out_ref[inner, group] = picked.astype(BF16)


def select_gates(spectra, index, gates, most_slots, owners, pack):
    rows = sum(spectrum.shape[1] for spectrum in spectra)
    gate_rows = spectra[0].shape[2]
    groups = most_slots // pack
    width = gates.shape[1]
    return pl.pallas_call(
        functools.partial(select_kernel, owners=owners, pack=pack),
        out_shape=jax.ShapeDtypeStruct((owners, groups, rows, width), BF16),
        grid=(owners,),
        in_specs=[pl.BlockSpec(memory_space=pltpu.SMEM)]
        + [pl.BlockSpec(memory_space=pltpu.VMEM)] * (1 + len(spectra)),
        out_specs=pl.BlockSpec((1, groups, rows, width), lambda i: (i, 0, 0, 0)),
        compiler_params=PARAMS,
        cost_estimate=pl.CostEstimate(
            flops=2 * owners * groups * pack * rows * gate_rows * width,
            bytes_accessed=owners * groups * rows * width * 2,
            transcendentals=0,
        ),
        name="select_gates",
    )(index, gates, *spectra)


def beam_kernel(index_ref, weights_ref, arrived_ref, *out_refs, first):
    sources, groups, rows, width = arrived_ref.shape
    ranges, share = len(out_refs), out_refs[0].shape[0]
    dof = weights_ref.shape[2]
    half = rows // 2
    for shift, out_ref in enumerate(out_refs):
        lead = lax.rem(index_ref[1] + shift, ranges) * (groups // ranges) + first
        packed = jnp.concatenate(
            [
                arrived_ref[:, lead + g, s * half : (s + 1) * half].reshape(sources * half, width)
                for s in range(2)
                for g in range(share)
            ],
            axis=1,
        )
        by_real, by_imag = [
            lax.dot_general(
                weights_ref[part], packed, (((0,), (0,)), ((), ())), preferred_element_type=F32
            )
            for part in range(2)
        ]
        middle = share * width
        real_part = by_real[:, :middle] + by_imag[:, middle:]
        imag_part = by_real[:, middle:] - by_imag[:, :middle]
        for g in range(share):
            span = slice(g * width, (g + 1) * width)
            out_ref[g, :dof] = real_part[:, span].astype(BF16)
            out_ref[g, dof:] = imag_part[:, span].astype(BF16)


def form_beams(arrived, weights, index, ranges, first, count):
    sources, _, rows, width = arrived.shape
    shape = (count, 2 * weights.shape[2], width)
    return pl.pallas_call(
        functools.partial(beam_kernel, first=first),
        out_shape=[jax.ShapeDtypeStruct(shape, BF16)] * ranges,
        in_specs=[
            pl.BlockSpec(memory_space=pltpu.SMEM),
            pl.BlockSpec(memory_space=pltpu.VMEM),
            pl.BlockSpec(memory_space=pltpu.VMEM),
        ],
        out_specs=[pl.BlockSpec(memory_space=pltpu.VMEM)] * ranges,
        compiler_params=PARAMS,
        cost_estimate=pl.CostEstimate(
            flops=4 * ranges * count * sources * rows * width * weights.shape[2],
            bytes_accessed=arrived.size * 2,
            transcendentals=0,
        ),
        name="form_beams",
    )(index, weights, arrived)


def exchange(arrays, axis):
    count = len(arrays)
    moved = [arrays[0]]
    for shift in range(1, count):
        pairs = [(i, (i + shift) % count) for i in range(count)]
        moved.append(lax.ppermute(arrays[shift], axis, pairs))
    return moved


def split_terms(array):
    high = array.astype(BF16)
    return high, (array - high.astype(F32)).astype(BF16)


def left_terms(array):
    high, low = split_terms(array)
    high, low = high.astype(F32), low.astype(F32)
    return jnp.concatenate([high, high, low], axis=0).T.astype(BF16)


def right_terms(array):
    high, low = split_terms(array)
    return jnp.concatenate([high, low, high], axis=0)


def product(left, right):
    return jnp.dot(left, right, preferred_element_type=F32)


def loaded_covariance(beams, pivot_row, part, pack, count_rows):
    dof = pivot_row.shape[1]
    width = beams[0].shape[1] // pack
    hot = lax.broadcasted_iota(jnp.int32, (dof, dof), 0) == pivot_row
    hot = jnp.where(hot, 1.0, 0.0).astype(BF16)
    own = jnp.concatenate([b[:, part * width : (part + 1) * width] for b in beams], axis=1)
    picked = [
        lax.dot_general(
            hot,
            own[half * dof : (half + 1) * dof],
            (((0,), (0,)), ((), ())),
            preferred_element_type=F32,
        )
        for half in range(2)
    ]
    upper = jnp.concatenate([picked[0], picked[1]], axis=1).astype(BF16)
    lower = jnp.concatenate([picked[1], -picked[0]], axis=1).astype(BF16)
    stacked = jnp.concatenate([upper, lower], axis=0)
    gram = lax.dot_general(
        stacked, stacked, (((1,), (1,)), ((), ())), preferred_element_type=F32
    )
    return gram * (1.0 / count_rows)


def lane_spread(piece, lane):
    return jnp.broadcast_to(piece[:, lane : lane + 1], piece.shape)


def refined_reciprocal(value):
    guess = pl.reciprocal(value, approx=True)
    return guess * (2.0 - value * guess)


def eliminate(rows):
    scales = []
    for first in range(0, PANEL, 8):
        span = range(first, first + 8)
        small = {(i, j): lane_spread(rows[i][0], j) for i in span for j in span if j >= i}
        for t in range(first, first + 8, 2):
            u = t + 1
            inverse = refined_reciprocal(small[t, t])
            cross = small[t, t] * small[u, u] - small[t, u] * small[t, u]
            second = refined_reciprocal(cross) * small[t, t]
            scales += [lax.rsqrt(small[t, t]), lax.rsqrt(cross * inverse)]
            factor = small[t, u] * inverse
            for j in range(u + 1, first + 8):
                small[u, j] = small[u, j] - factor * small[t, j]
            rows[u] = [x - factor * y for x, y in zip(rows[u], rows[t])]
            for i in range(u + 1, first + 8):
                one, two = small[t, i] * inverse, small[u, i] * second
                for j in range(i, first + 8):
                    small[i, j] = small[i, j] - one * small[t, j] - two * small[u, j]
                rows[i] = [
                    x - one * y - two * z for x, y, z in zip(rows[i], rows[t], rows[u])
                ]
        for t in span:
            rows[t] = [x * scales[t] for x in rows[t]]
        for i in range(first + 8, PANEL):
            for t in span:
                factor = lane_spread(rows[t][0], i)
                rows[i] = [x - factor * y for x, y in zip(rows[i], rows[t])]
    return rows


def factor_kernel(
    index_ref, pivots_ref, *refs, first, share_slots, ranges, waits, pack, count_rows
):
    beams_refs, refs = refs[:ranges], refs[ranges + waits :]
    out_refs = refs[:ranges]
    arriving, leaving, *scratch = refs[ranges:]
    slots = len(scratch) // 3
    work, lefts, rights = scratch[:slots], scratch[slots : 2 * slots], scratch[2 * slots :]
    order = work[0].shape[0]
    height = arriving.shape[1] // PANEL

    row = lax.broadcasted_iota(jnp.int32, (LANES, LANES), 0)
    col = lax.broadcasted_iota(jnp.int32, (LANES, LANES), 1)
    loading = jnp.where(row == col, LOADING, 0.0)
    owners = (index_ref.shape[0] - 2) // 2
    bin_lead = owner_start(index_ref, index_ref[0], owners) + index_ref[1] * share_slots + first
    for slot in range(slots):
        group, part = divmod(slot, pack)
        own_bin = jnp.minimum(bin_lead + slot, pivots_ref.shape[0] - 1)
        work[slot][...] = loaded_covariance(
            [ref[group] for ref in beams_refs],
            pivots_ref[pl.ds(own_bin, 1), :],
            part,
            pack,
            count_rows,
        )
        for start in range(0, order, LANES):
            work[slot][start : start + LANES, start : start + LANES] += loading

    eights = range(0, PANEL, 8)
    column = lax.broadcasted_iota(jnp.int32, (LANES, 3 * PANEL), 0)

    def spread_out(slot, rows):
        for i in eights:
            for w in range(rows.shape[1] // LANES):
                piece = rows[i : i + 8, w * LANES : (w + 1) * LANES]
                arriving[w, pl.ds(i * height + slot, 8, stride=height), :] = piece

    for slot in range(slots):
        spread_out(slot, work[slot][:PANEL, :])
    for start in range(0, order, LANES):
        chunks = (order - start) // LANES
        stop = start + LANES
        for slot in range(slots):
            lefts[slot][...] = jnp.zeros_like(lefts[slot])
            rights[slot][...] = jnp.zeros_like(rights[slot])

        def one_panel(p, carry, start=start, stop=stop, chunks=chunks):
            back = p * PANEL
            base = pl.multiple_of(start + back, PANEL)
            ahead = pl.multiple_of(jnp.minimum(back + PANEL, LANES - PANEL), PANEL)
            following = pl.multiple_of(start + ahead, PANEL)
            for slot in range(slots):
                left = jnp.where(column >= back + PANEL, lefts[slot][...], 0.0).astype(BF16)
                work[slot][start:stop, start:] -= product(left, rights[slot][:, start:])
            rows = []
            for t in range(PANEL):
                pieces = [arriving[w, t * height : (t + 1) * height, :] for w in range(chunks)]
                pieces[0] = pltpu.roll(pieces[0], (LANES - back) % LANES, 1)
                rows.append(pieces)
            rows = eliminate(rows)
            for t in range(PANEL):
                rows[t][0] = pltpu.roll(rows[t][0], back, 1)
                for w in range(chunks):
                    leaving[w, t * height : (t + 1) * height, :] = rows[t][w]
            for slot in range(slots):
                parts = []
                for w in range(chunks):
                    pieces = [
                        leaving[w, pl.ds(i * height + slot, 8, stride=height), :] for i in eights
                    ]
                    parts.append(jnp.concatenate(pieces, axis=0))
                panel = jnp.concatenate(parts, axis=1)
                work[slot][pl.ds(base, PANEL), start:] = panel
                lefts[slot][...] = left_terms(parts[0]).astype(F32)
                right = right_terms(panel)
                rights[slot][:, start:] = right
                left = lefts[slot][pl.ds(ahead, PANEL), :].astype(BF16)
                spread_out(slot, work[slot][pl.ds(following, PANEL), start:] - product(left, right))
            return carry

        lax.fori_loop(0, LANES // PANEL, one_panel, 0)
        if chunks > 1:
            terms = []
            for slot in range(slots):
                done = work[slot][start:stop, stop:]
                left = jnp.concatenate(
                    [left_terms(done[:, w * LANES : (w + 1) * LANES]) for w in range(chunks - 1)],
                    axis=0,
                )
                right = right_terms(done)
                ready = work[slot][stop : stop + PANEL, stop:] - product(left[:PANEL], right)
                spread_out(slot, ready)
                terms.append((left, right))
            for slot in range(slots):
                left, right = terms[slot]
                work[slot][stop + PANEL :, stop:] -= product(left[PANEL:], right)

    share = order // ranges
    row = lax.broadcasted_iota(jnp.int32, (share, order), 0)
    col = lax.broadcasted_iota(jnp.int32, (share, order), 1)
    for shift, out_ref in enumerate(out_refs):
        lead = pl.multiple_of(lax.rem(index_ref[1] + shift, ranges) * share, math.gcd(share, 16))
        upper = col >= row + lead
        for slot in range(slots):
            piece = work[slot][pl.ds(lead, share), :]
            out_ref[slot] = jnp.where(upper, piece, 0.0).astype(out_ref.dtype)


def factor_slots(beams, pivots, index, first, slots, share_slots, pack, count_rows, earlier):
    ranges = len(beams)
    order = beams[0].shape[1]
    height = -(-slots // 8) * 8
    return pl.pallas_call(
        functools.partial(
            factor_kernel,
            first=first,
            share_slots=share_slots,
            ranges=ranges,
            waits=len(earlier),
            pack=pack,
            count_rows=count_rows,
        ),
        out_shape=[jax.ShapeDtypeStruct((slots, order // ranges, order), BF16)] * ranges,
        in_specs=[pl.BlockSpec(memory_space=pltpu.SMEM)]
        + [pl.BlockSpec(memory_space=pltpu.VMEM)] * (1 + ranges)
        + [pl.BlockSpec(memory_space=pl.ANY)] * len(earlier),
        out_specs=[pl.BlockSpec(memory_space=pltpu.VMEM)] * ranges,
        scratch_shapes=[pltpu.VMEM((order // LANES, PANEL * height, LANES), F32)] * 2
        + [pltpu.VMEM((order, order), F32) for _ in range(slots)]
        + [pltpu.VMEM((LANES, 3 * PANEL), F32) for _ in range(slots)]
        + [pltpu.VMEM((3 * PANEL, order), BF16) for _ in range(slots)],
        compiler_params=PARAMS,
        cost_estimate=pl.CostEstimate(
            flops=slots * order**3,
            bytes_accessed=ranges * beams[0].size * 2,
            transcendentals=0,
        ),
        name="factor_slots",
    )(index, pivots, *beams, *earlier)


def place_kernel(index_ref, *refs, ranges, parts):
    *in_refs, out_ref = refs
    share_slots = out_ref.shape[0] // ranges
    for shift in range(ranges):
        lead = lax.rem(index_ref[1] + (ranges - shift), ranges) * share_slots
        for index, (first, count) in enumerate(parts):
            ref = in_refs[index * ranges + shift]
            for i in range(count):
                slot = lead + first + i
                keep = jnp.broadcast_to(slot < owner_count(index_ref, index_ref[0]), out_ref.shape[1:])
                out_ref[slot] = jnp.where(keep, ref[i].astype(F32), 0.0)


def place_rows(index, done, parts, most_slots):
    ranges = len(done[0])
    arrays = [array for part in done for array in part]
    return pl.pallas_call(
        functools.partial(place_kernel, ranges=ranges, parts=parts),
        out_shape=jax.ShapeDtypeStruct((most_slots,) + arrays[0].shape[1:], F32),
        in_specs=[pl.BlockSpec(memory_space=pltpu.SMEM)]
        + [pl.BlockSpec(memory_space=pltpu.VMEM)] * len(arrays),
        out_specs=pl.BlockSpec(memory_space=pltpu.VMEM),
        compiler_params=PARAMS,
        name="place_rows",
    )(index, *arrays)


def slot_parts(share_slots, pack):
    head = share_slots - pack
    return [(0, head), (head, pack)] if head > 0 else [(0, share_slots)]


def local(raw_echo, replica, beam_weights, pivots, owner_counts, train_gates):
    ch_local = raw_echo.shape[1]
    gate_rows = raw_echo.shape[2]
    pulse_count = raw_echo.shape[3]
    tap_count = replica.shape[1]
    train_local = train_gates.shape[1]
    owners = lax.axis_size("dop")
    ranges = lax.axis_size("rng")
    most_slots = 2 * (pulse_count // owners)
    share_slots = most_slots // ranges
    pack = max(1, min(LANES // train_local, share_slots))

    chunks = max(1, min(4, ch_local // 16))
    chunk_rows = ch_local // chunks
    rim = -(-(tap_count - 1) // 16) * 16
    filters = filter_rows(replica, gate_rows)
    table = doppler_table(pulse_count).transpose(0, 3, 1, 2)
    table = table.reshape(2 * pulse_count, -1).astype(BF16)
    following = [shifted(rim_rows(raw_echo, rim, c, chunks), "rng", -1) for c in range(chunks)]
    spectra = [
        form_spectrum(filters, table, raw_echo, following[c], c, chunks) for c in range(chunks)
    ]

    starts = jnp.cumsum(owner_counts, dtype=jnp.int32) - owner_counts
    places = jnp.stack([lax.axis_index("dop"), lax.axis_index("rng")]).astype(jnp.int32)
    index = jnp.concatenate([places, owner_counts, starts])
    local_gates = train_gates % gate_rows
    gates = jnp.concatenate([local_gates + part * gate_rows for part in range(pack)], axis=1)
    count_rows = float(train_local * ranges)

    outgoing = select_gates(spectra, index, gates, most_slots, owners, pack)
    arrived = lax.all_to_all(outgoing, "dop", split_axis=0, concat_axis=0, tiled=True)
    parts = slot_parts(share_slots, pack)
    formed = [
        form_beams(arrived, beam_weights, index, ranges, first // pack, count // pack)
        for first, count in parts
    ]
    beams = [exchange(arrays, "rng") for arrays in formed]
    done, earlier = [], [arrays[0] for arrays in formed[1:]]
    for (first, count), arrays in zip(parts, beams):
        factors = factor_slots(
            arrays, pivots, index, first, count, share_slots, pack, count_rows, earlier
        )
        earlier = factors[:1]
        done.append(exchange(factors, "rng"))
    return place_rows(index, done, parts, most_slots)


def solution(mesh):
    return jax.shard_map(
        local,
        mesh=mesh,
        in_specs=(P(None, "dop", "rng", None), P(), P(), P(), P(), P(None, "rng")),
        out_specs=P("dop", "rng", None),
        check_vma=False,
    )
```

```python
import functools
import math

import jax
import jax.numpy as jnp
from jax import lax
from jax.experimental import pallas as pl
from jax.experimental.pallas import tpu as pltpu
from jax.sharding import PartitionSpec as P

LOADING = 0.25
LANES = 128
PANEL = 32
BF16 = jnp.bfloat16
F32 = jnp.float32
PARAMS = pltpu.CompilerParams(vmem_limit_bytes=48 * 1024 * 1024)


def shifted(array, axis, by):
    count = lax.axis_size(axis)
    pairs = [(i, i + by) for i in range(count) if 0 <= i + by < count]
    return lax.ppermute(array, axis, pairs)


def complex_block(real_part, imag_part):
    upper_row = jnp.stack([real_part, imag_part])
    lower_row = jnp.stack([-imag_part, real_part])
    return jnp.stack([upper_row, lower_row])


def doppler_table(pulse_count):
    pulse_index = jnp.arange(pulse_count, dtype=jnp.int32)
    phase_index = pulse_index[:, None] * pulse_index[None, :] % pulse_count
    angle_table = phase_index.astype(jnp.float32) * (2.0 * math.pi / pulse_count)
    norm_scale = 1.0 / math.sqrt(pulse_count)
    return complex_block(jnp.cos(angle_table) * norm_scale, jnp.sin(angle_table) * norm_scale)


def filter_kernel(replica_ref, out_ref):
    gate_rows, span = out_ref.shape[0] // 2, replica_ref.shape[1]
    banded = [
        pltpu.roll(
            jnp.broadcast_to(replica_ref[part : part + 1, :], (gate_rows, span)),
            0,
            1,
            stride=1,
            stride_axis=0,
        )
        for part in range(2)
    ]
    out_ref[:gate_rows, :span] = banded[0].astype(BF16)
    out_ref[:gate_rows, span:] = banded[1].astype(BF16)
    out_ref[gate_rows:, :span] = (-banded[1]).astype(BF16)
    out_ref[gate_rows:, span:] = banded[0].astype(BF16)


def filter_rows(replica, gate_rows):
    tap_count = replica.shape[1]
    span = -(-(gate_rows + tap_count) // LANES) * LANES
    return pl.pallas_call(
        filter_kernel,
        out_shape=jax.ShapeDtypeStruct((2 * gate_rows, 2 * span), BF16),
        in_specs=[pl.BlockSpec(memory_space=pltpu.VMEM)],
        out_specs=pl.BlockSpec(memory_space=pltpu.VMEM),
        compiler_params=PARAMS,
        name="filter_rows",
    )(jnp.pad(replica, ((0, 0), (0, span - tap_count))))


def rim_kernel(echo_ref, out_ref):
    out_ref[...] = echo_ref[...].astype(BF16)


def rim_rows(raw_echo, rim, chunk, chunks):
    _, ch_local, _, pulses = raw_echo.shape
    shape = (2, ch_local // chunks, rim, pulses)
    return pl.pallas_call(
        rim_kernel,
        out_shape=jax.ShapeDtypeStruct(shape, BF16),
        grid=(1,),
        in_specs=[pl.BlockSpec(shape, lambda i: (0, chunk, 0, 0))],
        out_specs=pl.BlockSpec(shape, lambda i: (0, 0, 0, 0)),
        compiler_params=PARAMS,
        name="rim_rows",
    )(raw_echo)


def spectrum_kernel(rows_ref, table_ref, own_ref, next_ref, out_ref, turned):
    step = pl.program_id(0)
    _, channels, gate_rows, pulses = own_ref.shape
    bins, height, _ = out_ref.shape
    rim = next_ref.shape[2]
    span = rows_ref.shape[1] // 2
    each = range(channels)
    samples = []
    for part in range(2):
        samples += [
            jnp.concatenate([own_ref[part, c] for c in each], axis=1).astype(BF16),
            jnp.concatenate([next_ref[part, c] for c in each], axis=1),
        ]
        if span > gate_rows + rim:
            samples.append(jnp.zeros((span - gate_rows - rim, channels * pulses), BF16))
    samples = jnp.concatenate(samples, axis=0)
    matched = jnp.dot(rows_ref[...], samples, preferred_element_type=F32).astype(BF16)
    halves = [matched[:gate_rows], matched[gate_rows:]]
    stacked = jnp.concatenate(
        [
            jnp.concatenate([half[:, c * pulses : (c + 1) * pulses] for half in halves], axis=1)
            for c in each
        ],
        axis=0,
    )
    spectra = lax.dot_general(
        table_ref[...], stacked, (((1,), (1,)), ((), ())), preferred_element_type=F32
    )
    for part in range(2):
        turned_part = jnp.stack(
            [
                spectra[part * bins : (part + 1) * bins, c * gate_rows : (c + 1) * gate_rows]
                for c in each
            ],
            axis=0,
        )
        place = pl.multiple_of(part * (height // 2) + step * channels, channels)
        turned[:, pl.ds(place, channels), :] = jnp.swapaxes(turned_part, 0, 1)

    @pl.when(step == pl.num_programs(0) - 1)
    def _():
        out_ref[...] = turned[...].astype(BF16)


def form_spectrum(rows, table, raw_echo, next_rows, chunk, chunks):
    _, ch_local, gate_rows, pulses = raw_echo.shape
    channels = ch_local // chunks
    step = math.gcd(channels, 8)
    steps = channels // step
    height = 2 * channels
    bins = table.shape[0] // 2
    return pl.pallas_call(
        spectrum_kernel,
        out_shape=jax.ShapeDtypeStruct((bins, height, gate_rows), BF16),
        grid=(steps,),
        in_specs=[
            pl.BlockSpec(rows.shape, lambda i: (0, 0)),
            pl.BlockSpec(table.shape, lambda i: (0, 0)),
            pl.BlockSpec((2, step, gate_rows, pulses), lambda i: (0, chunk * steps + i, 0, 0)),
            pl.BlockSpec((2, step) + next_rows.shape[2:], lambda i: (0, i, 0, 0)),
        ],
        out_specs=pl.BlockSpec((bins, height, gate_rows), lambda i: (0, 0, 0)),
        scratch_shapes=[pltpu.VMEM((bins, height, gate_rows), F32)],
        compiler_params=PARAMS,
        cost_estimate=pl.CostEstimate(
            flops=2 * rows.size * channels * pulses + 2 * table.size * channels * gate_rows,
            bytes_accessed=8 * channels * gate_rows * pulses,
            transcendentals=0,
        ),
        name="form_spectrum",
    )(rows, table, raw_echo, next_rows)


def owner_count(index_ref, owner):
    return index_ref[2 + owner]


def owner_start(index_ref, owner, owners):
    return index_ref[2 + owners + owner]


def select_kernel(index_ref, gates_ref, *refs, owners, ranges, first, share_slots, pack):
    *spectrum_refs, out_ref = refs
    bin_count, height, gate_rows = spectrum_refs[0].shape
    some, groups, _, width = out_ref.shape
    half = height // 2
    gate_index = lax.broadcasted_iota(jnp.int32, (pack * gate_rows, width), 0)
    part_index = lax.broadcasted_iota(jnp.int32, (1, width), 1) // (width // pack)
    for inner in range(some):
        start = owner_start(index_ref, pl.program_id(0) * some + inner, owners)
        for group in range(groups):
            block, place = divmod(group, groups // ranges)
            slot = block * share_slots + first + place * pack
            bins = [jnp.minimum(start + slot + part, bin_count - 1) for part in range(pack)]
            gates = gates_ref[pl.ds(bins[0], 1), :]
            for part in range(1, pack):
                gates = jnp.where(part_index == part, gates_ref[pl.ds(bins[part], 1), :], gates)
            chooser = jnp.where(gate_index == gates, 1.0, 0.0).astype(BF16)
            spectra = jnp.concatenate(
                [
                    jnp.concatenate([ref[b, s * half : (s + 1) * half] for b in bins], axis=1)
                    for s in range(2)
                    for ref in spectrum_refs
                ],
                axis=0,
            )
            picked = jnp.dot(spectra, chooser, preferred_element_type=F32)
            out_ref[inner, group] = picked.astype(BF16)


def select_gates(spectra, index, gates, first, count, share_slots, owners, ranges, pack):
    rows = sum(spectrum.shape[1] for spectrum in spectra)
    gate_rows = spectra[0].shape[2]
    groups = ranges * count // pack
    width = gates.shape[1]
    some = math.gcd(owners, 2)
    return pl.pallas_call(
        functools.partial(
            select_kernel,
            owners=owners,
            ranges=ranges,
            first=first,
            share_slots=share_slots,
            pack=pack,
        ),
        out_shape=jax.ShapeDtypeStruct((owners, groups, rows, width), BF16),
        grid=(owners // some,),
        in_specs=[pl.BlockSpec(memory_space=pltpu.SMEM)]
        + [pl.BlockSpec(memory_space=pltpu.VMEM)] * (1 + len(spectra)),
        out_specs=pl.BlockSpec((some, groups, rows, width), lambda i: (i, 0, 0, 0)),
        compiler_params=PARAMS,
        cost_estimate=pl.CostEstimate(
            flops=2 * owners * groups * pack * rows * gate_rows * width,
            bytes_accessed=owners * groups * rows * width * 2,
            transcendentals=0,
        ),
        name="select_gates",
    )(index, gates, *spectra)


def beam_kernel(index_ref, weights_ref, arrived_ref, *refs, ranges):
    out_refs = refs[-ranges:]
    sources, groups, rows, width = arrived_ref.shape
    share = groups // ranges
    dof = weights_ref.shape[2]
    half = rows // 2
    for shift, out_ref in enumerate(out_refs):
        lead = lax.rem(index_ref[1] + shift, ranges) * share
        packed = jnp.concatenate(
            [
                arrived_ref[:, lead + g, s * half : (s + 1) * half].reshape(sources * half, width)
                for s in range(2)
                for g in range(share)
            ],
            axis=1,
        )
        by_real, by_imag = [
            lax.dot_general(
                weights_ref[part], packed, (((0,), (0,)), ((), ())), preferred_element_type=F32
            )
            for part in range(2)
        ]
        middle = share * width
        real_part = by_real[:, :middle] + by_imag[:, middle:]
        imag_part = by_real[:, middle:] - by_imag[:, :middle]
        for g in range(share):
            span = slice(g * width, (g + 1) * width)
            out_ref[g, :dof] = real_part[:, span].astype(BF16)
            out_ref[g, dof:] = imag_part[:, span].astype(BF16)


def form_beams(arrived, weights, index, ranges, earlier):
    _, groups, _, width = arrived.shape
    shape = (groups // ranges, 2 * weights.shape[2], width)
    return pl.pallas_call(
        functools.partial(beam_kernel, ranges=ranges),
        out_shape=[jax.ShapeDtypeStruct(shape, BF16)] * ranges,
        in_specs=[
            pl.BlockSpec(memory_space=pltpu.SMEM),
            pl.BlockSpec(memory_space=pltpu.VMEM),
            pl.BlockSpec(memory_space=pltpu.VMEM),
        ]
        + [pl.BlockSpec(memory_space=pl.ANY)] * len(earlier),
        out_specs=[pl.BlockSpec(memory_space=pltpu.VMEM)] * ranges,
        compiler_params=PARAMS,
        cost_estimate=pl.CostEstimate(
            flops=4 * arrived.size * weights.shape[2],
            bytes_accessed=arrived.size * 2,
            transcendentals=0,
        ),
        name="form_beams",
    )(index, weights, arrived, *earlier)


def exchange(arrays, axis):
    count = len(arrays)
    moved = [arrays[0]]
    for shift in range(1, count):
        pairs = [(i, (i + shift) % count) for i in range(count)]
        moved.append(lax.ppermute(arrays[shift], axis, pairs))
    return moved


def split_terms(array):
    high = array.astype(BF16)
    return high, (array - high.astype(F32)).astype(BF16)


def left_terms(array):
    high, low = split_terms(array)
    high, low = high.astype(F32), low.astype(F32)
    return jnp.concatenate([high, high, low], axis=0).T.astype(BF16)


def right_terms(array):
    high, low = split_terms(array)
    return jnp.concatenate([high, low, high], axis=0)


def product(left, right):
    return jnp.dot(left, right, preferred_element_type=F32)


def loaded_covariance(beams, pivot_row, part, pack, count_rows):
    dof = pivot_row.shape[1]
    width = beams[0].shape[1] // pack
    hot = lax.broadcasted_iota(jnp.int32, (dof, dof), 0) == pivot_row
    hot = jnp.where(hot, 1.0, 0.0).astype(BF16)
    own = jnp.concatenate([b[:, part * width : (part + 1) * width] for b in beams], axis=1)
    picked = [
        lax.dot_general(
            hot,
            own[half * dof : (half + 1) * dof],
            (((0,), (0,)), ((), ())),
            preferred_element_type=F32,
        )
        for half in range(2)
    ]
    upper = jnp.concatenate([picked[0], picked[1]], axis=1).astype(BF16)
    lower = jnp.concatenate([picked[1], -picked[0]], axis=1).astype(BF16)
    stacked = jnp.concatenate([upper, lower], axis=0)
    gram = lax.dot_general(
        stacked, stacked, (((1,), (1,)), ((), ())), preferred_element_type=F32
    )
    return gram * (1.0 / count_rows)


def lane_spread(piece, lane):
    return jnp.broadcast_to(piece[:, lane : lane + 1], piece.shape)


def refined_reciprocal(value):
    guess = pl.reciprocal(value, approx=True)
    return guess * (2.0 - value * guess)


def eliminate(rows):
    scales = []

    def diagonal_piece(first):
        span = range(first, first + 8)
        return {(i, j): lane_spread(rows[i][0], j) for i in span for j in span if j >= i}

    small = diagonal_piece(0)
    for first in range(0, PANEL, 8):
        stop = first + 8
        following = diagonal_piece(stop) if stop < PANEL else {}
        for t in range(first, stop, 2):
            u = t + 1
            inverse = refined_reciprocal(small[t, t])
            cross = small[t, t] * small[u, u] - small[t, u] * small[t, u]
            second = refined_reciprocal(cross) * small[t, t]
            scales += [lax.rsqrt(small[t, t]), lax.rsqrt(cross * inverse)]
            factor = small[t, u] * inverse
            for j in range(u + 1, stop):
                small[u, j] = small[u, j] - factor * small[t, j]
            rows[u] = [x - factor * y for x, y in zip(rows[u], rows[t])]
            upper = {i: (small[t, i], small[u, i]) for i in range(u + 1, stop)}
            for i in range(stop, PANEL):
                upper[i] = (lane_spread(rows[t][0], i), lane_spread(rows[u][0], i))
            scaled = {i: (x * inverse, y * second) for i, (x, y) in upper.items()}
            for piece in (small, following):
                for i, j in piece:
                    if i > u:
                        one, two = scaled[i]
                        x, y = upper[j]
                        piece[i, j] = piece[i, j] - one * x - two * y
            for i, (one, two) in scaled.items():
                rows[i] = [x - one * y - two * z for x, y, z in zip(rows[i], rows[t], rows[u])]
        small = following
    return [[x * scale for x in row] for row, scale in zip(rows, scales)]


def factor_kernel(
    index_ref, pivots_ref, *refs, first, share_slots, ranges, waits, pack, count_rows
):
    beams_refs, refs = refs[:ranges], refs[ranges + waits :]
    out_refs = refs[:ranges]
    arriving, leaving, *scratch = refs[ranges:]
    slots = len(scratch) // 3
    work, lefts, rights = scratch[:slots], scratch[slots : 2 * slots], scratch[2 * slots :]
    order = work[0].shape[0]
    height = arriving.shape[1] // PANEL

    row = lax.broadcasted_iota(jnp.int32, (LANES, LANES), 0)
    col = lax.broadcasted_iota(jnp.int32, (LANES, LANES), 1)
    loading = jnp.where(row == col, LOADING, 0.0)
    owners = (index_ref.shape[0] - 2) // 2
    bin_lead = owner_start(index_ref, index_ref[0], owners) + index_ref[1] * share_slots + first
    for slot in range(slots):
        group, part = divmod(slot, pack)
        own_bin = jnp.minimum(bin_lead + slot, pivots_ref.shape[0] - 1)
        work[slot][...] = loaded_covariance(
            [ref[group] for ref in beams_refs],
            pivots_ref[pl.ds(own_bin, 1), :],
            part,
            pack,
            count_rows,
        )
        for start in range(0, order, LANES):
            work[slot][start : start + LANES, start : start + LANES] += loading

    eights = range(0, PANEL, 8)
    column = lax.broadcasted_iota(jnp.int32, (LANES, 3 * PANEL), 0)

    def spread_out(slot, rows):
        for i in eights:
            for w in range(rows.shape[1] // LANES):
                piece = rows[i : i + 8, w * LANES : (w + 1) * LANES]
                arriving[w, pl.ds(i * height + slot, 8, stride=height), :] = piece

    for slot in range(slots):
        spread_out(slot, work[slot][:PANEL, :])
    for start in range(0, order, LANES):
        chunks = (order - start) // LANES
        stop = start + LANES
        for slot in range(slots):
            lefts[slot][...] = jnp.zeros_like(lefts[slot])
            rights[slot][...] = jnp.zeros_like(rights[slot])

        def one_panel(p, carry, start=start, stop=stop, chunks=chunks):
            back = p * PANEL
            base = pl.multiple_of(start + back, PANEL)
            ahead = pl.multiple_of(jnp.minimum(back + PANEL, LANES - PANEL), PANEL)
            following = pl.multiple_of(start + ahead, PANEL)
            for slot in range(slots):
                left = jnp.where(column >= back + PANEL, lefts[slot][...], 0.0).astype(BF16)
                work[slot][start:stop, start:] -= product(left, rights[slot][:, start:])
            rows = []
            for t in range(PANEL):
                pieces = [arriving[w, t * height : (t + 1) * height, :] for w in range(chunks)]
                pieces[0] = pltpu.roll(pieces[0], (LANES - back) % LANES, 1)
                rows.append(pieces)
            rows = eliminate(rows)
            for t in range(PANEL):
                rows[t][0] = pltpu.roll(rows[t][0], back, 1)
                for w in range(chunks):
                    leaving[w, t * height : (t + 1) * height, :] = rows[t][w]
            for slot in range(slots):
                parts = []
                for w in range(chunks):
                    pieces = [
                        leaving[w, pl.ds(i * height + slot, 8, stride=height), :] for i in eights
                    ]
                    parts.append(jnp.concatenate(pieces, axis=0))
                panel = jnp.concatenate(parts, axis=1)
                work[slot][pl.ds(base, PANEL), start:] = panel
                lefts[slot][...] = left_terms(parts[0]).astype(F32)
                right = right_terms(panel)
                rights[slot][:, start:] = right
                left = lefts[slot][pl.ds(ahead, PANEL), :].astype(BF16)
                spread_out(slot, work[slot][pl.ds(following, PANEL), start:] - product(left, right))
            return carry

        lax.fori_loop(0, LANES // PANEL, one_panel, 0)
        if chunks > 1:
            terms = []
            for slot in range(slots):
                done = work[slot][start:stop, stop:]
                left = jnp.concatenate(
                    [left_terms(done[:, w * LANES : (w + 1) * LANES]) for w in range(chunks - 1)],
                    axis=0,
                )
                right = right_terms(done)
                ready = work[slot][stop : stop + PANEL, stop:] - product(left[:PANEL], right)
                spread_out(slot, ready)
                terms.append((left, right))
            for slot in range(slots):
                left, right = terms[slot]
                work[slot][stop + PANEL :, stop:] -= product(left[PANEL:], right)

    share = order // ranges
    row = lax.broadcasted_iota(jnp.int32, (share, order), 0)
    col = lax.broadcasted_iota(jnp.int32, (share, order), 1)
    for shift, out_ref in enumerate(out_refs):
        lead = pl.multiple_of(lax.rem(index_ref[1] + shift, ranges) * share, math.gcd(share, 16))
        upper = col >= row + lead
        for slot in range(slots):
            piece = work[slot][pl.ds(lead, share), :]
            out_ref[slot] = jnp.where(upper, piece, 0.0).astype(out_ref.dtype)


def factor_slots(beams, pivots, index, first, slots, share_slots, pack, count_rows, earlier):
    ranges = len(beams)
    order = beams[0].shape[1]
    height = -(-slots // 8) * 8
    return pl.pallas_call(
        functools.partial(
            factor_kernel,
            first=first,
            share_slots=share_slots,
            ranges=ranges,
            waits=len(earlier),
            pack=pack,
            count_rows=count_rows,
        ),
        out_shape=[jax.ShapeDtypeStruct((slots, order // ranges, order), BF16)] * ranges,
        in_specs=[pl.BlockSpec(memory_space=pltpu.SMEM)]
        + [pl.BlockSpec(memory_space=pltpu.VMEM)] * (1 + ranges)
        + [pl.BlockSpec(memory_space=pl.ANY)] * len(earlier),
        out_specs=[pl.BlockSpec(memory_space=pltpu.VMEM)] * ranges,
        scratch_shapes=[pltpu.VMEM((order // LANES, PANEL * height, LANES), F32)] * 2
        + [pltpu.VMEM((order, order), F32) for _ in range(slots)]
        + [pltpu.VMEM((LANES, 3 * PANEL), F32) for _ in range(slots)]
        + [pltpu.VMEM((3 * PANEL, order), BF16) for _ in range(slots)],
        compiler_params=PARAMS,
        cost_estimate=pl.CostEstimate(
            flops=slots * order**3,
            bytes_accessed=ranges * beams[0].size * 2,
            transcendentals=0,
        ),
        name="factor_slots",
    )(index, pivots, *beams, *earlier)


def place_kernel(index_ref, *refs, first, share_slots, ranges):
    in_refs, out_ref = refs[:ranges], refs[-1]
    slots = out_ref.shape[0]
    steps = in_refs[0].shape[0] // slots
    step = pl.program_id(0)
    shift, place = step // steps, step % steps
    block = lax.rem(index_ref[1] + ranges - shift, ranges)
    lead = block * share_slots + first + place * slots
    for this, ref in enumerate(in_refs):

        @pl.when(shift == this)
        def _(ref=ref):
            for i in range(slots):
                keep = lead + i < owner_count(index_ref, index_ref[0])
                keep = jnp.broadcast_to(keep, out_ref.shape[1:])
                out_ref[i] = jnp.where(keep, ref[place * slots + i].astype(F32), 0.0)


def place_rows(index, arrays, first, share_slots, earlier):
    ranges = len(arrays)
    count = arrays[0].shape[0]
    slots = math.gcd(math.gcd(count, first), share_slots)
    steps = count // slots

    def out_index(step, index_ref):
        block = lax.rem(index_ref[1] + ranges - step // steps, ranges)
        return ((block * share_slots + first) // slots + step % steps, 0, 0)

    return pl.pallas_call(
        functools.partial(place_kernel, first=first, share_slots=share_slots, ranges=ranges),
        out_shape=jax.ShapeDtypeStruct((ranges * share_slots,) + arrays[0].shape[1:], F32),
        grid_spec=pltpu.PrefetchScalarGridSpec(
            num_scalar_prefetch=1,
            grid=(ranges * steps,),
            in_specs=[pl.BlockSpec(memory_space=pltpu.VMEM)] * ranges
            + [pl.BlockSpec(memory_space=pl.ANY)] * len(earlier),
            out_specs=pl.BlockSpec((slots,) + arrays[0].shape[1:], out_index),
        ),
        input_output_aliases={1 + ranges: 0} if earlier else {},
        compiler_params=PARAMS,
        name="place_rows",
    )(index, *arrays, *earlier)


def slot_parts(share_slots, pack):
    halves = 2 if share_slots % (2 * pack) == 0 else 1
    count = share_slots // halves
    return [(i * count, count) for i in range(halves)]


def local(raw_echo, replica, beam_weights, pivots, owner_counts, train_gates):
    ch_local = raw_echo.shape[1]
    gate_rows = raw_echo.shape[2]
    pulse_count = raw_echo.shape[3]
    tap_count = replica.shape[1]
    train_local = train_gates.shape[1]
    owners = lax.axis_size("dop")
    ranges = lax.axis_size("rng")
    most_slots = 2 * (pulse_count // owners)
    share_slots = most_slots // ranges
    pack = max(1, min(LANES // train_local, share_slots))

    chunks = max(1, min(4, ch_local // 16))
    chunk_rows = ch_local // chunks
    rim = -(-(tap_count - 1) // 16) * 16
    filters = filter_rows(replica, gate_rows)
    table = doppler_table(pulse_count).transpose(0, 3, 1, 2)
    table = table.reshape(2 * pulse_count, -1).astype(BF16)
    following = [shifted(rim_rows(raw_echo, rim, c, chunks), "rng", -1) for c in range(chunks)]
    spectra = [
        form_spectrum(filters, table, raw_echo, following[c], c, chunks) for c in range(chunks)
    ]

    starts = jnp.cumsum(owner_counts, dtype=jnp.int32) - owner_counts
    places = jnp.stack([lax.axis_index("dop"), lax.axis_index("rng")]).astype(jnp.int32)
    index = jnp.concatenate([places, owner_counts, starts])
    local_gates = train_gates % gate_rows
    gates = jnp.concatenate([local_gates + part * gate_rows for part in range(pack)], axis=1)
    count_rows = float(train_local * ranges)

    parts = slot_parts(share_slots, pack)
    outgoing = [
        select_gates(spectra, index, gates, first, count, share_slots, owners, ranges, pack)
        for first, count in parts
    ]
    sent = [
        lax.all_to_all(array, "dop", split_axis=0, concat_axis=0, tiled=True) for array in outgoing
    ]
    result, earlier = [], outgoing[1:]
    for (first, count), arrived in zip(parts, sent):
        beams = exchange(form_beams(arrived, beam_weights, index, ranges, earlier), "rng")
        factors = factor_slots(
            beams, pivots, index, first, count, share_slots, pack, count_rows, []
        )
        earlier = factors[:1]
        rows = exchange(factors, "rng")
        result = [place_rows(index, rows, first, share_slots, result)]
    return result[0]


def solution(mesh):
    return jax.shard_map(
        local,
        mesh=mesh,
        in_specs=(P(None, "dop", "rng", None), P(), P(), P(), P(), P(None, "rng")),
        out_specs=P("dop", "rng", None),
        check_vma=False,
    )
```

```python
import functools
import math

import jax
import jax.numpy as jnp
from jax import lax
from jax.experimental import pallas as pl
from jax.experimental.pallas import tpu as pltpu
from jax.sharding import PartitionSpec as P

LOADING = 0.25
LANES = 128
PANEL = 32
BF16 = jnp.bfloat16
F32 = jnp.float32
PARAMS = pltpu.CompilerParams(vmem_limit_bytes=48 * 1024 * 1024)


def shifted(array, axis, by):
    count = lax.axis_size(axis)
    pairs = [(i, i + by) for i in range(count) if 0 <= i + by < count]
    return lax.ppermute(array, axis, pairs)


def complex_block(real_part, imag_part):
    upper_row = jnp.stack([real_part, imag_part])
    lower_row = jnp.stack([-imag_part, real_part])
    return jnp.stack([upper_row, lower_row])


def doppler_table(pulse_count):
    pulse_index = jnp.arange(pulse_count, dtype=jnp.int32)
    phase_index = pulse_index[:, None] * pulse_index[None, :] % pulse_count
    angle_table = phase_index.astype(jnp.float32) * (2.0 * math.pi / pulse_count)
    norm_scale = 1.0 / math.sqrt(pulse_count)
    return complex_block(jnp.cos(angle_table) * norm_scale, jnp.sin(angle_table) * norm_scale)


def filter_kernel(replica_ref, out_ref):
    gate_rows, span = out_ref.shape[0] // 2, replica_ref.shape[1]
    banded = [
        pltpu.roll(
            jnp.broadcast_to(replica_ref[part : part + 1, :], (gate_rows, span)),
            0,
            1,
            stride=1,
            stride_axis=0,
        )
        for part in range(2)
    ]
    out_ref[:gate_rows, :span] = banded[0].astype(BF16)
    out_ref[:gate_rows, span:] = banded[1].astype(BF16)
    out_ref[gate_rows:, :span] = (-banded[1]).astype(BF16)
    out_ref[gate_rows:, span:] = banded[0].astype(BF16)


def filter_rows(replica, gate_rows):
    tap_count = replica.shape[1]
    span = -(-(gate_rows + tap_count) // LANES) * LANES
    return pl.pallas_call(
        filter_kernel,
        out_shape=jax.ShapeDtypeStruct((2 * gate_rows, 2 * span), BF16),
        in_specs=[pl.BlockSpec(memory_space=pltpu.VMEM)],
        out_specs=pl.BlockSpec(memory_space=pltpu.VMEM),
        compiler_params=PARAMS,
        name="filter_rows",
    )(jnp.pad(replica, ((0, 0), (0, span - tap_count))))


def rim_kernel(echo_ref, out_ref):
    out_ref[...] = echo_ref[...].astype(BF16)


def rim_rows(raw_echo, rim, chunk, chunks):
    _, ch_local, _, pulses = raw_echo.shape
    shape = (2, ch_local // chunks, rim, pulses)
    return pl.pallas_call(
        rim_kernel,
        out_shape=jax.ShapeDtypeStruct(shape, BF16),
        grid=(1,),
        in_specs=[pl.BlockSpec(shape, lambda i: (0, chunk, 0, 0))],
        out_specs=pl.BlockSpec(shape, lambda i: (0, 0, 0, 0)),
        compiler_params=PARAMS,
        name="rim_rows",
    )(raw_echo)


def spectrum_kernel(rows_ref, table_ref, own_ref, next_ref, out_ref, turned):
    step = pl.program_id(0)
    _, channels, gate_rows, pulses = own_ref.shape
    bins, height, _ = out_ref.shape
    rim = next_ref.shape[2]
    span = rows_ref.shape[1] // 2
    each = range(channels)
    samples = []
    for part in range(2):
        samples += [
            jnp.concatenate([own_ref[part, c] for c in each], axis=1).astype(BF16),
            jnp.concatenate([next_ref[part, c] for c in each], axis=1),
        ]
        if span > gate_rows + rim:
            samples.append(jnp.zeros((span - gate_rows - rim, channels * pulses), BF16))
    samples = jnp.concatenate(samples, axis=0)
    matched = jnp.dot(rows_ref[...], samples, preferred_element_type=F32).astype(BF16)
    halves = [matched[:gate_rows], matched[gate_rows:]]
    stacked = jnp.concatenate(
        [
            jnp.concatenate([half[:, c * pulses : (c + 1) * pulses] for half in halves], axis=1)
            for c in each
        ],
        axis=0,
    )
    spectra = lax.dot_general(
        table_ref[...], stacked, (((1,), (1,)), ((), ())), preferred_element_type=F32
    )
    for part in range(2):
        turned_part = jnp.stack(
            [
                spectra[part * bins : (part + 1) * bins, c * gate_rows : (c + 1) * gate_rows]
                for c in each
            ],
            axis=0,
        )
        place = pl.multiple_of(part * (height // 2) + step * channels, channels)
        turned[:, pl.ds(place, channels), :] = jnp.swapaxes(turned_part, 0, 1)

    @pl.when(step == pl.num_programs(0) - 1)
    def _():
        out_ref[...] = turned[...].astype(BF16)


def form_spectrum(rows, table, raw_echo, next_rows, chunk, chunks):
    _, ch_local, gate_rows, pulses = raw_echo.shape
    channels = ch_local // chunks
    step = math.gcd(channels, 8)
    steps = channels // step
    height = 2 * channels
    bins = table.shape[0] // 2
    return pl.pallas_call(
        spectrum_kernel,
        out_shape=jax.ShapeDtypeStruct((bins, height, gate_rows), BF16),
        grid=(steps,),
        in_specs=[
            pl.BlockSpec(rows.shape, lambda i: (0, 0)),
            pl.BlockSpec(table.shape, lambda i: (0, 0)),
            pl.BlockSpec((2, step, gate_rows, pulses), lambda i: (0, chunk * steps + i, 0, 0)),
            pl.BlockSpec((2, step) + next_rows.shape[2:], lambda i: (0, i, 0, 0)),
        ],
        out_specs=pl.BlockSpec((bins, height, gate_rows), lambda i: (0, 0, 0)),
        scratch_shapes=[pltpu.VMEM((bins, height, gate_rows), F32)],
        compiler_params=PARAMS,
        cost_estimate=pl.CostEstimate(
            flops=2 * rows.size * channels * pulses + 2 * table.size * channels * gate_rows,
            bytes_accessed=8 * channels * gate_rows * pulses,
            transcendentals=0,
        ),
        name="form_spectrum",
    )(rows, table, raw_echo, next_rows)


def owner_count(index_ref, owner):
    return index_ref[2 + owner]


def owner_start(index_ref, owner, owners):
    return index_ref[2 + owners + owner]


def select_kernel(index_ref, gates_ref, *refs, owners, ranges, first, share_slots, pack):
    *spectrum_refs, out_ref = refs
    bin_count, height, gate_rows = spectrum_refs[0].shape
    some, groups, _, width = out_ref.shape
    half = height // 2
    gate_index = lax.broadcasted_iota(jnp.int32, (pack * gate_rows, width), 0)
    part_index = lax.broadcasted_iota(jnp.int32, (1, width), 1) // (width // pack)
    for inner in range(some):
        start = owner_start(index_ref, pl.program_id(0) * some + inner, owners)
        for group in range(groups):
            block, place = divmod(group, groups // ranges)
            slot = block * share_slots + first + place * pack
            bins = [jnp.minimum(start + slot + part, bin_count - 1) for part in range(pack)]
            gates = gates_ref[pl.ds(bins[0], 1), :]
            for part in range(1, pack):
                gates = jnp.where(part_index == part, gates_ref[pl.ds(bins[part], 1), :], gates)
            chooser = jnp.where(gate_index == gates, 1.0, 0.0).astype(BF16)
            spectra = jnp.concatenate(
                [
                    jnp.concatenate([ref[b, s * half : (s + 1) * half] for b in bins], axis=1)
                    for s in range(2)
                    for ref in spectrum_refs
                ],
                axis=0,
            )
            picked = jnp.dot(spectra, chooser, preferred_element_type=F32)
            out_ref[inner, group] = picked.astype(BF16)


def select_gates(spectra, index, gates, first, count, share_slots, owners, ranges, pack):
    rows = sum(spectrum.shape[1] for spectrum in spectra)
    gate_rows = spectra[0].shape[2]
    groups = ranges * count // pack
    width = gates.shape[1]
    some = math.gcd(owners, 2)
    return pl.pallas_call(
        functools.partial(
            select_kernel,
            owners=owners,
            ranges=ranges,
            first=first,
            share_slots=share_slots,
            pack=pack,
        ),
        out_shape=jax.ShapeDtypeStruct((owners, groups, rows, width), BF16),
        grid=(owners // some,),
        in_specs=[pl.BlockSpec(memory_space=pltpu.SMEM)]
        + [pl.BlockSpec(memory_space=pltpu.VMEM)] * (1 + len(spectra)),
        out_specs=pl.BlockSpec((some, groups, rows, width), lambda i: (i, 0, 0, 0)),
        compiler_params=PARAMS,
        cost_estimate=pl.CostEstimate(
            flops=2 * owners * groups * pack * rows * gate_rows * width,
            bytes_accessed=owners * groups * rows * width * 2,
            transcendentals=0,
        ),
        name="select_gates",
    )(index, gates, *spectra)


def beam_kernel(weights_ref, arrived_ref, *refs):
    out_ref = refs[-1]
    sources, ranges, groups, rows, width = arrived_ref.shape
    dof = weights_ref.shape[2]
    half = rows // 2
    for block in range(ranges):
        packed = jnp.concatenate(
            [
                arrived_ref[:, block, g, s * half : (s + 1) * half].reshape(sources * half, width)
                for s in range(2)
                for g in range(groups)
            ],
            axis=1,
        )
        by_real, by_imag = [
            lax.dot_general(
                weights_ref[part], packed, (((0,), (0,)), ((), ())), preferred_element_type=F32
            )
            for part in range(2)
        ]
        middle = groups * width
        real_part = by_real[:, :middle] + by_imag[:, middle:]
        imag_part = by_real[:, middle:] - by_imag[:, :middle]
        for g in range(groups):
            span = slice(g * width, (g + 1) * width)
            out_ref[block, g, :dof] = real_part[:, span].astype(BF16)
            out_ref[block, g, dof:] = imag_part[:, span].astype(BF16)


def form_beams(arrived, weights, earlier):
    _, ranges, groups, _, width = arrived.shape
    shape = (ranges, groups, 2 * weights.shape[2], width)
    return pl.pallas_call(
        beam_kernel,
        out_shape=jax.ShapeDtypeStruct(shape, BF16),
        in_specs=[pl.BlockSpec(memory_space=pltpu.VMEM)] * 2
        + [pl.BlockSpec(memory_space=pl.ANY)] * len(earlier),
        out_specs=pl.BlockSpec(memory_space=pltpu.VMEM),
        compiler_params=PARAMS,
        cost_estimate=pl.CostEstimate(
            flops=4 * arrived.size * weights.shape[2],
            bytes_accessed=arrived.size * 2,
            transcendentals=0,
        ),
        name="form_beams",
    )(weights, arrived, *earlier)


def exchange(arrays, axis):
    count = len(arrays)
    moved = [arrays[0]]
    for shift in range(1, count):
        pairs = [(i, (i + shift) % count) for i in range(count)]
        moved.append(lax.ppermute(arrays[shift], axis, pairs))
    return moved


def split_terms(array):
    high = array.astype(BF16)
    return high, (array - high.astype(F32)).astype(BF16)


def left_terms(array):
    high, low = split_terms(array)
    high, low = high.astype(F32), low.astype(F32)
    return jnp.concatenate([high, high, low], axis=0).T.astype(BF16)


def right_terms(array):
    high, low = split_terms(array)
    return jnp.concatenate([high, low, high], axis=0)


def product(left, right):
    return jnp.dot(left, right, preferred_element_type=F32)


def loaded_covariance(beams, pivot_row, part, pack, count_rows):
    dof = pivot_row.shape[1]
    width = beams[0].shape[1] // pack
    hot = lax.broadcasted_iota(jnp.int32, (dof, dof), 0) == pivot_row
    hot = jnp.where(hot, 1.0, 0.0).astype(BF16)
    own = jnp.concatenate([b[:, part * width : (part + 1) * width] for b in beams], axis=1)
    picked = [
        lax.dot_general(
            hot,
            own[half * dof : (half + 1) * dof],
            (((0,), (0,)), ((), ())),
            preferred_element_type=F32,
        )
        for half in range(2)
    ]
    upper = jnp.concatenate([picked[0], picked[1]], axis=1).astype(BF16)
    lower = jnp.concatenate([picked[1], -picked[0]], axis=1).astype(BF16)
    stacked = jnp.concatenate([upper, lower], axis=0)
    gram = lax.dot_general(
        stacked, stacked, (((1,), (1,)), ((), ())), preferred_element_type=F32
    )
    return gram * (1.0 / count_rows)


def lane_spread(piece, lane):
    return jnp.broadcast_to(piece[:, lane : lane + 1], piece.shape)


def refined_reciprocal(value):
    guess = pl.reciprocal(value, approx=True)
    return guess * (2.0 - value * guess)


def tree_sum(terms):
    while len(terms) > 1:
        terms = [x + y for x, y in zip(terms[::2], terms[1::2])]
    return terms[0]


def eliminate(rows):
    scales = []
    for first in range(0, PANEL, 8):
        span = range(first, first + 8)
        small = {(i, j): lane_spread(rows[i][0], j) for i in span for j in span if j >= i}
        for t in range(first, first + 8, 2):
            u = t + 1
            inverse = refined_reciprocal(small[t, t])
            cross = small[t, t] * small[u, u] - small[t, u] * small[t, u]
            second = refined_reciprocal(cross) * small[t, t]
            scales += [lax.rsqrt(small[t, t]), lax.rsqrt(cross * inverse)]
            factor = small[t, u] * inverse
            for j in range(u + 1, first + 8):
                small[u, j] = small[u, j] - factor * small[t, j]
            rows[u] = [x - factor * y for x, y in zip(rows[u], rows[t])]
            for i in range(u + 1, first + 8):
                one, two = small[t, i] * inverse, small[u, i] * second
                for j in range(i, first + 8):
                    small[i, j] = small[i, j] - one * small[t, j] - two * small[u, j]
                rows[i] = [
                    x - one * y - two * z for x, y, z in zip(rows[i], rows[t], rows[u])
                ]
        for t in span:
            rows[t] = [x * scales[t] for x in rows[t]]
        for i in range(first + 8, PANEL):
            factors = [lane_spread(rows[t][0], i) for t in span]
            rows[i] = [
                x - tree_sum([f * rows[t][w] for f, t in zip(factors, span)])
                for w, x in enumerate(rows[i])
            ]
    return rows


def factor_kernel(
    index_ref, pivots_ref, beams_ref, *refs, first, share_slots, ranges, pack, count_rows
):
    out_refs = refs[:ranges]
    arriving, leaving, *scratch = refs[ranges:]
    slots = len(scratch) // 3
    work, lefts, rights = scratch[:slots], scratch[slots : 2 * slots], scratch[2 * slots :]
    order = work[0].shape[0]
    height = arriving.shape[1] // PANEL

    row = lax.broadcasted_iota(jnp.int32, (LANES, LANES), 0)
    col = lax.broadcasted_iota(jnp.int32, (LANES, LANES), 1)
    loading = jnp.where(row == col, LOADING, 0.0)
    owners = (index_ref.shape[0] - 2) // 2
    bin_lead = owner_start(index_ref, index_ref[0], owners) + index_ref[1] * share_slots + first
    for slot in range(slots):
        group, part = divmod(slot, pack)
        own_bin = jnp.minimum(bin_lead + slot, pivots_ref.shape[0] - 1)
        work[slot][...] = loaded_covariance(
            [beams_ref[r, group] for r in range(ranges)],
            pivots_ref[pl.ds(own_bin, 1), :],
            part,
            pack,
            count_rows,
        )
        for start in range(0, order, LANES):
            work[slot][start : start + LANES, start : start + LANES] += loading

    eights = range(0, PANEL, 8)
    column = lax.broadcasted_iota(jnp.int32, (LANES, 3 * PANEL), 0)

    def spread_out(slot, rows):
        for i in eights:
            for w in range(rows.shape[1] // LANES):
                piece = rows[i : i + 8, w * LANES : (w + 1) * LANES]
                arriving[w, pl.ds(i * height + slot, 8, stride=height), :] = piece

    for slot in range(slots):
        spread_out(slot, work[slot][:PANEL, :])
    for start in range(0, order, LANES):
        chunks = (order - start) // LANES
        stop = start + LANES
        for slot in range(slots):
            lefts[slot][...] = jnp.zeros_like(lefts[slot])
            rights[slot][...] = jnp.zeros_like(rights[slot])

        def one_panel(p, carry, start=start, stop=stop, chunks=chunks):
            back = p * PANEL
            base = pl.multiple_of(start + back, PANEL)
            ahead = pl.multiple_of(jnp.minimum(back + PANEL, LANES - PANEL), PANEL)
            following = pl.multiple_of(start + ahead, PANEL)
            for slot in range(slots):
                left = jnp.where(column >= back + PANEL, lefts[slot][...], 0.0).astype(BF16)
                work[slot][start:stop, start:] -= product(left, rights[slot][:, start:])
            rows = []
            for t in range(PANEL):
                pieces = [arriving[w, t * height : (t + 1) * height, :] for w in range(chunks)]
                pieces[0] = pltpu.roll(pieces[0], (LANES - back) % LANES, 1)
                rows.append(pieces)
            rows = eliminate(rows)
            for t in range(PANEL):
                rows[t][0] = pltpu.roll(rows[t][0], back, 1)
                for w in range(chunks):
                    leaving[w, t * height : (t + 1) * height, :] = rows[t][w]
            for slot in range(slots):
                parts = []
                for w in range(chunks):
                    pieces = [
                        leaving[w, pl.ds(i * height + slot, 8, stride=height), :] for i in eights
                    ]
                    parts.append(jnp.concatenate(pieces, axis=0))
                panel = jnp.concatenate(parts, axis=1)
                work[slot][pl.ds(base, PANEL), start:] = panel
                lefts[slot][...] = left_terms(parts[0]).astype(F32)
                right = right_terms(panel)
                rights[slot][:, start:] = right
                left = lefts[slot][pl.ds(ahead, PANEL), :].astype(BF16)
                spread_out(slot, work[slot][pl.ds(following, PANEL), start:] - product(left, right))
            return carry

        lax.fori_loop(0, LANES // PANEL, one_panel, 0)
        if chunks > 1:
            terms = []
            for slot in range(slots):
                done = work[slot][start:stop, stop:]
                left = jnp.concatenate(
                    [left_terms(done[:, w * LANES : (w + 1) * LANES]) for w in range(chunks - 1)],
                    axis=0,
                )
                right = right_terms(done)
                ready = work[slot][stop : stop + PANEL, stop:] - product(left[:PANEL], right)
                spread_out(slot, ready)
                terms.append((left, right))
            for slot in range(slots):
                left, right = terms[slot]
                work[slot][stop + PANEL :, stop:] -= product(left[PANEL:], right)

    share = order // ranges
    row = lax.broadcasted_iota(jnp.int32, (share, order), 0)
    col = lax.broadcasted_iota(jnp.int32, (share, order), 1)
    for shift, out_ref in enumerate(out_refs):
        lead = pl.multiple_of(lax.rem(index_ref[1] + shift, ranges) * share, math.gcd(share, 16))
        upper = col >= row + lead
        for slot in range(slots):
            piece = work[slot][pl.ds(lead, share), :]
            out_ref[slot] = jnp.where(upper, piece, 0.0).astype(out_ref.dtype)


def factor_slots(beams, pivots, index, first, slots, share_slots, pack, count_rows):
    ranges, _, order, _ = beams.shape
    height = -(-slots // 8) * 8
    return pl.pallas_call(
        functools.partial(
            factor_kernel,
            first=first,
            share_slots=share_slots,
            ranges=ranges,
            pack=pack,
            count_rows=count_rows,
        ),
        out_shape=[jax.ShapeDtypeStruct((slots, order // ranges, order), BF16)] * ranges,
        in_specs=[pl.BlockSpec(memory_space=pltpu.SMEM)]
        + [pl.BlockSpec(memory_space=pltpu.VMEM)] * 2,
        out_specs=[pl.BlockSpec(memory_space=pltpu.VMEM)] * ranges,
        scratch_shapes=[pltpu.VMEM((order // LANES, PANEL * height, LANES), F32)] * 2
        + [pltpu.VMEM((order, order), F32) for _ in range(slots)]
        + [pltpu.VMEM((LANES, 3 * PANEL), F32) for _ in range(slots)]
        + [pltpu.VMEM((3 * PANEL, order), BF16) for _ in range(slots)],
        compiler_params=PARAMS,
        cost_estimate=pl.CostEstimate(
            flops=slots * order**3,
            bytes_accessed=beams.size * 2,
            transcendentals=0,
        ),
        name="factor_slots",
    )(index, pivots, beams)


def place_kernel(index_ref, *refs, first, share_slots, ranges):
    in_refs, out_ref = refs[:ranges], refs[-1]
    slots = out_ref.shape[0]
    steps = in_refs[0].shape[0] // slots
    step = pl.program_id(0)
    shift, place = step // steps, step % steps
    block = lax.rem(index_ref[1] + ranges - shift, ranges)
    lead = block * share_slots + first + place * slots
    for this, ref in enumerate(in_refs):

        @pl.when(shift == this)
        def _(ref=ref):
            for i in range(slots):
                keep = lead + i < owner_count(index_ref, index_ref[0])
                keep = jnp.broadcast_to(keep, out_ref.shape[1:])
                out_ref[i] = jnp.where(keep, ref[place * slots + i].astype(F32), 0.0)


def place_rows(index, arrays, first, share_slots, earlier):
    ranges = len(arrays)
    count = arrays[0].shape[0]
    slots = math.gcd(math.gcd(count, first), share_slots)
    steps = count // slots

    def out_index(step, index_ref):
        block = lax.rem(index_ref[1] + ranges - step // steps, ranges)
        return ((block * share_slots + first) // slots + step % steps, 0, 0)

    return pl.pallas_call(
        functools.partial(place_kernel, first=first, share_slots=share_slots, ranges=ranges),
        out_shape=jax.ShapeDtypeStruct((ranges * share_slots,) + arrays[0].shape[1:], F32),
        grid_spec=pltpu.PrefetchScalarGridSpec(
            num_scalar_prefetch=1,
            grid=(ranges * steps,),
            in_specs=[pl.BlockSpec(memory_space=pltpu.VMEM)] * ranges
            + [pl.BlockSpec(memory_space=pl.ANY)] * len(earlier),
            out_specs=pl.BlockSpec((slots,) + arrays[0].shape[1:], out_index),
        ),
        input_output_aliases={1 + ranges: 0} if earlier else {},
        compiler_params=PARAMS,
        name="place_rows",
    )(index, *arrays, *earlier)


def slot_parts(share_slots, pack):
    head = share_slots - pack
    return [(0, head), (head, pack)] if head > 0 else [(0, share_slots)]


def local(raw_echo, replica, beam_weights, pivots, owner_counts, train_gates):
    ch_local = raw_echo.shape[1]
    gate_rows = raw_echo.shape[2]
    pulse_count = raw_echo.shape[3]
    tap_count = replica.shape[1]
    train_local = train_gates.shape[1]
    owners = lax.axis_size("dop")
    ranges = lax.axis_size("rng")
    most_slots = 2 * (pulse_count // owners)
    share_slots = most_slots // ranges
    pack = max(1, min(LANES // train_local, share_slots))

    chunks = max(1, min(4, ch_local // 16))
    chunk_rows = ch_local // chunks
    rim = -(-(tap_count - 1) // 16) * 16
    filters = filter_rows(replica, gate_rows)
    table = doppler_table(pulse_count).transpose(0, 3, 1, 2)
    table = table.reshape(2 * pulse_count, -1).astype(BF16)
    following = [shifted(rim_rows(raw_echo, rim, c, chunks), "rng", -1) for c in range(chunks)]
    spectra = [
        form_spectrum(filters, table, raw_echo, following[c], c, chunks) for c in range(chunks)
    ]

    starts = jnp.cumsum(owner_counts, dtype=jnp.int32) - owner_counts
    places = jnp.stack([lax.axis_index("dop"), lax.axis_index("rng")]).astype(jnp.int32)
    index = jnp.concatenate([places, owner_counts, starts])
    local_gates = train_gates % gate_rows
    gates = jnp.concatenate([local_gates + part * gate_rows for part in range(pack)], axis=1)
    count_rows = float(train_local * ranges)

    parts = slot_parts(share_slots, pack)
    outgoing = [
        select_gates(spectra, index, gates, first, count, share_slots, owners, ranges, pack)
        for first, count in parts
    ]
    axes = ("dop", "rng")
    sent = [
        lax.all_to_all(
            array.reshape(owners * ranges, -1, *array.shape[2:]),
            axes,
            split_axis=0,
            concat_axis=0,
            tiled=True,
        ).reshape(owners, ranges, -1, *array.shape[2:])
        for array in outgoing
    ]
    result, earlier = [], outgoing[1:]
    for (first, count), arrived in zip(parts, sent):
        beams = form_beams(arrived, beam_weights, earlier)
        factors = factor_slots(beams, pivots, index, first, count, share_slots, pack, count_rows)
        earlier = factors[:1]
        rows = exchange(factors, "rng")
        result = [place_rows(index, rows, first, share_slots, result)]
    return result[0]


def solution(mesh):
    return jax.shard_map(
        local,
        mesh=mesh,
        in_specs=(P(None, "dop", "rng", None), P(), P(), P(), P(), P(None, "rng")),
        out_specs=P("dop", "rng", None),
        check_vma=False,
    )
```

```python
import functools
import math

import jax
import jax.numpy as jnp
from jax import lax
from jax.experimental import pallas as pl
from jax.experimental.pallas import tpu as pltpu
from jax.sharding import PartitionSpec as P

LOADING = 0.25
LANES = 128
PANEL = 32
BF16 = jnp.bfloat16
F32 = jnp.float32
PARAMS = pltpu.CompilerParams(vmem_limit_bytes=48 * 1024 * 1024)


def shifted(array, axis, by):
    count = lax.axis_size(axis)
    pairs = [(i, i + by) for i in range(count) if 0 <= i + by < count]
    return lax.ppermute(array, axis, pairs)


def complex_block(real_part, imag_part):
    upper_row = jnp.stack([real_part, imag_part])
    lower_row = jnp.stack([-imag_part, real_part])
    return jnp.stack([upper_row, lower_row])


def doppler_table(pulse_count):
    pulse_index = jnp.arange(pulse_count, dtype=jnp.int32)
    phase_index = pulse_index[:, None] * pulse_index[None, :] % pulse_count
    angle_table = phase_index.astype(jnp.float32) * (2.0 * math.pi / pulse_count)
    norm_scale = 1.0 / math.sqrt(pulse_count)
    return complex_block(jnp.cos(angle_table) * norm_scale, jnp.sin(angle_table) * norm_scale)


def filter_kernel(replica_ref, out_ref):
    gate_rows, span = out_ref.shape[0] // 2, replica_ref.shape[1]
    banded = [
        pltpu.roll(
            jnp.broadcast_to(replica_ref[part : part + 1, :], (gate_rows, span)),
            0,
            1,
            stride=1,
            stride_axis=0,
        )
        for part in range(2)
    ]
    out_ref[:gate_rows, :span] = banded[0].astype(BF16)
    out_ref[:gate_rows, span:] = banded[1].astype(BF16)
    out_ref[gate_rows:, :span] = (-banded[1]).astype(BF16)
    out_ref[gate_rows:, span:] = banded[0].astype(BF16)


def filter_rows(replica, gate_rows):
    tap_count = replica.shape[1]
    span = -(-(gate_rows + tap_count) // LANES) * LANES
    return pl.pallas_call(
        filter_kernel,
        out_shape=jax.ShapeDtypeStruct((2 * gate_rows, 2 * span), BF16),
        in_specs=[pl.BlockSpec(memory_space=pltpu.VMEM)],
        out_specs=pl.BlockSpec(memory_space=pltpu.VMEM),
        compiler_params=PARAMS,
        name="filter_rows",
    )(jnp.pad(replica, ((0, 0), (0, span - tap_count))))


def rim_kernel(echo_ref, out_ref):
    out_ref[...] = echo_ref[...].astype(BF16)


def rim_rows(raw_echo, rim, chunk, chunks):
    _, ch_local, _, pulses = raw_echo.shape
    shape = (2, ch_local // chunks, rim, pulses)
    return pl.pallas_call(
        rim_kernel,
        out_shape=jax.ShapeDtypeStruct(shape, BF16),
        grid=(1,),
        in_specs=[pl.BlockSpec(shape, lambda i: (0, chunk, 0, 0))],
        out_specs=pl.BlockSpec(shape, lambda i: (0, 0, 0, 0)),
        compiler_params=PARAMS,
        name="rim_rows",
    )(raw_echo)


def spectrum_kernel(rows_ref, table_ref, own_ref, next_ref, out_ref, turned):
    step = pl.program_id(0)
    _, channels, gate_rows, pulses = own_ref.shape
    bins, height, _ = out_ref.shape
    rim = next_ref.shape[2]
    span = rows_ref.shape[1] // 2
    each = range(channels)
    samples = []
    for part in range(2):
        samples += [
            jnp.concatenate([own_ref[part, c] for c in each], axis=1).astype(BF16),
            jnp.concatenate([next_ref[part, c] for c in each], axis=1),
        ]
        if span > gate_rows + rim:
            samples.append(jnp.zeros((span - gate_rows - rim, channels * pulses), BF16))
    samples = jnp.concatenate(samples, axis=0)
    matched = jnp.dot(rows_ref[...], samples, preferred_element_type=F32)
    high, low = split_terms(matched)
    pieces = [
        term[part * gate_rows : (part + 1) * gate_rows]
        for term in (high, low, high)
        for part in range(2)
    ]
    stacked = jnp.concatenate(
        [
            jnp.concatenate([piece[:, c * pulses : (c + 1) * pulses] for piece in pieces], axis=1)
            for c in each
        ],
        axis=0,
    )
    spectra = lax.dot_general(
        table_ref[...], stacked, (((1,), (1,)), ((), ())), preferred_element_type=F32
    )
    for part in range(2):
        turned_part = jnp.stack(
            [
                spectra[part * bins : (part + 1) * bins, c * gate_rows : (c + 1) * gate_rows]
                for c in each
            ],
            axis=0,
        )
        place = pl.multiple_of(part * (height // 2) + step * channels, channels)
        turned[:, pl.ds(place, channels), :] = jnp.swapaxes(turned_part, 0, 1)

    @pl.when(step == pl.num_programs(0) - 1)
    def _():
        out_ref[...] = turned[...].astype(BF16)


def form_spectrum(rows, table, raw_echo, next_rows, chunk, chunks):
    _, ch_local, gate_rows, pulses = raw_echo.shape
    channels = ch_local // chunks
    step = math.gcd(channels, 8)
    steps = channels // step
    height = 2 * channels
    bins = table.shape[0] // 2
    return pl.pallas_call(
        spectrum_kernel,
        out_shape=jax.ShapeDtypeStruct((bins, height, gate_rows), BF16),
        grid=(steps,),
        in_specs=[
            pl.BlockSpec(rows.shape, lambda i: (0, 0)),
            pl.BlockSpec(table.shape, lambda i: (0, 0)),
            pl.BlockSpec((2, step, gate_rows, pulses), lambda i: (0, chunk * steps + i, 0, 0)),
            pl.BlockSpec((2, step) + next_rows.shape[2:], lambda i: (0, i, 0, 0)),
        ],
        out_specs=pl.BlockSpec((bins, height, gate_rows), lambda i: (0, 0, 0)),
        scratch_shapes=[pltpu.VMEM((bins, height, gate_rows), F32)],
        compiler_params=PARAMS,
        cost_estimate=pl.CostEstimate(
            flops=2 * rows.size * channels * pulses + 2 * table.size * channels * gate_rows,
            bytes_accessed=8 * channels * gate_rows * pulses,
            transcendentals=0,
        ),
        name="form_spectrum",
    )(rows, table, raw_echo, next_rows)


def owner_count(index_ref, owner):
    return index_ref[2 + owner]


def owner_start(index_ref, owner, owners):
    return index_ref[2 + owners + owner]


def select_kernel(
    index_ref, gates_ref, *refs, chunks, owners, ranges, first, share_slots, pack
):
    spectrum_refs, out_ref = refs[:chunks], refs[-1]
    bin_count, height, gate_rows = spectrum_refs[0].shape
    some, groups, _, width = out_ref.shape
    half = height // 2
    gate_index = lax.broadcasted_iota(jnp.int32, (pack * gate_rows, width), 0)
    part_index = lax.broadcasted_iota(jnp.int32, (1, width), 1) // (width // pack)
    for inner in range(some):
        start = owner_start(index_ref, pl.program_id(0) * some + inner, owners)
        for group in range(groups):
            block, place = divmod(group, groups // ranges)
            slot = block * share_slots + first + place * pack
            bins = [jnp.minimum(start + slot + part, bin_count - 1) for part in range(pack)]
            gates = gates_ref[pl.ds(bins[0], 1), :]
            for part in range(1, pack):
                gates = jnp.where(part_index == part, gates_ref[pl.ds(bins[part], 1), :], gates)
            chooser = jnp.where(gate_index == gates, 1.0, 0.0).astype(BF16)
            spectra = jnp.concatenate(
                [
                    jnp.concatenate([ref[b, s * half : (s + 1) * half] for b in bins], axis=1)
                    for s in range(2)
                    for ref in spectrum_refs
                ],
                axis=0,
            )
            picked = jnp.dot(spectra, chooser, preferred_element_type=F32)
            out_ref[inner, group] = picked.astype(BF16)


def select_gates(
    spectra, index, gates, first, count, share_slots, owners, ranges, pack, earlier
):
    rows = sum(spectrum.shape[1] for spectrum in spectra)
    gate_rows = spectra[0].shape[2]
    groups = ranges * count // pack
    width = gates.shape[1]
    some = math.gcd(owners, 2)
    return pl.pallas_call(
        functools.partial(
            select_kernel,
            chunks=len(spectra),
            owners=owners,
            ranges=ranges,
            first=first,
            share_slots=share_slots,
            pack=pack,
        ),
        out_shape=jax.ShapeDtypeStruct((owners, groups, rows, width), BF16),
        grid=(owners // some,),
        in_specs=[pl.BlockSpec(memory_space=pltpu.SMEM)]
        + [pl.BlockSpec(memory_space=pltpu.VMEM)] * (1 + len(spectra))
        + [pl.BlockSpec(memory_space=pl.ANY)] * len(earlier),
        out_specs=pl.BlockSpec((some, groups, rows, width), lambda i: (i, 0, 0, 0)),
        compiler_params=PARAMS,
        cost_estimate=pl.CostEstimate(
            flops=2 * owners * groups * pack * rows * gate_rows * width,
            bytes_accessed=owners * groups * rows * width * 2,
            transcendentals=0,
        ),
        name="select_gates",
    )(index, gates, *spectra, *earlier)


def beam_kernel(weights_ref, arrived_ref, *refs):
    out_ref = refs[-1]
    sources, ranges, groups, rows, width = arrived_ref.shape
    dof = weights_ref.shape[2]
    half = rows // 2
    for block in range(ranges):
        packed = jnp.concatenate(
            [
                arrived_ref[:, block, g, s * half : (s + 1) * half].reshape(sources * half, width)
                for s in range(2)
                for g in range(groups)
            ],
            axis=1,
        )
        by_real, by_imag = [
            lax.dot_general(
                weights_ref[part], packed, (((0,), (0,)), ((), ())), preferred_element_type=F32
            )
            for part in range(2)
        ]
        middle = groups * width
        real_part = by_real[:, :middle] + by_imag[:, middle:]
        imag_part = by_real[:, middle:] - by_imag[:, :middle]
        for g in range(groups):
            span = slice(g * width, (g + 1) * width)
            out_ref[block, g, :dof] = real_part[:, span].astype(BF16)
            out_ref[block, g, dof:] = imag_part[:, span].astype(BF16)


def form_beams(arrived, weights, earlier):
    _, ranges, groups, _, width = arrived.shape
    shape = (ranges, groups, 2 * weights.shape[2], width)
    return pl.pallas_call(
        beam_kernel,
        out_shape=jax.ShapeDtypeStruct(shape, BF16),
        in_specs=[pl.BlockSpec(memory_space=pltpu.VMEM)] * 2
        + [pl.BlockSpec(memory_space=pl.ANY)] * len(earlier),
        out_specs=pl.BlockSpec(memory_space=pltpu.VMEM),
        compiler_params=PARAMS,
        cost_estimate=pl.CostEstimate(
            flops=4 * arrived.size * weights.shape[2],
            bytes_accessed=arrived.size * 2,
            transcendentals=0,
        ),
        name="form_beams",
    )(weights, arrived, *earlier)


def exchange(arrays, axis):
    count = len(arrays)
    moved = [arrays[0]]
    for shift in range(1, count):
        pairs = [(i, (i + shift) % count) for i in range(count)]
        moved.append(lax.ppermute(arrays[shift], axis, pairs))
    return moved


def split_terms(array):
    high = array.astype(BF16)
    return high, (array - high.astype(F32)).astype(BF16)


def left_terms(array):
    high, low = split_terms(array)
    high, low = high.astype(F32), low.astype(F32)
    return jnp.concatenate([high, high, low], axis=0).T.astype(BF16)


def right_terms(array):
    high, low = split_terms(array)
    return jnp.concatenate([high, low, high], axis=0)


def product(left, right):
    return jnp.dot(left, right, preferred_element_type=F32)


def loaded_covariance(beams, pivot_row, part, pack, count_rows):
    dof = pivot_row.shape[1]
    width = beams[0].shape[1] // pack
    hot = lax.broadcasted_iota(jnp.int32, (dof, dof), 0) == pivot_row
    hot = jnp.where(hot, 1.0, 0.0).astype(BF16)
    own = jnp.concatenate([b[:, part * width : (part + 1) * width] for b in beams], axis=1)
    picked = [
        lax.dot_general(
            hot,
            own[half * dof : (half + 1) * dof],
            (((0,), (0,)), ((), ())),
            preferred_element_type=F32,
        )
        for half in range(2)
    ]
    upper = jnp.concatenate([picked[0], picked[1]], axis=1).astype(BF16)
    lower = jnp.concatenate([picked[1], -picked[0]], axis=1).astype(BF16)
    stacked = jnp.concatenate([upper, lower], axis=0)
    gram = lax.dot_general(
        stacked, stacked, (((1,), (1,)), ((), ())), preferred_element_type=F32
    )
    return gram * (1.0 / count_rows)


def lane_spread(piece, lane):
    return jnp.broadcast_to(piece[:, lane : lane + 1], piece.shape)


def refined_reciprocal(value):
    guess = pl.reciprocal(value, approx=True)
    return guess * (2.0 - value * guess)


def tree_sum(terms):
    while len(terms) > 1:
        terms = [x + y for x, y in zip(terms[::2], terms[1::2])]
    return terms[0]


def eliminate(rows):
    scales = []
    for first in range(0, PANEL, 8):
        span = range(first, first + 8)
        small = {(i, j): lane_spread(rows[i][0], j) for i in span for j in span if j >= i}
        for t in range(first, first + 8, 2):
            u = t + 1
            inverse = refined_reciprocal(small[t, t])
            cross = small[t, t] * small[u, u] - small[t, u] * small[t, u]
            guess = pl.reciprocal(cross, approx=True)
            second = (small[t, t] * guess) * (2.0 - cross * guess)
            scales += [lax.rsqrt(small[t, t]), lax.rsqrt(cross * inverse)]
            factor = small[t, u] * inverse
            for j in range(u + 1, first + 8):
                small[u, j] = small[u, j] - factor * small[t, j]
            rows[u] = [x - factor * y for x, y in zip(rows[u], rows[t])]
            for i in range(u + 1, first + 8):
                one, two = small[t, i] * inverse, small[u, i] * second
                for j in range(i, first + 8):
                    both = small[u, i] * small[u, j]
                    small[i, j] = (small[i, j] - one * small[t, j]) - both * second
                rows[i] = [
                    x - one * y - two * z for x, y, z in zip(rows[i], rows[t], rows[u])
                ]
        for t in span:
            rows[t] = [x * scales[t] for x in rows[t]]
        for i in range(first + 8, PANEL):
            factors = [lane_spread(rows[t][0], i) for t in span]
            rows[i] = [
                x - tree_sum([f * rows[t][w] for f, t in zip(factors, span)])
                for w, x in enumerate(rows[i])
            ]
    return rows


def factor_kernel(
    index_ref, pivots_ref, beams_ref, *refs, first, share_slots, ranges, pack, count_rows
):
    out_refs = refs[:ranges]
    arriving, leaving, *scratch = refs[ranges:]
    slots = len(scratch) // 3
    work, lefts, rights = scratch[:slots], scratch[slots : 2 * slots], scratch[2 * slots :]
    order = work[0].shape[0]
    height = arriving.shape[1] // PANEL

    row = lax.broadcasted_iota(jnp.int32, (LANES, LANES), 0)
    col = lax.broadcasted_iota(jnp.int32, (LANES, LANES), 1)
    loading = jnp.where(row == col, LOADING, 0.0)
    owners = (index_ref.shape[0] - 2) // 2
    bin_lead = owner_start(index_ref, index_ref[0], owners) + index_ref[1] * share_slots + first
    for slot in range(slots):
        group, part = divmod(slot, pack)
        own_bin = jnp.minimum(bin_lead + slot, pivots_ref.shape[0] - 1)
        work[slot][...] = loaded_covariance(
            [beams_ref[r, group] for r in range(ranges)],
            pivots_ref[pl.ds(own_bin, 1), :],
            part,
            pack,
            count_rows,
        )
        for start in range(0, order, LANES):
            work[slot][start : start + LANES, start : start + LANES] += loading

    eights = range(0, PANEL, 8)
    column = lax.broadcasted_iota(jnp.int32, (LANES, 3 * PANEL), 0)

    def spread_out(slot, rows):
        for i in eights:
            for w in range(rows.shape[1] // LANES):
                piece = rows[i : i + 8, w * LANES : (w + 1) * LANES]
                arriving[w, pl.ds(i * height + slot, 8, stride=height), :] = piece

    for slot in range(slots):
        spread_out(slot, work[slot][:PANEL, :])
    for start in range(0, order, LANES):
        chunks = (order - start) // LANES
        stop = start + LANES
        for slot in range(slots):
            lefts[slot][...] = jnp.zeros_like(lefts[slot])
            rights[slot][...] = jnp.zeros_like(rights[slot])

        def one_panel(p, carry, start=start, stop=stop, chunks=chunks):
            back = p * PANEL
            base = pl.multiple_of(start + back, PANEL)
            ahead = pl.multiple_of(jnp.minimum(back + PANEL, LANES - PANEL), PANEL)
            following = pl.multiple_of(start + ahead, PANEL)
            for slot in range(slots):
                left = jnp.where(column >= back + PANEL, lefts[slot][...], 0.0).astype(BF16)
                work[slot][start:stop, start:] -= product(left, rights[slot][:, start:])
            rows = []
            for t in range(PANEL):
                pieces = [arriving[w, t * height : (t + 1) * height, :] for w in range(chunks)]
                pieces[0] = pltpu.roll(pieces[0], (LANES - back) % LANES, 1)
                rows.append(pieces)
            rows = eliminate(rows)
            for t in range(PANEL):
                rows[t][0] = pltpu.roll(rows[t][0], back, 1)
                for w in range(chunks):
                    leaving[w, t * height : (t + 1) * height, :] = rows[t][w]
            for slot in range(slots):
                parts = []
                for w in range(chunks):
                    pieces = [
                        leaving[w, pl.ds(i * height + slot, 8, stride=height), :] for i in eights
                    ]
                    parts.append(jnp.concatenate(pieces, axis=0))
                panel = jnp.concatenate(parts, axis=1)
                work[slot][pl.ds(base, PANEL), start:] = panel
                lefts[slot][...] = left_terms(parts[0]).astype(F32)
                right = right_terms(panel)
                rights[slot][:, start:] = right
                left = lefts[slot][pl.ds(ahead, PANEL), :].astype(BF16)
                spread_out(slot, work[slot][pl.ds(following, PANEL), start:] - product(left, right))
            return carry

        lax.fori_loop(0, LANES // PANEL, one_panel, 0)
        if chunks > 1:
            terms = []
            for slot in range(slots):
                done = work[slot][start:stop, stop:]
                left = jnp.concatenate(
                    [left_terms(done[:, w * LANES : (w + 1) * LANES]) for w in range(chunks - 1)],
                    axis=0,
                )
                right = right_terms(done)
                ready = work[slot][stop : stop + PANEL, stop:] - product(left[:PANEL], right)
                spread_out(slot, ready)
                terms.append((left, right))
            for slot in range(slots):
                left, right = terms[slot]
                work[slot][stop + PANEL :, stop:] -= product(left[PANEL:], right)

    share = order // ranges
    row = lax.broadcasted_iota(jnp.int32, (share, order), 0)
    col = lax.broadcasted_iota(jnp.int32, (share, order), 1)
    for shift, out_ref in enumerate(out_refs):
        lead = pl.multiple_of(lax.rem(index_ref[1] + shift, ranges) * share, math.gcd(share, 16))
        upper = col >= row + lead
        for slot in range(slots):
            piece = work[slot][pl.ds(lead, share), :]
            out_ref[slot] = jnp.where(upper, piece, 0.0).astype(out_ref.dtype)


def factor_slots(beams, pivots, index, first, slots, share_slots, pack, count_rows):
    ranges, _, order, _ = beams.shape
    height = -(-slots // 8) * 8
    return pl.pallas_call(
        functools.partial(
            factor_kernel,
            first=first,
            share_slots=share_slots,
            ranges=ranges,
            pack=pack,
            count_rows=count_rows,
        ),
        out_shape=[jax.ShapeDtypeStruct((slots, order // ranges, order), BF16)] * ranges,
        in_specs=[pl.BlockSpec(memory_space=pltpu.SMEM)]
        + [pl.BlockSpec(memory_space=pltpu.VMEM)] * 2,
        out_specs=[pl.BlockSpec(memory_space=pltpu.VMEM)] * ranges,
        scratch_shapes=[pltpu.VMEM((order // LANES, PANEL * height, LANES), F32)] * 2
        + [pltpu.VMEM((order, order), F32) for _ in range(slots)]
        + [pltpu.VMEM((LANES, 3 * PANEL), F32) for _ in range(slots)]
        + [pltpu.VMEM((3 * PANEL, order), BF16) for _ in range(slots)],
        compiler_params=PARAMS,
        cost_estimate=pl.CostEstimate(
            flops=slots * order**3,
            bytes_accessed=beams.size * 2,
            transcendentals=0,
        ),
        name="factor_slots",
    )(index, pivots, beams)


def place_kernel(index_ref, *refs, first, share_slots, ranges):
    in_refs, out_ref = refs[:ranges], refs[-1]
    slots = out_ref.shape[0]
    steps = in_refs[0].shape[0] // slots
    step = pl.program_id(0)
    shift, place = step // steps, step % steps
    block = lax.rem(index_ref[1] + ranges - shift, ranges)
    lead = block * share_slots + first + place * slots
    for this, ref in enumerate(in_refs):

        @pl.when(shift == this)
        def _(ref=ref):
            for i in range(slots):
                keep = lead + i < owner_count(index_ref, index_ref[0])
                keep = jnp.broadcast_to(keep, out_ref.shape[1:])
                out_ref[i] = jnp.where(keep, ref[place * slots + i].astype(F32), 0.0)


def place_rows(index, arrays, first, share_slots, earlier):
    ranges = len(arrays)
    count = arrays[0].shape[0]
    slots = math.gcd(math.gcd(count, first), share_slots)
    steps = count // slots

    def out_index(step, index_ref):
        block = lax.rem(index_ref[1] + ranges - step // steps, ranges)
        return ((block * share_slots + first) // slots + step % steps, 0, 0)

    return pl.pallas_call(
        functools.partial(place_kernel, first=first, share_slots=share_slots, ranges=ranges),
        out_shape=jax.ShapeDtypeStruct((ranges * share_slots,) + arrays[0].shape[1:], F32),
        grid_spec=pltpu.PrefetchScalarGridSpec(
            num_scalar_prefetch=1,
            grid=(ranges * steps,),
            in_specs=[pl.BlockSpec(memory_space=pltpu.VMEM)] * ranges
            + [pl.BlockSpec(memory_space=pl.ANY)] * len(earlier),
            out_specs=pl.BlockSpec((slots,) + arrays[0].shape[1:], out_index),
        ),
        input_output_aliases={1 + ranges: 0} if earlier else {},
        compiler_params=PARAMS,
        name="place_rows",
    )(index, *arrays, *earlier)


def slot_parts(share_slots, pack):
    head = share_slots - pack
    return [(0, head), (head, pack)] if head > 0 else [(0, share_slots)]


def local(raw_echo, replica, beam_weights, pivots, owner_counts, train_gates):
    ch_local = raw_echo.shape[1]
    gate_rows = raw_echo.shape[2]
    pulse_count = raw_echo.shape[3]
    tap_count = replica.shape[1]
    train_local = train_gates.shape[1]
    owners = lax.axis_size("dop")
    ranges = lax.axis_size("rng")
    most_slots = 2 * (pulse_count // owners)
    share_slots = most_slots // ranges
    pack = max(1, min(LANES // train_local, share_slots))

    chunks = max(1, min(4, ch_local // 16))
    chunk_rows = ch_local // chunks
    rim = -(-(tap_count - 1) // 16) * 16
    filters = filter_rows(replica, gate_rows)
    table = doppler_table(pulse_count).transpose(0, 3, 1, 2)
    table = table.reshape(2 * pulse_count, -1)
    table_high = lax.reduce_precision(table, exponent_bits=8, mantissa_bits=7)
    table = jnp.concatenate([table_high, table_high, table - table_high], axis=1).astype(BF16)
    following = [shifted(rim_rows(raw_echo, rim, c, chunks), "rng", -1) for c in range(chunks)]
    spectra = [
        form_spectrum(filters, table, raw_echo, following[c], c, chunks) for c in range(chunks)
    ]

    starts = jnp.cumsum(owner_counts, dtype=jnp.int32) - owner_counts
    places = jnp.stack([lax.axis_index("dop"), lax.axis_index("rng")]).astype(jnp.int32)
    index = jnp.concatenate([places, owner_counts, starts])
    local_gates = train_gates % gate_rows
    gates = jnp.concatenate([local_gates + part * gate_rows for part in range(pack)], axis=1)
    count_rows = float(train_local * ranges)

    parts = slot_parts(share_slots, pack)
    outgoing = []
    for first, count in parts:
        earlier = [beam_weights] if first > 0 else []
        outgoing.append(
            select_gates(
                spectra, index, gates, first, count, share_slots, owners, ranges, pack, earlier
            )
        )
    axes = ("dop", "rng")
    sent = [
        lax.all_to_all(
            array.reshape(owners * ranges, -1, *array.shape[2:]),
            axes,
            split_axis=0,
            concat_axis=0,
            tiled=True,
        ).reshape(owners, ranges, -1, *array.shape[2:])
        for array in outgoing
    ]
    result, earlier = [], outgoing[1:]
    for (first, count), arrived in zip(parts, sent):
        beams = form_beams(arrived, beam_weights, earlier)
        factors = factor_slots(beams, pivots, index, first, count, share_slots, pack, count_rows)
        earlier = factors[:1]
        rows = exchange(factors, "rng")
        result = [place_rows(index, rows, first, share_slots, result)]
    return result[0]


def solution(mesh):
    return jax.shard_map(
        local,
        mesh=mesh,
        in_specs=(P(None, "dop", "rng", None), P(), P(), P(), P(), P(None, "rng")),
        out_specs=P("dop", "rng", None),
        check_vma=False,
    )
```

```python
import functools
import math

import jax
import jax.numpy as jnp
import numpy as np
from jax import lax
from jax.experimental import pallas as pl
from jax.experimental.pallas import tpu as pltpu
from jax.sharding import PartitionSpec as P

LOADING = 0.25
LANES = 128
PANEL = 32
BF16 = jnp.bfloat16
F32 = jnp.float32
PARAMS = pltpu.CompilerParams(vmem_limit_bytes=48 * 1024 * 1024)


def shifted(array, axis, by):
    count = lax.axis_size(axis)
    pairs = [(i, i + by) for i in range(count) if 0 <= i + by < count]
    return lax.ppermute(array, axis, pairs)


def doppler_table(pulse_count):
    pulse_index = np.arange(pulse_count)
    phase_index = pulse_index[:, None] * pulse_index[None, :] % pulse_count
    angle_table = phase_index.astype(np.float32) * np.float32(2.0 * math.pi / pulse_count)
    norm_scale = np.float32(1.0 / math.sqrt(pulse_count))
    real_part, imag_part = np.cos(angle_table) * norm_scale, np.sin(angle_table) * norm_scale
    table = np.block([[real_part.T, imag_part.T], [-imag_part.T, real_part.T]])
    high = table.astype(BF16)
    low = (table - high.astype(np.float32)).astype(BF16)
    return jnp.asarray(np.concatenate([high, high, low], axis=1))


def filter_kernel(replica_ref, out_ref):
    gate_rows, span = out_ref.shape[0] // 2, replica_ref.shape[1]
    banded = [
        pltpu.roll(
            jnp.broadcast_to(replica_ref[part : part + 1, :], (gate_rows, span)),
            0,
            1,
            stride=1,
            stride_axis=0,
        )
        for part in range(2)
    ]
    out_ref[:gate_rows, :span] = banded[0].astype(BF16)
    out_ref[:gate_rows, span:] = banded[1].astype(BF16)
    out_ref[gate_rows:, :span] = (-banded[1]).astype(BF16)
    out_ref[gate_rows:, span:] = banded[0].astype(BF16)


def filter_rows(replica, gate_rows):
    tap_count = replica.shape[1]
    span = -(-(gate_rows + tap_count) // LANES) * LANES
    return pl.pallas_call(
        filter_kernel,
        out_shape=jax.ShapeDtypeStruct((2 * gate_rows, 2 * span), BF16),
        in_specs=[pl.BlockSpec(memory_space=pltpu.VMEM)],
        out_specs=pl.BlockSpec(memory_space=pltpu.VMEM),
        compiler_params=PARAMS,
        name="filter_rows",
    )(jnp.pad(replica, ((0, 0), (0, span - tap_count))))


def rim_kernel(echo_ref, out_ref):
    out_ref[...] = echo_ref[...].astype(BF16)


def rim_rows(raw_echo, rim, chunk, chunks):
    _, ch_local, _, pulses = raw_echo.shape
    shape = (2, ch_local // chunks, rim, pulses)
    return pl.pallas_call(
        rim_kernel,
        out_shape=jax.ShapeDtypeStruct(shape, BF16),
        grid=(1,),
        in_specs=[pl.BlockSpec(shape, lambda i: (0, chunk, 0, 0))],
        out_specs=pl.BlockSpec(shape, lambda i: (0, 0, 0, 0)),
        compiler_params=PARAMS,
        name="rim_rows",
    )(raw_echo)


def spectrum_kernel(rows_ref, table_ref, own_ref, next_ref, out_ref, turned):
    step = pl.program_id(0)
    _, channels, gate_rows, pulses = own_ref.shape
    bins, height, _ = out_ref.shape
    rim = next_ref.shape[2]
    span = rows_ref.shape[1] // 2
    each = range(channels)
    samples = []
    for part in range(2):
        samples += [
            jnp.concatenate([own_ref[part, c] for c in each], axis=1).astype(BF16),
            jnp.concatenate([next_ref[part, c] for c in each], axis=1),
        ]
        if span > gate_rows + rim:
            samples.append(jnp.zeros((span - gate_rows - rim, channels * pulses), BF16))
    samples = jnp.concatenate(samples, axis=0)
    matched = jnp.dot(rows_ref[...], samples, preferred_element_type=F32)
    high, low = split_terms(matched)
    pieces = [
        term[part * gate_rows : (part + 1) * gate_rows]
        for term in (high, low, high)
        for part in range(2)
    ]
    stacked = jnp.concatenate(
        [
            jnp.concatenate([piece[:, c * pulses : (c + 1) * pulses] for piece in pieces], axis=1)
            for c in each
        ],
        axis=0,
    )
    spectra = lax.dot_general(
        table_ref[...], stacked, (((1,), (1,)), ((), ())), preferred_element_type=F32
    )
    for part in range(2):
        turned_part = jnp.stack(
            [
                spectra[part * bins : (part + 1) * bins, c * gate_rows : (c + 1) * gate_rows]
                for c in each
            ],
            axis=0,
        )
        place = pl.multiple_of(part * (height // 2) + step * channels, channels)
        turned[:, pl.ds(place, channels), :] = jnp.swapaxes(turned_part, 0, 1)

    @pl.when(step == pl.num_programs(0) - 1)
    def _():
        out_ref[...] = turned[...].astype(BF16)


def form_spectrum(rows, table, raw_echo, next_rows, chunk, chunks):
    _, ch_local, gate_rows, pulses = raw_echo.shape
    channels = ch_local // chunks
    step = math.gcd(channels, 8)
    steps = channels // step
    height = 2 * channels
    bins = table.shape[0] // 2
    return pl.pallas_call(
        spectrum_kernel,
        out_shape=jax.ShapeDtypeStruct((bins, height, gate_rows), BF16),
        grid=(steps,),
        in_specs=[
            pl.BlockSpec(rows.shape, lambda i: (0, 0)),
            pl.BlockSpec(table.shape, lambda i: (0, 0)),
            pl.BlockSpec((2, step, gate_rows, pulses), lambda i: (0, chunk * steps + i, 0, 0)),
            pl.BlockSpec((2, step) + next_rows.shape[2:], lambda i: (0, i, 0, 0)),
        ],
        out_specs=pl.BlockSpec((bins, height, gate_rows), lambda i: (0, 0, 0)),
        scratch_shapes=[pltpu.VMEM((bins, height, gate_rows), F32)],
        compiler_params=PARAMS,
        cost_estimate=pl.CostEstimate(
            flops=2 * rows.size * channels * pulses + 2 * table.size * channels * gate_rows,
            bytes_accessed=8 * channels * gate_rows * pulses,
            transcendentals=0,
        ),
        name="form_spectrum",
    )(rows, table, raw_echo, next_rows)


def owner_count(index_ref, owner):
    return index_ref[2 + owner]


def owner_start(index_ref, owner, owners):
    return index_ref[2 + owners + owner]


def select_kernel(
    index_ref, gates_ref, *refs, chunks, owners, ranges, first, share_slots, pack
):
    spectrum_refs, out_ref = refs[:chunks], refs[-1]
    bin_count, height, gate_rows = spectrum_refs[0].shape
    some, groups, _, width = out_ref.shape
    half = height // 2
    gate_index = lax.broadcasted_iota(jnp.int32, (pack * gate_rows, width), 0)
    part_index = lax.broadcasted_iota(jnp.int32, (1, width), 1) // (width // pack)
    for inner in range(some):
        start = owner_start(index_ref, pl.program_id(0) * some + inner, owners)
        for group in range(groups):
            block, place = divmod(group, groups // ranges)
            slot = block * share_slots + first + place * pack
            bins = [jnp.minimum(start + slot + part, bin_count - 1) for part in range(pack)]
            gates = gates_ref[pl.ds(bins[0], 1), :]
            for part in range(1, pack):
                gates = jnp.where(part_index == part, gates_ref[pl.ds(bins[part], 1), :], gates)
            chooser = jnp.where(gate_index == gates, 1.0, 0.0).astype(BF16)
            spectra = jnp.concatenate(
                [
                    jnp.concatenate([ref[b, s * half : (s + 1) * half] for b in bins], axis=1)
                    for s in range(2)
                    for ref in spectrum_refs
                ],
                axis=0,
            )
            picked = jnp.dot(spectra, chooser, preferred_element_type=F32)
            out_ref[inner, group] = picked.astype(BF16)


def select_gates(
    spectra, index, gates, first, count, share_slots, owners, ranges, pack, earlier
):
    rows = sum(spectrum.shape[1] for spectrum in spectra)
    gate_rows = spectra[0].shape[2]
    groups = ranges * count // pack
    width = gates.shape[1]
    some = math.gcd(owners, 2)
    return pl.pallas_call(
        functools.partial(
            select_kernel,
            chunks=len(spectra),
            owners=owners,
            ranges=ranges,
            first=first,
            share_slots=share_slots,
            pack=pack,
        ),
        out_shape=jax.ShapeDtypeStruct((owners, groups, rows, width), BF16),
        grid=(owners // some,),
        in_specs=[pl.BlockSpec(memory_space=pltpu.SMEM)]
        + [pl.BlockSpec(memory_space=pltpu.VMEM)] * (1 + len(spectra))
        + [pl.BlockSpec(memory_space=pl.ANY)] * len(earlier),
        out_specs=pl.BlockSpec((some, groups, rows, width), lambda i: (i, 0, 0, 0)),
        compiler_params=PARAMS,
        cost_estimate=pl.CostEstimate(
            flops=2 * owners * groups * pack * rows * gate_rows * width,
            bytes_accessed=owners * groups * rows * width * 2,
            transcendentals=0,
        ),
        name="select_gates",
    )(index, gates, *spectra, *earlier)


def beam_kernel(weights_ref, arrived_ref, *refs):
    out_ref = refs[-1]
    sources, _, groups, rows, width = arrived_ref.shape
    dof = weights_ref.shape[2]
    half = rows // 2
    packed = jnp.concatenate(
        [
            arrived_ref[:, 0, g, s * half : (s + 1) * half].reshape(sources * half, width)
            for s in range(2)
            for g in range(groups)
        ],
        axis=1,
    )
    by_real, by_imag = [
        lax.dot_general(
            weights_ref[part], packed, (((0,), (0,)), ((), ())), preferred_element_type=F32
        )
        for part in range(2)
    ]
    middle = groups * width
    real_part = by_real[:, :middle] + by_imag[:, middle:]
    imag_part = by_real[:, middle:] - by_imag[:, :middle]
    for g in range(groups):
        span = slice(g * width, (g + 1) * width)
        out_ref[0, g, :dof] = real_part[:, span].astype(BF16)
        out_ref[0, g, dof:] = imag_part[:, span].astype(BF16)


def form_beams(arrived, weights, earlier):
    sources, ranges, groups, rows, width = arrived.shape
    shape = (ranges, groups, 2 * weights.shape[2], width)
    return pl.pallas_call(
        beam_kernel,
        out_shape=jax.ShapeDtypeStruct(shape, BF16),
        grid=(ranges,),
        in_specs=[
            pl.BlockSpec(weights.shape, lambda i: (0, 0, 0)),
            pl.BlockSpec((sources, 1, groups, rows, width), lambda i: (0, i, 0, 0, 0)),
        ]
        + [pl.BlockSpec(memory_space=pl.ANY)] * len(earlier),
        out_specs=pl.BlockSpec((1,) + shape[1:], lambda i: (i, 0, 0, 0)),
        compiler_params=PARAMS,
        cost_estimate=pl.CostEstimate(
            flops=4 * arrived.size * weights.shape[2],
            bytes_accessed=arrived.size * 2,
            transcendentals=0,
        ),
        name="form_beams",
    )(weights, arrived, *earlier)


def exchange(arrays, axis):
    count = len(arrays)
    moved = [arrays[0]]
    for shift in range(1, count):
        pairs = [(i, (i + shift) % count) for i in range(count)]
        moved.append(lax.ppermute(arrays[shift], axis, pairs))
    return moved


def split_terms(array):
    high = array.astype(BF16)
    return high, (array - high.astype(F32)).astype(BF16)


def left_terms(array):
    high, low = split_terms(array)
    high, low = high.astype(F32), low.astype(F32)
    return jnp.concatenate([high, high, low], axis=0).T.astype(BF16)


def right_terms(array):
    high, low = split_terms(array)
    return jnp.concatenate([high, low, high], axis=0)


def product(left, right):
    return jnp.dot(left, right, preferred_element_type=F32)


def loaded_covariance(beams, pivot_row, part, pack, count_rows):
    dof = pivot_row.shape[1]
    width = beams[0].shape[1] // pack
    hot = lax.broadcasted_iota(jnp.int32, (dof, dof), 0) == pivot_row
    hot = jnp.where(hot, 1.0, 0.0).astype(BF16)
    own = jnp.concatenate([b[:, part * width : (part + 1) * width] for b in beams], axis=1)
    picked = [
        lax.dot_general(
            hot,
            own[half * dof : (half + 1) * dof],
            (((0,), (0,)), ((), ())),
            preferred_element_type=F32,
        )
        for half in range(2)
    ]
    upper = jnp.concatenate([picked[0], picked[1]], axis=1).astype(BF16)
    lower = jnp.concatenate([picked[1], -picked[0]], axis=1).astype(BF16)
    stacked = jnp.concatenate([upper, lower], axis=0)
    gram = lax.dot_general(
        stacked, stacked, (((1,), (1,)), ((), ())), preferred_element_type=F32
    )
    return gram * (1.0 / count_rows)


def lane_spread(piece, lane):
    lanes = jnp.full(piece.shape, lane, jnp.int32)
    return jnp.take_along_axis(piece, lanes, axis=1, mode="promise_in_bounds")


def refined_reciprocal(value):
    guess = pl.reciprocal(value, approx=True)
    return guess * (2.0 - value * guess)


def tree_sum(terms):
    while len(terms) > 1:
        terms = [x + y for x, y in zip(terms[::2], terms[1::2])]
    return terms[0]


def eliminate(rows):
    scales = []
    for first in range(0, PANEL, 8):
        span = range(first, first + 8)
        small = {(i, j): lane_spread(rows[i][0], j) for i in span for j in span if j >= i}
        for t in range(first, first + 8, 2):
            u = t + 1
            inverse = refined_reciprocal(small[t, t])
            cross = small[t, t] * small[u, u] - small[t, u] * small[t, u]
            guess = pl.reciprocal(cross, approx=True)
            second = (small[t, t] * guess) * (2.0 - cross * guess)
            scales += [lax.rsqrt(small[t, t]), lax.rsqrt(cross * inverse)]
            factor = small[t, u] * inverse
            for j in range(u + 1, first + 8):
                small[u, j] = small[u, j] - factor * small[t, j]
            rows[u] = [x - factor * y for x, y in zip(rows[u], rows[t])]
            for i in range(u + 1, first + 8):
                one, two = small[t, i] * inverse, small[u, i] * second
                for j in range(i, first + 8):
                    both = small[u, i] * small[u, j]
                    small[i, j] = (small[i, j] - one * small[t, j]) - both * second
                rows[i] = [
                    x - one * y - two * z for x, y, z in zip(rows[i], rows[t], rows[u])
                ]
        for t in span:
            rows[t] = [x * scales[t] for x in rows[t]]
        for i in range(first + 8, PANEL):
            factors = [lane_spread(rows[t][0], i) for t in span]
            rows[i] = [
                x - tree_sum([f * rows[t][w] for f, t in zip(factors, span)])
                for w, x in enumerate(rows[i])
            ]
    return rows


def factor_kernel(
    index_ref, pivots_ref, beams_ref, *refs, first, share_slots, ranges, pack, count_rows
):
    out_refs = refs[:ranges]
    arriving, leaving, *scratch = refs[ranges:]
    slots = len(scratch) // 3
    work, lefts, rights = scratch[:slots], scratch[slots : 2 * slots], scratch[2 * slots :]
    order = work[0].shape[0]
    height = arriving.shape[1] // PANEL

    row = lax.broadcasted_iota(jnp.int32, (LANES, LANES), 0)
    col = lax.broadcasted_iota(jnp.int32, (LANES, LANES), 1)
    loading = jnp.where(row == col, LOADING, 0.0)
    owners = (index_ref.shape[0] - 2) // 2
    bin_lead = owner_start(index_ref, index_ref[0], owners) + index_ref[1] * share_slots + first
    for slot in range(slots):
        group, part = divmod(slot, pack)
        own_bin = jnp.minimum(bin_lead + slot, pivots_ref.shape[0] - 1)
        work[slot][...] = loaded_covariance(
            [beams_ref[r, group] for r in range(ranges)],
            pivots_ref[pl.ds(own_bin, 1), :],
            part,
            pack,
            count_rows,
        )
        for start in range(0, order, LANES):
            work[slot][start : start + LANES, start : start + LANES] += loading

    eights = range(0, PANEL, 8)
    column = lax.broadcasted_iota(jnp.int32, (LANES, 3 * PANEL), 0)

    def spread_out(slot, rows):
        for i in eights:
            for w in range(rows.shape[1] // LANES):
                piece = rows[i : i + 8, w * LANES : (w + 1) * LANES]
                arriving[w, pl.ds(i * height + slot, 8, stride=height), :] = piece

    for slot in range(slots):
        spread_out(slot, work[slot][:PANEL, :])
    for start in range(0, order, LANES):
        chunks = (order - start) // LANES
        stop = start + LANES
        for slot in range(slots):
            lefts[slot][...] = jnp.zeros_like(lefts[slot])
            rights[slot][...] = jnp.zeros_like(rights[slot])

        def one_panel(p, carry, start=start, stop=stop, chunks=chunks):
            back = p * PANEL
            base = pl.multiple_of(start + back, PANEL)
            ahead = pl.multiple_of(jnp.minimum(back + PANEL, LANES - PANEL), PANEL)
            following = pl.multiple_of(start + ahead, PANEL)
            for slot in range(slots):
                left = jnp.where(column >= back + PANEL, lefts[slot][...], 0.0).astype(BF16)
                work[slot][start:stop, start:] -= product(left, rights[slot][:, start:])
            rows = []
            for t in range(PANEL):
                pieces = [arriving[w, t * height : (t + 1) * height, :] for w in range(chunks)]
                pieces[0] = pltpu.roll(pieces[0], (LANES - back) % LANES, 1)
                rows.append(pieces)
            rows = eliminate(rows)
            for t in range(PANEL):
                rows[t][0] = pltpu.roll(rows[t][0], back, 1)
                for w in range(chunks):
                    leaving[w, t * height : (t + 1) * height, :] = rows[t][w]
            for slot in range(slots):
                parts = []
                for w in range(chunks):
                    pieces = [
                        leaving[w, pl.ds(i * height + slot, 8, stride=height), :] for i in eights
                    ]
                    parts.append(jnp.concatenate(pieces, axis=0))
                panel = jnp.concatenate(parts, axis=1)
                work[slot][pl.ds(base, PANEL), start:] = panel
                lefts[slot][...] = left_terms(parts[0]).astype(F32)
                right = right_terms(panel)
                rights[slot][:, start:] = right
                left = lefts[slot][pl.ds(ahead, PANEL), :].astype(BF16)
                spread_out(slot, work[slot][pl.ds(following, PANEL), start:] - product(left, right))
            return carry

        lax.fori_loop(0, LANES // PANEL, one_panel, 0)
        if chunks > 1:
            terms = []
            for slot in range(slots):
                done = work[slot][start:stop, stop:]
                left = jnp.concatenate(
                    [left_terms(done[:, w * LANES : (w + 1) * LANES]) for w in range(chunks - 1)],
                    axis=0,
                )
                right = right_terms(done)
                ready = work[slot][stop : stop + PANEL, stop:] - product(left[:PANEL], right)
                spread_out(slot, ready)
                terms.append((left, right))
            for slot in range(slots):
                left, right = terms[slot]
                work[slot][stop + PANEL :, stop:] -= product(left[PANEL:], right)

    share = order // ranges
    row = lax.broadcasted_iota(jnp.int32, (share, order), 0)
    col = lax.broadcasted_iota(jnp.int32, (share, order), 1)
    for shift, out_ref in enumerate(out_refs):
        lead = pl.multiple_of(lax.rem(index_ref[1] + shift, ranges) * share, math.gcd(share, 16))
        upper = col >= row + lead
        for slot in range(slots):
            piece = work[slot][pl.ds(lead, share), :]
            out_ref[slot] = jnp.where(upper, piece, 0.0).astype(out_ref.dtype)


def factor_slots(beams, pivots, index, first, slots, share_slots, pack, count_rows):
    ranges, _, order, _ = beams.shape
    height = -(-slots // 8) * 8
    return pl.pallas_call(
        functools.partial(
            factor_kernel,
            first=first,
            share_slots=share_slots,
            ranges=ranges,
            pack=pack,
            count_rows=count_rows,
        ),
        out_shape=[jax.ShapeDtypeStruct((slots, order // ranges, order), BF16)] * ranges,
        in_specs=[pl.BlockSpec(memory_space=pltpu.SMEM)]
        + [pl.BlockSpec(memory_space=pltpu.VMEM)] * 2,
        out_specs=[pl.BlockSpec(memory_space=pltpu.VMEM)] * ranges,
        scratch_shapes=[pltpu.VMEM((order // LANES, PANEL * height, LANES), F32)] * 2
        + [pltpu.VMEM((order, order), F32) for _ in range(slots)]
        + [pltpu.VMEM((LANES, 3 * PANEL), F32) for _ in range(slots)]
        + [pltpu.VMEM((3 * PANEL, order), BF16) for _ in range(slots)],
        compiler_params=PARAMS,
        cost_estimate=pl.CostEstimate(
            flops=slots * order**3,
            bytes_accessed=beams.size * 2,
            transcendentals=0,
        ),
        name="factor_slots",
    )(index, pivots, beams)


def place_kernel(index_ref, *refs, first, share_slots, ranges):
    in_refs, out_ref = refs[:ranges], refs[-1]
    slots = out_ref.shape[0]
    steps = in_refs[0].shape[0] // slots
    step = pl.program_id(0)
    shift, place = step // steps, step % steps
    block = lax.rem(index_ref[1] + ranges - shift, ranges)
    lead = block * share_slots + first + place * slots
    for this, ref in enumerate(in_refs):

        @pl.when(shift == this)
        def _(ref=ref):
            for i in range(slots):
                keep = lead + i < owner_count(index_ref, index_ref[0])
                keep = jnp.broadcast_to(keep, out_ref.shape[1:])
                out_ref[i] = jnp.where(keep, ref[place * slots + i].astype(F32), 0.0)


def place_rows(index, arrays, first, share_slots, earlier):
    ranges = len(arrays)
    count = arrays[0].shape[0]
    slots = math.gcd(math.gcd(count, first), share_slots)
    steps = count // slots

    def out_index(step, index_ref):
        block = lax.rem(index_ref[1] + ranges - step // steps, ranges)
        return ((block * share_slots + first) // slots + step % steps, 0, 0)

    return pl.pallas_call(
        functools.partial(place_kernel, first=first, share_slots=share_slots, ranges=ranges),
        out_shape=jax.ShapeDtypeStruct((ranges * share_slots,) + arrays[0].shape[1:], F32),
        grid_spec=pltpu.PrefetchScalarGridSpec(
            num_scalar_prefetch=1,
            grid=(ranges * steps,),
            in_specs=[pl.BlockSpec(memory_space=pltpu.VMEM)] * ranges
            + [pl.BlockSpec(memory_space=pl.ANY)] * len(earlier),
            out_specs=pl.BlockSpec((slots,) + arrays[0].shape[1:], out_index),
        ),
        input_output_aliases={1 + ranges: 0} if earlier else {},
        compiler_params=PARAMS,
        name="place_rows",
    )(index, *arrays, *earlier)


def slot_parts(share_slots, pack):
    head = share_slots - pack
    return [(0, head), (head, pack)] if head > 0 else [(0, share_slots)]


def local(raw_echo, replica, beam_weights, pivots, owner_counts, train_gates):
    ch_local = raw_echo.shape[1]
    gate_rows = raw_echo.shape[2]
    pulse_count = raw_echo.shape[3]
    tap_count = replica.shape[1]
    train_local = train_gates.shape[1]
    owners = lax.axis_size("dop")
    ranges = lax.axis_size("rng")
    most_slots = 2 * (pulse_count // owners)
    share_slots = most_slots // ranges
    pack = max(1, min(LANES // train_local, share_slots))

    chunks = max(1, min(4, ch_local // 16))
    chunk_rows = ch_local // chunks
    rim = -(-(tap_count - 1) // 16) * 16
    filters = filter_rows(replica, gate_rows)
    table = doppler_table(pulse_count)
    following = [shifted(rim_rows(raw_echo, rim, c, chunks), "rng", -1) for c in range(chunks)]
    spectra = [
        form_spectrum(filters, table, raw_echo, following[c], c, chunks) for c in range(chunks)
    ]

    starts = jnp.cumsum(owner_counts, dtype=jnp.int32) - owner_counts
    places = jnp.stack([lax.axis_index("dop"), lax.axis_index("rng")]).astype(jnp.int32)
    index = jnp.concatenate([places, owner_counts, starts])
    local_gates = train_gates % gate_rows
    gates = jnp.concatenate([local_gates + part * gate_rows for part in range(pack)], axis=1)
    count_rows = float(train_local * ranges)

    parts = slot_parts(share_slots, pack)
    outgoing = []
    for first, count in parts:
        earlier = [beam_weights] if first > 0 else []
        outgoing.append(
            select_gates(
                spectra, index, gates, first, count, share_slots, owners, ranges, pack, earlier
            )
        )
    axes = ("dop", "rng")
    sent = [
        lax.all_to_all(
            array.reshape(owners * ranges, -1, *array.shape[2:]),
            axes,
            split_axis=0,
            concat_axis=0,
            tiled=True,
        ).reshape(owners, ranges, -1, *array.shape[2:])
        for array in outgoing
    ]
    result, earlier = [], outgoing[1:]
    for (first, count), arrived in zip(parts, sent):
        beams = form_beams(arrived, beam_weights, earlier)
        factors = factor_slots(beams, pivots, index, first, count, share_slots, pack, count_rows)
        earlier = factors[:1]
        rows = exchange(factors, "rng")
        result = [place_rows(index, rows, first, share_slots, result)]
    return result[0]


def solution(mesh):
    return jax.shard_map(
        local,
        mesh=mesh,
        in_specs=(P(None, "dop", "rng", None), P(), P(), P(), P(), P(None, "rng")),
        out_specs=P("dop", "rng", None),
        check_vma=False,
    )
```

```python
import functools
import math

import jax
import jax.numpy as jnp
import numpy as np
from jax import lax
from jax.experimental import pallas as pl
from jax.experimental.pallas import tpu as pltpu
from jax.sharding import PartitionSpec as P

LOADING = 0.25
LANES = 128
PANEL = 32
BF16 = jnp.bfloat16
F32 = jnp.float32
PARAMS = pltpu.CompilerParams(vmem_limit_bytes=48 * 1024 * 1024)


def shifted(array, axis, by):
    count = lax.axis_size(axis)
    pairs = [(i, i + by) for i in range(count) if 0 <= i + by < count]
    return lax.ppermute(array, axis, pairs)


def doppler_table(pulse_count):
    pulse_index = np.arange(pulse_count)
    phase_index = pulse_index[:, None] * pulse_index[None, :] % pulse_count
    angle_table = phase_index.astype(np.float32) * np.float32(2.0 * math.pi / pulse_count)
    norm_scale = np.float32(1.0 / math.sqrt(pulse_count))
    real_part, imag_part = np.cos(angle_table) * norm_scale, np.sin(angle_table) * norm_scale
    table = np.block([[real_part.T, imag_part.T], [-imag_part.T, real_part.T]])
    high = table.astype(BF16)
    low = (table - high.astype(np.float32)).astype(BF16)
    return jnp.asarray(np.concatenate([high, high, low], axis=1))


def filter_kernel(replica_ref, out_ref):
    gate_rows, span = out_ref.shape[0] // 2, replica_ref.shape[1]
    banded = [
        pltpu.roll(
            jnp.broadcast_to(replica_ref[part : part + 1, :], (gate_rows, span)),
            0,
            1,
            stride=1,
            stride_axis=0,
        )
        for part in range(2)
    ]
    out_ref[:gate_rows, :span] = banded[0].astype(BF16)
    out_ref[:gate_rows, span:] = banded[1].astype(BF16)
    out_ref[gate_rows:, :span] = (-banded[1]).astype(BF16)
    out_ref[gate_rows:, span:] = banded[0].astype(BF16)


def filter_rows(replica, gate_rows):
    tap_count = replica.shape[1]
    span = -(-(gate_rows + tap_count) // LANES) * LANES
    return pl.pallas_call(
        filter_kernel,
        out_shape=jax.ShapeDtypeStruct((2 * gate_rows, 2 * span), BF16),
        in_specs=[pl.BlockSpec(memory_space=pltpu.VMEM)],
        out_specs=pl.BlockSpec(memory_space=pltpu.VMEM),
        compiler_params=PARAMS,
        name="filter_rows",
    )(jnp.pad(replica, ((0, 0), (0, span - tap_count))))


def rim_kernel(echo_ref, out_ref):
    out_ref[...] = echo_ref[...].astype(BF16)


def rim_rows(raw_echo, rim, chunk, chunks):
    _, ch_local, _, pulses = raw_echo.shape
    shape = (2, ch_local // chunks, rim, pulses)
    return pl.pallas_call(
        rim_kernel,
        out_shape=jax.ShapeDtypeStruct(shape, BF16),
        grid=(1,),
        in_specs=[pl.BlockSpec(shape, lambda i: (0, chunk, 0, 0))],
        out_specs=pl.BlockSpec(shape, lambda i: (0, 0, 0, 0)),
        compiler_params=PARAMS,
        name="rim_rows",
    )(raw_echo)


def spectrum_kernel(rows_ref, table_ref, own_ref, next_ref, out_ref, turned):
    step = pl.program_id(0)
    _, channels, gate_rows, pulses = own_ref.shape
    bins, height, _ = out_ref.shape
    rim = next_ref.shape[2]
    span = rows_ref.shape[1] // 2
    each = range(channels)
    samples = []
    for part in range(2):
        samples += [
            jnp.concatenate([own_ref[part, c] for c in each], axis=1).astype(BF16),
            jnp.concatenate([next_ref[part, c] for c in each], axis=1),
        ]
        if span > gate_rows + rim:
            samples.append(jnp.zeros((span - gate_rows - rim, channels * pulses), BF16))
    samples = jnp.concatenate(samples, axis=0)
    matched = jnp.dot(rows_ref[...], samples, preferred_element_type=F32)
    high, low = split_terms(matched)
    pieces = [
        term[part * gate_rows : (part + 1) * gate_rows]
        for term in (high, low, high)
        for part in range(2)
    ]
    stacked = jnp.concatenate(
        [
            jnp.concatenate([piece[:, c * pulses : (c + 1) * pulses] for piece in pieces], axis=1)
            for c in each
        ],
        axis=0,
    )
    spectra = lax.dot_general(
        table_ref[...], stacked, (((1,), (1,)), ((), ())), preferred_element_type=F32
    )
    for part in range(2):
        turned_part = jnp.stack(
            [
                spectra[part * bins : (part + 1) * bins, c * gate_rows : (c + 1) * gate_rows]
                for c in each
            ],
            axis=0,
        )
        place = pl.multiple_of(part * (height // 2) + step * channels, channels)
        turned[:, pl.ds(place, channels), :] = jnp.swapaxes(turned_part, 0, 1)

    @pl.when(step == pl.num_programs(0) - 1)
    def _():
        out_ref[...] = turned[...].astype(BF16)


def form_spectrum(rows, table, raw_echo, next_rows, chunk, chunks):
    _, ch_local, gate_rows, pulses = raw_echo.shape
    channels = ch_local // chunks
    step = math.gcd(channels, 8)
    steps = channels // step
    height = 2 * channels
    bins = table.shape[0] // 2
    return pl.pallas_call(
        spectrum_kernel,
        out_shape=jax.ShapeDtypeStruct((bins, height, gate_rows), BF16),
        grid=(steps,),
        in_specs=[
            pl.BlockSpec(rows.shape, lambda i: (0, 0)),
            pl.BlockSpec(table.shape, lambda i: (0, 0)),
            pl.BlockSpec((2, step, gate_rows, pulses), lambda i: (0, chunk * steps + i, 0, 0)),
            pl.BlockSpec((2, step) + next_rows.shape[2:], lambda i: (0, i, 0, 0)),
        ],
        out_specs=pl.BlockSpec((bins, height, gate_rows), lambda i: (0, 0, 0)),
        scratch_shapes=[pltpu.VMEM((bins, height, gate_rows), F32)],
        compiler_params=PARAMS,
        cost_estimate=pl.CostEstimate(
            flops=2 * rows.size * channels * pulses + 2 * table.size * channels * gate_rows,
            bytes_accessed=8 * channels * gate_rows * pulses,
            transcendentals=0,
        ),
        name="form_spectrum",
    )(rows, table, raw_echo, next_rows)


def owner_count(index_ref, owner):
    return index_ref[2 + owner]


def owner_start(index_ref, owner, owners):
    return index_ref[2 + owners + owner]


def select_kernel(
    index_ref, gates_ref, *refs, chunks, owners, ranges, first, share_slots, pack
):
    spectrum_refs, out_ref, token_ref = refs[:chunks], refs[-2], refs[-1]
    token_ref[...] = jnp.zeros_like(token_ref)
    bin_count, height, gate_rows = spectrum_refs[0].shape
    some, groups, _, width = out_ref.shape
    half = height // 2
    gate_index = lax.broadcasted_iota(jnp.int32, (pack * gate_rows, width), 0)
    part_index = lax.broadcasted_iota(jnp.int32, (1, width), 1) // (width // pack)
    for inner in range(some):
        start = owner_start(index_ref, pl.program_id(0) * some + inner, owners)
        for group in range(groups):
            block, place = divmod(group, groups // ranges)
            slot = block * share_slots + first + place * pack
            bins = [jnp.minimum(start + slot + part, bin_count - 1) for part in range(pack)]
            gates = gates_ref[pl.ds(bins[0], 1), :]
            for part in range(1, pack):
                gates = jnp.where(part_index == part, gates_ref[pl.ds(bins[part], 1), :], gates)
            chooser = jnp.where(gate_index == gates, 1.0, 0.0).astype(BF16)
            spectra = jnp.concatenate(
                [
                    jnp.concatenate([ref[b, s * half : (s + 1) * half] for b in bins], axis=1)
                    for s in range(2)
                    for ref in spectrum_refs
                ],
                axis=0,
            )
            picked = jnp.dot(spectra, chooser, preferred_element_type=F32)
            out_ref[inner, group] = picked.astype(BF16)


def select_gates(
    spectra, index, gates, first, count, share_slots, owners, ranges, pack, earlier
):
    rows = sum(spectrum.shape[1] for spectrum in spectra)
    gate_rows = spectra[0].shape[2]
    groups = ranges * count // pack
    width = gates.shape[1]
    some = math.gcd(owners, 2)
    return pl.pallas_call(
        functools.partial(
            select_kernel,
            chunks=len(spectra),
            owners=owners,
            ranges=ranges,
            first=first,
            share_slots=share_slots,
            pack=pack,
        ),
        out_shape=[
            jax.ShapeDtypeStruct((owners, groups, rows, width), BF16),
            jax.ShapeDtypeStruct((8, LANES), jnp.int32),
        ],
        grid=(owners // some,),
        in_specs=[pl.BlockSpec(memory_space=pltpu.SMEM)]
        + [pl.BlockSpec(memory_space=pltpu.VMEM)] * (1 + len(spectra))
        + [pl.BlockSpec(memory_space=pl.ANY)] * len(earlier),
        out_specs=[
            pl.BlockSpec((some, groups, rows, width), lambda i: (i, 0, 0, 0)),
            pl.BlockSpec((8, LANES), lambda i: (0, 0)),
        ],
        compiler_params=PARAMS,
        cost_estimate=pl.CostEstimate(
            flops=2 * owners * groups * pack * rows * gate_rows * width,
            bytes_accessed=owners * groups * rows * width * 2,
            transcendentals=0,
        ),
        name="select_gates",
    )(index, gates, *spectra, *earlier)


def beam_kernel(weights_ref, arrived_ref, *refs):
    out_ref = refs[-1]
    sources, ranges, groups, rows, width = arrived_ref.shape
    dof = weights_ref.shape[2]
    half = rows // 2
    for block in range(ranges):
        packed = jnp.concatenate(
            [
                arrived_ref[:, block, g, s * half : (s + 1) * half].reshape(sources * half, width)
                for s in range(2)
                for g in range(groups)
            ],
            axis=1,
        )
        by_real, by_imag = [
            lax.dot_general(
                weights_ref[part], packed, (((0,), (0,)), ((), ())), preferred_element_type=F32
            )
            for part in range(2)
        ]
        middle = groups * width
        real_part = by_real[:, :middle] + by_imag[:, middle:]
        imag_part = by_real[:, middle:] - by_imag[:, :middle]
        for g in range(groups):
            span = slice(g * width, (g + 1) * width)
            out_ref[block, g, :dof] = real_part[:, span].astype(BF16)
            out_ref[block, g, dof:] = imag_part[:, span].astype(BF16)


def form_beams(arrived, weights, earlier):
    _, ranges, groups, _, width = arrived.shape
    shape = (ranges, groups, 2 * weights.shape[2], width)
    return pl.pallas_call(
        beam_kernel,
        out_shape=jax.ShapeDtypeStruct(shape, BF16),
        in_specs=[pl.BlockSpec(memory_space=pltpu.VMEM)] * 2
        + [pl.BlockSpec(memory_space=pl.ANY)] * len(earlier),
        out_specs=pl.BlockSpec(memory_space=pltpu.VMEM),
        compiler_params=PARAMS,
        cost_estimate=pl.CostEstimate(
            flops=4 * arrived.size * weights.shape[2],
            bytes_accessed=arrived.size * 2,
            transcendentals=0,
        ),
        name="form_beams",
    )(weights, arrived, *earlier)


def exchange(arrays, axis):
    count = len(arrays)
    moved = [arrays[0]]
    for shift in range(1, count):
        pairs = [(i, (i + shift) % count) for i in range(count)]
        moved.append(lax.ppermute(arrays[shift], axis, pairs))
    return moved


def split_terms(array):
    high = array.astype(BF16)
    return high, (array - high.astype(F32)).astype(BF16)


def left_terms(array):
    high, low = split_terms(array)
    high, low = high.astype(F32), low.astype(F32)
    return jnp.concatenate([high, high, low], axis=0).T.astype(BF16)


def right_terms(array):
    high, low = split_terms(array)
    return jnp.concatenate([high, low, high], axis=0)


def product(left, right):
    return jnp.dot(left, right, preferred_element_type=F32)


def loaded_covariance(beams, pivot_row, part, pack, count_rows):
    dof = pivot_row.shape[1]
    width = beams[0].shape[1] // pack
    hot = lax.broadcasted_iota(jnp.int32, (dof, dof), 0) == pivot_row
    hot = jnp.where(hot, 1.0, 0.0).astype(BF16)
    own = jnp.concatenate([b[:, part * width : (part + 1) * width] for b in beams], axis=1)
    picked = [
        lax.dot_general(
            hot,
            own[half * dof : (half + 1) * dof],
            (((0,), (0,)), ((), ())),
            preferred_element_type=F32,
        )
        for half in range(2)
    ]
    upper = jnp.concatenate([picked[0], picked[1]], axis=1).astype(BF16)
    lower = jnp.concatenate([picked[1], -picked[0]], axis=1).astype(BF16)
    stacked = jnp.concatenate([upper, lower], axis=0)
    gram = lax.dot_general(
        stacked, stacked, (((1,), (1,)), ((), ())), preferred_element_type=F32
    )
    return gram * (1.0 / count_rows)


def lane_spread(piece, lane):
    return jnp.broadcast_to(piece[:, lane : lane + 1], piece.shape)


def refined_reciprocal(value):
    guess = pl.reciprocal(value, approx=True)
    return guess * (2.0 - value * guess)


def tree_sum(terms):
    while len(terms) > 1:
        terms = [x + y for x, y in zip(terms[::2], terms[1::2])]
    return terms[0]


def eliminate(rows):
    scales = []
    for first in range(0, PANEL, 8):
        span = range(first, first + 8)
        small = {(i, j): lane_spread(rows[i][0], j) for i in span for j in span if j >= i}
        inverses = []
        for t in range(first, first + 8, 2):
            u = t + 1
            inverse = refined_reciprocal(small[t, t])
            cross = small[t, t] * small[u, u] - small[t, u] * small[t, u]
            guess = pl.reciprocal(cross, approx=True)
            second = (small[t, t] * guess) * (2.0 - cross * guess)
            inverses += [inverse, second]
            scales += [lax.rsqrt(small[t, t]), lax.rsqrt(cross * inverse)]
            factor = small[t, u] * inverse
            for j in range(u + 1, first + 8):
                small[u, j] = small[u, j] - factor * small[t, j]
            rows[u] = [x - factor * y for x, y in zip(rows[u], rows[t])]
            for i in range(u + 1, first + 8):
                one, two = small[t, i] * inverse, small[u, i] * second
                for j in range(i, first + 8):
                    both = small[u, i] * small[u, j]
                    small[i, j] = (small[i, j] - one * small[t, j]) - both * second
                rows[i] = [
                    x - one * y - two * z for x, y, z in zip(rows[i], rows[t], rows[u])
                ]
        ratios = [rows[t][0] * inverse for t, inverse in zip(span, inverses)]
        for i in range(first + 8, PANEL):
            factors = [lane_spread(ratio, i) for ratio in ratios]
            rows[i] = [
                x - tree_sum([f * rows[t][w] for f, t in zip(factors, span)])
                for w, x in enumerate(rows[i])
            ]
    return [[x * scale for x in row] for row, scale in zip(rows, scales)]


def factor_kernel(
    index_ref, pivots_ref, beams_ref, *refs, first, share_slots, ranges, pack, count_rows
):
    out_refs = refs[:ranges]
    arriving, leaving, *scratch = refs[ranges:]
    slots = len(scratch) // 3
    work, lefts, rights = scratch[:slots], scratch[slots : 2 * slots], scratch[2 * slots :]
    order = work[0].shape[0]
    height = arriving.shape[1] // PANEL

    row = lax.broadcasted_iota(jnp.int32, (LANES, LANES), 0)
    col = lax.broadcasted_iota(jnp.int32, (LANES, LANES), 1)
    loading = jnp.where(row == col, LOADING, 0.0)
    owners = (index_ref.shape[0] - 2) // 2
    bin_lead = owner_start(index_ref, index_ref[0], owners) + index_ref[1] * share_slots + first
    for slot in range(slots):
        group, part = divmod(slot, pack)
        own_bin = jnp.minimum(bin_lead + slot, pivots_ref.shape[0] - 1)
        work[slot][...] = loaded_covariance(
            [beams_ref[r, group] for r in range(ranges)],
            pivots_ref[pl.ds(own_bin, 1), :],
            part,
            pack,
            count_rows,
        )
        for start in range(0, order, LANES):
            work[slot][start : start + LANES, start : start + LANES] += loading

    eights = range(0, PANEL, 8)
    column = lax.broadcasted_iota(jnp.int32, (LANES, 3 * PANEL), 0)

    def spread_out(slot, rows):
        for i in eights:
            for w in range(rows.shape[1] // LANES):
                piece = rows[i : i + 8, w * LANES : (w + 1) * LANES]
                arriving[w, pl.ds(i * height + slot, 8, stride=height), :] = piece

    for slot in range(slots):
        spread_out(slot, work[slot][:PANEL, :])
    for start in range(0, order, LANES):
        chunks = (order - start) // LANES
        stop = start + LANES
        for slot in range(slots):
            lefts[slot][...] = jnp.zeros_like(lefts[slot])
            rights[slot][...] = jnp.zeros_like(rights[slot])

        def one_panel(p, carry, start=start, stop=stop, chunks=chunks):
            back = p * PANEL
            base = pl.multiple_of(start + back, PANEL)
            ahead = pl.multiple_of(jnp.minimum(back + PANEL, LANES - PANEL), PANEL)
            following = pl.multiple_of(start + ahead, PANEL)
            for slot in range(slots):
                left = jnp.where(column >= back + PANEL, lefts[slot][...], 0.0).astype(BF16)
                work[slot][start:stop, start:] -= product(left, rights[slot][:, start:])
            rows = []
            for t in range(PANEL):
                pieces = [arriving[w, t * height : (t + 1) * height, :] for w in range(chunks)]
                pieces[0] = pltpu.roll(pieces[0], (LANES - back) % LANES, 1)
                rows.append(pieces)
            rows = eliminate(rows)
            for t in range(PANEL):
                rows[t][0] = pltpu.roll(rows[t][0], back, 1)
                for w in range(chunks):
                    leaving[w, t * height : (t + 1) * height, :] = rows[t][w]
            for slot in range(slots):
                parts = []
                for w in range(chunks):
                    pieces = [
                        leaving[w, pl.ds(i * height + slot, 8, stride=height), :] for i in eights
                    ]
                    parts.append(jnp.concatenate(pieces, axis=0))
                panel = jnp.concatenate(parts, axis=1)
                work[slot][pl.ds(base, PANEL), start:] = panel
                lefts[slot][...] = left_terms(parts[0]).astype(F32)
                right = right_terms(panel)
                rights[slot][:, start:] = right
                left = lefts[slot][pl.ds(ahead, PANEL), :].astype(BF16)
                spread_out(slot, work[slot][pl.ds(following, PANEL), start:] - product(left, right))
            return carry

        lax.fori_loop(0, LANES // PANEL, one_panel, 0)
        if chunks > 1:
            terms = []
            for slot in range(slots):
                done = work[slot][start:stop, stop:]
                left = jnp.concatenate(
                    [left_terms(done[:, w * LANES : (w + 1) * LANES]) for w in range(chunks - 1)],
                    axis=0,
                )
                right = right_terms(done)
                ready = work[slot][stop : stop + PANEL, stop:] - product(left[:PANEL], right)
                spread_out(slot, ready)
                terms.append((left, right))
            for slot in range(slots):
                left, right = terms[slot]
                work[slot][stop + PANEL :, stop:] -= product(left[PANEL:], right)

    share = order // ranges
    row = lax.broadcasted_iota(jnp.int32, (share, order), 0)
    col = lax.broadcasted_iota(jnp.int32, (share, order), 1)
    for shift, out_ref in enumerate(out_refs):
        lead = pl.multiple_of(lax.rem(index_ref[1] + shift, ranges) * share, math.gcd(share, 16))
        upper = col >= row + lead
        for slot in range(slots):
            piece = work[slot][pl.ds(lead, share), :]
            out_ref[slot] = jnp.where(upper, piece, 0.0).astype(out_ref.dtype)


def factor_slots(beams, pivots, index, first, slots, share_slots, pack, count_rows):
    ranges, _, order, _ = beams.shape
    height = -(-slots // 8) * 8
    return pl.pallas_call(
        functools.partial(
            factor_kernel,
            first=first,
            share_slots=share_slots,
            ranges=ranges,
            pack=pack,
            count_rows=count_rows,
        ),
        out_shape=[jax.ShapeDtypeStruct((slots, order // ranges, order), BF16)] * ranges,
        in_specs=[pl.BlockSpec(memory_space=pltpu.SMEM)]
        + [pl.BlockSpec(memory_space=pltpu.VMEM)] * 2,
        out_specs=[pl.BlockSpec(memory_space=pltpu.VMEM)] * ranges,
        scratch_shapes=[pltpu.VMEM((order // LANES, PANEL * height, LANES), F32)] * 2
        + [pltpu.VMEM((order, order), F32) for _ in range(slots)]
        + [pltpu.VMEM((LANES, 3 * PANEL), F32) for _ in range(slots)]
        + [pltpu.VMEM((3 * PANEL, order), BF16) for _ in range(slots)],
        compiler_params=PARAMS,
        cost_estimate=pl.CostEstimate(
            flops=slots * order**3,
            bytes_accessed=beams.size * 2,
            transcendentals=0,
        ),
        name="factor_slots",
    )(index, pivots, beams)


def place_kernel(index_ref, *refs, first, share_slots, ranges):
    in_refs, out_ref = refs[:ranges], refs[-1]
    slots = out_ref.shape[0]
    steps = in_refs[0].shape[0] // slots
    step = pl.program_id(0)
    shift, place = step // steps, step % steps
    block = lax.rem(index_ref[1] + ranges - shift, ranges)
    lead = block * share_slots + first + place * slots
    for this, ref in enumerate(in_refs):

        @pl.when(shift == this)
        def _(ref=ref):
            for i in range(slots):
                keep = lead + i < owner_count(index_ref, index_ref[0])
                keep = jnp.broadcast_to(keep, out_ref.shape[1:])
                out_ref[i] = jnp.where(keep, ref[place * slots + i].astype(F32), 0.0)


def place_rows(index, arrays, first, share_slots, earlier):
    ranges = len(arrays)
    count = arrays[0].shape[0]
    slots = math.gcd(math.gcd(count, first), share_slots)
    steps = count // slots

    def out_index(step, index_ref):
        block = lax.rem(index_ref[1] + ranges - step // steps, ranges)
        return ((block * share_slots + first) // slots + step % steps, 0, 0)

    return pl.pallas_call(
        functools.partial(place_kernel, first=first, share_slots=share_slots, ranges=ranges),
        out_shape=jax.ShapeDtypeStruct((ranges * share_slots,) + arrays[0].shape[1:], F32),
        grid_spec=pltpu.PrefetchScalarGridSpec(
            num_scalar_prefetch=1,
            grid=(ranges * steps,),
            in_specs=[pl.BlockSpec(memory_space=pltpu.VMEM)] * ranges
            + [pl.BlockSpec(memory_space=pl.ANY)] * len(earlier),
            out_specs=pl.BlockSpec((slots,) + arrays[0].shape[1:], out_index),
        ),
        input_output_aliases={1 + ranges: 0} if earlier else {},
        compiler_params=PARAMS,
        name="place_rows",
    )(index, *arrays, *earlier)


def slot_parts(share_slots, pack):
    head = share_slots - pack
    return [(0, head), (head, pack)] if head > 0 else [(0, share_slots)]


def local(raw_echo, replica, beam_weights, pivots, owner_counts, train_gates):
    ch_local = raw_echo.shape[1]
    gate_rows = raw_echo.shape[2]
    pulse_count = raw_echo.shape[3]
    tap_count = replica.shape[1]
    train_local = train_gates.shape[1]
    owners = lax.axis_size("dop")
    ranges = lax.axis_size("rng")
    most_slots = 2 * (pulse_count // owners)
    share_slots = most_slots // ranges
    pack = max(1, min(LANES // train_local, share_slots))

    chunks = max(1, min(4, ch_local // 16))
    chunk_rows = ch_local // chunks
    rim = -(-(tap_count - 1) // 16) * 16
    filters = filter_rows(replica, gate_rows)
    table = doppler_table(pulse_count)
    following = [shifted(rim_rows(raw_echo, rim, c, chunks), "rng", -1) for c in range(chunks)]
    spectra = [
        form_spectrum(filters, table, raw_echo, following[c], c, chunks) for c in range(chunks)
    ]

    starts = jnp.cumsum(owner_counts, dtype=jnp.int32) - owner_counts
    places = jnp.stack([lax.axis_index("dop"), lax.axis_index("rng")]).astype(jnp.int32)
    index = jnp.concatenate([places, owner_counts, starts])
    local_gates = train_gates % gate_rows
    gates = jnp.concatenate([local_gates + part * gate_rows for part in range(pack)], axis=1)
    count_rows = float(train_local * ranges)

    parts = slot_parts(share_slots, pack)
    outgoing, tokens = [], []
    for first, count in parts:
        earlier = [beam_weights] if first > 0 else []
        array, token = select_gates(
            spectra, index, gates, first, count, share_slots, owners, ranges, pack, earlier
        )
        outgoing.append(array)
        tokens.append(token)
    axes = ("dop", "rng")
    sent = [
        lax.all_to_all(
            array.reshape(owners * ranges, -1, *array.shape[2:]),
            axes,
            split_axis=0,
            concat_axis=0,
            tiled=True,
        ).reshape(owners, ranges, -1, *array.shape[2:])
        for array in outgoing
    ]
    result, earlier = [], tokens[1:]
    for (first, count), arrived in zip(parts, sent):
        beams = form_beams(arrived, beam_weights, earlier)
        factors = factor_slots(beams, pivots, index, first, count, share_slots, pack, count_rows)
        earlier = factors[:1]
        rows = exchange(factors, "rng")
        result = [place_rows(index, rows, first, share_slots, result)]
    return result[0]


def solution(mesh):
    return jax.shard_map(
        local,
        mesh=mesh,
        in_specs=(P(None, "dop", "rng", None), P(), P(), P(), P(), P(None, "rng")),
        out_specs=P("dop", "rng", None),
        check_vma=False,
    )
```

```python
import functools
import math

import jax
import jax.numpy as jnp
import numpy as np
from jax import lax
from jax.experimental import pallas as pl
from jax.experimental.pallas import tpu as pltpu
from jax.sharding import PartitionSpec as P

LOADING = 0.25
LANES = 128
PANEL = 32
BF16 = jnp.bfloat16
F32 = jnp.float32
PARAMS = pltpu.CompilerParams(vmem_limit_bytes=48 * 1024 * 1024)
SMALL_PARAMS = pltpu.CompilerParams(vmem_limit_bytes=24 * 1024 * 1024)


def shifted(array, axis, by):
    count = lax.axis_size(axis)
    pairs = [(i, i + by) for i in range(count) if 0 <= i + by < count]
    return lax.ppermute(array, axis, pairs)


def doppler_table(pulse_count):
    pulse_index = np.arange(pulse_count)
    phase_index = pulse_index[:, None] * pulse_index[None, :] % pulse_count
    angle_table = phase_index.astype(np.float32) * np.float32(2.0 * math.pi / pulse_count)
    norm_scale = np.float32(1.0 / math.sqrt(pulse_count))
    real_part, imag_part = np.cos(angle_table) * norm_scale, np.sin(angle_table) * norm_scale
    table = np.block([[real_part.T, imag_part.T], [-imag_part.T, real_part.T]])
    high = table.astype(BF16)
    low = (table - high.astype(np.float32)).astype(BF16)
    return jnp.asarray(np.concatenate([high, high, low], axis=1))


def filter_kernel(replica_ref, out_ref):
    gate_rows, span = out_ref.shape[0] // 2, replica_ref.shape[1]
    banded = [
        pltpu.roll(
            jnp.broadcast_to(replica_ref[part : part + 1, :], (gate_rows, span)),
            0,
            1,
            stride=1,
            stride_axis=0,
        )
        for part in range(2)
    ]
    out_ref[:gate_rows, :span] = banded[0].astype(BF16)
    out_ref[:gate_rows, span:] = banded[1].astype(BF16)
    out_ref[gate_rows:, :span] = (-banded[1]).astype(BF16)
    out_ref[gate_rows:, span:] = banded[0].astype(BF16)


def filter_rows(replica, gate_rows):
    tap_count = replica.shape[1]
    span = -(-(gate_rows + tap_count) // LANES) * LANES
    return pl.pallas_call(
        filter_kernel,
        out_shape=jax.ShapeDtypeStruct((2 * gate_rows, 2 * span), BF16),
        in_specs=[pl.BlockSpec(memory_space=pltpu.VMEM)],
        out_specs=pl.BlockSpec(memory_space=pltpu.VMEM),
        compiler_params=PARAMS,
        name="filter_rows",
    )(jnp.pad(replica, ((0, 0), (0, span - tap_count))))


def rim_kernel(echo_ref, out_ref):
    out_ref[...] = echo_ref[...].astype(BF16)


def rim_rows(raw_echo, rim, chunk, chunks):
    _, ch_local, _, pulses = raw_echo.shape
    shape = (2, ch_local // chunks, rim, pulses)
    return pl.pallas_call(
        rim_kernel,
        out_shape=jax.ShapeDtypeStruct(shape, BF16),
        grid=(1,),
        in_specs=[pl.BlockSpec(shape, lambda i: (0, chunk, 0, 0))],
        out_specs=pl.BlockSpec(shape, lambda i: (0, 0, 0, 0)),
        compiler_params=PARAMS,
        name="rim_rows",
    )(raw_echo)


def spectrum_kernel(rows_ref, table_ref, own_ref, next_ref, out_ref, turned):
    step = pl.program_id(0)
    _, channels, gate_rows, pulses = own_ref.shape
    bins, height, _ = out_ref.shape
    rim = next_ref.shape[2]
    span = rows_ref.shape[1] // 2
    each = range(channels)
    samples = []
    for part in range(2):
        samples += [
            jnp.concatenate([own_ref[part, c] for c in each], axis=1).astype(BF16),
            jnp.concatenate([next_ref[part, c] for c in each], axis=1),
        ]
        if span > gate_rows + rim:
            samples.append(jnp.zeros((span - gate_rows - rim, channels * pulses), BF16))
    samples = jnp.concatenate(samples, axis=0)
    matched = jnp.dot(rows_ref[...], samples, preferred_element_type=F32)
    high, low = split_terms(matched)
    pieces = [
        term[part * gate_rows : (part + 1) * gate_rows]
        for term in (high, low, high)
        for part in range(2)
    ]
    stacked = jnp.concatenate(
        [
            jnp.concatenate([piece[:, c * pulses : (c + 1) * pulses] for piece in pieces], axis=1)
            for c in each
        ],
        axis=0,
    )
    spectra = lax.dot_general(
        table_ref[...], stacked, (((1,), (1,)), ((), ())), preferred_element_type=F32
    )
    for part in range(2):
        turned_part = jnp.stack(
            [
                spectra[part * bins : (part + 1) * bins, c * gate_rows : (c + 1) * gate_rows]
                for c in each
            ],
            axis=0,
        )
        place = pl.multiple_of(part * (height // 2) + step * channels, channels)
        turned[:, pl.ds(place, channels), :] = jnp.swapaxes(turned_part, 0, 1)

    @pl.when(step == pl.num_programs(0) - 1)
    def _():
        out_ref[...] = turned[...].astype(BF16)


def form_spectrum(rows, table, raw_echo, next_rows, chunk, chunks):
    _, ch_local, gate_rows, pulses = raw_echo.shape
    channels = ch_local // chunks
    step = math.gcd(channels, 8)
    steps = channels // step
    height = 2 * channels
    bins = table.shape[0] // 2
    return pl.pallas_call(
        spectrum_kernel,
        out_shape=jax.ShapeDtypeStruct((bins, height, gate_rows), BF16),
        grid=(steps,),
        in_specs=[
            pl.BlockSpec(rows.shape, lambda i: (0, 0)),
            pl.BlockSpec(table.shape, lambda i: (0, 0)),
            pl.BlockSpec((2, step, gate_rows, pulses), lambda i: (0, chunk * steps + i, 0, 0)),
            pl.BlockSpec((2, step) + next_rows.shape[2:], lambda i: (0, i, 0, 0)),
        ],
        out_specs=pl.BlockSpec((bins, height, gate_rows), lambda i: (0, 0, 0)),
        scratch_shapes=[pltpu.VMEM((bins, height, gate_rows), F32)],
        compiler_params=PARAMS,
        cost_estimate=pl.CostEstimate(
            flops=2 * rows.size * channels * pulses + 2 * table.size * channels * gate_rows,
            bytes_accessed=8 * channels * gate_rows * pulses,
            transcendentals=0,
        ),
        name="form_spectrum",
    )(rows, table, raw_echo, next_rows)


def owner_count(index_ref, owner):
    return index_ref[2 + owner]


def owner_start(index_ref, owner, owners):
    return index_ref[2 + owners + owner]


def select_kernel(
    index_ref, gates_ref, *refs, chunks, owners, ranges, first, share_slots, pack
):
    spectrum_refs, out_ref, token_ref = refs[:chunks], refs[-2], refs[-1]
    token_ref[...] = jnp.zeros_like(token_ref)
    bin_count, height, gate_rows = spectrum_refs[0].shape
    some, groups, _, width = out_ref.shape
    half = height // 2
    gate_index = lax.broadcasted_iota(jnp.int32, (pack * gate_rows, width), 0)
    part_index = lax.broadcasted_iota(jnp.int32, (1, width), 1) // (width // pack)
    for inner in range(some):
        start = owner_start(index_ref, pl.program_id(0) * some + inner, owners)
        for group in range(groups):
            block, place = divmod(group, groups // ranges)
            slot = block * share_slots + first + place * pack
            bins = [jnp.minimum(start + slot + part, bin_count - 1) for part in range(pack)]
            gates = gates_ref[pl.ds(bins[0], 1), :]
            for part in range(1, pack):
                gates = jnp.where(part_index == part, gates_ref[pl.ds(bins[part], 1), :], gates)
            chooser = jnp.where(gate_index == gates, 1.0, 0.0).astype(BF16)
            spectra = jnp.concatenate(
                [
                    jnp.concatenate([ref[b, s * half : (s + 1) * half] for b in bins], axis=1)
                    for s in range(2)
                    for ref in spectrum_refs
                ],
                axis=0,
            )
            picked = jnp.dot(spectra, chooser, preferred_element_type=F32)
            out_ref[inner, group] = picked.astype(BF16)


def select_gates(
    spectra, index, gates, first, count, share_slots, owners, ranges, pack, earlier
):
    rows = sum(spectrum.shape[1] for spectrum in spectra)
    gate_rows = spectra[0].shape[2]
    groups = ranges * count // pack
    width = gates.shape[1]
    some = math.gcd(owners, 2)
    return pl.pallas_call(
        functools.partial(
            select_kernel,
            chunks=len(spectra),
            owners=owners,
            ranges=ranges,
            first=first,
            share_slots=share_slots,
            pack=pack,
        ),
        out_shape=[
            jax.ShapeDtypeStruct((owners, groups, rows, width), BF16),
            jax.ShapeDtypeStruct((8, LANES), jnp.int32),
        ],
        grid=(owners // some,),
        in_specs=[pl.BlockSpec(memory_space=pltpu.SMEM)]
        + [pl.BlockSpec(memory_space=pltpu.VMEM)] * (1 + len(spectra))
        + [pl.BlockSpec(memory_space=pl.ANY)] * len(earlier),
        out_specs=[
            pl.BlockSpec((some, groups, rows, width), lambda i: (i, 0, 0, 0)),
            pl.BlockSpec((8, LANES), lambda i: (0, 0)),
        ],
        compiler_params=PARAMS,
        cost_estimate=pl.CostEstimate(
            flops=2 * owners * groups * pack * rows * gate_rows * width,
            bytes_accessed=owners * groups * rows * width * 2,
            transcendentals=0,
        ),
        name="select_gates",
    )(index, gates, *spectra, *earlier)


def beam_kernel(weights_ref, arrived_ref, *refs):
    out_ref = refs[-1]
    sources, ranges, groups, rows, width = arrived_ref.shape
    dof = weights_ref.shape[2]
    half = rows // 2
    for block in range(ranges):
        packed = jnp.concatenate(
            [
                arrived_ref[:, block, g, s * half : (s + 1) * half].reshape(sources * half, width)
                for s in range(2)
                for g in range(groups)
            ],
            axis=1,
        )
        by_real, by_imag = [
            lax.dot_general(
                weights_ref[part], packed, (((0,), (0,)), ((), ())), preferred_element_type=F32
            )
            for part in range(2)
        ]
        middle = groups * width
        real_part = by_real[:, :middle] + by_imag[:, middle:]
        imag_part = by_real[:, middle:] - by_imag[:, :middle]
        for g in range(groups):
            span = slice(g * width, (g + 1) * width)
            out_ref[block, g, :dof] = real_part[:, span].astype(BF16)
            out_ref[block, g, dof:] = imag_part[:, span].astype(BF16)


def form_beams(arrived, weights, earlier):
    _, ranges, groups, _, width = arrived.shape
    shape = (ranges, groups, 2 * weights.shape[2], width)
    return pl.pallas_call(
        beam_kernel,
        out_shape=jax.ShapeDtypeStruct(shape, BF16),
        in_specs=[pl.BlockSpec(memory_space=pltpu.VMEM)] * 2
        + [pl.BlockSpec(memory_space=pl.ANY)] * len(earlier),
        out_specs=pl.BlockSpec(memory_space=pltpu.VMEM),
        compiler_params=SMALL_PARAMS,
        cost_estimate=pl.CostEstimate(
            flops=4 * arrived.size * weights.shape[2],
            bytes_accessed=arrived.size * 2,
            transcendentals=0,
        ),
        name="form_beams",
    )(weights, arrived, *earlier)


def exchange(arrays, axis):
    count = len(arrays)
    moved = [arrays[0]]
    for shift in range(1, count):
        pairs = [(i, (i + shift) % count) for i in range(count)]
        moved.append(lax.ppermute(arrays[shift], axis, pairs))
    return moved


def split_terms(array):
    high = array.astype(BF16)
    return high, (array - high.astype(F32)).astype(BF16)


def left_terms(array):
    high, low = split_terms(array)
    high, low = high.astype(F32), low.astype(F32)
    return jnp.concatenate([high, high, low], axis=0).T.astype(BF16)


def right_terms(array):
    high, low = split_terms(array)
    return jnp.concatenate([high, low, high], axis=0)


def product(left, right):
    return jnp.dot(left, right, preferred_element_type=F32)


def loaded_covariance(beams, pivot_row, part, pack, count_rows):
    dof = pivot_row.shape[1]
    width = beams[0].shape[1] // pack
    hot = lax.broadcasted_iota(jnp.int32, (dof, dof), 0) == pivot_row
    hot = jnp.where(hot, 1.0, 0.0).astype(BF16)
    own = jnp.concatenate([b[:, part * width : (part + 1) * width] for b in beams], axis=1)
    picked = [
        lax.dot_general(
            hot,
            own[half * dof : (half + 1) * dof],
            (((0,), (0,)), ((), ())),
            preferred_element_type=F32,
        )
        for half in range(2)
    ]
    upper = jnp.concatenate([picked[0], picked[1]], axis=1).astype(BF16)
    lower = jnp.concatenate([picked[1], -picked[0]], axis=1).astype(BF16)
    stacked = jnp.concatenate([upper, lower], axis=0)
    gram = lax.dot_general(
        stacked, stacked, (((1,), (1,)), ((), ())), preferred_element_type=F32
    )
    return gram * (1.0 / count_rows)


def lane_spread(piece, lane):
    return jnp.broadcast_to(piece[:, lane : lane + 1], piece.shape)


def refined_reciprocal(value):
    guess = pl.reciprocal(value, approx=True)
    return guess * (2.0 - value * guess)


def tree_sum(terms):
    while len(terms) > 1:
        terms = [x + y for x, y in zip(terms[::2], terms[1::2])]
    return terms[0]


def eliminate(rows):
    scales = []
    for first in range(0, PANEL, 8):
        span = range(first, first + 8)
        small = {(i, j): lane_spread(rows[i][0], j) for i in span for j in span if j >= i}
        inverses = []
        for t in range(first, first + 8, 2):
            u = t + 1
            inverse = refined_reciprocal(small[t, t])
            cross = small[t, t] * small[u, u] - small[t, u] * small[t, u]
            guess = pl.reciprocal(cross, approx=True)
            second = (small[t, t] * guess) * (2.0 - cross * guess)
            inverses += [inverse, second]
            scales += [lax.rsqrt(small[t, t]), lax.rsqrt(cross * inverse)]
            factor = small[t, u] * inverse
            for j in range(u + 1, first + 8):
                small[u, j] = small[u, j] - factor * small[t, j]
            rows[u] = [x - factor * y for x, y in zip(rows[u], rows[t])]
            for i in range(u + 1, first + 8):
                one, two = small[t, i] * inverse, small[u, i] * second
                for j in range(i, first + 8):
                    both = small[u, i] * small[u, j]
                    small[i, j] = (small[i, j] - one * small[t, j]) - both * second
                rows[i] = [
                    x - one * y - two * z for x, y, z in zip(rows[i], rows[t], rows[u])
                ]
        ratios = [rows[t][0] * inverse for t, inverse in zip(span, inverses)]
        for i in range(first + 8, PANEL):
            factors = [lane_spread(ratio, i) for ratio in ratios]
            rows[i] = [
                x - tree_sum([f * rows[t][w] for f, t in zip(factors, span)])
                for w, x in enumerate(rows[i])
            ]
    return [[x * scale for x in row] for row, scale in zip(rows, scales)]


def factor_kernel(
    index_ref, pivots_ref, beams_ref, *refs, first, share_slots, ranges, pack, count_rows
):
    out_refs = refs[:ranges]
    arriving, leaving, *scratch = refs[ranges:]
    slots = len(scratch) // 3
    work, lefts, rights = scratch[:slots], scratch[slots : 2 * slots], scratch[2 * slots :]
    order = work[0].shape[0]
    height = arriving.shape[1] // PANEL

    row = lax.broadcasted_iota(jnp.int32, (LANES, LANES), 0)
    col = lax.broadcasted_iota(jnp.int32, (LANES, LANES), 1)
    loading = jnp.where(row == col, LOADING, 0.0)
    owners = (index_ref.shape[0] - 2) // 2
    bin_lead = owner_start(index_ref, index_ref[0], owners) + index_ref[1] * share_slots + first
    for slot in range(slots):
        group, part = divmod(slot, pack)
        own_bin = jnp.minimum(bin_lead + slot, pivots_ref.shape[0] - 1)
        work[slot][...] = loaded_covariance(
            [beams_ref[r, group] for r in range(ranges)],
            pivots_ref[pl.ds(own_bin, 1), :],
            part,
            pack,
            count_rows,
        )
        for start in range(0, order, LANES):
            work[slot][start : start + LANES, start : start + LANES] += loading

    eights = range(0, PANEL, 8)
    column = lax.broadcasted_iota(jnp.int32, (LANES, 3 * PANEL), 0)

    def spread_out(slot, rows):
        for i in eights:
            for w in range(rows.shape[1] // LANES):
                piece = rows[i : i + 8, w * LANES : (w + 1) * LANES]
                arriving[w, pl.ds(i * height + slot, 8, stride=height), :] = piece

    for slot in range(slots):
        spread_out(slot, work[slot][:PANEL, :])
    for start in range(0, order, LANES):
        chunks = (order - start) // LANES
        stop = start + LANES
        for slot in range(slots):
            lefts[slot][...] = jnp.zeros_like(lefts[slot])
            rights[slot][...] = jnp.zeros_like(rights[slot])

        def one_panel(p, carry, start=start, stop=stop, chunks=chunks):
            back = p * PANEL
            base = pl.multiple_of(start + back, PANEL)
            ahead = pl.multiple_of(jnp.minimum(back + PANEL, LANES - PANEL), PANEL)
            following = pl.multiple_of(start + ahead, PANEL)
            for slot in range(slots):
                left = jnp.where(column >= back + PANEL, lefts[slot][...], 0.0).astype(BF16)
                work[slot][start:stop, start:] -= product(left, rights[slot][:, start:])
            rows = []
            for t in range(PANEL):
                pieces = [arriving[w, t * height : (t + 1) * height, :] for w in range(chunks)]
                pieces[0] = pltpu.roll(pieces[0], (LANES - back) % LANES, 1)
                rows.append(pieces)
            rows = eliminate(rows)
            for t in range(PANEL):
                rows[t][0] = pltpu.roll(rows[t][0], back, 1)
                for w in range(chunks):
                    leaving[w, t * height : (t + 1) * height, :] = rows[t][w]
            for slot in range(slots):
                parts = []
                for w in range(chunks):
                    pieces = [
                        leaving[w, pl.ds(i * height + slot, 8, stride=height), :] for i in eights
                    ]
                    parts.append(jnp.concatenate(pieces, axis=0))
                panel = jnp.concatenate(parts, axis=1)
                work[slot][pl.ds(base, PANEL), start:] = panel
                lefts[slot][...] = left_terms(parts[0]).astype(F32)
                right = right_terms(panel)
                rights[slot][:, start:] = right
                left = lefts[slot][pl.ds(ahead, PANEL), :].astype(BF16)
                spread_out(slot, work[slot][pl.ds(following, PANEL), start:] - product(left, right))
            return carry

        lax.fori_loop(0, LANES // PANEL, one_panel, 0)
        if chunks > 1:
            terms = []
            for slot in range(slots):
                done = work[slot][start:stop, stop:]
                left = jnp.concatenate(
                    [left_terms(done[:, w * LANES : (w + 1) * LANES]) for w in range(chunks - 1)],
                    axis=0,
                )
                right = right_terms(done)
                ready = work[slot][stop : stop + PANEL, stop:] - product(left[:PANEL], right)
                spread_out(slot, ready)
                terms.append((left, right))
            for slot in range(slots):
                left, right = terms[slot]
                work[slot][stop + PANEL :, stop:] -= product(left[PANEL:], right)

    share = order // ranges
    row = lax.broadcasted_iota(jnp.int32, (share, order), 0)
    col = lax.broadcasted_iota(jnp.int32, (share, order), 1)
    for shift, out_ref in enumerate(out_refs):
        lead = pl.multiple_of(lax.rem(index_ref[1] + shift, ranges) * share, math.gcd(share, 16))
        upper = col >= row + lead
        for slot in range(slots):
            piece = work[slot][pl.ds(lead, share), :]
            out_ref[slot] = jnp.where(upper, piece, 0.0).astype(out_ref.dtype)


def factor_slots(beams, pivots, index, first, slots, share_slots, pack, count_rows):
    ranges, _, order, _ = beams.shape
    height = -(-slots // 8) * 8
    return pl.pallas_call(
        functools.partial(
            factor_kernel,
            first=first,
            share_slots=share_slots,
            ranges=ranges,
            pack=pack,
            count_rows=count_rows,
        ),
        out_shape=[jax.ShapeDtypeStruct((slots, order // ranges, order), BF16)] * ranges,
        in_specs=[pl.BlockSpec(memory_space=pltpu.SMEM)]
        + [pl.BlockSpec(memory_space=pltpu.VMEM)] * 2,
        out_specs=[pl.BlockSpec(memory_space=pltpu.VMEM)] * ranges,
        scratch_shapes=[pltpu.VMEM((order // LANES, PANEL * height, LANES), F32)] * 2
        + [pltpu.VMEM((order, order), F32) for _ in range(slots)]
        + [pltpu.VMEM((LANES, 3 * PANEL), F32) for _ in range(slots)]
        + [pltpu.VMEM((3 * PANEL, order), BF16) for _ in range(slots)],
        compiler_params=SMALL_PARAMS,
        cost_estimate=pl.CostEstimate(
            flops=slots * order**3,
            bytes_accessed=beams.size * 2,
            transcendentals=0,
        ),
        name="factor_slots",
    )(index, pivots, beams)


def place_kernel(index_ref, *refs, first, share_slots, ranges):
    in_refs, out_ref = refs[:ranges], refs[-1]
    slots = out_ref.shape[0]
    steps = in_refs[0].shape[0] // slots
    step = pl.program_id(0)
    shift, place = step // steps, step % steps
    block = lax.rem(index_ref[1] + ranges - shift, ranges)
    lead = block * share_slots + first + place * slots
    for this, ref in enumerate(in_refs):

        @pl.when(shift == this)
        def _(ref=ref):
            for i in range(slots):
                keep = lead + i < owner_count(index_ref, index_ref[0])
                keep = jnp.broadcast_to(keep, out_ref.shape[1:])
                out_ref[i] = jnp.where(keep, ref[place * slots + i].astype(F32), 0.0)


def place_rows(index, arrays, first, share_slots, earlier):
    ranges = len(arrays)
    count = arrays[0].shape[0]
    slots = math.gcd(math.gcd(count, first), share_slots)
    steps = count // slots

    def out_index(step, index_ref):
        block = lax.rem(index_ref[1] + ranges - step // steps, ranges)
        return ((block * share_slots + first) // slots + step % steps, 0, 0)

    return pl.pallas_call(
        functools.partial(place_kernel, first=first, share_slots=share_slots, ranges=ranges),
        out_shape=jax.ShapeDtypeStruct((ranges * share_slots,) + arrays[0].shape[1:], F32),
        grid_spec=pltpu.PrefetchScalarGridSpec(
            num_scalar_prefetch=1,
            grid=(ranges * steps,),
            in_specs=[pl.BlockSpec(memory_space=pltpu.VMEM)] * ranges
            + [pl.BlockSpec(memory_space=pl.ANY)] * len(earlier),
            out_specs=pl.BlockSpec((slots,) + arrays[0].shape[1:], out_index),
        ),
        input_output_aliases={1 + ranges: 0} if earlier else {},
        compiler_params=SMALL_PARAMS,
        name="place_rows",
    )(index, *arrays, *earlier)


def slot_parts(share_slots, pack):
    head = share_slots - pack
    return [(0, head), (head, pack)] if head > 0 else [(0, share_slots)]


def local(raw_echo, replica, beam_weights, pivots, owner_counts, train_gates):
    ch_local = raw_echo.shape[1]
    gate_rows = raw_echo.shape[2]
    pulse_count = raw_echo.shape[3]
    tap_count = replica.shape[1]
    train_local = train_gates.shape[1]
    owners = lax.axis_size("dop")
    ranges = lax.axis_size("rng")
    most_slots = 2 * (pulse_count // owners)
    share_slots = most_slots // ranges
    pack = max(1, min(LANES // train_local, share_slots))

    chunks = max(1, min(4, ch_local // 16))
    chunk_rows = ch_local // chunks
    rim = -(-(tap_count - 1) // 16) * 16
    filters = filter_rows(replica, gate_rows)
    table = doppler_table(pulse_count)
    following = [shifted(rim_rows(raw_echo, rim, c, chunks), "rng", -1) for c in range(chunks)]
    spectra = [
        form_spectrum(filters, table, raw_echo, following[c], c, chunks) for c in range(chunks)
    ]

    starts = jnp.cumsum(owner_counts, dtype=jnp.int32) - owner_counts
    places = jnp.stack([lax.axis_index("dop"), lax.axis_index("rng")]).astype(jnp.int32)
    index = jnp.concatenate([places, owner_counts, starts])
    local_gates = train_gates % gate_rows
    gates = jnp.concatenate([local_gates + part * gate_rows for part in range(pack)], axis=1)
    count_rows = float(train_local * ranges)

    parts = slot_parts(share_slots, pack)
    outgoing, tokens = [], []
    for first, count in parts:
        earlier = [beam_weights] if first > 0 else []
        array, token = select_gates(
            spectra, index, gates, first, count, share_slots, owners, ranges, pack, earlier
        )
        outgoing.append(array)
        tokens.append(token)
    axes = ("dop", "rng")
    sent = [
        lax.all_to_all(
            array.reshape(owners * ranges, -1, *array.shape[2:]),
            axes,
            split_axis=0,
            concat_axis=0,
            tiled=True,
        ).reshape(owners, ranges, -1, *array.shape[2:])
        for array in outgoing
    ]
    result, earlier = [], tokens[1:]
    for (first, count), arrived in zip(parts, sent):
        beams = form_beams(arrived, beam_weights, earlier)
        factors = factor_slots(beams, pivots, index, first, count, share_slots, pack, count_rows)
        earlier = factors[:1]
        rows = exchange(factors, "rng")
        result = [place_rows(index, rows, first, share_slots, result)]
    return result[0]


def solution(mesh):
    return jax.shard_map(
        local,
        mesh=mesh,
        in_specs=(P(None, "dop", "rng", None), P(), P(), P(), P(), P(None, "rng")),
        out_specs=P("dop", "rng", None),
        check_vma=False,
    )
```

```python
import functools
import math

import jax
import jax.numpy as jnp
import numpy as np
from jax import lax
from jax.experimental import pallas as pl
from jax.experimental.pallas import tpu as pltpu
from jax.sharding import PartitionSpec as P

LOADING = 0.25
LANES = 128
PANEL = 32
BF16 = jnp.bfloat16
F32 = jnp.float32
PARAMS = pltpu.CompilerParams(vmem_limit_bytes=48 * 1024 * 1024)
SMALL_PARAMS = pltpu.CompilerParams(vmem_limit_bytes=24 * 1024 * 1024)


def shifted(array, axis, by):
    count = lax.axis_size(axis)
    pairs = [(i, i + by) for i in range(count) if 0 <= i + by < count]
    return lax.ppermute(array, axis, pairs)


def doppler_table(pulse_count):
    pulse_index = np.arange(pulse_count)
    phase_index = pulse_index[:, None] * pulse_index[None, :] % pulse_count
    angle_table = phase_index.astype(np.float32) * np.float32(2.0 * math.pi / pulse_count)
    norm_scale = np.float32(1.0 / math.sqrt(pulse_count))
    real_part, imag_part = np.cos(angle_table) * norm_scale, np.sin(angle_table) * norm_scale
    table = np.block([[real_part.T, imag_part.T], [-imag_part.T, real_part.T]])
    high = table.astype(BF16)
    low = (table - high.astype(np.float32)).astype(BF16)
    return jnp.asarray(np.concatenate([high, high, low], axis=1))


def filter_kernel(replica_ref, out_ref):
    gate_rows, span = out_ref.shape[0] // 2, replica_ref.shape[1]
    banded = [
        pltpu.roll(
            jnp.broadcast_to(replica_ref[part : part + 1, :], (gate_rows, span)),
            0,
            1,
            stride=1,
            stride_axis=0,
        )
        for part in range(2)
    ]
    out_ref[:gate_rows, :span] = banded[0].astype(BF16)
    out_ref[:gate_rows, span:] = banded[1].astype(BF16)
    out_ref[gate_rows:, :span] = (-banded[1]).astype(BF16)
    out_ref[gate_rows:, span:] = banded[0].astype(BF16)


def filter_rows(replica, gate_rows):
    tap_count = replica.shape[1]
    span = -(-(gate_rows + tap_count) // LANES) * LANES
    return pl.pallas_call(
        filter_kernel,
        out_shape=jax.ShapeDtypeStruct((2 * gate_rows, 2 * span), BF16),
        in_specs=[pl.BlockSpec(memory_space=pltpu.VMEM)],
        out_specs=pl.BlockSpec(memory_space=pltpu.VMEM),
        compiler_params=PARAMS,
        name="filter_rows",
    )(jnp.pad(replica, ((0, 0), (0, span - tap_count))))


def rim_kernel(echo_ref, out_ref):
    out_ref[...] = echo_ref[...].astype(BF16)


def rim_rows(raw_echo, rim, chunk, chunks):
    _, ch_local, _, pulses = raw_echo.shape
    shape = (2, ch_local // chunks, rim, pulses)
    return pl.pallas_call(
        rim_kernel,
        out_shape=jax.ShapeDtypeStruct(shape, BF16),
        grid=(1,),
        in_specs=[pl.BlockSpec(shape, lambda i: (0, chunk, 0, 0))],
        out_specs=pl.BlockSpec(shape, lambda i: (0, 0, 0, 0)),
        compiler_params=PARAMS,
        name="rim_rows",
    )(raw_echo)


def spectrum_kernel(rows_ref, table_ref, own_ref, next_ref, out_ref, turned):
    step = pl.program_id(0)
    _, channels, gate_rows, pulses = own_ref.shape
    bins, height, _ = out_ref.shape
    rim = next_ref.shape[2]
    span = rows_ref.shape[1] // 2
    each = range(channels)
    samples = []
    for part in range(2):
        samples += [
            jnp.concatenate([own_ref[part, c] for c in each], axis=1).astype(BF16),
            jnp.concatenate([next_ref[part, c] for c in each], axis=1),
        ]
        if span > gate_rows + rim:
            samples.append(jnp.zeros((span - gate_rows - rim, channels * pulses), BF16))
    samples = jnp.concatenate(samples, axis=0)
    matched = jnp.dot(rows_ref[...], samples, preferred_element_type=F32)
    high, low = split_terms(matched)
    pieces = [
        term[part * gate_rows : (part + 1) * gate_rows]
        for term in (high, low, high)
        for part in range(2)
    ]
    stacked = jnp.concatenate(
        [
            jnp.concatenate([piece[:, c * pulses : (c + 1) * pulses] for piece in pieces], axis=1)
            for c in each
        ],
        axis=0,
    )
    spectra = lax.dot_general(
        table_ref[...], stacked, (((1,), (1,)), ((), ())), preferred_element_type=F32
    )
    for part in range(2):
        turned_part = jnp.stack(
            [
                spectra[part * bins : (part + 1) * bins, c * gate_rows : (c + 1) * gate_rows]
                for c in each
            ],
            axis=0,
        )
        place = pl.multiple_of(part * (height // 2) + step * channels, channels)
        turned[:, pl.ds(place, channels), :] = jnp.swapaxes(turned_part, 0, 1)

    @pl.when(step == pl.num_programs(0) - 1)
    def _():
        out_ref[...] = turned[...].astype(BF16)


def form_spectrum(rows, table, raw_echo, next_rows, chunk, chunks):
    _, ch_local, gate_rows, pulses = raw_echo.shape
    channels = ch_local // chunks
    step = math.gcd(channels, 8)
    steps = channels // step
    height = 2 * channels
    bins = table.shape[0] // 2
    return pl.pallas_call(
        spectrum_kernel,
        out_shape=jax.ShapeDtypeStruct((bins, height, gate_rows), BF16),
        grid=(steps,),
        in_specs=[
            pl.BlockSpec(rows.shape, lambda i: (0, 0)),
            pl.BlockSpec(table.shape, lambda i: (0, 0)),
            pl.BlockSpec((2, step, gate_rows, pulses), lambda i: (0, chunk * steps + i, 0, 0)),
            pl.BlockSpec((2, step) + next_rows.shape[2:], lambda i: (0, i, 0, 0)),
        ],
        out_specs=pl.BlockSpec((bins, height, gate_rows), lambda i: (0, 0, 0)),
        scratch_shapes=[pltpu.VMEM((bins, height, gate_rows), F32)],
        compiler_params=PARAMS,
        cost_estimate=pl.CostEstimate(
            flops=2 * rows.size * channels * pulses + 2 * table.size * channels * gate_rows,
            bytes_accessed=8 * channels * gate_rows * pulses,
            transcendentals=0,
        ),
        name="form_spectrum",
    )(rows, table, raw_echo, next_rows)


def owner_count(index_ref, owner):
    return index_ref[2 + owner]


def owner_start(index_ref, owner, owners):
    return index_ref[2 + owners + owner]


def select_kernel(
    index_ref, gates_ref, *refs, chunks, owners, ranges, first, share_slots, pack
):
    spectrum_refs, out_ref, token_ref = refs[:chunks], refs[-2], refs[-1]
    token_ref[...] = jnp.zeros_like(token_ref)
    bin_count, height, gate_rows = spectrum_refs[0].shape
    some, groups, _, width = out_ref.shape
    half = height // 2
    gate_index = lax.broadcasted_iota(jnp.int32, (pack * gate_rows, width), 0)
    part_index = lax.broadcasted_iota(jnp.int32, (1, width), 1) // (width // pack)
    for inner in range(some):
        start = owner_start(index_ref, pl.program_id(0) * some + inner, owners)
        for group in range(groups):
            block, place = divmod(group, groups // ranges)
            slot = block * share_slots + first + place * pack
            bins = [jnp.minimum(start + slot + part, bin_count - 1) for part in range(pack)]
            gates = gates_ref[pl.ds(bins[0], 1), :]
            for part in range(1, pack):
                gates = jnp.where(part_index == part, gates_ref[pl.ds(bins[part], 1), :], gates)
            chooser = jnp.where(gate_index == gates, 1.0, 0.0).astype(BF16)
            spectra = jnp.concatenate(
                [
                    jnp.concatenate([ref[b, s * half : (s + 1) * half] for b in bins], axis=1)
                    for s in range(2)
                    for ref in spectrum_refs
                ],
                axis=0,
            )
            picked = jnp.dot(spectra, chooser, preferred_element_type=F32)
            out_ref[inner, group] = picked.astype(BF16)


def select_gates(
    spectra, index, gates, first, count, share_slots, owners, ranges, pack, earlier
):
    rows = sum(spectrum.shape[1] for spectrum in spectra)
    gate_rows = spectra[0].shape[2]
    groups = ranges * count // pack
    width = gates.shape[1]
    some = math.gcd(owners, 4)
    return pl.pallas_call(
        functools.partial(
            select_kernel,
            chunks=len(spectra),
            owners=owners,
            ranges=ranges,
            first=first,
            share_slots=share_slots,
            pack=pack,
        ),
        out_shape=[
            jax.ShapeDtypeStruct((owners, groups, rows, width), BF16),
            jax.ShapeDtypeStruct((8, LANES), jnp.int32),
        ],
        grid=(owners // some,),
        in_specs=[pl.BlockSpec(memory_space=pltpu.SMEM)]
        + [pl.BlockSpec(memory_space=pltpu.VMEM)] * (1 + len(spectra))
        + [pl.BlockSpec(memory_space=pl.ANY)] * len(earlier),
        out_specs=[
            pl.BlockSpec((some, groups, rows, width), lambda i: (i, 0, 0, 0)),
            pl.BlockSpec((8, LANES), lambda i: (0, 0)),
        ],
        compiler_params=PARAMS,
        cost_estimate=pl.CostEstimate(
            flops=2 * owners * groups * pack * rows * gate_rows * width,
            bytes_accessed=owners * groups * rows * width * 2,
            transcendentals=0,
        ),
        name="select_gates",
    )(index, gates, *spectra, *earlier)


def beam_kernel(weights_ref, arrived_ref, *refs):
    out_ref = refs[-1]
    sources, ranges, groups, rows, width = arrived_ref.shape
    dof = weights_ref.shape[2]
    half = rows // 2
    for block in range(ranges):
        packed = jnp.concatenate(
            [
                arrived_ref[:, block, g, s * half : (s + 1) * half].reshape(sources * half, width)
                for s in range(2)
                for g in range(groups)
            ],
            axis=1,
        )
        by_real, by_imag = [
            lax.dot_general(
                weights_ref[part], packed, (((0,), (0,)), ((), ())), preferred_element_type=F32
            )
            for part in range(2)
        ]
        middle = groups * width
        real_part = by_real[:, :middle] + by_imag[:, middle:]
        imag_part = by_real[:, middle:] - by_imag[:, :middle]
        for g in range(groups):
            span = slice(g * width, (g + 1) * width)
            out_ref[block, g, :dof] = real_part[:, span].astype(BF16)
            out_ref[block, g, dof:] = imag_part[:, span].astype(BF16)


def form_beams(arrived, weights, earlier):
    _, ranges, groups, _, width = arrived.shape
    shape = (ranges, groups, 2 * weights.shape[2], width)
    return pl.pallas_call(
        beam_kernel,
        out_shape=jax.ShapeDtypeStruct(shape, BF16),
        in_specs=[pl.BlockSpec(memory_space=pltpu.VMEM)] * 2
        + [pl.BlockSpec(memory_space=pl.ANY)] * len(earlier),
        out_specs=pl.BlockSpec(memory_space=pltpu.VMEM),
        compiler_params=SMALL_PARAMS,
        cost_estimate=pl.CostEstimate(
            flops=4 * arrived.size * weights.shape[2],
            bytes_accessed=arrived.size * 2,
            transcendentals=0,
        ),
        name="form_beams",
    )(weights, arrived, *earlier)


def exchange(arrays, axis):
    count = len(arrays)
    moved = [arrays[0]]
    for shift in range(1, count):
        pairs = [(i, (i + shift) % count) for i in range(count)]
        moved.append(lax.ppermute(arrays[shift], axis, pairs))
    return moved


def split_terms(array):
    high = array.astype(BF16)
    return high, (array - high.astype(F32)).astype(BF16)


def left_terms(array):
    high, low = split_terms(array)
    high, low = high.astype(F32), low.astype(F32)
    return jnp.concatenate([high, high, low], axis=0).T.astype(BF16)


def right_terms(array):
    high, low = split_terms(array)
    return jnp.concatenate([high, low, high], axis=0)


def product(left, right):
    return jnp.dot(left, right, preferred_element_type=F32)


def loaded_covariance(beams, pivot_row, part, pack, count_rows):
    dof = pivot_row.shape[1]
    width = beams[0].shape[1] // pack
    hot = lax.broadcasted_iota(jnp.int32, (dof, dof), 0) == pivot_row
    hot = jnp.where(hot, 1.0, 0.0).astype(BF16)
    own = jnp.concatenate([b[:, part * width : (part + 1) * width] for b in beams], axis=1)
    picked = [
        lax.dot_general(
            hot,
            own[half * dof : (half + 1) * dof],
            (((0,), (0,)), ((), ())),
            preferred_element_type=F32,
        )
        for half in range(2)
    ]
    upper = jnp.concatenate([picked[0], picked[1]], axis=1).astype(BF16)
    lower = jnp.concatenate([picked[1], -picked[0]], axis=1).astype(BF16)
    stacked = jnp.concatenate([upper, lower], axis=0)
    gram = lax.dot_general(
        stacked, stacked, (((1,), (1,)), ((), ())), preferred_element_type=F32
    )
    return gram * (1.0 / count_rows)


def lane_spread(piece, lane):
    return jnp.broadcast_to(piece[:, lane : lane + 1], piece.shape)


def refined_reciprocal(value):
    guess = pl.reciprocal(value, approx=True)
    return guess * (2.0 - value * guess)


def tree_sum(terms):
    while len(terms) > 1:
        terms = [x + y for x, y in zip(terms[::2], terms[1::2])]
    return terms[0]


def eliminate(rows):
    scales = []
    for first in range(0, PANEL, 8):
        span = range(first, first + 8)
        small = {(i, j): lane_spread(rows[i][0], j) for i in span for j in span if j >= i}
        inverses = []
        for t in range(first, first + 8, 2):
            u = t + 1
            inverse = refined_reciprocal(small[t, t])
            cross = small[t, t] * small[u, u] - small[t, u] * small[t, u]
            guess = pl.reciprocal(cross, approx=True)
            second = (small[t, t] * guess) * (2.0 - cross * guess)
            inverses += [inverse, second]
            scales += [lax.rsqrt(small[t, t]), lax.rsqrt(cross * inverse)]
            factor = small[t, u] * inverse
            for j in range(u + 1, first + 8):
                small[u, j] = small[u, j] - factor * small[t, j]
            rows[u] = [x - factor * y for x, y in zip(rows[u], rows[t])]
            for i in range(u + 1, first + 8):
                one, two = small[t, i] * inverse, small[u, i] * second
                for j in range(i, first + 8):
                    both = small[u, i] * small[u, j]
                    small[i, j] = (small[i, j] - one * small[t, j]) - both * second
                rows[i] = [
                    x - one * y - two * z for x, y, z in zip(rows[i], rows[t], rows[u])
                ]
        ratios = [rows[t][0] * inverse for t, inverse in zip(span, inverses)]
        for i in range(first + 8, PANEL):
            factors = [lane_spread(ratio, i) for ratio in ratios]
            rows[i] = [
                x - tree_sum([f * rows[t][w] for f, t in zip(factors, span)])
                for w, x in enumerate(rows[i])
            ]
    return [[x * scale for x in row] for row, scale in zip(rows, scales)]


def factor_kernel(
    index_ref, pivots_ref, beams_ref, *refs, first, share_slots, ranges, pack, count_rows
):
    out_refs = refs[:ranges]
    arriving, leaving, *scratch = refs[ranges:]
    slots = len(scratch) // 3
    work, lefts, rights = scratch[:slots], scratch[slots : 2 * slots], scratch[2 * slots :]
    order = work[0].shape[0]
    height = arriving.shape[1] // PANEL

    row = lax.broadcasted_iota(jnp.int32, (LANES, LANES), 0)
    col = lax.broadcasted_iota(jnp.int32, (LANES, LANES), 1)
    loading = jnp.where(row == col, LOADING, 0.0)
    owners = (index_ref.shape[0] - 2) // 2
    bin_lead = owner_start(index_ref, index_ref[0], owners) + index_ref[1] * share_slots + first
    for slot in range(slots):
        group, part = divmod(slot, pack)
        own_bin = jnp.minimum(bin_lead + slot, pivots_ref.shape[0] - 1)
        work[slot][...] = loaded_covariance(
            [beams_ref[r, group] for r in range(ranges)],
            pivots_ref[pl.ds(own_bin, 1), :],
            part,
            pack,
            count_rows,
        )
        for start in range(0, order, LANES):
            work[slot][start : start + LANES, start : start + LANES] += loading

    eights = range(0, PANEL, 8)
    column = lax.broadcasted_iota(jnp.int32, (LANES, 3 * PANEL), 0)

    def spread_out(slot, rows):
        for i in eights:
            for w in range(rows.shape[1] // LANES):
                piece = rows[i : i + 8, w * LANES : (w + 1) * LANES]
                arriving[w, pl.ds(i * height + slot, 8, stride=height), :] = piece

    for slot in range(slots):
        spread_out(slot, work[slot][:PANEL, :])
    for start in range(0, order, LANES):
        chunks = (order - start) // LANES
        stop = start + LANES
        for slot in range(slots):
            lefts[slot][...] = jnp.zeros_like(lefts[slot])
            rights[slot][...] = jnp.zeros_like(rights[slot])

        def one_panel(p, carry, start=start, stop=stop, chunks=chunks):
            back = p * PANEL
            base = pl.multiple_of(start + back, PANEL)
            ahead = pl.multiple_of(jnp.minimum(back + PANEL, LANES - PANEL), PANEL)
            following = pl.multiple_of(start + ahead, PANEL)
            for slot in range(slots):
                left = jnp.where(column >= back + PANEL, lefts[slot][...], 0.0).astype(BF16)
                work[slot][start:stop, start:] -= product(left, rights[slot][:, start:])
            rows = []
            for t in range(PANEL):
                pieces = [arriving[w, t * height : (t + 1) * height, :] for w in range(chunks)]
                pieces[0] = pltpu.roll(pieces[0], (LANES - back) % LANES, 1)
                rows.append(pieces)
            rows = eliminate(rows)
            for t in range(PANEL):
                rows[t][0] = pltpu.roll(rows[t][0], back, 1)
                for w in range(chunks):
                    leaving[w, t * height : (t + 1) * height, :] = rows[t][w]
            for slot in range(slots):
                parts = []
                for w in range(chunks):
                    pieces = [
                        leaving[w, pl.ds(i * height + slot, 8, stride=height), :] for i in eights
                    ]
                    parts.append(jnp.concatenate(pieces, axis=0))
                panel = jnp.concatenate(parts, axis=1)
                work[slot][pl.ds(base, PANEL), start:] = panel
                lefts[slot][...] = left_terms(parts[0]).astype(F32)
                right = right_terms(panel)
                rights[slot][:, start:] = right
                left = lefts[slot][pl.ds(ahead, PANEL), :].astype(BF16)
                spread_out(slot, work[slot][pl.ds(following, PANEL), start:] - product(left, right))
            return carry

        lax.fori_loop(0, LANES // PANEL, one_panel, 0)
        if chunks > 1:
            terms = []
            for slot in range(slots):
                done = work[slot][start:stop, stop:]
                left = jnp.concatenate(
                    [left_terms(done[:, w * LANES : (w + 1) * LANES]) for w in range(chunks - 1)],
                    axis=0,
                )
                right = right_terms(done)
                ready = work[slot][stop : stop + PANEL, stop:] - product(left[:PANEL], right)
                spread_out(slot, ready)
                terms.append((left, right))
            for slot in range(slots):
                left, right = terms[slot]
                work[slot][stop + PANEL :, stop:] -= product(left[PANEL:], right)

    share = order // ranges
    row = lax.broadcasted_iota(jnp.int32, (share, order), 0)
    col = lax.broadcasted_iota(jnp.int32, (share, order), 1)
    for shift, out_ref in enumerate(out_refs):
        lead = pl.multiple_of(lax.rem(index_ref[1] + shift, ranges) * share, math.gcd(share, 16))
        upper = col >= row + lead
        for slot in range(slots):
            piece = work[slot][pl.ds(lead, share), :]
            out_ref[slot] = jnp.where(upper, piece, 0.0).astype(out_ref.dtype)


def factor_slots(beams, pivots, index, first, slots, share_slots, pack, count_rows):
    ranges, _, order, _ = beams.shape
    height = -(-slots // 8) * 8
    return pl.pallas_call(
        functools.partial(
            factor_kernel,
            first=first,
            share_slots=share_slots,
            ranges=ranges,
            pack=pack,
            count_rows=count_rows,
        ),
        out_shape=[jax.ShapeDtypeStruct((slots, order // ranges, order), BF16)] * ranges,
        in_specs=[pl.BlockSpec(memory_space=pltpu.SMEM)]
        + [pl.BlockSpec(memory_space=pltpu.VMEM)] * 2,
        out_specs=[pl.BlockSpec(memory_space=pltpu.VMEM)] * ranges,
        scratch_shapes=[pltpu.VMEM((order // LANES, PANEL * height, LANES), F32)] * 2
        + [pltpu.VMEM((order, order), F32) for _ in range(slots)]
        + [pltpu.VMEM((LANES, 3 * PANEL), F32) for _ in range(slots)]
        + [pltpu.VMEM((3 * PANEL, order), BF16) for _ in range(slots)],
        compiler_params=SMALL_PARAMS,
        cost_estimate=pl.CostEstimate(
            flops=slots * order**3,
            bytes_accessed=beams.size * 2,
            transcendentals=0,
        ),
        name="factor_slots",
    )(index, pivots, beams)


def place_kernel(index_ref, *refs, first, share_slots, ranges):
    in_refs, out_ref = refs[:ranges], refs[-1]
    slots = out_ref.shape[0]
    steps = in_refs[0].shape[0] // slots
    step = pl.program_id(0)
    shift, place = step // steps, step % steps
    block = lax.rem(index_ref[1] + ranges - shift, ranges)
    lead = block * share_slots + first + place * slots
    for this, ref in enumerate(in_refs):

        @pl.when(shift == this)
        def _(ref=ref):
            for i in range(slots):
                keep = lead + i < owner_count(index_ref, index_ref[0])
                keep = jnp.broadcast_to(keep, out_ref.shape[1:])
                out_ref[i] = jnp.where(keep, ref[place * slots + i].astype(F32), 0.0)


def place_rows(index, arrays, first, share_slots, earlier):
    ranges = len(arrays)
    count = arrays[0].shape[0]
    slots = math.gcd(math.gcd(count, first), share_slots)
    steps = count // slots

    def out_index(step, index_ref):
        block = lax.rem(index_ref[1] + ranges - step // steps, ranges)
        return ((block * share_slots + first) // slots + step % steps, 0, 0)

    return pl.pallas_call(
        functools.partial(place_kernel, first=first, share_slots=share_slots, ranges=ranges),
        out_shape=jax.ShapeDtypeStruct((ranges * share_slots,) + arrays[0].shape[1:], F32),
        grid_spec=pltpu.PrefetchScalarGridSpec(
            num_scalar_prefetch=1,
            grid=(ranges * steps,),
            in_specs=[pl.BlockSpec(memory_space=pltpu.VMEM)] * ranges
            + [pl.BlockSpec(memory_space=pl.ANY)] * len(earlier),
            out_specs=pl.BlockSpec((slots,) + arrays[0].shape[1:], out_index),
        ),
        input_output_aliases={1 + ranges: 0} if earlier else {},
        compiler_params=SMALL_PARAMS,
        name="place_rows",
    )(index, *arrays, *earlier)


def slot_parts(share_slots, pack):
    head = share_slots - pack
    return [(0, head), (head, pack)] if head > 0 else [(0, share_slots)]


def local(raw_echo, replica, beam_weights, pivots, owner_counts, train_gates):
    ch_local = raw_echo.shape[1]
    gate_rows = raw_echo.shape[2]
    pulse_count = raw_echo.shape[3]
    tap_count = replica.shape[1]
    train_local = train_gates.shape[1]
    owners = lax.axis_size("dop")
    ranges = lax.axis_size("rng")
    most_slots = 2 * (pulse_count // owners)
    share_slots = most_slots // ranges
    pack = max(1, min(LANES // train_local, share_slots))

    chunks = max(1, min(4, ch_local // 16))
    chunk_rows = ch_local // chunks
    rim = -(-(tap_count - 1) // 16) * 16
    filters = filter_rows(replica, gate_rows)
    table = doppler_table(pulse_count)
    following = [shifted(rim_rows(raw_echo, rim, c, chunks), "rng", -1) for c in range(chunks)]
    spectra = [
        form_spectrum(filters, table, raw_echo, following[c], c, chunks) for c in range(chunks)
    ]

    starts = jnp.cumsum(owner_counts, dtype=jnp.int32) - owner_counts
    places = jnp.stack([lax.axis_index("dop"), lax.axis_index("rng")]).astype(jnp.int32)
    index = jnp.concatenate([places, owner_counts, starts])
    local_gates = train_gates % gate_rows
    gates = jnp.concatenate([local_gates + part * gate_rows for part in range(pack)], axis=1)
    count_rows = float(train_local * ranges)

    parts = slot_parts(share_slots, pack)
    outgoing, tokens = [], []
    for first, count in parts:
        earlier = [beam_weights] if first > 0 else []
        array, token = select_gates(
            spectra, index, gates, first, count, share_slots, owners, ranges, pack, earlier
        )
        outgoing.append(array)
        tokens.append(token)
    axes = ("dop", "rng")
    sent = [
        lax.all_to_all(
            array.reshape(owners * ranges, -1, *array.shape[2:]),
            axes,
            split_axis=0,
            concat_axis=0,
            tiled=True,
        ).reshape(owners, ranges, -1, *array.shape[2:])
        for array in outgoing
    ]
    result, earlier = [], tokens[1:]
    for (first, count), arrived in zip(parts, sent):
        beams = form_beams(arrived, beam_weights, earlier)
        factors = factor_slots(beams, pivots, index, first, count, share_slots, pack, count_rows)
        earlier = factors[:1]
        rows = exchange(factors, "rng")
        result = [place_rows(index, rows, first, share_slots, result)]
    return result[0]


def solution(mesh):
    return jax.shard_map(
        local,
        mesh=mesh,
        in_specs=(P(None, "dop", "rng", None), P(), P(), P(), P(), P(None, "rng")),
        out_specs=P("dop", "rng", None),
        check_vma=False,
    )
```

```python
import functools
import math

import jax
import jax.numpy as jnp
import numpy as np
from jax import lax
from jax.experimental import pallas as pl
from jax.experimental.pallas import tpu as pltpu
from jax.sharding import PartitionSpec as P

LOADING = 0.25
LANES = 128
PANEL = 16
BF16 = jnp.bfloat16
F32 = jnp.float32
PARAMS = pltpu.CompilerParams(vmem_limit_bytes=48 * 1024 * 1024)
SMALL_PARAMS = pltpu.CompilerParams(vmem_limit_bytes=24 * 1024 * 1024)


def shifted(array, axis, by):
    count = lax.axis_size(axis)
    pairs = [(i, i + by) for i in range(count) if 0 <= i + by < count]
    return lax.ppermute(array, axis, pairs)


def doppler_table(pulse_count):
    pulse_index = np.arange(pulse_count)
    phase_index = pulse_index[:, None] * pulse_index[None, :] % pulse_count
    angle_table = phase_index.astype(np.float32) * np.float32(2.0 * math.pi / pulse_count)
    norm_scale = np.float32(1.0 / math.sqrt(pulse_count))
    real_part, imag_part = np.cos(angle_table) * norm_scale, np.sin(angle_table) * norm_scale
    table = np.block([[real_part.T, imag_part.T], [-imag_part.T, real_part.T]])
    high = table.astype(BF16)
    low = (table - high.astype(np.float32)).astype(BF16)
    return jnp.asarray(np.concatenate([high, high, low], axis=1))


def filter_kernel(replica_ref, out_ref):
    gate_rows, span = out_ref.shape[0] // 2, replica_ref.shape[1]
    banded = [
        pltpu.roll(
            jnp.broadcast_to(replica_ref[part : part + 1, :], (gate_rows, span)),
            0,
            1,
            stride=1,
            stride_axis=0,
        )
        for part in range(2)
    ]
    out_ref[:gate_rows, :span] = banded[0].astype(BF16)
    out_ref[:gate_rows, span:] = banded[1].astype(BF16)
    out_ref[gate_rows:, :span] = (-banded[1]).astype(BF16)
    out_ref[gate_rows:, span:] = banded[0].astype(BF16)


def filter_rows(replica, gate_rows):
    tap_count = replica.shape[1]
    span = -(-(gate_rows + tap_count) // LANES) * LANES
    return pl.pallas_call(
        filter_kernel,
        out_shape=jax.ShapeDtypeStruct((2 * gate_rows, 2 * span), BF16),
        in_specs=[pl.BlockSpec(memory_space=pltpu.VMEM)],
        out_specs=pl.BlockSpec(memory_space=pltpu.VMEM),
        compiler_params=PARAMS,
        name="filter_rows",
    )(jnp.pad(replica, ((0, 0), (0, span - tap_count))))


def rim_kernel(echo_ref, out_ref):
    out_ref[...] = echo_ref[...].astype(BF16)


def rim_rows(raw_echo, rim, chunk, chunks):
    _, ch_local, _, pulses = raw_echo.shape
    shape = (2, ch_local // chunks, rim, pulses)
    return pl.pallas_call(
        rim_kernel,
        out_shape=jax.ShapeDtypeStruct(shape, BF16),
        grid=(1,),
        in_specs=[pl.BlockSpec(shape, lambda i: (0, chunk, 0, 0))],
        out_specs=pl.BlockSpec(shape, lambda i: (0, 0, 0, 0)),
        compiler_params=PARAMS,
        name="rim_rows",
    )(raw_echo)


def spectrum_kernel(rows_ref, table_ref, own_ref, next_ref, out_ref, turned):
    step = pl.program_id(0)
    _, channels, gate_rows, pulses = own_ref.shape
    bins, height, _ = out_ref.shape
    rim = next_ref.shape[2]
    span = rows_ref.shape[1] // 2
    each = range(channels)
    samples = []
    for part in range(2):
        samples += [
            jnp.concatenate([own_ref[part, c] for c in each], axis=1).astype(BF16),
            jnp.concatenate([next_ref[part, c] for c in each], axis=1),
        ]
        if span > gate_rows + rim:
            samples.append(jnp.zeros((span - gate_rows - rim, channels * pulses), BF16))
    samples = jnp.concatenate(samples, axis=0)
    matched = jnp.dot(rows_ref[...], samples, preferred_element_type=F32)
    high, low = split_terms(matched)
    pieces = [
        term[part * gate_rows : (part + 1) * gate_rows]
        for term in (high, low, high)
        for part in range(2)
    ]
    stacked = jnp.concatenate(
        [
            jnp.concatenate([piece[:, c * pulses : (c + 1) * pulses] for piece in pieces], axis=1)
            for c in each
        ],
        axis=0,
    )
    spectra = lax.dot_general(
        table_ref[...], stacked, (((1,), (1,)), ((), ())), preferred_element_type=F32
    )
    for part in range(2):
        turned_part = jnp.stack(
            [
                spectra[part * bins : (part + 1) * bins, c * gate_rows : (c + 1) * gate_rows]
                for c in each
            ],
            axis=0,
        )
        place = pl.multiple_of(part * (height // 2) + step * channels, channels)
        turned[:, pl.ds(place, channels), :] = jnp.swapaxes(turned_part, 0, 1)

    @pl.when(step == pl.num_programs(0) - 1)
    def _():
        out_ref[...] = turned[...].astype(BF16)


def form_spectrum(rows, table, raw_echo, next_rows, chunk, chunks):
    _, ch_local, gate_rows, pulses = raw_echo.shape
    channels = ch_local // chunks
    step = math.gcd(channels, 8)
    steps = channels // step
    height = 2 * channels
    bins = table.shape[0] // 2
    return pl.pallas_call(
        spectrum_kernel,
        out_shape=jax.ShapeDtypeStruct((bins, height, gate_rows), BF16),
        grid=(steps,),
        in_specs=[
            pl.BlockSpec(rows.shape, lambda i: (0, 0)),
            pl.BlockSpec(table.shape, lambda i: (0, 0)),
            pl.BlockSpec((2, step, gate_rows, pulses), lambda i: (0, chunk * steps + i, 0, 0)),
            pl.BlockSpec((2, step) + next_rows.shape[2:], lambda i: (0, i, 0, 0)),
        ],
        out_specs=pl.BlockSpec((bins, height, gate_rows), lambda i: (0, 0, 0)),
        scratch_shapes=[pltpu.VMEM((bins, height, gate_rows), F32)],
        compiler_params=PARAMS,
        cost_estimate=pl.CostEstimate(
            flops=2 * rows.size * channels * pulses + 2 * table.size * channels * gate_rows,
            bytes_accessed=8 * channels * gate_rows * pulses,
            transcendentals=0,
        ),
        name="form_spectrum",
    )(rows, table, raw_echo, next_rows)


def owner_count(index_ref, owner):
    return index_ref[2 + owner]


def owner_start(index_ref, owner, owners):
    return index_ref[2 + owners + owner]


def select_kernel(
    index_ref, gates_ref, *refs, chunks, owners, ranges, first, share_slots, pack
):
    spectrum_refs, out_ref, token_ref = refs[:chunks], refs[-2], refs[-1]
    token_ref[...] = jnp.zeros_like(token_ref)
    bin_count, height, gate_rows = spectrum_refs[0].shape
    some, groups, _, width = out_ref.shape
    half = height // 2
    gate_index = lax.broadcasted_iota(jnp.int32, (pack * gate_rows, width), 0)
    part_index = lax.broadcasted_iota(jnp.int32, (1, width), 1) // (width // pack)
    for inner in range(some):
        start = owner_start(index_ref, pl.program_id(0) * some + inner, owners)
        for group in range(groups):
            block, place = divmod(group, groups // ranges)
            slot = block * share_slots + first + place * pack
            bins = [jnp.minimum(start + slot + part, bin_count - 1) for part in range(pack)]
            gates = gates_ref[pl.ds(bins[0], 1), :]
            for part in range(1, pack):
                gates = jnp.where(part_index == part, gates_ref[pl.ds(bins[part], 1), :], gates)
            chooser = jnp.where(gate_index == gates, 1.0, 0.0).astype(BF16)
            spectra = jnp.concatenate(
                [
                    jnp.concatenate([ref[b, s * half : (s + 1) * half] for b in bins], axis=1)
                    for s in range(2)
                    for ref in spectrum_refs
                ],
                axis=0,
            )
            picked = jnp.dot(spectra, chooser, preferred_element_type=F32)
            out_ref[inner, group] = picked.astype(BF16)


def select_gates(
    spectra, index, gates, first, count, share_slots, owners, ranges, pack, earlier
):
    rows = sum(spectrum.shape[1] for spectrum in spectra)
    gate_rows = spectra[0].shape[2]
    groups = ranges * count // pack
    width = gates.shape[1]
    some = math.gcd(owners, 4)
    return pl.pallas_call(
        functools.partial(
            select_kernel,
            chunks=len(spectra),
            owners=owners,
            ranges=ranges,
            first=first,
            share_slots=share_slots,
            pack=pack,
        ),
        out_shape=[
            jax.ShapeDtypeStruct((owners, groups, rows, width), BF16),
            jax.ShapeDtypeStruct((8, LANES), jnp.int32),
        ],
        grid=(owners // some,),
        in_specs=[pl.BlockSpec(memory_space=pltpu.SMEM)]
        + [pl.BlockSpec(memory_space=pltpu.VMEM)] * (1 + len(spectra))
        + [pl.BlockSpec(memory_space=pl.ANY)] * len(earlier),
        out_specs=[
            pl.BlockSpec((some, groups, rows, width), lambda i: (i, 0, 0, 0)),
            pl.BlockSpec((8, LANES), lambda i: (0, 0)),
        ],
        compiler_params=PARAMS,
        cost_estimate=pl.CostEstimate(
            flops=2 * owners * groups * pack * rows * gate_rows * width,
            bytes_accessed=owners * groups * rows * width * 2,
            transcendentals=0,
        ),
        name="select_gates",
    )(index, gates, *spectra, *earlier)


def beam_kernel(weights_ref, arrived_ref, *refs):
    out_ref = refs[-1]
    sources, ranges, groups, rows, width = arrived_ref.shape
    dof = weights_ref.shape[2]
    half = rows // 2
    for block in range(ranges):
        packed = jnp.concatenate(
            [
                arrived_ref[:, block, g, s * half : (s + 1) * half].reshape(sources * half, width)
                for s in range(2)
                for g in range(groups)
            ],
            axis=1,
        )
        by_real, by_imag = [
            lax.dot_general(
                weights_ref[part], packed, (((0,), (0,)), ((), ())), preferred_element_type=F32
            )
            for part in range(2)
        ]
        middle = groups * width
        real_part = by_real[:, :middle] + by_imag[:, middle:]
        imag_part = by_real[:, middle:] - by_imag[:, :middle]
        for g in range(groups):
            span = slice(g * width, (g + 1) * width)
            out_ref[block, g, :dof] = real_part[:, span].astype(BF16)
            out_ref[block, g, dof:] = imag_part[:, span].astype(BF16)


def form_beams(arrived, weights, earlier):
    _, ranges, groups, _, width = arrived.shape
    shape = (ranges, groups, 2 * weights.shape[2], width)
    return pl.pallas_call(
        beam_kernel,
        out_shape=jax.ShapeDtypeStruct(shape, BF16),
        in_specs=[pl.BlockSpec(memory_space=pltpu.VMEM)] * 2
        + [pl.BlockSpec(memory_space=pl.ANY)] * len(earlier),
        out_specs=pl.BlockSpec(memory_space=pltpu.VMEM),
        compiler_params=SMALL_PARAMS,
        cost_estimate=pl.CostEstimate(
            flops=4 * arrived.size * weights.shape[2],
            bytes_accessed=arrived.size * 2,
            transcendentals=0,
        ),
        name="form_beams",
    )(weights, arrived, *earlier)


def exchange(arrays, axis):
    count = len(arrays)
    moved = [arrays[0]]
    for shift in range(1, count):
        pairs = [(i, (i + shift) % count) for i in range(count)]
        moved.append(lax.ppermute(arrays[shift], axis, pairs))
    return moved


def split_terms(array):
    high = array.astype(BF16)
    return high, (array - high.astype(F32)).astype(BF16)


def left_terms(array):
    high, low = split_terms(array)
    high, low = high.astype(F32), low.astype(F32)
    return jnp.concatenate([high, high, low], axis=0).T.astype(BF16)


def right_terms(array):
    high, low = split_terms(array)
    return jnp.concatenate([high, low, high], axis=0)


def product(left, right):
    return jnp.dot(left, right, preferred_element_type=F32)


def loaded_covariance(beams, pivot_row, part, pack, count_rows):
    dof = pivot_row.shape[1]
    width = beams[0].shape[1] // pack
    hot = lax.broadcasted_iota(jnp.int32, (dof, dof), 0) == pivot_row
    hot = jnp.where(hot, 1.0, 0.0).astype(BF16)
    own = jnp.concatenate([b[:, part * width : (part + 1) * width] for b in beams], axis=1)
    picked = [
        lax.dot_general(
            hot,
            own[half * dof : (half + 1) * dof],
            (((0,), (0,)), ((), ())),
            preferred_element_type=F32,
        )
        for half in range(2)
    ]
    upper = jnp.concatenate([picked[0], picked[1]], axis=1).astype(BF16)
    lower = jnp.concatenate([picked[1], -picked[0]], axis=1).astype(BF16)
    stacked = jnp.concatenate([upper, lower], axis=0)
    gram = lax.dot_general(
        stacked, stacked, (((1,), (1,)), ((), ())), preferred_element_type=F32
    )
    return gram * (1.0 / count_rows)


def lane_spread(piece, lane):
    return jnp.broadcast_to(piece[:, lane : lane + 1], piece.shape)


def refined_reciprocal(value):
    guess = pl.reciprocal(value, approx=True)
    return guess * (2.0 - value * guess)


def tree_sum(terms):
    while len(terms) > 1:
        terms = [x + y for x, y in zip(terms[::2], terms[1::2])]
    return terms[0]


def eliminate(rows):
    scales = []
    for first in range(0, PANEL, 8):
        span = range(first, first + 8)
        small = {(i, j): lane_spread(rows[i][0], j) for i in span for j in span if j >= i}
        inverses = []
        for t in range(first, first + 8, 2):
            u = t + 1
            inverse = refined_reciprocal(small[t, t])
            cross = small[t, t] * small[u, u] - small[t, u] * small[t, u]
            guess = pl.reciprocal(cross, approx=True)
            second = (small[t, t] * guess) * (2.0 - cross * guess)
            inverses += [inverse, second]
            scales += [lax.rsqrt(small[t, t]), lax.rsqrt(cross * inverse)]
            factor = small[t, u] * inverse
            for j in range(u + 1, first + 8):
                small[u, j] = small[u, j] - factor * small[t, j]
            rows[u] = [x - factor * y for x, y in zip(rows[u], rows[t])]
            for i in range(u + 1, first + 8):
                one, two = small[t, i] * inverse, small[u, i] * second
                for j in range(i, first + 8):
                    both = small[u, i] * small[u, j]
                    small[i, j] = (small[i, j] - one * small[t, j]) - both * second
                rows[i] = [
                    x - one * y - two * z for x, y, z in zip(rows[i], rows[t], rows[u])
                ]
        ratios = [rows[t][0] * inverse for t, inverse in zip(span, inverses)]
        for i in range(first + 8, PANEL):
            factors = [lane_spread(ratio, i) for ratio in ratios]
            rows[i] = [
                x - tree_sum([f * rows[t][w] for f, t in zip(factors, span)])
                for w, x in enumerate(rows[i])
            ]
    return [[x * scale for x in row] for row, scale in zip(rows, scales)]


def factor_kernel(
    index_ref, pivots_ref, beams_ref, *refs, first, share_slots, ranges, pack, count_rows
):
    out_refs = refs[:ranges]
    arriving, leaving, *scratch = refs[ranges:]
    slots = len(scratch) // 3
    work, lefts, rights = scratch[:slots], scratch[slots : 2 * slots], scratch[2 * slots :]
    order = work[0].shape[0]
    height = arriving.shape[1] // PANEL

    row = lax.broadcasted_iota(jnp.int32, (LANES, LANES), 0)
    col = lax.broadcasted_iota(jnp.int32, (LANES, LANES), 1)
    loading = jnp.where(row == col, LOADING, 0.0)
    owners = (index_ref.shape[0] - 2) // 2
    bin_lead = owner_start(index_ref, index_ref[0], owners) + index_ref[1] * share_slots + first
    for slot in range(slots):
        group, part = divmod(slot, pack)
        own_bin = jnp.minimum(bin_lead + slot, pivots_ref.shape[0] - 1)
        work[slot][...] = loaded_covariance(
            [beams_ref[r, group] for r in range(ranges)],
            pivots_ref[pl.ds(own_bin, 1), :],
            part,
            pack,
            count_rows,
        )
        for start in range(0, order, LANES):
            work[slot][start : start + LANES, start : start + LANES] += loading

    eights = range(0, PANEL, 8)
    column = lax.broadcasted_iota(jnp.int32, (LANES, 3 * PANEL), 0)

    def spread_out(slot, rows):
        for i in eights:
            for w in range(rows.shape[1] // LANES):
                piece = rows[i : i + 8, w * LANES : (w + 1) * LANES]
                arriving[w, pl.ds(i * height + slot, 8, stride=height), :] = piece

    for slot in range(slots):
        spread_out(slot, work[slot][:PANEL, :])
    for start in range(0, order, LANES):
        chunks = (order - start) // LANES
        stop = start + LANES
        for slot in range(slots):
            lefts[slot][...] = jnp.zeros_like(lefts[slot])
            rights[slot][...] = jnp.zeros_like(rights[slot])

        def one_panel(p, carry, start=start, stop=stop, chunks=chunks):
            back = p * PANEL
            base = pl.multiple_of(start + back, PANEL)
            ahead = pl.multiple_of(jnp.minimum(back + PANEL, LANES - PANEL), PANEL)
            following = pl.multiple_of(start + ahead, PANEL)
            for slot in range(slots):
                left = jnp.where(column >= back + PANEL, lefts[slot][...], 0.0).astype(BF16)
                work[slot][start:stop, start:] -= product(left, rights[slot][:, start:])
            rows = []
            for t in range(PANEL):
                pieces = [arriving[w, t * height : (t + 1) * height, :] for w in range(chunks)]
                pieces[0] = pltpu.roll(pieces[0], (LANES - back) % LANES, 1)
                rows.append(pieces)
            rows = eliminate(rows)
            for t in range(PANEL):
                rows[t][0] = pltpu.roll(rows[t][0], back, 1)
                for w in range(chunks):
                    leaving[w, t * height : (t + 1) * height, :] = rows[t][w]
            for slot in range(slots):
                parts = []
                for w in range(chunks):
                    pieces = [
                        leaving[w, pl.ds(i * height + slot, 8, stride=height), :] for i in eights
                    ]
                    parts.append(jnp.concatenate(pieces, axis=0))
                panel = jnp.concatenate(parts, axis=1)
                work[slot][pl.ds(base, PANEL), start:] = panel
                lefts[slot][...] = left_terms(parts[0]).astype(F32)
                right = right_terms(panel)
                rights[slot][:, start:] = right
                left = lefts[slot][pl.ds(ahead, PANEL), :].astype(BF16)
                spread_out(slot, work[slot][pl.ds(following, PANEL), start:] - product(left, right))
            return carry

        lax.fori_loop(0, LANES // PANEL, one_panel, 0)
        if chunks > 1:
            terms = []
            for slot in range(slots):
                done = work[slot][start:stop, stop:]
                left = jnp.concatenate(
                    [left_terms(done[:, w * LANES : (w + 1) * LANES]) for w in range(chunks - 1)],
                    axis=0,
                )
                right = right_terms(done)
                ready = work[slot][stop : stop + PANEL, stop:] - product(left[:PANEL], right)
                spread_out(slot, ready)
                terms.append((left, right))
            for slot in range(slots):
                left, right = terms[slot]
                work[slot][stop + PANEL :, stop:] -= product(left[PANEL:], right)

    share = order // ranges
    row = lax.broadcasted_iota(jnp.int32, (share, order), 0)
    col = lax.broadcasted_iota(jnp.int32, (share, order), 1)
    for shift, out_ref in enumerate(out_refs):
        lead = pl.multiple_of(lax.rem(index_ref[1] + shift, ranges) * share, math.gcd(share, 16))
        upper = col >= row + lead
        for slot in range(slots):
            piece = work[slot][pl.ds(lead, share), :]
            out_ref[slot] = jnp.where(upper, piece, 0.0).astype(out_ref.dtype)


def factor_slots(beams, pivots, index, first, slots, share_slots, pack, count_rows):
    ranges, _, order, _ = beams.shape
    height = -(-slots // 8) * 8
    return pl.pallas_call(
        functools.partial(
            factor_kernel,
            first=first,
            share_slots=share_slots,
            ranges=ranges,
            pack=pack,
            count_rows=count_rows,
        ),
        out_shape=[jax.ShapeDtypeStruct((slots, order // ranges, order), BF16)] * ranges,
        in_specs=[pl.BlockSpec(memory_space=pltpu.SMEM)]
        + [pl.BlockSpec(memory_space=pltpu.VMEM)] * 2,
        out_specs=[pl.BlockSpec(memory_space=pltpu.VMEM)] * ranges,
        scratch_shapes=[pltpu.VMEM((order // LANES, PANEL * height, LANES), F32)] * 2
        + [pltpu.VMEM((order, order), F32) for _ in range(slots)]
        + [pltpu.VMEM((LANES, 3 * PANEL), F32) for _ in range(slots)]
        + [pltpu.VMEM((3 * PANEL, order), BF16) for _ in range(slots)],
        compiler_params=SMALL_PARAMS,
        cost_estimate=pl.CostEstimate(
            flops=slots * order**3,
            bytes_accessed=beams.size * 2,
            transcendentals=0,
        ),
        name="factor_slots",
    )(index, pivots, beams)


def place_kernel(index_ref, *refs, first, share_slots, ranges):
    in_refs, out_ref = refs[:ranges], refs[-1]
    slots = out_ref.shape[0]
    steps = in_refs[0].shape[0] // slots
    step = pl.program_id(0)
    shift, place = step // steps, step % steps
    block = lax.rem(index_ref[1] + ranges - shift, ranges)
    lead = block * share_slots + first + place * slots
    for this, ref in enumerate(in_refs):

        @pl.when(shift == this)
        def _(ref=ref):
            for i in range(slots):
                keep = lead + i < owner_count(index_ref, index_ref[0])
                keep = jnp.broadcast_to(keep, out_ref.shape[1:])
                out_ref[i] = jnp.where(keep, ref[place * slots + i].astype(F32), 0.0)


def place_rows(index, arrays, first, share_slots, earlier):
    ranges = len(arrays)
    count = arrays[0].shape[0]
    slots = math.gcd(math.gcd(count, first), share_slots)
    steps = count // slots

    def out_index(step, index_ref):
        block = lax.rem(index_ref[1] + ranges - step // steps, ranges)
        return ((block * share_slots + first) // slots + step % steps, 0, 0)

    return pl.pallas_call(
        functools.partial(place_kernel, first=first, share_slots=share_slots, ranges=ranges),
        out_shape=jax.ShapeDtypeStruct((ranges * share_slots,) + arrays[0].shape[1:], F32),
        grid_spec=pltpu.PrefetchScalarGridSpec(
            num_scalar_prefetch=1,
            grid=(ranges * steps,),
            in_specs=[pl.BlockSpec(memory_space=pltpu.VMEM)] * ranges
            + [pl.BlockSpec(memory_space=pl.ANY)] * len(earlier),
            out_specs=pl.BlockSpec((slots,) + arrays[0].shape[1:], out_index),
        ),
        input_output_aliases={1 + ranges: 0} if earlier else {},
        compiler_params=SMALL_PARAMS,
        name="place_rows",
    )(index, *arrays, *earlier)


def slot_parts(share_slots, pack):
    head = share_slots - pack
    return [(0, head), (head, pack)] if head > 0 else [(0, share_slots)]


def local(raw_echo, replica, beam_weights, pivots, owner_counts, train_gates):
    ch_local = raw_echo.shape[1]
    gate_rows = raw_echo.shape[2]
    pulse_count = raw_echo.shape[3]
    tap_count = replica.shape[1]
    train_local = train_gates.shape[1]
    owners = lax.axis_size("dop")
    ranges = lax.axis_size("rng")
    most_slots = 2 * (pulse_count // owners)
    share_slots = most_slots // ranges
    pack = max(1, min(LANES // train_local, share_slots))

    chunks = max(1, min(4, ch_local // 16))
    chunk_rows = ch_local // chunks
    rim = -(-(tap_count - 1) // 16) * 16
    filters = filter_rows(replica, gate_rows)
    table = doppler_table(pulse_count)
    following = [shifted(rim_rows(raw_echo, rim, c, chunks), "rng", -1) for c in range(chunks)]
    spectra = [
        form_spectrum(filters, table, raw_echo, following[c], c, chunks) for c in range(chunks)
    ]

    starts = jnp.cumsum(owner_counts, dtype=jnp.int32) - owner_counts
    places = jnp.stack([lax.axis_index("dop"), lax.axis_index("rng")]).astype(jnp.int32)
    index = jnp.concatenate([places, owner_counts, starts])
    local_gates = train_gates % gate_rows
    gates = jnp.concatenate([local_gates + part * gate_rows for part in range(pack)], axis=1)
    count_rows = float(train_local * ranges)

    parts = slot_parts(share_slots, pack)
    outgoing, tokens = [], []
    for first, count in parts:
        earlier = [beam_weights] if first > 0 else []
        array, token = select_gates(
            spectra, index, gates, first, count, share_slots, owners, ranges, pack, earlier
        )
        outgoing.append(array)
        tokens.append(token)
    axes = ("dop", "rng")
    sent = [
        lax.all_to_all(
            array.reshape(owners * ranges, -1, *array.shape[2:]),
            axes,
            split_axis=0,
            concat_axis=0,
            tiled=True,
        ).reshape(owners, ranges, -1, *array.shape[2:])
        for array in outgoing
    ]
    result, earlier = [], tokens[1:]
    for (first, count), arrived in zip(parts, sent):
        beams = form_beams(arrived, beam_weights, earlier)
        factors = factor_slots(beams, pivots, index, first, count, share_slots, pack, count_rows)
        earlier = factors[:1]
        rows = exchange(factors, "rng")
        result = [place_rows(index, rows, first, share_slots, result)]
    return result[0]


def solution(mesh):
    return jax.shard_map(
        local,
        mesh=mesh,
        in_specs=(P(None, "dop", "rng", None), P(), P(), P(), P(), P(None, "rng")),
        out_specs=P("dop", "rng", None),
        check_vma=False,
    )
```

```python
import functools
import math

import jax
import jax.numpy as jnp
import numpy as np
from jax import lax
from jax.experimental import pallas as pl
from jax.experimental.pallas import tpu as pltpu
from jax.sharding import PartitionSpec as P

LOADING = 0.25
LANES = 128
PANEL = 32
BF16 = jnp.bfloat16
F32 = jnp.float32
PARAMS = pltpu.CompilerParams(vmem_limit_bytes=48 * 1024 * 1024)
SMALL_PARAMS = pltpu.CompilerParams(vmem_limit_bytes=24 * 1024 * 1024)


def shifted(array, axis, by):
    count = lax.axis_size(axis)
    pairs = [(i, i + by) for i in range(count) if 0 <= i + by < count]
    return lax.ppermute(array, axis, pairs)


def doppler_table(pulse_count):
    pulse_index = np.arange(pulse_count)
    phase_index = pulse_index[:, None] * pulse_index[None, :] % pulse_count
    angle_table = phase_index.astype(np.float32) * np.float32(2.0 * math.pi / pulse_count)
    norm_scale = np.float32(1.0 / math.sqrt(pulse_count))
    real_part, imag_part = np.cos(angle_table) * norm_scale, np.sin(angle_table) * norm_scale
    table = np.block([[real_part.T, imag_part.T], [-imag_part.T, real_part.T]])
    high = table.astype(BF16)
    low = (table - high.astype(np.float32)).astype(BF16)
    return jnp.asarray(np.concatenate([high, high, low], axis=1))


def filter_kernel(replica_ref, out_ref):
    gate_rows, span = out_ref.shape[0] // 2, replica_ref.shape[1]
    banded = [
        pltpu.roll(
            jnp.broadcast_to(replica_ref[part : part + 1, :], (gate_rows, span)),
            0,
            1,
            stride=1,
            stride_axis=0,
        )
        for part in range(2)
    ]
    out_ref[:gate_rows, :span] = banded[0].astype(BF16)
    out_ref[:gate_rows, span:] = banded[1].astype(BF16)
    out_ref[gate_rows:, :span] = (-banded[1]).astype(BF16)
    out_ref[gate_rows:, span:] = banded[0].astype(BF16)


def filter_rows(replica, gate_rows):
    tap_count = replica.shape[1]
    span = -(-(gate_rows + tap_count) // LANES) * LANES
    return pl.pallas_call(
        filter_kernel,
        out_shape=jax.ShapeDtypeStruct((2 * gate_rows, 2 * span), BF16),
        in_specs=[pl.BlockSpec(memory_space=pltpu.VMEM)],
        out_specs=pl.BlockSpec(memory_space=pltpu.VMEM),
        compiler_params=PARAMS,
        name="filter_rows",
    )(jnp.pad(replica, ((0, 0), (0, span - tap_count))))


def rim_kernel(echo_ref, out_ref):
    out_ref[...] = echo_ref[...].astype(BF16)


def rim_rows(raw_echo, rim, chunk, chunks):
    _, ch_local, _, pulses = raw_echo.shape
    shape = (2, ch_local // chunks, rim, pulses)
    return pl.pallas_call(
        rim_kernel,
        out_shape=jax.ShapeDtypeStruct(shape, BF16),
        grid=(1,),
        in_specs=[pl.BlockSpec(shape, lambda i: (0, chunk, 0, 0))],
        out_specs=pl.BlockSpec(shape, lambda i: (0, 0, 0, 0)),
        compiler_params=PARAMS,
        name="rim_rows",
    )(raw_echo)


def spectrum_kernel(rows_ref, table_ref, own_ref, next_ref, out_ref, turned):
    step = pl.program_id(0)
    _, channels, gate_rows, pulses = own_ref.shape
    bins, height, _ = out_ref.shape
    rim = next_ref.shape[2]
    span = rows_ref.shape[1] // 2
    each = range(channels)
    samples = []
    for part in range(2):
        samples += [
            jnp.concatenate([own_ref[part, c] for c in each], axis=1).astype(BF16),
            jnp.concatenate([next_ref[part, c] for c in each], axis=1),
        ]
        if span > gate_rows + rim:
            samples.append(jnp.zeros((span - gate_rows - rim, channels * pulses), BF16))
    samples = jnp.concatenate(samples, axis=0)
    matched = jnp.dot(rows_ref[...], samples, preferred_element_type=F32)
    high, low = split_terms(matched)
    pieces = [
        term[part * gate_rows : (part + 1) * gate_rows]
        for term in (high, low, high)
        for part in range(2)
    ]
    stacked = jnp.concatenate(
        [
            jnp.concatenate([piece[:, c * pulses : (c + 1) * pulses] for piece in pieces], axis=1)
            for c in each
        ],
        axis=0,
    )
    spectra = lax.dot_general(
        table_ref[...], stacked, (((1,), (1,)), ((), ())), preferred_element_type=F32
    )
    for part in range(2):
        turned_part = jnp.stack(
            [
                spectra[part * bins : (part + 1) * bins, c * gate_rows : (c + 1) * gate_rows]
                for c in each
            ],
            axis=0,
        )
        place = pl.multiple_of(part * (height // 2) + step * channels, channels)
        turned[:, pl.ds(place, channels), :] = jnp.swapaxes(turned_part, 0, 1)

    @pl.when(step == pl.num_programs(0) - 1)
    def _():
        out_ref[...] = turned[...].astype(BF16)


def form_spectrum(rows, table, raw_echo, next_rows, chunk, chunks):
    _, ch_local, gate_rows, pulses = raw_echo.shape
    channels = ch_local // chunks
    step = math.gcd(channels, 16)
    steps = channels // step
    height = 2 * channels
    bins = table.shape[0] // 2
    return pl.pallas_call(
        spectrum_kernel,
        out_shape=jax.ShapeDtypeStruct((bins, height, gate_rows), BF16),
        grid=(steps,),
        in_specs=[
            pl.BlockSpec(rows.shape, lambda i: (0, 0)),
            pl.BlockSpec(table.shape, lambda i: (0, 0)),
            pl.BlockSpec((2, step, gate_rows, pulses), lambda i: (0, chunk * steps + i, 0, 0)),
            pl.BlockSpec((2, step) + next_rows.shape[2:], lambda i: (0, i, 0, 0)),
        ],
        out_specs=pl.BlockSpec((bins, height, gate_rows), lambda i: (0, 0, 0)),
        scratch_shapes=[pltpu.VMEM((bins, height, gate_rows), F32)],
        compiler_params=PARAMS,
        cost_estimate=pl.CostEstimate(
            flops=2 * rows.size * channels * pulses + 2 * table.size * channels * gate_rows,
            bytes_accessed=8 * channels * gate_rows * pulses,
            transcendentals=0,
        ),
        name="form_spectrum",
    )(rows, table, raw_echo, next_rows)


def owner_count(index_ref, owner):
    return index_ref[2 + owner]


def owner_start(index_ref, owner, owners):
    return index_ref[2 + owners + owner]


def select_kernel(
    index_ref, gates_ref, *refs, chunks, owners, ranges, first, share_slots, pack
):
    spectrum_refs, out_ref, token_ref = refs[:chunks], refs[-2], refs[-1]
    token_ref[...] = jnp.zeros_like(token_ref)
    bin_count, height, gate_rows = spectrum_refs[0].shape
    some, groups, _, width = out_ref.shape
    half = height // 2
    gate_index = lax.broadcasted_iota(jnp.int32, (pack * gate_rows, width), 0)
    part_index = lax.broadcasted_iota(jnp.int32, (1, width), 1) // (width // pack)
    for inner in range(some):
        start = owner_start(index_ref, pl.program_id(0) * some + inner, owners)
        for group in range(groups):
            block, place = divmod(group, groups // ranges)
            slot = block * share_slots + first + place * pack
            bins = [jnp.minimum(start + slot + part, bin_count - 1) for part in range(pack)]
            gates = gates_ref[pl.ds(bins[0], 1), :]
            for part in range(1, pack):
                gates = jnp.where(part_index == part, gates_ref[pl.ds(bins[part], 1), :], gates)
            chooser = jnp.where(gate_index == gates, 1.0, 0.0).astype(BF16)
            spectra = jnp.concatenate(
                [
                    jnp.concatenate([ref[b, s * half : (s + 1) * half] for b in bins], axis=1)
                    for s in range(2)
                    for ref in spectrum_refs
                ],
                axis=0,
            )
            picked = jnp.dot(spectra, chooser, preferred_element_type=F32)
            out_ref[inner, group] = picked.astype(BF16)


def select_gates(
    spectra, index, gates, first, count, share_slots, owners, ranges, pack, earlier
):
    rows = sum(spectrum.shape[1] for spectrum in spectra)
    gate_rows = spectra[0].shape[2]
    groups = ranges * count // pack
    width = gates.shape[1]
    some = math.gcd(owners, 4)
    return pl.pallas_call(
        functools.partial(
            select_kernel,
            chunks=len(spectra),
            owners=owners,
            ranges=ranges,
            first=first,
            share_slots=share_slots,
            pack=pack,
        ),
        out_shape=[
            jax.ShapeDtypeStruct((owners, groups, rows, width), BF16),
            jax.ShapeDtypeStruct((8, LANES), jnp.int32),
        ],
        grid=(owners // some,),
        in_specs=[pl.BlockSpec(memory_space=pltpu.SMEM)]
        + [pl.BlockSpec(memory_space=pltpu.VMEM)] * (1 + len(spectra))
        + [pl.BlockSpec(memory_space=pl.ANY)] * len(earlier),
        out_specs=[
            pl.BlockSpec((some, groups, rows, width), lambda i: (i, 0, 0, 0)),
            pl.BlockSpec((8, LANES), lambda i: (0, 0)),
        ],
        compiler_params=PARAMS,
        cost_estimate=pl.CostEstimate(
            flops=2 * owners * groups * pack * rows * gate_rows * width,
            bytes_accessed=owners * groups * rows * width * 2,
            transcendentals=0,
        ),
        name="select_gates",
    )(index, gates, *spectra, *earlier)


def beam_kernel(weights_ref, arrived_ref, *refs):
    out_ref = refs[-1]
    sources, ranges, groups, rows, width = arrived_ref.shape
    dof = weights_ref.shape[2]
    half = rows // 2
    for block in range(ranges):
        packed = jnp.concatenate(
            [
                arrived_ref[:, block, g, s * half : (s + 1) * half].reshape(sources * half, width)
                for s in range(2)
                for g in range(groups)
            ],
            axis=1,
        )
        by_real, by_imag = [
            lax.dot_general(
                weights_ref[part], packed, (((0,), (0,)), ((), ())), preferred_element_type=F32
            )
            for part in range(2)
        ]
        middle = groups * width
        real_part = by_real[:, :middle] + by_imag[:, middle:]
        imag_part = by_real[:, middle:] - by_imag[:, :middle]
        for g in range(groups):
            span = slice(g * width, (g + 1) * width)
            out_ref[block, g, :dof] = real_part[:, span].astype(BF16)
            out_ref[block, g, dof:] = imag_part[:, span].astype(BF16)


def form_beams(arrived, weights, earlier):
    _, ranges, groups, _, width = arrived.shape
    shape = (ranges, groups, 2 * weights.shape[2], width)
    return pl.pallas_call(
        beam_kernel,
        out_shape=jax.ShapeDtypeStruct(shape, BF16),
        in_specs=[pl.BlockSpec(memory_space=pltpu.VMEM)] * 2
        + [pl.BlockSpec(memory_space=pl.ANY)] * len(earlier),
        out_specs=pl.BlockSpec(memory_space=pltpu.VMEM),
        compiler_params=SMALL_PARAMS,
        cost_estimate=pl.CostEstimate(
            flops=4 * arrived.size * weights.shape[2],
            bytes_accessed=arrived.size * 2,
            transcendentals=0,
        ),
        name="form_beams",
    )(weights, arrived, *earlier)


def exchange(arrays, axis):
    count = len(arrays)
    moved = [arrays[0]]
    for shift in range(1, count):
        pairs = [(i, (i + shift) % count) for i in range(count)]
        moved.append(lax.ppermute(arrays[shift], axis, pairs))
    return moved


def split_terms(array):
    high = array.astype(BF16)
    return high, (array - high.astype(F32)).astype(BF16)


def left_terms(array):
    high, low = split_terms(array)
    high, low = high.astype(F32), low.astype(F32)
    return jnp.concatenate([high, high, low], axis=0).T.astype(BF16)


def right_terms(array):
    high, low = split_terms(array)
    return jnp.concatenate([high, low, high], axis=0)


def product(left, right):
    return jnp.dot(left, right, preferred_element_type=F32)


def loaded_covariance(beams, pivot_row, part, pack, count_rows):
    dof = pivot_row.shape[1]
    width = beams[0].shape[1] // pack
    hot = lax.broadcasted_iota(jnp.int32, (dof, dof), 0) == pivot_row
    hot = jnp.where(hot, 1.0, 0.0).astype(BF16)
    own = jnp.concatenate([b[:, part * width : (part + 1) * width] for b in beams], axis=1)
    picked = [
        lax.dot_general(
            hot,
            own[half * dof : (half + 1) * dof],
            (((0,), (0,)), ((), ())),
            preferred_element_type=F32,
        )
        for half in range(2)
    ]
    upper = jnp.concatenate([picked[0], picked[1]], axis=1).astype(BF16)
    lower = jnp.concatenate([picked[1], -picked[0]], axis=1).astype(BF16)
    stacked = jnp.concatenate([upper, lower], axis=0)
    gram = lax.dot_general(
        stacked, stacked, (((1,), (1,)), ((), ())), preferred_element_type=F32
    )
    return gram * (1.0 / count_rows)


def lane_spread(piece, lane):
    return jnp.broadcast_to(piece[:, lane : lane + 1], piece.shape)


def refined_reciprocal(value):
    guess = pl.reciprocal(value, approx=True)
    return guess * (2.0 - value * guess)


def tree_sum(terms):
    while len(terms) > 1:
        terms = [x + y for x, y in zip(terms[::2], terms[1::2])]
    return terms[0]


def eliminate(rows):
    scales = []
    for first in range(0, PANEL, 8):
        span = range(first, first + 8)
        small = {(i, j): lane_spread(rows[i][0], j) for i in span for j in span if j >= i}
        inverses = []
        for t in range(first, first + 8, 2):
            u = t + 1
            inverse = refined_reciprocal(small[t, t])
            cross = small[t, t] * small[u, u] - small[t, u] * small[t, u]
            guess = pl.reciprocal(cross, approx=True)
            second = (small[t, t] * guess) * (2.0 - cross * guess)
            inverses += [inverse, second]
            scales += [lax.rsqrt(small[t, t]), lax.rsqrt(cross * inverse)]
            factor = small[t, u] * inverse
            for j in range(u + 1, first + 8):
                small[u, j] = small[u, j] - factor * small[t, j]
            rows[u] = [x - factor * y for x, y in zip(rows[u], rows[t])]
            for i in range(u + 1, first + 8):
                one, two = small[t, i] * inverse, small[u, i] * second
                for j in range(i, first + 8):
                    both = small[u, i] * small[u, j]
                    small[i, j] = (small[i, j] - one * small[t, j]) - both * second
                rows[i] = [
                    x - one * y - two * z for x, y, z in zip(rows[i], rows[t], rows[u])
                ]
        ratios = [rows[t][0] * inverse for t, inverse in zip(span, inverses)]
        for i in range(first + 8, PANEL):
            factors = [lane_spread(ratio, i) for ratio in ratios]
            rows[i] = [
                x - tree_sum([f * rows[t][w] for f, t in zip(factors, span)])
                for w, x in enumerate(rows[i])
            ]
    return [[x * scale for x in row] for row, scale in zip(rows, scales)]


def factor_kernel(
    index_ref, pivots_ref, beams_ref, *refs, first, share_slots, ranges, pack, count_rows
):
    out_refs = refs[:ranges]
    arriving, leaving, *scratch = refs[ranges:]
    slots = len(scratch) // 3
    work, lefts, rights = scratch[:slots], scratch[slots : 2 * slots], scratch[2 * slots :]
    order = work[0].shape[0]
    height = arriving.shape[1] // PANEL

    row = lax.broadcasted_iota(jnp.int32, (LANES, LANES), 0)
    col = lax.broadcasted_iota(jnp.int32, (LANES, LANES), 1)
    loading = jnp.where(row == col, LOADING, 0.0)
    owners = (index_ref.shape[0] - 2) // 2
    bin_lead = owner_start(index_ref, index_ref[0], owners) + index_ref[1] * share_slots + first
    for slot in range(slots):
        group, part = divmod(slot, pack)
        own_bin = jnp.minimum(bin_lead + slot, pivots_ref.shape[0] - 1)
        work[slot][...] = loaded_covariance(
            [beams_ref[r, group] for r in range(ranges)],
            pivots_ref[pl.ds(own_bin, 1), :],
            part,
            pack,
            count_rows,
        )
        for start in range(0, order, LANES):
            work[slot][start : start + LANES, start : start + LANES] += loading

    eights = range(0, PANEL, 8)
    column = lax.broadcasted_iota(jnp.int32, (LANES, 3 * PANEL), 0)

    def spread_out(slot, rows):
        for i in eights:
            for w in range(rows.shape[1] // LANES):
                piece = rows[i : i + 8, w * LANES : (w + 1) * LANES]
                arriving[w, pl.ds(i * height + slot, 8, stride=height), :] = piece

    for slot in range(slots):
        spread_out(slot, work[slot][:PANEL, :])
    for start in range(0, order, LANES):
        chunks = (order - start) // LANES
        stop = start + LANES
        for slot in range(slots):
            lefts[slot][...] = jnp.zeros_like(lefts[slot])
            rights[slot][...] = jnp.zeros_like(rights[slot])

        def one_panel(p, carry, start=start, stop=stop, chunks=chunks):
            back = p * PANEL
            base = pl.multiple_of(start + back, PANEL)
            ahead = pl.multiple_of(jnp.minimum(back + PANEL, LANES - PANEL), PANEL)
            following = pl.multiple_of(start + ahead, PANEL)
            for slot in range(slots):
                left = jnp.where(column >= back + PANEL, lefts[slot][...], 0.0).astype(BF16)
                work[slot][start:stop, start:] -= product(left, rights[slot][:, start:])
            rows = []
            for t in range(PANEL):
                pieces = [arriving[w, t * height : (t + 1) * height, :] for w in range(chunks)]
                pieces[0] = pltpu.roll(pieces[0], (LANES - back) % LANES, 1)
                rows.append(pieces)
            rows = eliminate(rows)
            for t in range(PANEL):
                rows[t][0] = pltpu.roll(rows[t][0], back, 1)
                for w in range(chunks):
                    leaving[w, t * height : (t + 1) * height, :] = rows[t][w]
            for slot in range(slots):
                parts = []
                for w in range(chunks):
                    pieces = [
                        leaving[w, pl.ds(i * height + slot, 8, stride=height), :] for i in eights
                    ]
                    parts.append(jnp.concatenate(pieces, axis=0))
                panel = jnp.concatenate(parts, axis=1)
                work[slot][pl.ds(base, PANEL), start:] = panel
                lefts[slot][...] = left_terms(parts[0]).astype(F32)
                right = right_terms(panel)
                rights[slot][:, start:] = right
                left = lefts[slot][pl.ds(ahead, PANEL), :].astype(BF16)
                spread_out(slot, work[slot][pl.ds(following, PANEL), start:] - product(left, right))
            return carry

        lax.fori_loop(0, LANES // PANEL, one_panel, 0)
        if chunks > 1:
            terms = []
            for slot in range(slots):
                done = work[slot][start:stop, stop:]
                left = jnp.concatenate(
                    [left_terms(done[:, w * LANES : (w + 1) * LANES]) for w in range(chunks - 1)],
                    axis=0,
                )
                right = right_terms(done)
                ready = work[slot][stop : stop + PANEL, stop:] - product(left[:PANEL], right)
                spread_out(slot, ready)
                terms.append((left, right))
            for slot in range(slots):
                left, right = terms[slot]
                work[slot][stop + PANEL :, stop:] -= product(left[PANEL:], right)

    share = order // ranges
    row = lax.broadcasted_iota(jnp.int32, (share, order), 0)
    col = lax.broadcasted_iota(jnp.int32, (share, order), 1)
    for shift, out_ref in enumerate(out_refs):
        lead = pl.multiple_of(lax.rem(index_ref[1] + shift, ranges) * share, math.gcd(share, 16))
        upper = col >= row + lead
        for slot in range(slots):
            piece = work[slot][pl.ds(lead, share), :]
            out_ref[slot] = jnp.where(upper, piece, 0.0).astype(out_ref.dtype)


def factor_slots(beams, pivots, index, first, slots, share_slots, pack, count_rows):
    ranges, _, order, _ = beams.shape
    height = -(-slots // 8) * 8
    return pl.pallas_call(
        functools.partial(
            factor_kernel,
            first=first,
            share_slots=share_slots,
            ranges=ranges,
            pack=pack,
            count_rows=count_rows,
        ),
        out_shape=[jax.ShapeDtypeStruct((slots, order // ranges, order), BF16)] * ranges,
        in_specs=[pl.BlockSpec(memory_space=pltpu.SMEM)]
        + [pl.BlockSpec(memory_space=pltpu.VMEM)] * 2,
        out_specs=[pl.BlockSpec(memory_space=pltpu.VMEM)] * ranges,
        scratch_shapes=[pltpu.VMEM((order // LANES, PANEL * height, LANES), F32)] * 2
        + [pltpu.VMEM((order, order), F32) for _ in range(slots)]
        + [pltpu.VMEM((LANES, 3 * PANEL), F32) for _ in range(slots)]
        + [pltpu.VMEM((3 * PANEL, order), BF16) for _ in range(slots)],
        compiler_params=SMALL_PARAMS,
        cost_estimate=pl.CostEstimate(
            flops=slots * order**3,
            bytes_accessed=beams.size * 2,
            transcendentals=0,
        ),
        name="factor_slots",
    )(index, pivots, beams)


def place_kernel(index_ref, *refs, first, share_slots, ranges):
    in_refs, out_ref = refs[:ranges], refs[-1]
    slots = out_ref.shape[0]
    steps = in_refs[0].shape[0] // slots
    step = pl.program_id(0)
    shift, place = step // steps, step % steps
    block = lax.rem(index_ref[1] + ranges - shift, ranges)
    lead = block * share_slots + first + place * slots
    for this, ref in enumerate(in_refs):

        @pl.when(shift == this)
        def _(ref=ref):
            for i in range(slots):
                keep = lead + i < owner_count(index_ref, index_ref[0])
                keep = jnp.broadcast_to(keep, out_ref.shape[1:])
                out_ref[i] = jnp.where(keep, ref[place * slots + i].astype(F32), 0.0)


def place_rows(index, arrays, first, share_slots, earlier):
    ranges = len(arrays)
    count = arrays[0].shape[0]
    slots = math.gcd(math.gcd(count, first), share_slots)
    steps = count // slots

    def out_index(step, index_ref):
        block = lax.rem(index_ref[1] + ranges - step // steps, ranges)
        return ((block * share_slots + first) // slots + step % steps, 0, 0)

    return pl.pallas_call(
        functools.partial(place_kernel, first=first, share_slots=share_slots, ranges=ranges),
        out_shape=jax.ShapeDtypeStruct((ranges * share_slots,) + arrays[0].shape[1:], F32),
        grid_spec=pltpu.PrefetchScalarGridSpec(
            num_scalar_prefetch=1,
            grid=(ranges * steps,),
            in_specs=[pl.BlockSpec(memory_space=pltpu.VMEM)] * ranges
            + [pl.BlockSpec(memory_space=pl.ANY)] * len(earlier),
            out_specs=pl.BlockSpec((slots,) + arrays[0].shape[1:], out_index),
        ),
        input_output_aliases={1 + ranges: 0} if earlier else {},
        compiler_params=SMALL_PARAMS,
        name="place_rows",
    )(index, *arrays, *earlier)


def slot_parts(share_slots, pack):
    head = share_slots - pack
    return [(0, head), (head, pack)] if head > 0 else [(0, share_slots)]


def local(raw_echo, replica, beam_weights, pivots, owner_counts, train_gates):
    ch_local = raw_echo.shape[1]
    gate_rows = raw_echo.shape[2]
    pulse_count = raw_echo.shape[3]
    tap_count = replica.shape[1]
    train_local = train_gates.shape[1]
    owners = lax.axis_size("dop")
    ranges = lax.axis_size("rng")
    most_slots = 2 * (pulse_count // owners)
    share_slots = most_slots // ranges
    pack = max(1, min(LANES // train_local, share_slots))

    chunks = max(1, min(4, ch_local // 16))
    chunk_rows = ch_local // chunks
    rim = -(-(tap_count - 1) // 16) * 16
    filters = filter_rows(replica, gate_rows)
    table = doppler_table(pulse_count)
    following = [shifted(rim_rows(raw_echo, rim, c, chunks), "rng", -1) for c in range(chunks)]
    spectra = [
        form_spectrum(filters, table, raw_echo, following[c], c, chunks) for c in range(chunks)
    ]

    starts = jnp.cumsum(owner_counts, dtype=jnp.int32) - owner_counts
    places = jnp.stack([lax.axis_index("dop"), lax.axis_index("rng")]).astype(jnp.int32)
    index = jnp.concatenate([places, owner_counts, starts])
    local_gates = train_gates % gate_rows
    gates = jnp.concatenate([local_gates + part * gate_rows for part in range(pack)], axis=1)
    count_rows = float(train_local * ranges)

    parts = slot_parts(share_slots, pack)
    outgoing, tokens = [], []
    for first, count in parts:
        earlier = [beam_weights] if first > 0 else []
        array, token = select_gates(
            spectra, index, gates, first, count, share_slots, owners, ranges, pack, earlier
        )
        outgoing.append(array)
        tokens.append(token)
    axes = ("dop", "rng")
    sent = [
        lax.all_to_all(
            array.reshape(owners * ranges, -1, *array.shape[2:]),
            axes,
            split_axis=0,
            concat_axis=0,
            tiled=True,
        ).reshape(owners, ranges, -1, *array.shape[2:])
        for array in outgoing
    ]
    result, earlier = [], tokens[1:]
    for (first, count), arrived in zip(parts, sent):
        beams = form_beams(arrived, beam_weights, earlier)
        factors = factor_slots(beams, pivots, index, first, count, share_slots, pack, count_rows)
        earlier = factors[:1]
        rows = exchange(factors, "rng")
        result = [place_rows(index, rows, first, share_slots, result)]
    return result[0]


def solution(mesh):
    return jax.shard_map(
        local,
        mesh=mesh,
        in_specs=(P(None, "dop", "rng", None), P(), P(), P(), P(), P(None, "rng")),
        out_specs=P("dop", "rng", None),
        check_vma=False,
    )
```
